128 devices in a mesh: dp: 64 (over y_lo, x, z, core), seq: 2 (over y_hi).
Axes of the slice: x: 4, y: 4 (y_hi: 2, y_lo: 2; y = y_hi * 2 + y_lo), z: 4, core: 2. Of those that a mesh axis runs over, the one named last changes fastest.
Arguments:
- tokens: bfloat16 [3, 64, 512, 768], P(None, 'dp', 'seq'), may hold values from -6 to 6
- lengths: int32 [3, 64], P(None, 'dp'), may hold values from 257 to 512, as said below
- cotangent: bfloat16 [3, 64, 512, 768], P(None, 'dp', 'seq'), may hold values from -6 to 6
- w_qkv: bfloat16 [768, 2304], P(('dp', 'seq')), may hold values from -0.21875 to 0.21875
- b_qv: bfloat16 [1536], P(('dp', 'seq')), may hold values from -3 to 3
- w_out: bfloat16 [768, 768], P(('dp', 'seq')), may hold values from -0.875 to 0.875
- b_out: bfloat16 [768], P(('dp', 'seq')), may hold values from -2 to 2
- w_in: bfloat16 [768, 3072], P(('dp', 'seq')), may hold values from -0.21875 to 0.21875
- b_in: bfloat16 [3072], P(('dp', 'seq')), may hold values from -2 to 2
- w_back: bfloat16 [3072, 768], P(('dp', 'seq')), may hold values from -0.109375 to 0.109375
- b_back: bfloat16 [768], P(('dp', 'seq')), may hold values from -2 to 2
- gain_one: bfloat16 [768], P(('dp', 'seq')), may hold values from 0.5 to 1.5
- shift_one: bfloat16 [768], P(('dp', 'seq')), may hold values from -2 to 2
- gain_two: bfloat16 [768], P(('dp', 'seq')), may hold values from 0.5 to 1.5
- shift_two: bfloat16 [768], P(('dp', 'seq')), may hold values from -2 to 2
Outputs:
- block_out: bfloat16 [3, 64, 512, 768], P(None, 'dp', 'seq')
- tokens_grad: float32 [3, 64, 512, 768], P(None, 'dp', 'seq')
- grad_qkv: float32 [768, 2304], P(('dp', 'seq'))
- grad_qv_bias: float32 [1536], P(('dp', 'seq'))
- grad_out: float32 [768, 768], P(('dp', 'seq'))
- grad_out_bias: float32 [768], P(('dp', 'seq'))
- grad_in: float32 [768, 3072], P(('dp', 'seq'))
- grad_in_bias: float32 [3072], P(('dp', 'seq'))
- grad_back: float32 [3072, 768], P(('dp', 'seq'))
- grad_back_bias: float32 [768], P(('dp', 'seq'))
- grad_gain_one: float32 [768], P(('dp', 'seq'))
- grad_shift_one: float32 [768], P(('dp', 'seq'))
- grad_gain_two: float32 [768], P(('dp', 'seq'))
- grad_shift_two: float32 [768], P(('dp', 'seq'))
The draws below stay inside these ranges and needn't reach their ends.
Inputs may be any that keep to these rules, and one draw needn't show every extreme that they name: `lengths`: tokens of a pair at positions from its length on are padding; no query attends to them.
All inputs are finite; a program needn't handle non-finite values.
Results may differ from the reference program's by a relative error of at most 0.014.
Values may be sent and summed in bfloat16 or wider, within the bound.
No kernel may reach another device: no remote copies, remote signals or barrier semaphores. Data moves between devices by JAX's collectives and lax.ppermute only.
A program may use at most 192 MiB of HBM per device.

```python
import jax
import jax.numpy as jnp
from jax import lax

D = 768
HD = 64
FF = 3072
SEQ = 512
MICRO = 3
SPAN = 256
PAIRS_MB = 64


def draw_lengths(key, part):
    key = jax.random.fold_in(key, 7)
    valid = jax.random.randint(key, (MICRO, PAIRS_MB), SEQ - SPAN + 1, SEQ + 1)
    valid = valid.at[0, 0].set(SEQ)
    valid = valid.at[MICRO - 1, PAIRS_MB - 1].set(SEQ - SPAN + 1)
    return valid.astype(jnp.int32)


def level_of(rng, shape, shards, smallest, largest):
    level, own = 1.0, jax.random.fold_in(rng, 6)
    for dim, parts in shards:
        draws = jnp.exp(jax.random.uniform(jax.random.fold_in(own, dim), (parts,), jnp.float32, smallest / len(shards), largest / len(shards)))
        level = level * jnp.repeat(draws, shape[dim] // parts).reshape([-1 if axis == dim else 1 for axis in range(len(shape))])
    return level


def normal_values(rng, extent, scale, limit, cuts=(), kind=jnp.bfloat16):
    array = scale * jax.random.normal(rng, extent, jnp.float32)
    if cuts:
        array = array * level_of(rng, extent, cuts, -0.22, 0.18)
    return jnp.clip(array, -limit, limit).astype(kind)


def setup_inputs(seed: int = 0) -> dict:
    seeds = jax.random.split(jax.random.key(seed), 16)
    tokens = normal_values(seeds[0], (MICRO, PAIRS_MB, SEQ, D), 1.0, 6.0, ((1, 64), (2, 2)))
    lengths = draw_lengths(jax.random.fold_in(seeds[15], 71), 0)
    cotangent = normal_values(seeds[2], (MICRO, PAIRS_MB, SEQ, D), 1.0, 6.0, ((1, 64), (2, 2)))
    w_qkv = normal_values(seeds[3], (D, 3 * D), D ** -0.5, 0.21875, ((0, 128),))
    b_qv = normal_values(seeds[4], (2 * D,), 0.5, 3.0, ((0, 128),))
    w_out = normal_values(seeds[5], (D, D), (D // 16) ** -0.5, 0.875, ((0, 128),))
    b_out = normal_values(seeds[6], (D,), 0.3, 2.0, ((0, 128),))
    w_in = normal_values(seeds[7], (D, FF), D ** -0.5, 0.21875, ((0, 128),))
    b_in = normal_values(seeds[8], (FF,), 0.3, 2.0, ((0, 128),))
    w_back = normal_values(seeds[9], (FF, D), FF ** -0.5, 0.109375, ((0, 128),))
    b_back = normal_values(seeds[10], (D,), 0.3, 2.0, ((0, 128),))
    gain_one = jnp.clip(1.0 + 0.1 * jax.random.normal(seeds[11], (D,), jnp.float32), 0.5, 1.5).astype(jnp.bfloat16)
    shift_one = normal_values(seeds[12], (D,), 0.3, 2.0, ((0, 128),))
    gain_two = jnp.clip(1.0 + 0.1 * jax.random.normal(seeds[13], (D,), jnp.float32), 0.5, 1.5).astype(jnp.bfloat16)
    shift_two = normal_values(seeds[14], (D,), 0.3, 2.0, ((0, 128),))
    return dict(tokens=tokens, lengths=lengths, cotangent=cotangent, w_qkv=w_qkv, b_qv=b_qv, w_out=w_out, b_out=b_out, w_in=w_in, b_in=b_in, w_back=w_back, b_back=b_back, gain_one=gain_one, shift_one=shift_one, gain_two=gain_two, shift_two=shift_two)


@jax.custom_vjp
def low(v):
    return lax.optimization_barrier(v.astype(jnp.bfloat16)).astype(jnp.float32)

@jax.custom_vjp
def low_back(v):
    return v

def low_keep(v):
    return (low(v), None)

def low_pass(kept, grad):
    return (grad,)

def back_keep(v):
    return (v, None)

def back_low(kept, grad):
    return (low(grad),)
low.defvjp(low_keep, low_pass)
low_back.defvjp(back_keep, back_low)
epsilon = 1e-05
highest = lax.Precision.HIGHEST

def layer_norm(value, gain, shift):
    centre = value - lax.optimization_barrier(jnp.mean(value, axis=-1, keepdims=True))
    spread = lax.optimization_barrier(jnp.mean(centre * centre, axis=-1, keepdims=True))
    return centre * lax.rsqrt(spread + epsilon) * gain + shift

def project(value, weight):
    return jnp.einsum('bsd,de->bse', value, weight, precision=highest)

def block_forward(tokens, w_qkv, b_qv, w_out, b_out, w_in, b_in, w_back, b_back, gain_one, shift_one, gain_two, shift_two, valid):
    batch, length, width = tokens.shape
    heads = width // HD
    middle = jnp.zeros((width,), jnp.float32)
    bias_all = jnp.concatenate([b_qv[:width], middle, b_qv[width:]])
    mixed = low(low_back(project(tokens, w_qkv) + bias_all))
    queries = mixed[..., :width].reshape(batch, length, heads, HD)
    keys = mixed[..., width:2 * width].reshape(batch, length, heads, HD)
    values = mixed[..., 2 * width:].reshape(batch, length, heads, HD)
    scores = jnp.einsum('bqhe,bkhe->bhqk', queries, keys, precision=highest) * (1.0 / HD ** 0.5)
    scores = low_back(scores)
    position = jnp.arange(length, dtype=jnp.int32)
    visible = position[None, None, None, :] < valid[:, None, None, None]
    scores = jnp.where(visible, scores, -1e+30)
    probs = low(jax.nn.softmax(scores, axis=-1))
    context = jnp.einsum('bhqk,bkhe->bqhe', probs, values, precision=highest).reshape(batch, length, width)
    context = low(low_back(context))
    branch = low_back(project(context, w_out) + b_out)
    normed = layer_norm(tokens + branch, gain_one, shift_one)
    inner = low_back(project(low(normed), w_in) + b_in)
    active = low(jax.nn.gelu(inner, approximate=False))
    outer = low_back(project(active, w_back) + b_back)
    return layer_norm(normed + outer, gain_two, shift_two)

def reference(tokens, lengths, cotangent, w_qkv, b_qv, w_out, b_out, w_in, b_in, w_back, b_back, gain_one, shift_one, gain_two, shift_two):
    total_seqs = MICRO * PAIRS_MB
    per_step = max((divisor for divisor in range(1, 9) if total_seqs % divisor == 0))
    step_count = total_seqs // per_step
    inputs = tokens.astype(jnp.float32).reshape(step_count, per_step, SEQ, D)
    grads_in = cotangent.astype(jnp.float32).reshape(step_count, per_step, SEQ, D)
    valid_all = lengths.astype(jnp.int32).reshape(step_count, per_step)
    params = (w_qkv.astype(jnp.float32), b_qv.astype(jnp.float32), w_out.astype(jnp.float32), b_out.astype(jnp.float32), w_in.astype(jnp.float32), b_in.astype(jnp.float32), w_back.astype(jnp.float32), b_back.astype(jnp.float32), gain_one.astype(jnp.float32), shift_one.astype(jnp.float32), gain_two.astype(jnp.float32), shift_two.astype(jnp.float32))

    def one_step(totals, items):
        block_tokens, block_valid, block_cot = items

        def wrapped(inputs_here, *weights):
            return block_forward(inputs_here, *weights, block_valid)
        output, pullback = jax.vjp(wrapped, block_tokens, *params)
        grads = pullback(block_cot)
        totals = tuple((running + fresh for running, fresh in zip(totals, grads[1:])))
        return (totals, (output.astype(jnp.bfloat16), grads[0]))
    start = tuple((jnp.zeros_like(weight) for weight in params))
    totals, (outputs, input_grads) = lax.scan(one_step, start, (inputs, valid_all, grads_in))
    outputs = outputs.reshape(MICRO, PAIRS_MB, SEQ, D)
    input_grads = input_grads.reshape(MICRO, PAIRS_MB, SEQ, D)
    return (outputs, input_grads, totals[0], totals[1], totals[2], totals[3], totals[4], totals[5], totals[6], totals[7], totals[8], totals[9], totals[10], totals[11])
```

```python
import jax
import jax.numpy as jnp
from jax import lax
from jax.experimental import pallas as pl
from jax.experimental.pallas import tpu as pltpu
from jax.sharding import Mesh, PartitionSpec as P

HD = 64
EPS = 1e-05
F32 = jnp.float32
BF = jnp.bfloat16
DEVICES = ("yl", "x", "z", "c", "yh")
SWAP = ((0, 1), (1, 0))
STEPS = (0, 1, 3, 2)
V_OUT, V_BACK, V_GAIN1, V_SHIFT1, V_GAIN2, V_SHIFT2, V_IN, V_QV = 0, 1, 2, 3, 4, 5, 6, 10


def mm(a, b):
    return lax.dot_general(a, b, (((1,), (0,)), ((), ())), preferred_element_type=F32)


def mm_nt(a, b):
    return lax.dot_general(a, b, (((1,), (1,)), ((), ())), preferred_element_type=F32)


def mm_tn(a, b):
    return lax.dot_general(a, b, (((0,), (0,)), ((), ())), preferred_element_type=F32)


def vmem(mib, flops=0, moved=0):
    return dict(
        compiler_params=pltpu.CompilerParams(vmem_limit_bytes=mib << 20),
        cost_estimate=pl.CostEstimate(flops=flops, bytes_accessed=moved, transcendentals=0),
    )


def gather_ring(block, axis):
    parts = [block]
    for step in STEPS[1:]:
        parts.append(lax.ppermute(block, axis, [(j, (j - step) % 4) for j in range(4)]))
    return jnp.concatenate(parts, axis=0)


def column_pairs(flip_c, flip_y):
    pairs = []
    for a in (0, 1):
        for b in (0, 1):
            for d in (0, 1):
                pairs.append((b * 4 + (a ^ flip_c) * 2 + (d ^ flip_y), a * 4 + b * 2 + d))
    return pairs


FLIPS = ((0, 0), (0, 1), (1, 0), (1, 1))


def gather_column(shard):
    parts = [lax.ppermute(shard, ("yl", "c", "yh"), column_pairs(*flip)) for flip in FLIPS]
    return jnp.concatenate(parts, axis=0)


def arrival(first):
    yl, x, z, c, yh = (lax.axis_index(name) for name in DEVICES)
    j = jnp.arange(768)
    half, r = j // 384, j % 384
    steps = jnp.array(STEPS)
    last, early, flip = steps[r // 96], steps[(r % 96) // 24], (r % 24) // 6
    if first == "z":
        zz, xx = (z + early) % 4, (x + last) % 4
    else:
        xx, zz = (x + early) % 4, (z + last) % 4
    row = (c ^ half) * 384 + xx * 96 + zz * 24 + (yl ^ (flip // 2)) * 12 + (yh ^ (flip % 2)) * 6 + r % 6
    return (jnp.arange(768)[:, None] == row[None, :]).astype(BF)


def gather_xz(block, first):
    block = gather_ring(block, first)
    block = gather_ring(block, "x" if first == "z" else "z")
    both = jnp.concatenate([block, lax.ppermute(block, "c", SWAP)], axis=0)
    return mm(arrival(first), both).astype(BF)


def scatter_pieces(parts, axis, dim):
    me = lax.axis_index(axis)

    def piece(step):
        return sum(
            lax.dynamic_index_in_dim(part, (me + step) % 4, dim, keepdims=False).astype(F32)
            for part in parts
        )

    return tuple(piece(step).astype(BF) for step in STEPS[1:]), piece(0)


def scatter_ring(pieces, axis):
    sent, _ = pieces
    return tuple(
        lax.ppermute(out, axis, [(j, (j + step) % 4) for j in range(4)])
        for step, out in zip(STEPS[1:], sent)
    )


def first_pieces(mine, away, first):
    recv = lax.ppermute(away, "c", SWAP)
    shape = (4, 4, mine.shape[0] // 16, mine.shape[1])
    return scatter_pieces((mine.reshape(shape), recv.reshape(shape)), first, 0 if first == "x" else 1)


def second_pieces(pieces, received, first):
    total = pieces[1]
    for part in received:
        total += part.astype(F32)
    return scatter_pieces((total,), "z" if first == "x" else "x", 0)


def ring_sum(pieces, received):
    total = pieces[1]
    for part in received:
        total += part.astype(F32)
    return total


def scatter_column(block):
    yl, yh = lax.axis_index("yl"), lax.axis_index("yh")
    blocks = block.reshape((2, 2, block.shape[0] // 4) + block.shape[1:])
    total = None
    for flip_c, flip_y in FLIPS:
        pairs = [(user, owner) for owner, user in column_pairs(flip_c, flip_y)]
        out = lax.dynamic_slice(
            blocks, (yl ^ flip_c, yh ^ flip_y, 0, 0), (1, 1) + blocks.shape[2:]
        )[0, 0]
        part = lax.ppermute(out, ("yl", "c", "yh"), pairs)
        total = part if total is None else total + part
    return total


def attend_kernel(limits, x_own, x_oth, w_qkv, bias, own, oth, context, probs):
    g = pl.program_id(0)
    span, width = context.shape
    lane = lax.broadcasted_iota(jnp.int32, (span, 128), 1)
    key = lax.broadcasted_iota(jnp.int32, (span, span), 0)
    see_own = key < limits[g, 0]
    see_oth = key < limits[g, 1]
    for j in range(3):
        at = pl.ds(j * width, width)
        own[:, at] = (mm(x_own[...], w_qkv[:, at]) + bias[:, at]).astype(BF)
        if j:
            oth[:, pl.ds((j - 1) * width, width)] = (
                mm(x_oth[...], w_qkv[:, at]) + bias[:, at]
            ).astype(BF)

    def pair(p, carry):
        at = pl.multiple_of(p * 128, 128)
        q = own[:, pl.ds(at, 128)] * jnp.asarray(0.125, BF)
        k_own = own[:, pl.ds(at + width, 128)]
        k_oth = oth[:, pl.ds(at, 128)]
        v = jnp.concatenate(
            [own[:, pl.ds(at + 2 * width, 128)], oth[:, pl.ds(at + width, 128)]], axis=0
        )
        v_t = v.T
        outs = []
        for h in (0, 1):
            q_h = jnp.where((lane >= 64) == (h == 1), q, jnp.zeros_like(q))
            s_own = jnp.where(see_own, mm_nt(k_own, q_h), -1e30)
            s_oth = jnp.where(see_oth, mm_nt(k_oth, q_h), -1e30)
            peak = jnp.maximum(
                jnp.max(s_own, axis=0, keepdims=True), jnp.max(s_oth, axis=0, keepdims=True)
            )
            e_own = jnp.exp(s_own - peak)
            e_oth = jnp.exp(s_oth - peak)
            scale = 1.0 / (
                jnp.sum(e_own, axis=0, keepdims=True) + jnp.sum(e_oth, axis=0, keepdims=True)
            )
            p_t = jnp.concatenate([(e_own * scale).astype(BF), (e_oth * scale).astype(BF)], axis=0)
            probs[2 * p + h] = p_t
            outs.append(mm(v_t[h * HD : (h + 1) * HD], p_t))
        context[:, pl.ds(at, 128)] = jnp.concatenate(outs, axis=0).T.astype(BF)
        return carry

    lax.fori_loop(0, width // 128, pair, 0)


def attend(limits, x_own, x_oth, w_qkv, bias):
    micro = limits.shape[0]
    rows, width = x_own.shape
    span, heads = rows // micro, width // HD

    def block(n):
        return pl.BlockSpec((span, n), lambda g, *_: (g, 0))

    def whole(*shape):
        return pl.BlockSpec(shape, lambda g, *_: (0,) * len(shape))

    return pl.pallas_call(
        attend_kernel,
        grid_spec=pltpu.PrefetchScalarGridSpec(
            num_scalar_prefetch=1,
            grid=(micro,),
            in_specs=[block(width), block(width), whole(width, 3 * width), whole(1, 3 * width)],
            out_specs=[
                block(3 * width),
                block(2 * width),
                block(width),
                pl.BlockSpec((None, heads, 2 * span, span), lambda g, *_: (g, 0, 0, 0)),
            ],
        ),
        out_shape=[
            jax.ShapeDtypeStruct((rows, 3 * width), BF),
            jax.ShapeDtypeStruct((rows, 2 * width), BF),
            jax.ShapeDtypeStruct((rows, width), BF),
            jax.ShapeDtypeStruct((micro, heads, 2 * span, span), BF),
        ],
        name="attend",
        **vmem(60, 28 << 30, 20 << 20),
    )(limits, x_own, x_oth, w_qkv, bias)


def attend_back_kernel(own, oth, probs, d_context, w_qkv, *rest):
    d_own, d_oth, x_part = rest[-3:]
    span, width = d_context.shape
    lane = lax.broadcasted_iota(jnp.int32, (span, 128), 1)
    lane2 = lax.broadcasted_iota(jnp.int32, (2 * span, 128), 1)

    def pair(p, carry):
        at = pl.multiple_of(p * 128, 128)
        q = own[:, pl.ds(at, 128)]
        k = jnp.concatenate([own[:, pl.ds(at + width, 128)], oth[:, pl.ds(at, 128)]], axis=0)
        v = jnp.concatenate(
            [own[:, pl.ds(at + 2 * width, 128)], oth[:, pl.ds(at + width, 128)]], axis=0
        )
        k_t = k.T
        d_c = d_context[:, pl.ds(at, 128)]
        d_q, d_k, d_v = [], [], []
        for h in (0, 1):
            d_h = jnp.where((lane >= 64) == (h == 1), d_c, jnp.zeros_like(d_c))
            p_b = probs[2 * p + h]
            p_f = p_b.astype(F32)
            d_p = mm_nt(v, d_h)
            weighted = jnp.sum(p_f * d_p, axis=0, keepdims=True)
            d_s = (p_f * (d_p - weighted)).astype(BF)
            d_q.append(mm(k_t[h * HD : (h + 1) * HD], d_s))
            d_k.append(mm(d_s, q))
            d_v.append(mm(p_b, d_c))
        d_own[:, pl.ds(at, 128)] = (jnp.concatenate(d_q, axis=0).T * 0.125).astype(BF)
        d_k = (jnp.where(lane2 < HD, d_k[0], d_k[1]) * 0.125).astype(BF)
        d_v = jnp.where(lane2 < HD, d_v[0], d_v[1]).astype(BF)
        d_own[:, pl.ds(at + width, 128)] = d_k[:span]
        d_own[:, pl.ds(at + 2 * width, 128)] = d_v[:span]
        d_oth[:, pl.ds(at, 128)] = d_k[span:]
        d_oth[:, pl.ds(at + width, 128)] = d_v[span:]
        return carry

    lax.fori_loop(0, width // 128, pair, 0)
    x_part[...] = (
        mm_nt(d_oth[:, :width], w_qkv[:, width : 2 * width])
        + mm_nt(d_oth[:, width:], w_qkv[:, 2 * width :])
    ).astype(BF)


def attend_back(own, oth, probs, d_context, w_qkv, after):
    micro, heads, _, span = probs.shape
    rows, width = d_context.shape

    def block(n):
        return pl.BlockSpec((span, n), lambda g: (g, 0))

    return pl.pallas_call(
        attend_back_kernel,
        grid=(micro,),
        in_specs=[
            block(3 * width),
            block(2 * width),
            pl.BlockSpec((None, heads, 2 * span, span), lambda g: (g, 0, 0, 0)),
            block(width),
            pl.BlockSpec((width, 3 * width), lambda g: (0, 0)),
        ]
        + [pl.BlockSpec(memory_space=pl.ANY)] * len(after),
        out_specs=[block(3 * width), block(2 * width), block(width)],
        out_shape=[
            jax.ShapeDtypeStruct((rows, 3 * width), BF),
            jax.ShapeDtypeStruct((rows, 2 * width), BF),
            jax.ShapeDtypeStruct((rows, width), BF),
        ],
        name="attend_back",
        **vmem(60, 28 << 30, 20 << 20),
    )(own, oth, probs, d_context, w_qkv, *after)


def norm_parts(value):
    centre = value - jnp.mean(value, axis=-1, keepdims=True)
    inverse = lax.rsqrt(jnp.mean(centre * centre, axis=-1, keepdims=True) + EPS)
    return centre * inverse, inverse


def norm_back(grad, hat, inverse, gain):
    scaled = grad * gain
    return inverse * (
        scaled
        - jnp.mean(scaled, axis=-1, keepdims=True)
        - hat * jnp.mean(scaled * hat, axis=-1, keepdims=True)
    )


def rows_of(*terms):
    return jnp.concatenate(terms + (jnp.zeros((8 - len(terms), terms[0].shape[1]), F32),), axis=0)


def middle_kernel(
    core, x, context, cot, w_out, vec, b_in, w_in, w_back,
    block_out, in_mine, in_away, back_mine, back_away, d_normed, hat_one, inv_one, sums, in_sums,
    normed, normed_b, outer, active, slope, d_outer,
):
    phase, l = pl.program_id(0), pl.program_id(1)
    rows, width = x.shape
    half = width // 2
    mine, away = pl.multiple_of(core[0] * half, half), pl.multiple_of((1 - core[0]) * half, half)
    step = 256

    def row(i):
        return vec[i : i + 1, :]

    @pl.when((phase == 0) & (l == 0))
    def _():
        for r in range(0, rows, step):
            at = pl.ds(r, step)
            hat, inverse = norm_parts(x[at].astype(F32) + mm(context[at], w_out[...]) + row(V_OUT))
            hat_one[at] = hat
            inv_one[at] = jnp.broadcast_to(inverse, (step, 128))
            value = hat * row(V_GAIN1) + row(V_SHIFT1)
            normed[at] = value
            normed_b[at] = value.astype(BF)
            outer[at] = value + row(V_BACK)

    @pl.when(phase == 0)
    def _():
        for r in range(0, rows, step):
            at = pl.ds(r, step)
            inner = mm(normed_b[at], w_in[...]) + b_in[0]
            phi = 0.5 + 0.5 * lax.erf(inner * (0.5**0.5))
            act = (inner * phi).astype(BF)
            active[l, at] = act
            slope[l, at] = phi + inner * jnp.exp(-0.5 * inner * inner) * 0.3989422804014327
            outer[at] += mm(act, w_back[...])

    @pl.when((phase == 1) & (l == 0))
    def _():
        total = [jnp.zeros((1, width), F32) for _ in range(3)]
        for r in range(0, rows, step):
            at = pl.ds(r, step)
            hat, inverse = norm_parts(outer[at])
            block_out[at] = (hat * row(V_GAIN2) + row(V_SHIFT2)).astype(BF)
            grad = cot[at].astype(F32)
            d_second = norm_back(grad, hat, inverse, row(V_GAIN2))
            d_b = d_second.astype(BF)
            d_outer[at] = d_b
            d_normed[at] = d_second
            for i, term in enumerate((d_b.astype(F32), grad * hat, grad)):
                total[i] += jnp.sum(term, axis=0, keepdims=True)
        sums[...] = rows_of(*total)

    @pl.when(phase == 1)
    def _():
        pieces = []
        bias = jnp.zeros((1, width), F32)
        for r in range(0, rows, step):
            at = pl.ds(r, step)
            d_inner = (mm_nt(d_outer[at], w_back[...]) * slope[l, at]).astype(BF)
            pieces.append(d_inner)
            bias += jnp.sum(d_inner.astype(F32), axis=0, keepdims=True)
            d_normed[at] += mm_nt(d_inner, w_in[...])
        d_inner = jnp.concatenate(pieces, axis=0)
        in_sums[0] = bias
        for start, into_in, into_back in ((mine, in_mine, back_mine), (away, in_away, back_away)):
            cols = pl.ds(start, half)
            into_back[...] = mm_tn(active[l, :, cols], d_outer[...]).astype(BF)
            into_in[...] = mm_tn(normed_b[:, cols], d_inner).astype(BF)


def middle(core, x, context, cot, w_out, vec, b_in, w_in, w_back):
    rows, width = x.shape
    parts = w_in.shape[1] // width
    half = width // 2

    def whole(*shape):
        return pl.BlockSpec(shape, lambda p, l, *_: (0,) * len(shape))

    chunk = pl.BlockSpec((width, width), lambda p, l, *_: (0, l))
    late = pl.BlockSpec((half, width), lambda p, l, *_: (0, p * l))
    grads = ((half, parts * width), BF)
    return pl.pallas_call(
        middle_kernel,
        grid_spec=pltpu.PrefetchScalarGridSpec(
            num_scalar_prefetch=1,
            grid=(2, parts),
            in_specs=[whole(rows, width)] * 3
            + [
                whole(width, width),
                whole(16, width),
                pl.BlockSpec((1, 1, width), lambda p, l, *_: (l, 0, 0)),
                chunk,
                chunk,
            ],
            out_specs=[whole(rows, width), late, late, late, late, whole(rows, width)]
            + [whole(rows, width), whole(rows, 128), whole(8, width)]
            + [pl.BlockSpec((1, 1, width), lambda p, l, *_: (p * l, 0, 0))],
            scratch_shapes=[
                pltpu.VMEM((rows, width), F32),
                pltpu.VMEM((rows, width), BF),
                pltpu.VMEM((rows, width), F32),
                pltpu.VMEM((parts, rows, width), BF),
                pltpu.VMEM((parts, rows, width), F32),
                pltpu.VMEM((rows, width), BF),
            ],
        ),
        out_shape=[
            jax.ShapeDtypeStruct(shape, kind)
            for shape, kind in (
                ((rows, width), BF), grads, grads, grads, grads, ((rows, width), F32),
                ((rows, width), F32), ((rows, 128), F32), ((8, width), F32), ((parts, 1, width), F32),
            )
        ],
        name="middle",
        **vmem(62, 40 << 30, 40 << 20),
    )(core, x, context, cot, w_out, vec, b_in, w_in, w_back)


def branch_back_kernel(
    core, d_normed, hat_one, inv_one, context, w_out, vec, d_first, d_context, mine, away, sums, d_branch
):
    rows, width = d_normed.shape
    half = width // 2
    step = 256
    total = [jnp.zeros((1, width), F32) for _ in range(3)]
    for r in range(0, rows, step):
        at = pl.ds(r, step)
        grad, hat = d_normed[at], hat_one[at]
        back = norm_back(grad, hat, inv_one[at, 0:1], vec[V_GAIN1 : V_GAIN1 + 1, :])
        d_first[at] = back
        d_b = back.astype(BF)
        d_branch[at] = d_b
        for i, term in enumerate((d_b.astype(F32), grad * hat, grad)):
            total[i] += jnp.sum(term, axis=0, keepdims=True)
        d_context[at] = mm_nt(d_b, w_out[...]).astype(BF)
    sums[...] = rows_of(*total)
    for start, out in ((core[0] * half, mine), ((1 - core[0]) * half, away)):
        out[...] = mm_tn(context[:, pl.ds(pl.multiple_of(start, half), half)], d_branch[...]).astype(BF)


def branch_back(core, d_normed, hat_one, inv_one, context, w_out, vec):
    rows, width = d_normed.shape
    shapes = (
        ((rows, width), F32), ((rows, width), BF), ((width // 2, width), BF), ((width // 2, width), BF),
        ((8, width), F32),
    )
    return pl.pallas_call(
        branch_back_kernel,
        in_specs=[pl.BlockSpec(memory_space=pltpu.SMEM)]
        + [pl.BlockSpec(memory_space=pltpu.VMEM)] * 6,
        out_specs=[pl.BlockSpec(memory_space=pltpu.VMEM)] * 5,
        out_shape=[jax.ShapeDtypeStruct(*shape) for shape in shapes],
        scratch_shapes=[pltpu.VMEM((rows, width), BF)],
        name="branch_back",
        **vmem(60, 2 << 30, 12 << 20),
    )(core, d_normed, hat_one, inv_one, context, w_out, vec)


def mixed_back_kernel(core, x_own, x_oth, d_own, d_oth, w_qkv, d_first, *rest):
    mine, away, d_tokens, sums = rest[-4:]
    j = pl.program_id(0)
    width = x_own.shape[1]
    half = width // 2

    @pl.when(j == 0)
    def _():
        d_tokens[...] = d_first[...]
        sums[...] = jnp.zeros_like(sums)

    d_tokens[...] += mm_nt(d_own[...], w_qkv[...])
    total = jnp.sum(d_own[...].astype(F32), axis=0, keepdims=True)
    far = jnp.sum(d_oth[...].astype(F32), axis=0, keepdims=True)
    place = lax.broadcasted_iota(jnp.int32, sums.shape, 0)
    sums[...] += jnp.where(place == j, total, 0.0) + jnp.where((place == j) & (j > 0), far, 0.0)
    for start, out in ((core[0] * half, mine), ((1 - core[0]) * half, away)):
        cols = pl.ds(pl.multiple_of(start, half), half)

        @pl.when(j == 0)
        def _():
            out[...] = mm_tn(x_own[:, cols], d_own[...]).astype(BF)

        @pl.when(j > 0)
        def _():
            out[...] = (
                mm_tn(x_own[:, cols], d_own[...]) + mm_tn(x_oth[:, cols], d_oth[...])
            ).astype(BF)


def mixed_back(core, x_own, x_oth, d_own, d_oth, w_qkv, d_first, after):
    rows, width = x_own.shape
    half = width // 2

    def whole(*shape):
        return pl.BlockSpec(shape, lambda j, *_: (0,) * len(shape))

    own = pl.BlockSpec((rows, width), lambda j, *_: (0, j))
    oth = pl.BlockSpec((rows, width), lambda j, *_: (0, jnp.maximum(j - 1, 0)))
    grad = pl.BlockSpec((half, width), lambda j, *_: (0, j))
    return pl.pallas_call(
        mixed_back_kernel,
        grid_spec=pltpu.PrefetchScalarGridSpec(
            num_scalar_prefetch=1,
            grid=(3,),
            in_specs=[whole(rows, width), whole(rows, width), own, oth]
            + [pl.BlockSpec((width, width), lambda j, *_: (0, j)), whole(rows, width)]
            + [pl.BlockSpec(memory_space=pl.ANY)] * len(after),
            out_specs=[grad, grad, whole(rows, width), whole(8, width)],
        ),
        out_shape=[
            jax.ShapeDtypeStruct((half, 3 * width), BF),
            jax.ShapeDtypeStruct((half, 3 * width), BF),
            jax.ShapeDtypeStruct((rows, width), F32),
            jax.ShapeDtypeStruct((8, width), F32),
        ],
        name="mixed_back",
        **vmem(60, 10 << 30, 20 << 20),
    )(core, x_own, x_oth, d_own, d_oth, w_qkv, d_first, *after)


def on_device(
    tokens, lengths, cotangent, w_qkv, b_qv, w_out, b_out, w_in, b_in, w_back, b_back,
    gain_one, shift_one, gain_two, shift_two,
):
    micro, _, span, width = tokens.shape
    ff = w_in.shape[1]
    rows = micro * span
    yh = lax.axis_index("yh")
    c = lax.axis_index("c")
    core = c.reshape(1)
    x_own = tokens.reshape(rows, width)
    x_oth = lax.ppermute(x_own, "yh", SWAP)

    vectors = jnp.concatenate(
        [v.reshape(6, -1) for v in (b_out, b_back, gain_one, shift_one, gain_two, shift_two, b_in, b_qv)]
        + [jnp.zeros((6, 116), BF)],
        axis=1,
    )
    first = gather_column(jnp.concatenate([w_qkv, vectors, w_out], axis=1))
    w_in = w_in.reshape(6, width, 4).transpose(0, 2, 1).reshape(6, ff)
    rest = gather_column(jnp.concatenate([w_in, w_back.reshape(6, ff)], axis=1))
    cut = 12 * 128
    first_a = gather_xz(first[:, :cut], "z")
    first_b = gather_xz(first[:, cut:], "x")
    w_in = gather_xz(rest[:, :ff], "z")
    w_back = gather_xz(rest[:, ff:], "x")
    w_qkv = jnp.concatenate([first_a, first_b[:, : 3 * width - cut]], axis=1)
    vec = first_b[:, 3 * width - cut : 3 * width - cut + 16].astype(F32).T
    w_out = first_b[:, 3 * width - cut + 128 :]
    b_in = vec[V_IN : V_IN + 4].reshape(4, 1, width)
    b_qv = vec[V_QV : V_QV + 2].T.reshape(1, 2 * width)
    bias_all = jnp.concatenate([b_qv[:, :width], jnp.zeros((1, width), F32), b_qv[:, width:]], axis=1)

    limits = jnp.stack([lengths[:, 0] - yh * span, lengths[:, 0] - (1 - yh) * span], axis=1)
    mixed, mixed_oth, context, probs = attend(limits, x_own, x_oth, w_qkv, bias_all)
    (
        block_out, in_mine, in_away, back_mine, back_away, d_normed, hat_one, inv_one, sums_two, in_sums
    ) = middle(core, x_own, context, cotangent.reshape(rows, width), w_out, vec, b_in, w_in, w_back)
    in_one = first_pieces(in_mine, in_away, "x")
    back_one = first_pieces(back_mine, back_away, "z")
    d_first, d_context, out_mine, out_away, sums_one = branch_back(
        core, d_normed, hat_one, inv_one, context, w_out, vec
    )
    d_own, d_oth, x_part = attend_back(
        mixed, mixed_oth, probs, d_context, w_qkv, in_one[0] + back_one[0]
    )
    x_part = lax.ppermute(x_part, "yh", SWAP)
    in_two = second_pieces(in_one, scatter_ring(in_one, "x"), "x")
    back_two = second_pieces(back_one, scatter_ring(back_one, "z"), "z")
    qkv_mine, qkv_away, d_tokens, sums_qkv = mixed_back(
        core, x_own, x_oth, d_own, d_oth, w_qkv, d_first, in_two[0] + back_two[0]
    )
    g_qv = jnp.stack([sums_qkv[0], sums_qkv[2]]).reshape(width, 2).T
    g_vectors = jnp.concatenate(
        [sums_one[0:1], sums_two[0:1], sums_one[1:3], sums_two[1:3], in_sums[:, 0], g_qv]
        + [jnp.zeros((116, width), F32)],
        axis=0,
    ).T.astype(BF).reshape(2, width // 2, 128)
    vec_mine = lax.dynamic_index_in_dim(g_vectors, c, 0, keepdims=False)
    vec_away = lax.dynamic_index_in_dim(g_vectors, 1 - c, 0, keepdims=False)
    cut_mine, cut_away = qkv_mine[:, cut:], qkv_away[:, cut:]
    a_one = first_pieces(qkv_mine[:, :cut], qkv_away[:, :cut], "x")
    b_one = first_pieces(
        jnp.concatenate([cut_mine, vec_mine, out_mine], axis=1),
        jnp.concatenate([cut_away, vec_away, out_away], axis=1),
        "z",
    )
    a_two = second_pieces(a_one, scatter_ring(a_one, "x"), "x")
    b_two = second_pieces(b_one, scatter_ring(b_one, "z"), "z")
    early = scatter_column(
        jnp.concatenate(
            [ring_sum(in_two, scatter_ring(in_two, "z")), ring_sum(back_two, scatter_ring(back_two, "x"))],
            axis=1,
        )
    )
    late = scatter_column(
        jnp.concatenate(
            [ring_sum(a_two, scatter_ring(a_two, "z")), ring_sum(b_two, scatter_ring(b_two, "x"))],
            axis=1,
        )
    )
    o_in = early[:, :ff].reshape(6, 4, width).transpose(0, 2, 1).reshape(6, ff)
    o_back = early[:, ff:].reshape(24, width)
    o_vec = late[:, 3 * width : 3 * width + 12]
    return (
        block_out.reshape(tokens.shape),
        (d_tokens + x_part.astype(F32)).reshape(tokens.shape),
        late[:, : 3 * width],
        o_vec[:, V_QV : V_QV + 2].reshape(12),
        late[:, 3 * width + 128 :],
        o_vec[:, V_OUT],
        o_in,
        o_vec[:, V_IN : V_IN + 4].reshape(24),
        o_back,
        o_vec[:, V_BACK],
        o_vec[:, V_GAIN1],
        o_vec[:, V_SHIFT1],
        o_vec[:, V_GAIN2],
        o_vec[:, V_SHIFT2],
    )


def solution(mesh):
    fine = Mesh(mesh.devices.reshape(2, 4, 4, 2, 2), DEVICES)
    pairs = ("yl", "x", "z", "c")
    data = P(None, pairs, "yh", None)
    weight, vector = P(DEVICES, None), P(DEVICES)
    kinds = (weight, vector) * 4
    return jax.shard_map(
        on_device,
        mesh=fine,
        in_specs=(data, P(None, pairs), data) + kinds + (vector,) * 4,
        out_specs=(data, data) + kinds + (vector,) * 4,
        check_vma=False,
    )
```

```python
import functools

import jax
import jax.numpy as jnp
import numpy as np
from jax import lax
from jax.experimental import pallas as pl
from jax.experimental.pallas import tpu as pltpu
from jax.sharding import Mesh, PartitionSpec as P

HD = 64
EPS = 1e-05
F32 = jnp.float32
BF = jnp.bfloat16
DEVICES = ("yl", "x", "z", "c", "yh")
SWAP = ((0, 1), (1, 0))
STEPS = (0, 1, 3, 2)
AT_OUT, AT_VEC = 3 * 768, 4 * 768
ONE = AT_VEC + 128
V_OUT, V_BACK, V_GAIN1, V_SHIFT1, V_GAIN2, V_SHIFT2, V_IN, V_QV = 0, 1, 2, 3, 4, 5, 6, 10


def mm(a, b):
    return lax.dot_general(a, b, (((1,), (0,)), ((), ())), preferred_element_type=F32)


def mm_nt(a, b):
    return lax.dot_general(a, b, (((1,), (1,)), ((), ())), preferred_element_type=F32)


def mm_tn(a, b):
    return lax.dot_general(a, b, (((0,), (0,)), ((), ())), preferred_element_type=F32)


def vmem(mib, flops=0, moved=0):
    return dict(
        compiler_params=pltpu.CompilerParams(vmem_limit_bytes=mib << 20),
        cost_estimate=pl.CostEstimate(flops=flops, bytes_accessed=moved, transcendentals=0),
    )


ROW = [i % 6 for i in range(36)] + [i // 4 for i in range(24)] + [i // 2 for i in range(12)]
COLUMN = [i // 6 for i in range(36)] + [V_IN + i % 4 for i in range(24)] + [V_QV + i % 2 for i in range(12)]


def vector_maps():
    rows, columns = np.zeros((8, 128), np.float32), np.zeros((128, 128), np.float32)
    for i, (r, l) in enumerate(zip(ROW, COLUMN)):
        rows[r, i] = columns[i, l] = 1
    return rows, columns


def pack_kernel(w_qkv, w_out, line, rows, columns, out):
    width = w_out.shape[1]
    out[:, : 3 * width] = w_qkv[...]
    out[:, AT_OUT:AT_VEC] = w_out[...]
    out[:, AT_VEC:] = mm((line[...].astype(F32) * rows[...]).astype(BF), columns[...])[:6].astype(BF)


def pack(w_qkv, w_out, vectors):
    line = jnp.concatenate(vectors + (jnp.zeros((56,), BF),)).reshape(1, 128)
    rows, columns = vector_maps()
    return pl.pallas_call(
        pack_kernel,
        out_shape=jax.ShapeDtypeStruct((6, ONE), BF),
        name="pack",
    )(w_qkv, w_out, line, jnp.asarray(rows), jnp.asarray(columns, BF))


def finish_kernel(a, b, d, e, rows, columns, g_qkv, g_out, line):
    total = (a[...] + b[...]) + (d[...] + e[...])
    g_qkv[...] = total[:, :AT_OUT]
    g_out[...] = total[:, AT_OUT:AT_VEC]
    spread = lax.dot_general(
        total[:, AT_VEC:], columns[...], (((1,), (1,)), ((), ())),
        precision=lax.Precision.HIGHEST, preferred_element_type=F32,
    )
    line[...] = jnp.sum(spread * rows[:6], axis=0, keepdims=True)


def finish(parts):
    rows, columns = vector_maps()
    g_qkv, g_out, line = pl.pallas_call(
        finish_kernel,
        out_shape=[
            jax.ShapeDtypeStruct(shape, F32) for shape in ((6, AT_OUT), (6, AT_VEC - AT_OUT), (1, 128))
        ],
        name="finish",
    )(*parts, jnp.asarray(rows), jnp.asarray(columns))
    line = line.reshape(128)
    return g_qkv, g_out, [line[6 * i : 6 * i + 6] for i in range(6)] + [line[36:60], line[60:72]]


def interleave(parity):
    row = lax.broadcasted_iota(jnp.int32, (384, 768), 0)
    return (lax.broadcasted_iota(jnp.int32, (384, 768), 1) == 2 * row + parity).astype(BF)


def column_pairs(flip_c, flip_y):
    pairs = []
    for a in (0, 1):
        for b in (0, 1):
            for d in (0, 1):
                pairs.append((b * 4 + (a ^ flip_c) * 2 + (d ^ flip_y), a * 4 + b * 2 + d))
    return pairs


FLIPS = ((0, 0), (0, 1), (1, 0), (1, 1))


def gather_column(shard):
    parts = [lax.ppermute(shard, ("yl", "c", "yh"), column_pairs(*flip)) for flip in FLIPS]
    return jnp.concatenate(parts, axis=0)


def plane_pairs(step, stage):
    pairs = []
    for x in range(4):
        for z in range(4):
            for c in range(2):
                near = (x, (z + step) % 4) if c == stage else ((x + step) % 4, z)
                pairs.append(((near[0] * 4 + near[1]) * 2 + c, (x * 4 + z) * 2 + c))
    return pairs


def from_ring(block, stage):
    return [lax.ppermute(block, ("x", "z", "c"), plane_pairs(step, stage)) for step in STEPS[1:]]


def arrival():
    yl, x, z, c, yh = (lax.axis_index(name) for name in DEVICES)
    j = jnp.arange(384)
    steps = jnp.array(STEPS)
    last, early, flip = steps[j // 96], steps[(j % 96) // 24], (j % 24) // 6
    xx = (x + jnp.where(c == 0, last, early)) % 4
    zz = (z + jnp.where(c == 0, early, last)) % 4
    row = xx * 96 + zz * 24 + (yl ^ (flip // 2)) * 12 + (yh ^ (flip % 2)) * 6 + j % 6
    return (jnp.arange(384)[:, None] == row[None, :]).astype(BF)


def sort_kernel(order, *refs):
    blocks, out = refs[:-1], refs[-1]
    out[...] = mm(order[...], jnp.concatenate([b[...] for b in blocks], axis=0)).astype(BF)


def sort_rows(order, blocks):
    rows, columns = blocks[0].shape
    lanes = 640 if columns % 768 else 768
    return pl.pallas_call(
        sort_kernel,
        grid=(columns // lanes,),
        in_specs=[pl.BlockSpec(order.shape, lambda j: (0, 0))]
        + [pl.BlockSpec((rows, lanes), lambda j: (0, j))] * 4,
        out_specs=pl.BlockSpec((4 * rows, lanes), lambda j: (0, j)),
        out_shape=jax.ShapeDtypeStruct((4 * rows, columns), BF),
        name="sort_rows",
        **vmem(24, 2 * 384 * 384 * columns, 2 * 2 * 384 * columns),
    )(order, *blocks)


def split_kernel(order, mine, recv, *pieces):
    total = (mine[...].astype(F32) + recv[...].astype(F32)).astype(BF)
    rows = mm_tn(order[...], total)
    size = pieces[0].shape[0]
    for i, piece in enumerate(pieces):
        piece[...] = rows[i * size : (i + 1) * size].astype(piece.dtype)


def split_rows(order, mine, recv):
    if mine.ndim == 2:
        mine, recv = mine[None], recv[None]
    parts, rows, columns = mine.shape
    lanes = 640 if columns % 768 else 768
    chunks = columns // lanes
    half = pl.BlockSpec((None, rows, lanes), lambda p, j: (p, 0, j))
    piece = pl.BlockSpec((rows // 4, lanes), lambda p, j: (0, p * chunks + j))
    shape = (rows // 4, parts * columns)
    return pl.pallas_call(
        split_kernel,
        grid=(parts, chunks),
        in_specs=[pl.BlockSpec(order.shape, lambda p, j: (0, 0)), half, half],
        out_specs=[piece] * 4,
        out_shape=[jax.ShapeDtypeStruct(shape, kind) for kind in (F32, BF, BF, BF)],
        name="split_rows",
        **vmem(24, 2 * 384 * 384 * parts * columns, 3 * 2 * 384 * parts * columns),
    )(order, mine, recv)


def fold_kernel(own, a, b, d, *pieces):
    total = own[...] + a[...].astype(F32) + b[...].astype(F32) + d[...].astype(F32)
    size = pieces[0].shape[0]
    for i, piece in enumerate(pieces):
        piece[...] = total[i * size : (i + 1) * size].astype(piece.dtype)


def fold_rows(own, received):
    rows, columns = own.shape
    lanes = 640 if columns % 768 else 768
    block = pl.BlockSpec((rows, lanes), lambda j: (0, j))
    piece = pl.BlockSpec((rows // 4, lanes), lambda j: (0, j))
    return pl.pallas_call(
        fold_kernel,
        grid=(columns // lanes,),
        in_specs=[block] * 4,
        out_specs=[piece] * 4,
        out_shape=[jax.ShapeDtypeStruct((rows // 4, columns), kind) for kind in (F32, BF, BF, BF)],
        name="fold_rows",
        **vmem(24, 4 * rows * columns, 11 * rows * columns),
    )(own, *received)


def to_ring(pieces, stage):
    return [
        lax.ppermute(piece, ("x", "z", "c"), [(b, a) for a, b in plane_pairs(step, stage)])
        for step, piece in zip(STEPS[1:], pieces)
    ]


def column_parts(own, received):
    total = own
    for part in received:
        total += part.astype(F32)
    size = total.shape[0] // 4
    parts = []
    for i, flip in enumerate(FLIPS):
        pairs = [(user, owner) for owner, user in column_pairs(*flip)]
        parts.append(lax.ppermute(total[i * size : (i + 1) * size], ("yl", "c", "yh"), pairs))
    return parts


def sum_parts(parts):
    return (parts[0] + parts[1]) + (parts[2] + parts[3])


def attend_body(g, limits, x_own, x_oth, w_qkv, bias, own, oth, context, probs):
    span, width = context.shape
    lane = lax.broadcasted_iota(jnp.int32, (span, 128), 1)
    key = lax.broadcasted_iota(jnp.int32, (span, span), 0)
    see_own = key < limits[g, 0]
    see_oth = key < limits[g, 1]
    for j in range(3):
        at = pl.ds(j * width, width)
        own[:, at] = (mm(x_own[...], w_qkv[:, at]) + bias[0:1, at]).astype(BF)
        if j:
            oth[:, pl.ds((j - 1) * width, width)] = (
                mm(x_oth[...], w_qkv[:, at]) + bias[0:1, at]
            ).astype(BF)

    def pair(p, carry):
        at = pl.multiple_of(p * 128, 128)
        q = own[:, pl.ds(at, 128)] * jnp.asarray(0.125, BF)
        k_own = own[:, pl.ds(at + width, 128)]
        k_oth = oth[:, pl.ds(at, 128)]
        v = jnp.concatenate(
            [own[:, pl.ds(at + 2 * width, 128)], oth[:, pl.ds(at + width, 128)]], axis=0
        )
        v_t = v.T
        outs = []
        for h in (0, 1):
            q_h = jnp.where((lane >= 64) == (h == 1), q, jnp.zeros_like(q))
            s_own = jnp.where(see_own, mm_nt(k_own, q_h), -1e30)
            s_oth = jnp.where(see_oth, mm_nt(k_oth, q_h), -1e30)
            peak = jnp.maximum(
                jnp.max(s_own, axis=0, keepdims=True), jnp.max(s_oth, axis=0, keepdims=True)
            )
            e_own = jnp.exp(s_own - peak)
            e_oth = jnp.exp(s_oth - peak)
            scale = 1.0 / (
                jnp.sum(e_own, axis=0, keepdims=True) + jnp.sum(e_oth, axis=0, keepdims=True)
            )
            p_t = jnp.concatenate([(e_own * scale).astype(BF), (e_oth * scale).astype(BF)], axis=0)
            probs[2 * p + h] = p_t
            outs.append(mm(v_t[h * HD : (h + 1) * HD], p_t))
        context[:, pl.ds(at, 128)] = jnp.concatenate(outs, axis=0).T.astype(BF)
        return carry

    lax.fori_loop(0, width // 128, pair, 0)


def attend_first_kernel(
    core, limits, x_own, x_oth, here, there, own, oth, context, probs, weights, bias, vec, arrived
):
    width = context.shape[1]
    half = width // 2

    @pl.when(pl.program_id(0) == 0)
    def _():
        copies = [
            pltpu.make_async_copy(
                source, weights.at[pl.ds(pl.multiple_of(start * half, half), half)], arrived.at[i]
            )
            for i, (source, start) in enumerate(((here, core[0]), (there, 1 - core[0])))
        ]
        for copy in copies:
            copy.start()
        for copy in copies:
            copy.wait()
        rows = weights[:, AT_VEC:].astype(F32).T[:16]
        vec[...] = rows
        pairs = rows[V_QV : V_QV + 2].astype(BF)
        sides = [
            mm(pairs[0:1, k : k + half], interleave(0)) + mm(pairs[1:2, k : k + half], interleave(1))
            for k in (0, half)
        ]
        line = jnp.concatenate([sides[0], jnp.zeros((1, width), F32), sides[1]], axis=1)
        bias[...] = jnp.broadcast_to(line, bias.shape)

    attend_body(
        pl.program_id(0), limits, x_own, x_oth, weights, bias, own, oth, context, probs
    )


def attend_more_kernel(first, limits, x_own, x_oth, weights, bias, *rest):
    attend_body(pl.program_id(0) + first, limits, x_own, x_oth, weights, bias, *rest[-4:])


def attend_specs(micro, rows, width, first):
    span, heads = rows // micro, width // HD

    def block(n):
        return pl.BlockSpec((span, n), lambda g, *_: (g + first, 0))

    specs = [
        block(3 * width),
        block(2 * width),
        block(width),
        pl.BlockSpec((None, heads, 2 * span, span), lambda g, *_: (g + first, 0, 0, 0)),
    ]
    shapes = [
        jax.ShapeDtypeStruct((rows, 3 * width), BF),
        jax.ShapeDtypeStruct((rows, 2 * width), BF),
        jax.ShapeDtypeStruct((rows, width), BF),
        jax.ShapeDtypeStruct((micro, heads, 2 * span, span), BF),
    ]
    return block(width), specs, shapes


def attend_first(core, limits, x_own, x_oth, here, there, count):
    rows, width = x_own.shape
    block, specs, shapes = attend_specs(limits.shape[0], rows, width, 0)

    def whole(*shape):
        return pl.BlockSpec(shape, lambda g, *_: (0,) * len(shape))

    return pl.pallas_call(
        attend_first_kernel,
        grid_spec=pltpu.PrefetchScalarGridSpec(
            num_scalar_prefetch=2,
            grid=(count,),
            in_specs=[block, block] + [pl.BlockSpec(memory_space=pl.ANY)] * 2,
            out_specs=specs + [whole(width, ONE), whole(8, 3 * width), whole(16, width)],
            scratch_shapes=[pltpu.SemaphoreType.DMA((2,))],
        ),
        out_shape=shapes
        + [
            jax.ShapeDtypeStruct((width, ONE), BF),
            jax.ShapeDtypeStruct((8, 3 * width), F32),
            jax.ShapeDtypeStruct((16, width), F32),
        ],
        name="attend_first",
        **vmem(60, 10 * count << 30, 8 * count << 20),
    )(core, limits, x_own, x_oth, here, there)


def attend_more(limits, x_own, x_oth, weights, bias, first, earlier):
    micro = limits.shape[0]
    rows, width = x_own.shape
    block, specs, shapes = attend_specs(micro, rows, width, first)

    def whole(*shape):
        return pl.BlockSpec(shape, lambda g, *_: (0,) * len(shape))

    count = micro - first
    return pl.pallas_call(
        functools.partial(attend_more_kernel, first),
        grid_spec=pltpu.PrefetchScalarGridSpec(
            num_scalar_prefetch=1,
            grid=(count,),
            in_specs=[block, block, whole(width, 3 * width), whole(8, 3 * width)]
            + [pl.BlockSpec(memory_space=pl.ANY)] * len(earlier),
            out_specs=specs,
        ),
        out_shape=shapes,
        input_output_aliases={5 + i: i for i in range(len(earlier))},
        name="attend_more",
        **vmem(60, 10 * count << 30, 8 * count << 20),
    )(limits, x_own, x_oth, weights, bias, *earlier)


def attend_back_kernel(own, oth, probs, d_context, w_qkv, d_own, d_oth, x_part, sums):
    span, width = d_context.shape
    lane = lax.broadcasted_iota(jnp.int32, (span, 128), 1)
    lane2 = lax.broadcasted_iota(jnp.int32, (2 * span, 128), 1)

    def pair(p, carry):
        at = pl.multiple_of(p * 128, 128)
        q = own[:, pl.ds(at, 128)]
        k = jnp.concatenate([own[:, pl.ds(at + width, 128)], oth[:, pl.ds(at, 128)]], axis=0)
        v = jnp.concatenate(
            [own[:, pl.ds(at + 2 * width, 128)], oth[:, pl.ds(at + width, 128)]], axis=0
        )
        k_t = k.T
        d_c = d_context[:, pl.ds(at, 128)]
        d_q, d_k, d_v = [], [], []
        for h in (0, 1):
            d_h = jnp.where((lane >= 64) == (h == 1), d_c, jnp.zeros_like(d_c))
            p_b = probs[2 * p + h]
            p_f = p_b.astype(F32)
            d_p = mm_nt(v, d_h)
            weighted = jnp.sum(p_f * d_p, axis=0, keepdims=True)
            d_s = (p_f * (d_p - weighted)).astype(BF)
            d_q.append(mm(k_t[h * HD : (h + 1) * HD], d_s))
            d_k.append(mm(d_s, q))
            d_v.append(mm(p_b, d_c))
        d_own[:, pl.ds(at, 128)] = (jnp.concatenate(d_q, axis=0).T * 0.125).astype(BF)
        d_k = (jnp.where(lane2 < HD, d_k[0], d_k[1]) * 0.125).astype(BF)
        d_v = jnp.where(lane2 < HD, d_v[0], d_v[1]).astype(BF)
        d_own[:, pl.ds(at + width, 128)] = d_k[:span]
        d_own[:, pl.ds(at + 2 * width, 128)] = d_v[:span]
        d_oth[:, pl.ds(at, 128)] = d_k[span:]
        d_oth[:, pl.ds(at + width, 128)] = d_v[span:]
        return carry

    lax.fori_loop(0, width // 128, pair, 0)
    x_part[...] = (
        mm_nt(d_oth[:, :width], w_qkv[:, width : 2 * width])
        + mm_nt(d_oth[:, width:], w_qkv[:, 2 * width :])
    ).astype(BF)
    of_queries = jnp.sum(d_own[:, :width].astype(F32), axis=0, keepdims=True)
    of_values = jnp.sum(
        d_own[:, 2 * width :].astype(F32) + d_oth[:, width:].astype(F32), axis=0, keepdims=True
    )
    sums[0] = rows_of(of_queries, of_values)


def attend_back(own, oth, probs, d_context, w_qkv):
    micro, heads, _, span = probs.shape
    rows, width = d_context.shape

    def block(n):
        return pl.BlockSpec((span, n), lambda g: (g, 0))

    return pl.pallas_call(
        attend_back_kernel,
        grid=(micro,),
        in_specs=[
            block(3 * width),
            block(2 * width),
            pl.BlockSpec((None, heads, 2 * span, span), lambda g: (g, 0, 0, 0)),
            block(width),
            pl.BlockSpec((width, 3 * width), lambda g: (0, 0)),
        ],
        out_specs=[block(3 * width), block(2 * width), block(width)]
        + [pl.BlockSpec((1, 8, width), lambda g: (g, 0, 0))],
        out_shape=[
            jax.ShapeDtypeStruct((rows, 3 * width), BF),
            jax.ShapeDtypeStruct((rows, 2 * width), BF),
            jax.ShapeDtypeStruct((rows, width), BF),
            jax.ShapeDtypeStruct((micro, 8, width), F32),
        ],
        name="attend_back",
        **vmem(60, 28 << 30, 20 << 20),
    )(own, oth, probs, d_context, w_qkv)


def norm_parts(value):
    centre = value - jnp.mean(value, axis=-1, keepdims=True)
    inverse = lax.rsqrt(jnp.mean(centre * centre, axis=-1, keepdims=True) + EPS)
    return centre * inverse, inverse


def norm_back(grad, hat, inverse, gain):
    scaled = grad * gain
    return inverse * (
        scaled
        - jnp.mean(scaled, axis=-1, keepdims=True)
        - hat * jnp.mean(scaled * hat, axis=-1, keepdims=True)
    )


def rows_of(*terms):
    return jnp.concatenate(terms + (jnp.zeros((8 - len(terms), terms[0].shape[1]), F32),), axis=0)


def middle_kernel(
    core, x, context, cot, w_out, vec, b_in, w_mine, w_away,
    block_out, grad_mine, grad_away, d_normed, hat_one, inv_one, sums, in_sums,
    normed, normed_b, outer, active, slope, d_outer, weights, arrived,
):
    phase, l = pl.program_id(0), pl.program_id(1)
    rows, width = x.shape
    half = width // 2
    parts = active.shape[0]
    w_in, w_back = weights.at[l], weights.at[parts + l]
    mine, away = pl.multiple_of(core[0] * half, half), pl.multiple_of((1 - core[0]) * half, half)
    step = 256

    def row(i):
        return vec[i : i + 1, :]

    def fetch(i):
        lanes = pl.ds(i * width, width)
        return [
            pltpu.make_async_copy(
                source.at[:, lanes], weights.at[i, pl.ds(start, half)], arrived.at[i, k]
            )
            for k, (source, start) in enumerate(((w_mine, mine), (w_away, away)))
        ]

    @pl.when((phase == 0) & (l == 0))
    def _():
        for i in range(parts):
            for copy in fetch(i) + fetch(parts + i):
                copy.start()
        for r in range(0, rows, step):
            at = pl.ds(r, step)
            hat, inverse = norm_parts(x[at].astype(F32) + mm(context[at], w_out[...]) + row(V_OUT))
            hat_one[at] = hat
            inv_one[at] = jnp.broadcast_to(inverse, (step, 128))
            value = hat * row(V_GAIN1) + row(V_SHIFT1)
            normed[at] = value
            normed_b[at] = value.astype(BF)
            outer[at] = value + row(V_BACK)

    @pl.when(phase == 0)
    def _():
        for i in range(parts):

            @pl.when(l == i)
            def _():
                for copy in fetch(i) + fetch(parts + i):
                    copy.wait()

        for r in range(0, rows, step):
            at = pl.ds(r, step)
            inner = mm(normed_b[at], w_in[...]) + b_in[0]
            phi = 0.5 + 0.5 * lax.erf(inner * (0.5**0.5))
            act = (inner * phi).astype(BF)
            active[l, at] = act
            slope[l, at] = phi + inner * jnp.exp(-0.5 * inner * inner) * 0.3989422804014327
            outer[at] += mm(act, w_back[...])

    @pl.when((phase == 1) & (l == 0))
    def _():
        total = [jnp.zeros((1, width), F32) for _ in range(3)]
        for r in range(0, rows, step):
            at = pl.ds(r, step)
            hat, inverse = norm_parts(outer[at])
            block_out[at] = (hat * row(V_GAIN2) + row(V_SHIFT2)).astype(BF)
            grad = cot[at].astype(F32)
            d_second = norm_back(grad, hat, inverse, row(V_GAIN2))
            d_b = d_second.astype(BF)
            d_outer[at] = d_b
            d_normed[at] = d_second
            for i, term in enumerate((d_b.astype(F32), grad * hat, grad)):
                total[i] += jnp.sum(term, axis=0, keepdims=True)
        sums[...] = rows_of(*total)

    @pl.when(phase == 1)
    def _():
        pieces = []
        bias = jnp.zeros((1, width), F32)
        for r in range(0, rows, step):
            at = pl.ds(r, step)
            d_inner = (mm_nt(d_outer[at], w_back[...]) * slope[l, at]).astype(BF)
            pieces.append(d_inner)
            bias += jnp.sum(d_inner.astype(F32), axis=0, keepdims=True)
            d_normed[at] += mm_nt(d_inner, w_in[...])
        d_inner = jnp.concatenate(pieces, axis=0)
        in_sums[0] = bias
        for start, out in ((mine, grad_mine), (away, grad_away)):
            cols = pl.ds(start, half)
            out[0] = mm_tn(normed_b[:, cols], d_inner).astype(BF)
            out[1] = mm_tn(active[l, :, cols], d_outer[...]).astype(BF)


def middle(core, x, context, cot, w_out, vec, b_in, w_mine, w_away):
    rows, width = x.shape
    parts = b_in.shape[0]
    half = width // 2

    def whole(*shape):
        return pl.BlockSpec(shape, lambda p, l, *_: (0,) * len(shape))

    late = pl.BlockSpec((2, half, width), lambda p, l, *_: (0, 0, p * l))
    grads = ((2, half, parts * width), BF)
    return pl.pallas_call(
        middle_kernel,
        grid_spec=pltpu.PrefetchScalarGridSpec(
            num_scalar_prefetch=1,
            grid=(2, parts),
            in_specs=[whole(rows, width)] * 3
            + [
                pl.BlockSpec((width, width), lambda p, l, *_: (0, AT_OUT // width)),
                whole(16, width),
                pl.BlockSpec((1, 1, width), lambda p, l, *_: (l, 0, 0)),
                pl.BlockSpec(memory_space=pl.ANY),
                pl.BlockSpec(memory_space=pl.ANY),
            ],
            out_specs=[whole(rows, width), late, late, whole(rows, width)]
            + [whole(rows, width), whole(rows, 128), whole(8, width)]
            + [pl.BlockSpec((1, 1, width), lambda p, l, *_: (p * l, 0, 0))],
            scratch_shapes=[
                pltpu.VMEM((rows, width), F32),
                pltpu.VMEM((rows, width), BF),
                pltpu.VMEM((rows, width), F32),
                pltpu.VMEM((parts, rows, width), BF),
                pltpu.VMEM((parts, rows, width), F32),
                pltpu.VMEM((rows, width), BF),
                pltpu.VMEM((2 * parts, width, width), BF),
                pltpu.SemaphoreType.DMA((2 * parts, 2)),
            ],
        ),
        out_shape=[
            jax.ShapeDtypeStruct(shape, kind)
            for shape, kind in (
                ((rows, width), BF), grads, grads, ((rows, width), F32),
                ((rows, width), F32), ((rows, 128), F32), ((8, width), F32), ((parts, 1, width), F32),
            )
        ],
        name="middle",
        **vmem(62, 40 << 30, 40 << 20),
    )(core, x, context, cot, w_out, vec, b_in, w_mine, w_away)


def branch_back_kernel(
    core, d_normed, hat_one, inv_one, context, w_out, vec, d_first, d_context, mine, away, sums, d_branch
):
    rows, width = d_normed.shape
    half = width // 2
    step = 256
    total = [jnp.zeros((1, width), F32) for _ in range(3)]
    for r in range(0, rows, step):
        at = pl.ds(r, step)
        grad, hat = d_normed[at], hat_one[at]
        back = norm_back(grad, hat, inv_one[at, 0:1], vec[V_GAIN1 : V_GAIN1 + 1, :])
        d_first[at] = back
        d_b = back.astype(BF)
        d_branch[at] = d_b
        for i, term in enumerate((d_b.astype(F32), grad * hat, grad)):
            total[i] += jnp.sum(term, axis=0, keepdims=True)
        d_context[at] = mm_nt(d_b, w_out[...]).astype(BF)
    sums[...] = rows_of(*total)
    for start, out in ((core[0] * half, mine), ((1 - core[0]) * half, away)):
        out[...] = mm_tn(context[:, pl.ds(pl.multiple_of(start, half), half)], d_branch[...]).astype(BF)


def branch_back(core, d_normed, hat_one, inv_one, context, w_out, vec):
    rows, width = d_normed.shape
    shapes = (
        ((rows, width), F32), ((rows, width), BF), ((width // 2, width), BF), ((width // 2, width), BF),
        ((8, width), F32),
    )

    def whole(*shape):
        return pl.BlockSpec(shape, lambda i, *_: (0,) * len(shape))

    return pl.pallas_call(
        branch_back_kernel,
        grid_spec=pltpu.PrefetchScalarGridSpec(
            num_scalar_prefetch=1,
            grid=(1,),
            in_specs=[whole(rows, width), whole(rows, width), whole(rows, 128), whole(rows, width)]
            + [pl.BlockSpec((width, width), lambda i, *_: (0, AT_OUT // width)), whole(16, width)],
            out_specs=[whole(*shape) for shape, _ in shapes],
            scratch_shapes=[pltpu.VMEM((rows, width), BF)],
        ),
        out_shape=[jax.ShapeDtypeStruct(*shape) for shape in shapes],
        name="branch_back",
        **vmem(60, 2 << 30, 12 << 20),
    )(core, d_normed, hat_one, inv_one, context, w_out, vec)


def mixed_grads_kernel(
    core, x_own, x_oth, d_own, d_oth, out_mine, out_away, sums_one, sums_two, in_sums, sums_qv,
    mine, away, columns,
):
    j = pl.program_id(0)
    width = x_own.shape[1]
    half = width // 2
    sides = ((core[0], out_mine, mine), (1 - core[0], out_away, away))

    @pl.when(j == 0)
    def _():
        qv = (sums_qv[0] + sums_qv[1] + sums_qv[2]).astype(BF)
        apart = [
            jnp.concatenate([mm_nt(qv[i : i + 1], interleave(parity)) for i in (0, 1)], axis=1)
            for parity in (0, 1)
        ]
        one, two = sums_one[...], sums_two[...]
        rows = [one[0:1], two[0:1], one[1:3], two[1:3]] + [in_sums[i] for i in range(4)] + apart
        columns[...] = jnp.concatenate(rows + [jnp.zeros((116, width), F32)], axis=0).T.astype(BF)
        for side, from_out, out in sides:
            out[:, AT_OUT:AT_VEC] = from_out[...]
            out[:, AT_VEC:] = columns[pl.ds(pl.multiple_of(side * half, half), half)]

    for side, _, out in sides:
        cols = pl.ds(pl.multiple_of(side * half, half), half)

        @pl.when(j == 0)
        def _():
            out[:, pl.ds(0, width)] = mm_tn(x_own[:, cols], d_own[...]).astype(BF)

        @pl.when(j > 0)
        def _():
            both = mm_tn(x_own[:, cols], d_own[...]) + mm_tn(x_oth[:, cols], d_oth[...])
            out[:, pl.ds(pl.multiple_of(j * width, width), width)] = both.astype(BF)


def mixed_grads(core, x_own, x_oth, d_own, d_oth, out_mine, out_away, *sums):
    rows, width = x_own.shape
    half = width // 2

    def whole(*shape):
        return pl.BlockSpec(shape, lambda j, *_: (0,) * len(shape))

    own = pl.BlockSpec((rows, width), lambda j, *_: (0, j))
    oth = pl.BlockSpec((rows, width), lambda j, *_: (0, jnp.maximum(j - 1, 0)))
    return pl.pallas_call(
        mixed_grads_kernel,
        grid_spec=pltpu.PrefetchScalarGridSpec(
            num_scalar_prefetch=1,
            grid=(3,),
            in_specs=[whole(rows, width), whole(rows, width), own, oth]
            + [whole(half, width), whole(half, width)]
            + [whole(*part.shape) for part in sums],
            out_specs=[whole(half, ONE), whole(half, ONE)],
            scratch_shapes=[pltpu.VMEM((width, 128), BF)],
        ),
        out_shape=[jax.ShapeDtypeStruct((half, ONE), BF)] * 2,
        name="mixed_grads",
        **vmem(60, 6 << 30, 14 << 20),
    )(core, x_own, x_oth, d_own, d_oth, out_mine, out_away, *sums)


def tokens_back_kernel(d_first, x_back, d_own, weights, d_tokens):
    d_tokens[...] = d_first[...] + x_back[...].astype(F32) + mm_nt(d_own[...], weights[...])


def tokens_back(d_first, x_back, d_own, weights, micro):
    rows, width = d_first.shape

    def block(n):
        return pl.BlockSpec((rows // micro, n), lambda g: (g, 0))

    return pl.pallas_call(
        tokens_back_kernel,
        grid=(micro,),
        in_specs=[block(width), block(width), block(3 * width)]
        + [pl.BlockSpec((width, 3 * width), lambda g: (0, 0))],
        out_specs=block(width),
        out_shape=jax.ShapeDtypeStruct((rows, width), F32),
        name="tokens_back",
        **vmem(40, 3 << 30, 14 << 20),
    )(d_first, x_back, d_own, weights)


def on_device(
    tokens, lengths, cotangent, w_qkv, b_qv, w_out, b_out, w_in, b_in, w_back, b_back,
    gain_one, shift_one, gain_two, shift_two,
):
    micro, _, span, width = tokens.shape
    ff = w_in.shape[1]
    rows = micro * span
    yh = lax.axis_index("yh")
    c = lax.axis_index("c")
    core = c.reshape(1)
    x_own = tokens.reshape(rows, width)
    tie = lax.optimization_barrier
    order = arrival()

    packed = pack(w_qkv, w_out, (b_out, b_back, gain_one, shift_one, gain_two, shift_two, b_in, b_qv))
    packed, w_in, w_back, x_sent = tie((packed, w_in, w_back, x_own))
    one = gather_column(packed)
    w_in = w_in.reshape(6, width, 4).transpose(0, 2, 1).reshape(6, ff)
    two = jnp.concatenate([w_in, w_back.reshape(6, ff)], axis=1)
    one, two, x_sent = tie((one, two, x_sent))
    x_oth = lax.ppermute(x_sent, "yh", SWAP)
    one = jnp.concatenate([one] + from_ring(one, 0), axis=0)
    two = gather_column(two)
    one, two = tie((one, two))
    one_parts = [one] + from_ring(one, 1)
    two = jnp.concatenate([two] + from_ring(two, 0), axis=0)
    one_parts, two, x_oth = tie((one_parts, two, x_oth))
    one = sort_rows(order, one_parts)
    one, two = tie((one, two))
    one_away = lax.ppermute(one, "c", SWAP)
    two_parts = [two] + from_ring(two, 1)

    limits = jnp.stack([lengths[:, 0] - yh * span, lengths[:, 0] - (1 - yh) * span], axis=1)
    *seen, weights, bias, vec = attend_first(core, limits, x_own, x_oth, one, one_away, micro - 1)
    seen, two_parts = tie((seen, two_parts))
    two = sort_rows(order, two_parts)
    seen, two = tie((seen, two))
    two_away = lax.ppermute(two, "c", SWAP)
    mixed, mixed_oth, context, probs = attend_more(
        limits, x_own, x_oth, weights, bias, micro - 1, seen
    )
    b_in = vec[V_IN : V_IN + 4].reshape(4, 1, width)
    block_out, ff_mine, ff_away, d_normed, hat_one, inv_one, sums_two, in_sums = middle(
        core, x_own, context, cotangent.reshape(rows, width), weights, vec, b_in, two, two_away
    )
    ff_recv = lax.ppermute(ff_away, "c", SWAP)
    d_first, d_context, out_mine, out_away, sums_one = branch_back(
        core, d_normed, hat_one, inv_one, context, weights, vec
    )
    ff_recv, d_context = tie((ff_recv, d_context))
    ff_own, *ff_sent = split_rows(order, ff_mine, ff_recv)
    ff_sent, d_context = tie((ff_sent, d_context))
    ff_got = to_ring(ff_sent, 1)
    d_own, d_oth, x_part, sums_qv = attend_back(mixed, mixed_oth, probs, d_context, weights)
    ff_got, d_own, x_part = tie((ff_got, d_own, x_part))
    ff_own, *ff_sent = fold_rows(ff_own, ff_got)
    ff_sent, d_own, x_part = tie((ff_sent, d_own, x_part))
    ff_got = to_ring(ff_sent, 0)
    x_back = lax.ppermute(x_part, "yh", SWAP)
    g_mine, g_away = mixed_grads(
        core, x_own, x_oth, d_own, d_oth, out_mine, out_away, sums_one, sums_two, in_sums, sums_qv
    )
    ff_got, g_away = tie((ff_got, g_away))
    g_recv = lax.ppermute(g_away, "c", SWAP)
    ff_parts = column_parts(ff_own, ff_got)
    g_recv, ff_parts = tie((g_recv, ff_parts))
    g_own, *g_sent = split_rows(order, g_mine, g_recv)
    g_sent, d_own, ff_parts = tie((g_sent, d_own, ff_parts))
    g_got = to_ring(g_sent, 1)
    d_tokens = tokens_back(d_first, x_back, d_own, weights, micro)
    early = sum_parts(ff_parts)
    o_in = early[:, :ff].reshape(6, 4, width).transpose(0, 2, 1).reshape(6, ff)
    o_back = early[:, ff:].reshape(24, width)
    g_got, d_tokens, o_in, o_back = tie((g_got, d_tokens, o_in, o_back))
    g_own, *g_sent = fold_rows(g_own, g_got)
    g_qkv, g_out, lines = finish(column_parts(g_own, to_ring(g_sent, 0)))
    return (
        block_out.reshape(tokens.shape),
        d_tokens.reshape(tokens.shape),
        g_qkv,
        lines[7],
        g_out,
        lines[0],
        o_in,
        lines[6],
        o_back,
        lines[1],
        lines[2],
        lines[3],
        lines[4],
        lines[5],
    )


def solution(mesh):
    fine = Mesh(mesh.devices.reshape(2, 4, 4, 2, 2), DEVICES)
    pairs = ("yl", "x", "z", "c")
    data = P(None, pairs, "yh", None)
    weight, vector = P(DEVICES, None), P(DEVICES)
    kinds = (weight, vector) * 4
    return jax.shard_map(
        on_device,
        mesh=fine,
        in_specs=(data, P(None, pairs), data) + kinds + (vector,) * 4,
        out_specs=(data, data) + kinds + (vector,) * 4,
        check_vma=False,
    )
```

```python
import functools

import jax
import jax.numpy as jnp
import numpy as np
from jax import lax
from jax.experimental import pallas as pl
from jax.experimental.pallas import tpu as pltpu
from jax.sharding import Mesh, PartitionSpec as P

HD = 64
EPS = 1e-05
F32 = jnp.float32
BF = jnp.bfloat16
DEVICES = ("yl", "x", "z", "c", "yh")
SWAP = ((0, 1), (1, 0))
STEPS = (0, 1, 3, 2)
AT_OUT, AT_VEC = 3 * 768, 4 * 768
LATE = AT_VEC + 128
ONE, TWO = 3 * 768 + 128, 9 * 768
V_OUT, V_BACK, V_GAIN1, V_SHIFT1, V_GAIN2, V_SHIFT2, V_IN, V_QV = 0, 1, 2, 3, 4, 5, 6, 10


def mm(a, b):
    return lax.dot_general(a, b, (((1,), (0,)), ((), ())), preferred_element_type=F32)


def mm_nt(a, b):
    return lax.dot_general(a, b, (((1,), (1,)), ((), ())), preferred_element_type=F32)


def mm_tn(a, b):
    return lax.dot_general(a, b, (((0,), (0,)), ((), ())), preferred_element_type=F32)


def vmem(mib, flops=0, moved=0):
    return dict(
        compiler_params=pltpu.CompilerParams(vmem_limit_bytes=mib << 20),
        cost_estimate=pl.CostEstimate(flops=flops, bytes_accessed=moved, transcendentals=0),
    )


ROW = [i % 6 for i in range(36)] + [i // 4 for i in range(24)] + [i // 2 for i in range(12)]
COLUMN = [i // 6 for i in range(36)] + [V_IN + i % 4 for i in range(24)] + [V_QV + i % 2 for i in range(12)]


SIZES = (6, 6, 6, 6, 6, 6, 24, 12)


def maps():
    rows, columns = np.zeros((8, 128), np.float32), np.zeros((128, 128), np.float32)
    for i, (r, l) in enumerate(zip(ROW, COLUMN)):
        rows[r, i] = columns[i, l] = 1
    f, place = np.arange(768)[:, None], np.arange(768)[None, :]
    units = (f == 4 * (place % 192) + place // 192).astype(np.float32)
    r, f = np.arange(32)[:, None], np.arange(24)[None, :]
    spread = ((r % 8 < 6) & (f == 4 * (r % 8) + r // 8)).astype(np.float32)
    return rows, columns, units, spread


def pack_kernel(*refs):
    w_qkv, w_out, w_in, w_back = refs[:4]
    vectors = refs[4:12]
    rows, columns, units, spread, out, line, stack = refs[12:]
    width = w_out.shape[1]
    line[...] = jnp.zeros_like(line)
    stack[...] = jnp.zeros_like(stack)
    at = 0
    for size, vector in zip(SIZES, vectors):
        line[0:1, at : at + size] = vector[...].astype(F32).reshape(1, size)
        at += size
    out[:, : 3 * width] = w_qkv[...]
    out[:, 3 * width : ONE] = mm((line[0:1] * rows[...]).astype(BF), columns[...])[:6].astype(BF)
    for b in range(4):
        stack[8 * b : 8 * b + 6] = w_in[:, b * width : (b + 1) * width].astype(F32)
    moved = mm(stack[...].astype(BF), units[...])
    merged = mm(spread[...], w_back[...])
    for l in range(4):
        for b in range(4):
            start = ONE + l * width + 192 * b
            out[:, start : start + 192] = moved[8 * b : 8 * b + 6, 192 * l : 192 * (l + 1)].astype(BF)
        start = ONE + (4 + l) * width
        out[:, start : start + width] = merged[8 * l : 8 * l + 6].astype(BF)
    out[:, ONE + 8 * width :] = w_out[...]


def pack(w_qkv, w_out, w_in, w_back, vectors):
    rows, columns, units, spread = maps()
    return pl.pallas_call(
        pack_kernel,
        out_shape=jax.ShapeDtypeStruct((6, ONE + TWO), BF),
        scratch_shapes=[pltpu.VMEM((8, 128), F32), pltpu.VMEM((32, 768), F32)],
        name="pack",
    )(
        w_qkv, w_out, w_in, w_back, *vectors, jnp.asarray(rows),
        *(jnp.asarray(part, BF) for part in (columns, units, spread)),
    )


def exact_nt(a, b):
    return lax.dot_general(
        a, b, (((1,), (1,)), ((), ())), precision=lax.Precision.HIGHEST, preferred_element_type=F32
    )


def exact_tn(a, b):
    return lax.dot_general(
        a, b, (((0,), (0,)), ((), ())), precision=lax.Precision.HIGHEST, preferred_element_type=F32
    )


def finish_hidden_kernel(a, b, d, e, units, spread, g_in, g_back, stack, rows):
    width = g_back.shape[1]
    total = (a[...] + b[...]) + (d[...] + e[...])
    stack[...] = jnp.zeros_like(stack)
    rows[...] = jnp.zeros_like(rows)
    for l in range(4):
        for b in range(4):
            start = l * width + 192 * b
            stack[8 * b : 8 * b + 6, 192 * l : 192 * (l + 1)] = total[:, start : start + 192]
        rows[8 * l : 8 * l + 6] = total[:, (4 + l) * width : (5 + l) * width]
    moved = exact_nt(stack[...], units[...])
    for b in range(4):
        g_in[:, b * width : (b + 1) * width] = moved[8 * b : 8 * b + 6]
    g_back[...] = exact_tn(spread[...], rows[...])


def finish_hidden(parts):
    _, _, units, spread = maps()
    return pl.pallas_call(
        finish_hidden_kernel,
        out_shape=[jax.ShapeDtypeStruct((6, 3072), F32), jax.ShapeDtypeStruct((24, 768), F32)],
        scratch_shapes=[pltpu.VMEM((32, 768), F32)] * 2,
        name="finish_hidden",
    )(*parts, jnp.asarray(units), jnp.asarray(spread))


def finish_kernel(*refs):
    a, b, d, e, rows, columns, g_qkv, g_out = refs[:8]
    vectors, line = refs[8:-1], refs[-1]
    total = (a[...] + b[...]) + (d[...] + e[...])
    g_qkv[...] = total[:, :AT_OUT]
    g_out[...] = total[:, AT_OUT:AT_VEC]
    line[...] = exact_nt(total[:, AT_VEC:], columns[...]) * rows[:6]
    line[0:1] = jnp.sum(line[...], axis=0, keepdims=True)
    at = 0
    for size, vector in zip(SIZES, vectors):
        vector[...] = line[0:1, at : at + size].reshape(size)
        at += size


def finish(parts):
    rows, columns, _, _ = maps()
    g_qkv, g_out, *vectors = pl.pallas_call(
        finish_kernel,
        out_shape=[
            jax.ShapeDtypeStruct(shape, F32)
            for shape in ((6, AT_OUT), (6, AT_VEC - AT_OUT)) + tuple((size,) for size in SIZES)
        ],
        scratch_shapes=[pltpu.VMEM((6, 128), F32)],
        name="finish",
    )(*parts, jnp.asarray(rows), jnp.asarray(columns))
    return g_qkv, g_out, vectors


def interleave(parity):
    row = lax.broadcasted_iota(jnp.int32, (384, 768), 0)
    return (lax.broadcasted_iota(jnp.int32, (384, 768), 1) == 2 * row + parity).astype(BF)


def column_pairs(flip_c, flip_y):
    pairs = []
    for a in (0, 1):
        for b in (0, 1):
            for d in (0, 1):
                pairs.append((b * 4 + (a ^ flip_c) * 2 + (d ^ flip_y), a * 4 + b * 2 + d))
    return pairs


FLIPS = ((0, 0), (0, 1), (1, 0), (1, 1))


def gather_column(shard):
    parts = [lax.ppermute(shard, ("yl", "c", "yh"), column_pairs(*flip)) for flip in FLIPS]
    return jnp.concatenate(parts, axis=0)


def plane_pairs(step, stage):
    pairs = []
    for x in range(4):
        for z in range(4):
            for c in range(2):
                near = (x, (z + step) % 4) if c == stage else ((x + step) % 4, z)
                pairs.append(((near[0] * 4 + near[1]) * 2 + c, (x * 4 + z) * 2 + c))
    return pairs


def from_ring(block, stage):
    return [lax.ppermute(block, ("x", "z", "c"), plane_pairs(step, stage)) for step in STEPS[1:]]


def arrival():
    yl, x, z, c, yh = (lax.axis_index(name) for name in DEVICES)
    j = jnp.arange(384)
    steps = jnp.array(STEPS)
    last, early, flip = steps[j // 96], steps[(j % 96) // 24], (j % 24) // 6
    xx = (x + jnp.where(c == 0, last, early)) % 4
    zz = (z + jnp.where(c == 0, early, last)) % 4
    row = xx * 96 + zz * 24 + (yl ^ (flip // 2)) * 12 + (yh ^ (flip % 2)) * 6 + j % 6
    return (jnp.arange(384)[:, None] == row[None, :]).astype(BF)


def wide(columns):
    return next(n for n in (2304, 3072, columns) if columns % n == 0)


def sort_kernel(order, *refs):
    blocks, out = refs[:-1], refs[-1]
    out[...] = mm(order[...], jnp.concatenate([b[...] for b in blocks], axis=0)).astype(BF)


def sort_rows(order, blocks):
    rows, columns = blocks[0].shape
    lanes = wide(columns)
    return pl.pallas_call(
        sort_kernel,
        grid=(columns // lanes,),
        in_specs=[pl.BlockSpec(order.shape, lambda j: (0, 0))]
        + [pl.BlockSpec((rows, lanes), lambda j: (0, j))] * 4,
        out_specs=pl.BlockSpec((4 * rows, lanes), lambda j: (0, j)),
        out_shape=jax.ShapeDtypeStruct((4 * rows, columns), BF),
        name="sort_rows",
        **vmem(60, 2 * 384 * 384 * columns, 2 * 2 * 384 * columns),
    )(order, *blocks)


def split_kernel(order, mine, recv, *pieces):
    total = (mine[...].astype(F32) + recv[...].astype(F32)).astype(BF)
    rows = mm_tn(order[...], total)
    size = pieces[0].shape[0]
    for i, piece in enumerate(pieces):
        piece[...] = rows[i * size : (i + 1) * size].astype(piece.dtype)


def split_rows(order, mine, recv):
    if mine.ndim == 2:
        mine, recv = mine[None], recv[None]
    parts, rows, columns = mine.shape
    lanes = wide(columns)
    chunks = columns // lanes
    half = pl.BlockSpec((None, rows, lanes), lambda p, j: (p, 0, j))
    piece = pl.BlockSpec((rows // 4, lanes), lambda p, j: (0, p * chunks + j))
    shape = (rows // 4, parts * columns)
    return pl.pallas_call(
        split_kernel,
        grid=(parts, chunks),
        in_specs=[pl.BlockSpec(order.shape, lambda p, j: (0, 0)), half, half],
        out_specs=[piece] * 4,
        out_shape=[jax.ShapeDtypeStruct(shape, kind) for kind in (F32, BF, BF, BF)],
        name="split_rows",
        **vmem(60, 2 * 384 * 384 * parts * columns, 3 * 2 * 384 * parts * columns),
    )(order, mine, recv)


def fold_kernel(own, a, b, d, *pieces):
    total = own[...] + a[...].astype(F32) + b[...].astype(F32) + d[...].astype(F32)
    size = pieces[0].shape[0]
    for i, piece in enumerate(pieces):
        piece[...] = total[i * size : (i + 1) * size].astype(piece.dtype)


def fold_rows(own, received):
    rows, columns = own.shape
    lanes = wide(columns)
    block = pl.BlockSpec((rows, lanes), lambda j: (0, j))
    piece = pl.BlockSpec((rows // 4, lanes), lambda j: (0, j))
    return pl.pallas_call(
        fold_kernel,
        grid=(columns // lanes,),
        in_specs=[block] * 4,
        out_specs=[piece] * 4,
        out_shape=[jax.ShapeDtypeStruct((rows // 4, columns), kind) for kind in (F32, BF, BF, BF)],
        name="fold_rows",
        **vmem(60, 4 * rows * columns, 11 * rows * columns),
    )(own, *received)


def to_ring(pieces, stage):
    return [
        lax.ppermute(piece, ("x", "z", "c"), [(b, a) for a, b in plane_pairs(step, stage)])
        for step, piece in zip(STEPS[1:], pieces)
    ]


def column_parts(own, received):
    total = own
    for part in received:
        total += part.astype(F32)
    size = total.shape[0] // 4
    parts = []
    for i, flip in enumerate(FLIPS):
        pairs = [(user, owner) for owner, user in column_pairs(*flip)]
        parts.append(lax.ppermute(total[i * size : (i + 1) * size], ("yl", "c", "yh"), pairs))
    return parts


def sum_parts(parts):
    return (parts[0] + parts[1]) + (parts[2] + parts[3])


def apart(pair):
    lane = lax.broadcasted_iota(jnp.int32, pair.shape, 1)
    zero = jnp.zeros_like(pair)
    return jnp.concatenate(
        [jnp.where(lane < HD, pair, zero), jnp.where(lane < HD, zero, pair)], axis=0
    )


def beside(rows, span):
    return jnp.concatenate([rows[:HD, :span], rows[HD:, span:]], axis=0)


def attend_body(g, limits, x_own, x_oth, w_qkv, bias, own, oth, context, probs):
    span, width = context.shape
    key = lax.broadcasted_iota(jnp.int32, (span, 128), 0)
    lane = lax.broadcasted_iota(jnp.int32, (span, 128), 1)
    hidden = jnp.concatenate(
        [jnp.where((key >= limits[g, i]) & (lane == 0), -1e30, 0.0).astype(BF) for i in (0, 1)],
        axis=0,
    )
    unit = (lax.broadcasted_iota(jnp.int32, (2 * span, 128), 1) == 0).astype(BF)
    for j in range(3):
        at = pl.ds(j * width, width)
        own[:, at] = (mm(x_own[...], w_qkv[:, at]) + bias[0:1, at]).astype(BF)
        if j:
            oth[:, pl.ds((j - 1) * width, width)] = (
                mm(x_oth[...], w_qkv[:, at]) + bias[0:1, at]
            ).astype(BF)

    for at in range(0, width, 128):
        q = apart(own[:, pl.ds(at, 128)] * jnp.asarray(0.125, BF))
        k = jnp.concatenate([own[:, pl.ds(at + width, 128)], oth[:, pl.ds(at, 128)]], axis=0)
        v = jnp.concatenate(
            [own[:, pl.ds(at + 2 * width, 128)], oth[:, pl.ds(at + width, 128)]], axis=0
        )
        s = mm_nt(jnp.concatenate([k, hidden], axis=1), jnp.concatenate([q, unit], axis=1))
        e = jnp.exp(s - jnp.max(s, axis=0, keepdims=True))
        p_t = (e * (1.0 / jnp.sum(e, axis=0, keepdims=True))).astype(BF)
        probs[at // HD] = p_t[:, :span]
        probs[at // HD + 1] = p_t[:, span:]
        context[:, pl.ds(at, 128)] = beside(mm(v.T, p_t), span).T.astype(BF)


def attend_first_kernel(
    core, limits, x_own, x_oth, here, there, own, oth, context, probs, weights, bias, vec, arrived
):
    width = context.shape[1]
    half = width // 2

    @pl.when(pl.program_id(0) == 0)
    def _():
        copies = [
            pltpu.make_async_copy(
                source, weights.at[pl.ds(pl.multiple_of(start * half, half), half)], arrived.at[i]
            )
            for i, (source, start) in enumerate(((here, core[0]), (there, 1 - core[0])))
        ]
        for copy in copies:
            copy.start()
        for copy in copies:
            copy.wait()
        rows = weights[:, 3 * width :].astype(F32).T[:16]
        vec[...] = rows
        pairs = rows[V_QV : V_QV + 2].astype(BF)
        sides = [
            mm(pairs[0:1, k : k + half], interleave(0)) + mm(pairs[1:2, k : k + half], interleave(1))
            for k in (0, half)
        ]
        line = jnp.concatenate([sides[0], jnp.zeros((1, width), F32), sides[1]], axis=1)
        bias[...] = jnp.broadcast_to(line, bias.shape)

    attend_body(
        pl.program_id(0), limits, x_own, x_oth, weights, bias, own, oth, context, probs
    )


def attend_more_kernel(first, limits, x_own, x_oth, weights, bias, *rest):
    attend_body(pl.program_id(0) + first, limits, x_own, x_oth, weights, bias, *rest[-4:])


def attend_specs(micro, rows, width, first):
    span, heads = rows // micro, width // HD

    def block(n):
        return pl.BlockSpec((span, n), lambda g, *_: (g + first, 0))

    specs = [
        block(3 * width),
        block(2 * width),
        block(width),
        pl.BlockSpec((None, heads, 2 * span, span), lambda g, *_: (g + first, 0, 0, 0)),
    ]
    shapes = [
        jax.ShapeDtypeStruct((rows, 3 * width), BF),
        jax.ShapeDtypeStruct((rows, 2 * width), BF),
        jax.ShapeDtypeStruct((rows, width), BF),
        jax.ShapeDtypeStruct((micro, heads, 2 * span, span), BF),
    ]
    return block(width), specs, shapes


def attend_first(core, limits, x_own, x_oth, here, there, count):
    rows, width = x_own.shape
    block, specs, shapes = attend_specs(limits.shape[0], rows, width, 0)

    def whole(*shape):
        return pl.BlockSpec(shape, lambda g, *_: (0,) * len(shape))

    return pl.pallas_call(
        attend_first_kernel,
        grid_spec=pltpu.PrefetchScalarGridSpec(
            num_scalar_prefetch=2,
            grid=(count,),
            in_specs=[block, block] + [pl.BlockSpec(memory_space=pl.ANY)] * 2,
            out_specs=specs + [whole(width, ONE), whole(8, 3 * width), whole(16, width)],
            scratch_shapes=[pltpu.SemaphoreType.DMA((2,))],
        ),
        out_shape=shapes
        + [
            jax.ShapeDtypeStruct((width, ONE), BF),
            jax.ShapeDtypeStruct((8, 3 * width), F32),
            jax.ShapeDtypeStruct((16, width), F32),
        ],
        name="attend_first",
        **vmem(60, 10 * count << 30, 8 * count << 20),
    )(core, limits, x_own, x_oth, here, there)


def attend_more(limits, x_own, x_oth, weights, bias, first, earlier):
    micro = limits.shape[0]
    rows, width = x_own.shape
    block, specs, shapes = attend_specs(micro, rows, width, first)

    def whole(*shape):
        return pl.BlockSpec(shape, lambda g, *_: (0,) * len(shape))

    count = micro - first
    return pl.pallas_call(
        functools.partial(attend_more_kernel, first),
        grid_spec=pltpu.PrefetchScalarGridSpec(
            num_scalar_prefetch=1,
            grid=(count,),
            in_specs=[block, block, whole(width, 3 * width), whole(8, 3 * width)]
            + [pl.BlockSpec(memory_space=pl.ANY)] * len(earlier),
            out_specs=specs,
        ),
        out_shape=shapes,
        input_output_aliases={5 + i: i for i in range(len(earlier))},
        name="attend_more",
        **vmem(60, 10 * count << 30, 8 * count << 20),
    )(limits, x_own, x_oth, weights, bias, *earlier)


def attend_back_kernel(own, oth, probs, d_context, w_qkv, *rest):
    d_own, d_oth, x_part, sums = rest[-4:]
    span, width = d_context.shape
    for at in range(0, width, 128):
        q = apart(own[:, pl.ds(at, 128)] * jnp.asarray(0.125, BF))
        k = jnp.concatenate([own[:, pl.ds(at + width, 128)], oth[:, pl.ds(at, 128)]], axis=0)
        v = jnp.concatenate(
            [own[:, pl.ds(at + 2 * width, 128)], oth[:, pl.ds(at + width, 128)]], axis=0
        )
        d_c = apart(d_context[:, pl.ds(at, 128)])
        p_b = jnp.concatenate([probs[at // HD], probs[at // HD + 1]], axis=1)
        p_f = p_b.astype(F32)
        d_p = mm_nt(v, d_c)
        weighted = jnp.sum(p_f * d_p, axis=0, keepdims=True)
        d_s = (p_f * (d_p - weighted)).astype(BF)
        d_own[:, pl.ds(at, 128)] = (beside(mm(k.T, d_s), span).T * 0.125).astype(BF)
        d_k = mm(d_s, q).astype(BF)
        d_v = mm(p_b, d_c).astype(BF)
        d_own[:, pl.ds(at + width, 128)] = d_k[:span]
        d_own[:, pl.ds(at + 2 * width, 128)] = d_v[:span]
        d_oth[:, pl.ds(at, 128)] = d_k[span:]
        d_oth[:, pl.ds(at + width, 128)] = d_v[span:]
    x_part[...] = (
        mm_nt(d_oth[:, :width], w_qkv[:, width : 2 * width])
        + mm_nt(d_oth[:, width:], w_qkv[:, 2 * width :])
    ).astype(BF)
    of_queries = jnp.sum(d_own[:, :width].astype(F32), axis=0, keepdims=True)
    of_values = jnp.sum(
        d_own[:, 2 * width :].astype(F32) + d_oth[:, width:].astype(F32), axis=0, keepdims=True
    )
    sums[0] = rows_of(of_queries, of_values)


def attend_back(own, oth, probs, d_context, w_qkv, first, count, earlier=()):
    micro, heads, _, span = probs.shape
    rows, width = d_context.shape

    def block(n):
        return pl.BlockSpec((span, n), lambda g: (g + first, 0))

    return pl.pallas_call(
        attend_back_kernel,
        grid=(count,),
        in_specs=[
            block(3 * width),
            block(2 * width),
            pl.BlockSpec((None, heads, 2 * span, span), lambda g: (g + first, 0, 0, 0)),
            block(width),
            pl.BlockSpec((width, 3 * width), lambda g: (0, 0)),
        ]
        + [pl.BlockSpec(memory_space=pl.ANY)] * len(earlier),
        out_specs=[block(3 * width), block(2 * width), block(width)]
        + [pl.BlockSpec((1, 8, width), lambda g: (g + first, 0, 0))],
        out_shape=[
            jax.ShapeDtypeStruct((rows, 3 * width), BF),
            jax.ShapeDtypeStruct((rows, 2 * width), BF),
            jax.ShapeDtypeStruct((rows, width), BF),
            jax.ShapeDtypeStruct((micro, 8, width), F32),
        ],
        input_output_aliases={5 + i: i for i in range(len(earlier))},
        name="attend_back",
        **vmem(60, 9 * count << 30, 8 * count << 20),
    )(own, oth, probs, d_context, w_qkv, *earlier)


def norm_parts(value):
    centre = value - jnp.mean(value, axis=-1, keepdims=True)
    inverse = lax.rsqrt(jnp.mean(centre * centre, axis=-1, keepdims=True) + EPS)
    return centre * inverse, inverse


def norm_back(grad, hat, inverse, gain):
    scaled = grad * gain
    return inverse * (
        scaled
        - jnp.mean(scaled, axis=-1, keepdims=True)
        - hat * jnp.mean(scaled * hat, axis=-1, keepdims=True)
    )


def rows_of(*terms):
    return jnp.concatenate(terms + (jnp.zeros((8 - len(terms), terms[0].shape[1]), F32),), axis=0)


def middle_kernel(
    core, vec, b_in, x, context, cot, w_mine, w_away,
    grad_mine, grad_away, out_mine, out_away, sums, in_sums, block_out, d_first, d_context,
    x_in, c_in, cot_in, normed_b, hat_one, inv_one, outer, active, slope, d_outer, d_normed, result,
    d_ctx, weights, from_rows, from_weights, to_rows,
):
    t = pl.program_id(0)
    rows, width = x_in.shape
    half, parts, step = width // 2, active.shape[0], rows // 3
    mine, away = pl.multiple_of(core[0] * half, half), pl.multiple_of((1 - core[0]) * half, half)
    blocks = [pl.ds(r * step, step) for r in range(3)]
    w_out = weights.at[2 * parts]

    def row(i):
        return vec[i : i + 1, :]

    def fetch(i):
        lanes = pl.ds(i * width, width)
        return [
            pltpu.make_async_copy(
                source.at[:, lanes], weights.at[i, pl.ds(start, half)], from_weights.at[i, k]
            )
            for k, (source, start) in enumerate(((w_mine, mine), (w_away, away)))
        ]

    def rows_in(r, *which):
        ends = ((context, c_in), (x, x_in), (cot, cot_in))
        return [
            pltpu.make_async_copy(ends[k][0].at[blocks[r]], ends[k][1].at[blocks[r]], from_rows.at[k, r])
            for k in which
        ]

    def rows_out(k, r):
        source, into = ((result, block_out), (d_normed, d_first), (d_ctx, d_context))[k]
        return pltpu.make_async_copy(source.at[blocks[r]], into.at[blocks[r]], to_rows.at[k, r])

    def wait_part(i):
        for copy in fetch(i) + fetch(parts + i):
            copy.wait()

    def forward(l):
        w_in, w_back = weights.at[l], weights.at[parts + l]

        def hidden(r):
            return mm(normed_b[blocks[r]], w_in[...]) + b_in[0]

        def bend(r, inner):
            phi = 0.5 + 0.5 * lax.erf(inner * (0.5**0.5))
            act = (inner * phi).astype(BF)
            active[l, blocks[r]] = act
            slope[l, blocks[r]] = phi + inner * jnp.exp(-0.5 * inner * inner) * 0.3989422804014327
            return act

        inner = [hidden(0), hidden(1)]
        for r in range(3):
            act = bend(r, inner[r])
            if r == 0:
                inner.append(hidden(2))
            outer[blocks[r]] += mm(act, w_back[...])

    def backward(l):
        w_in, w_back = weights.at[l], weights.at[parts + l]

        def back(r):
            return mm_nt(d_outer[blocks[r]], w_back[...])

        d_act = [back(0), back(1)]
        pieces = []
        bias = jnp.zeros((1, width), F32)
        for r, at in enumerate(blocks):
            d_inner = (d_act[r] * slope[l, at]).astype(BF)
            pieces.append(d_inner)
            if r == 0:
                d_act.append(back(2))
            bias += jnp.sum(d_inner.astype(F32), axis=0, keepdims=True)
            d_normed[at] += mm_nt(d_inner, w_in[...])
        d_inner = jnp.concatenate(pieces, axis=0)
        in_sums[0] = bias
        for start, out in ((mine, grad_mine), (away, grad_away)):
            cols = pl.ds(start, half)
            out[0] = mm_tn(normed_b[:, cols], d_inner).astype(BF)
            out[1] = mm_tn(active[l, :, cols], d_outer[...]).astype(BF)

    @pl.when(t == 0)
    def _():
        for copy in fetch(2 * parts):
            copy.start()
        for r in range(3):
            for copy in rows_in(r, 0, 1):
                copy.start()
        for i in range(parts):
            for copy in fetch(i) + fetch(parts + i):
                copy.start()
        for r in range(3):
            rows_in(r, 2)[0].start()
        for copy in fetch(2 * parts):
            copy.wait()
        wait_part(0)
        for r, at in enumerate(blocks):
            for copy in rows_in(r, 0, 1):
                copy.wait()
            hat, inverse = norm_parts(x_in[at].astype(F32) + mm(c_in[at], w_out[...]) + row(V_OUT))
            hat_one[at] = hat
            inv_one[at] = jnp.broadcast_to(inverse, (step, 128))
            value = hat * row(V_GAIN1) + row(V_SHIFT1)
            normed_b[at] = value.astype(BF)
            outer[at] = value + row(V_BACK)
        forward(0)

    @pl.when((t > 0) & (t < parts))
    def _():
        for i in range(1, parts):

            @pl.when(t == i)
            def _():
                wait_part(i)

        forward(t)

    @pl.when(t == parts)
    def _():
        total = [jnp.zeros((1, width), F32) for _ in range(3)]
        for r, at in enumerate(blocks):
            rows_in(r, 2)[0].wait()
            hat, inverse = norm_parts(outer[at])
            result[at] = (hat * row(V_GAIN2) + row(V_SHIFT2)).astype(BF)
            rows_out(0, r).start()
            grad = cot_in[at].astype(F32)
            d_second = norm_back(grad, hat, inverse, row(V_GAIN2))
            d_b = d_second.astype(BF)
            d_outer[at] = d_b
            d_normed[at] = d_second
            for i, term in enumerate((d_b.astype(F32), grad * hat, grad)):
                total[i] += jnp.sum(term, axis=0, keepdims=True)
        for i, term in zip((V_BACK, V_GAIN2, V_SHIFT2), total):
            sums[i : i + 1] = term
        backward(0)

    @pl.when((t > parts) & (t < 2 * parts))
    def _():
        backward(t - parts)

    @pl.when(t == 2 * parts)
    def _():
        total = [jnp.zeros((1, width), F32) for _ in range(3)]
        for r, at in enumerate(blocks):
            grad, hat = d_normed[at], hat_one[at]
            back = norm_back(grad, hat, inv_one[at, 0:1], row(V_GAIN1))
            d_normed[at] = back
            rows_out(1, r).start()
            d_b = back.astype(BF)
            d_outer[at] = d_b
            for i, term in enumerate((d_b.astype(F32), grad * hat, grad)):
                total[i] += jnp.sum(term, axis=0, keepdims=True)
            d_ctx[at] = mm_nt(d_b, w_out[...]).astype(BF)
            rows_out(2, r).start()
        for i, term in zip((V_OUT, V_GAIN1, V_SHIFT1), total):
            sums[i : i + 1] = term
        for start, out in ((mine, out_mine), (away, out_away)):
            out[...] = mm_tn(c_in[:, pl.ds(start, half)], d_outer[...]).astype(BF)
        for k in range(3):
            for r in range(3):
                rows_out(k, r).wait()


def middle(core, vec, b_in, x, context, cot, w_mine, w_away):
    rows, width = x.shape
    parts = b_in.shape[0]
    half = width // 2

    def whole(*shape):
        return pl.BlockSpec(shape, lambda t, *_: (0,) * len(shape))

    def later(t):
        return jnp.clip(t - parts, 0, parts - 1)

    anywhere = pl.BlockSpec(memory_space=pl.ANY)
    late = pl.BlockSpec((2, half, width), lambda t, *_: (0, 0, later(t)))
    shapes = (
        ((2, half, parts * width), BF), ((2, half, parts * width), BF),
        ((half, width), BF), ((half, width), BF), ((8, width), F32), ((parts, 1, width), F32),
        ((rows, width), BF), ((rows, width), F32), ((rows, width), BF),
    )
    return pl.pallas_call(
        middle_kernel,
        grid_spec=pltpu.PrefetchScalarGridSpec(
            num_scalar_prefetch=1,
            grid=(2 * parts + 1,),
            in_specs=[
                whole(16, width),
                pl.BlockSpec((1, 1, width), lambda t, *_: (jnp.minimum(t, parts - 1), 0, 0)),
            ]
            + [anywhere] * 5,
            out_specs=[late, late, whole(half, width), whole(half, width), whole(8, width)]
            + [pl.BlockSpec((1, 1, width), lambda t, *_: (later(t), 0, 0))]
            + [anywhere] * 3,
            scratch_shapes=[pltpu.VMEM((rows, width), BF)] * 4
            + [pltpu.VMEM((rows, width), F32), pltpu.VMEM((rows, 128), F32)]
            + [pltpu.VMEM((rows, width), F32)]
            + [pltpu.VMEM((parts, rows, width), BF), pltpu.VMEM((parts, rows, width), F32)]
            + [pltpu.VMEM((rows, width), BF), pltpu.VMEM((rows, width), F32)]
            + [pltpu.VMEM((rows, width), BF)] * 2
            + [
                pltpu.VMEM((2 * parts + 1, width, width), BF),
                pltpu.SemaphoreType.DMA((3, 3)),
                pltpu.SemaphoreType.DMA((2 * parts + 1, 2)),
                pltpu.SemaphoreType.DMA((3, 3)),
            ],
        ),
        out_shape=[jax.ShapeDtypeStruct(*shape) for shape in shapes],
        name="middle",
        **vmem(62, 24 << 30, 30 << 20),
    )(core, vec, b_in, x, context, cot, w_mine, w_away)


def mixed_grads_kernel(
    core, x_own, x_oth, d_own, d_oth, out_mine, out_away, sums, in_sums, sums_qv,
    mine, away, columns, result, done,
):
    j = pl.program_id(0)
    width = x_own.shape[1]
    half = width // 2
    sides = (core[0], 1 - core[0])

    def send(k, start, lanes):
        return pltpu.make_async_copy(
            result.at[k, :, pl.ds(start, lanes)], (mine, away)[k].at[:, pl.ds(start, lanes)],
            done.at[k, start // width],
        )

    def sends():
        return [
            send(k, i * width, width if i < 4 else LATE - AT_VEC) for k in (0, 1) for i in range(5)
        ]

    def place(k):
        return pl.ds(pl.multiple_of(sides[k] * half, half), half)

    @pl.when(j == 0)
    def _():
        qv = (sums_qv[0] + sums_qv[1] + sums_qv[2]).astype(BF)
        split = [
            jnp.concatenate([mm_nt(qv[i : i + 1], interleave(parity)) for i in (0, 1)], axis=1)
            for parity in (0, 1)
        ]
        rows = [sums[0:6]] + [in_sums[i] for i in range(4)] + split
        columns[...] = jnp.concatenate(rows + [jnp.zeros((116, width), F32)], axis=0).T.astype(BF)
        for k, from_out in enumerate((out_mine, out_away)):
            result[k, :, AT_OUT:AT_VEC] = from_out[...]
            result[k, :, AT_VEC:] = columns[place(k)]
            result[k, :, :width] = mm_tn(x_own[:, place(k)], d_own[...]).astype(BF)
            for start, lanes in ((AT_OUT, width), (AT_VEC, LATE - AT_VEC), (0, width)):
                send(k, start, lanes).start()

    for i in (1, 2):

        @pl.when(j == i)
        def _():
            for k in (0, 1):
                both = mm_tn(x_own[:, place(k)], d_own[...]) + mm_tn(x_oth[:, place(k)], d_oth[...])
                result[k, :, i * width : (i + 1) * width] = both.astype(BF)
                send(k, i * width, width).start()

    @pl.when(j == 2)
    def _():
        for copy in sends():
            copy.wait()


def mixed_grads(core, x_own, x_oth, d_own, d_oth, out_mine, out_away, *sums):
    rows, width = x_own.shape
    half = width // 2

    def whole(*shape):
        return pl.BlockSpec(shape, lambda j, *_: (0,) * len(shape))

    own = pl.BlockSpec((rows, width), lambda j, *_: (0, j))
    oth = pl.BlockSpec((rows, width), lambda j, *_: (0, jnp.maximum(j - 1, 0)))
    return pl.pallas_call(
        mixed_grads_kernel,
        grid_spec=pltpu.PrefetchScalarGridSpec(
            num_scalar_prefetch=1,
            grid=(3,),
            in_specs=[whole(rows, width), whole(rows, width), own, oth]
            + [whole(half, width), whole(half, width)]
            + [whole(*part.shape) for part in sums],
            out_specs=[pl.BlockSpec(memory_space=pl.ANY)] * 2,
            scratch_shapes=[
                pltpu.VMEM((width, 128), BF),
                pltpu.VMEM((2, half, LATE), BF),
                pltpu.SemaphoreType.DMA((2, 5)),
            ],
        ),
        out_shape=[jax.ShapeDtypeStruct((half, LATE), BF)] * 2,
        name="mixed_grads",
        **vmem(60, 6 << 30, 14 << 20),
    )(core, x_own, x_oth, d_own, d_oth, out_mine, out_away, *sums)


def tokens_back_kernel(d_first, x_back, d_own, weights, d_tokens):
    d_tokens[...] = d_first[...] + x_back[...].astype(F32) + mm_nt(d_own[...], weights[...])


def tokens_back(d_first, x_back, d_own, weights, micro):
    rows, width = d_first.shape

    def block(n):
        return pl.BlockSpec((rows // micro, n), lambda g: (g, 0))

    return pl.pallas_call(
        tokens_back_kernel,
        grid=(micro,),
        in_specs=[block(width), block(width), block(3 * width)]
        + [pl.BlockSpec((width, 3 * width), lambda g: (0, 0))],
        out_specs=block(width),
        out_shape=jax.ShapeDtypeStruct((rows, width), F32),
        name="tokens_back",
        **vmem(40, 3 << 30, 14 << 20),
    )(d_first, x_back, d_own, weights)


def on_device(
    tokens, lengths, cotangent, w_qkv, b_qv, w_out, b_out, w_in, b_in, w_back, b_back,
    gain_one, shift_one, gain_two, shift_two,
):
    micro, _, span, width = tokens.shape
    ff = w_in.shape[1]
    rows = micro * span
    yh = lax.axis_index("yh")
    c = lax.axis_index("c")
    core = c.reshape(1)
    x_own = tokens.reshape(rows, width)
    tie = lax.optimization_barrier
    order = arrival()

    packed = pack(
        w_qkv, w_out, w_in, w_back,
        (b_out, b_back, gain_one, shift_one, gain_two, shift_two, b_in, b_qv),
    )
    x_oth = lax.ppermute(x_own, "yh", SWAP)
    column = gather_column(packed)
    near = [column] + from_ring(column, 0)
    one = jnp.concatenate([part[:, :ONE] for part in near], axis=0)
    two = jnp.concatenate([part[:, ONE:] for part in near], axis=0)
    one_parts = [one] + from_ring(one, 1)
    one_parts, two, x_oth = tie((one_parts, two, x_oth))
    one = sort_rows(order, one_parts)
    one, two = tie((one, two))
    one_away = lax.ppermute(one, "c", SWAP)
    two_parts = [two] + from_ring(two, 1)

    limits = jnp.stack([lengths[:, 0] - yh * span, lengths[:, 0] - (1 - yh) * span], axis=1)
    *seen, weights, bias, vec = attend_first(core, limits, x_own, x_oth, one, one_away, micro - 1)
    seen, two_parts = tie((seen, two_parts))
    two = sort_rows(order, two_parts)
    seen, two = tie((seen, two))
    two_away = lax.ppermute(two, "c", SWAP)
    mixed, mixed_oth, context, probs = attend_more(
        limits, x_own, x_oth, weights, bias, micro - 1, seen
    )
    b_in = vec[V_IN : V_IN + 4].reshape(4, 1, width)
    (
        ff_mine, ff_away, out_mine, out_away, sums, in_sums, block_out, d_first, d_context
    ) = middle(core, vec, b_in, x_own, context, cotangent.reshape(rows, width), two, two_away)
    ff_recv = lax.ppermute(ff_away, "c", SWAP)
    part = attend_back(mixed, mixed_oth, probs, d_context, weights, 0, 1)
    ff_recv, part = tie((ff_recv, part))
    ff_own, *ff_sent = split_rows(order, ff_mine, ff_recv)
    ff_sent, part = tie((ff_sent, part))
    ff_got = to_ring(ff_sent, 1)
    d_own, d_oth, x_part, sums_qv = attend_back(
        mixed, mixed_oth, probs, d_context, weights, 1, micro - 1, part
    )
    x_back = lax.ppermute(x_part, "yh", SWAP)
    g_mine, g_away = mixed_grads(
        core, x_own, x_oth, d_own, d_oth, out_mine, out_away, sums, in_sums, sums_qv
    )
    ff_got, g_away = tie((ff_got, g_away))
    g_recv = lax.ppermute(g_away, "c", SWAP)
    ff_own, *ff_sent = fold_rows(ff_own, ff_got)
    ff_got = to_ring(ff_sent, 0)
    g_recv, ff_sent = tie((g_recv, ff_sent))
    g_own, *g_sent = split_rows(order, g_mine, g_recv)
    g_sent, ff_got, x_back = tie((g_sent, ff_got, x_back))
    g_got = to_ring(g_sent, 1)
    o_in, o_back = finish_hidden(column_parts(ff_own, ff_got))
    d_tokens = tokens_back(d_first, x_back, d_own, weights, micro)
    g_got, d_tokens, o_in, o_back = tie((g_got, d_tokens, o_in, o_back))
    g_own, *g_sent = fold_rows(g_own, g_got)
    g_qkv, g_out, lines = finish(column_parts(g_own, to_ring(g_sent, 0)))
    return (
        block_out.reshape(tokens.shape),
        d_tokens.reshape(tokens.shape),
        g_qkv,
        lines[7],
        g_out,
        lines[0],
        o_in,
        lines[6],
        o_back,
        lines[1],
        lines[2],
        lines[3],
        lines[4],
        lines[5],
    )


def solution(mesh):
    fine = Mesh(mesh.devices.reshape(2, 4, 4, 2, 2), DEVICES)
    pairs = ("yl", "x", "z", "c")
    data = P(None, pairs, "yh", None)
    weight, vector = P(DEVICES, None), P(DEVICES)
    kinds = (weight, vector) * 4
    return jax.shard_map(
        on_device,
        mesh=fine,
        in_specs=(data, P(None, pairs), data) + kinds + (vector,) * 4,
        out_specs=(data, data) + kinds + (vector,) * 4,
        check_vma=False,
    )
```

```python
import functools

import jax
import jax.numpy as jnp
import numpy as np
from jax import lax
from jax.experimental import pallas as pl
from jax.experimental.pallas import tpu as pltpu
from jax.sharding import Mesh, PartitionSpec as P

HD = 64
EPS = 1e-05
F32 = jnp.float32
BF = jnp.bfloat16
DEVICES = ("yl", "x", "z", "c", "yh")
SWAP = ((0, 1), (1, 0))
STEPS = (0, 1, 3, 2)
AT_VEC = 3 * 768
ONE, TWO = AT_VEC + 128, 9 * 768
V_OUT, V_BACK, V_GAIN1, V_SHIFT1, V_GAIN2, V_SHIFT2, V_IN, V_QV = 0, 1, 2, 3, 4, 5, 6, 10


def mm(a, b):
    return lax.dot_general(a, b, (((1,), (0,)), ((), ())), preferred_element_type=F32)


def mm_nt(a, b):
    return lax.dot_general(a, b, (((1,), (1,)), ((), ())), preferred_element_type=F32)


def mm_tn(a, b):
    return lax.dot_general(a, b, (((0,), (0,)), ((), ())), preferred_element_type=F32)


def vmem(mib, flops=0, moved=0):
    return dict(
        compiler_params=pltpu.CompilerParams(vmem_limit_bytes=mib << 20),
        cost_estimate=pl.CostEstimate(flops=flops, bytes_accessed=moved, transcendentals=0),
    )


ROW = [i % 6 for i in range(36)] + [i // 4 for i in range(24)] + [i // 2 for i in range(12)]
COLUMN = [i // 6 for i in range(36)] + [V_IN + i % 4 for i in range(24)] + [V_QV + i % 2 for i in range(12)]


SIZES = (6, 6, 6, 6, 6, 6, 24, 12)


def maps():
    rows, columns = np.zeros((8, 128), np.float32), np.zeros((128, 128), np.float32)
    for i, (r, l) in enumerate(zip(ROW, COLUMN)):
        rows[r, i] = columns[i, l] = 1
    f, place = np.arange(768)[:, None], np.arange(768)[None, :]
    units = (f == 4 * (place % 192) + place // 192).astype(np.float32)
    r, f = np.arange(32)[:, None], np.arange(24)[None, :]
    spread = ((r % 8 < 6) & (f == 4 * (r % 8) + r // 8)).astype(np.float32)
    return rows, columns, units, spread


def pack_kernel(*refs):
    w_qkv, w_out, w_in, w_back = refs[:4]
    vectors = refs[4:12]
    rows, columns, units, spread, out, line, stack = refs[12:]
    width = w_out.shape[1]
    line[...] = jnp.zeros_like(line)
    stack[...] = jnp.zeros_like(stack)
    at = 0
    for size, vector in zip(SIZES, vectors):
        line[0:1, at : at + size] = vector[...].astype(F32).reshape(1, size)
        at += size
    out[:, : 3 * width] = w_qkv[...]
    out[:, AT_VEC:ONE] = mm((line[0:1] * rows[...]).astype(BF), columns[...])[:6].astype(BF)
    for b in range(4):
        stack[8 * b : 8 * b + 6] = w_in[:, b * width : (b + 1) * width].astype(F32)
    moved = mm(stack[...].astype(BF), units[...])
    merged = mm(spread[...], w_back[...])
    for l in range(4):
        for b in range(4):
            start = ONE + l * width + 192 * b
            out[:, start : start + 192] = moved[8 * b : 8 * b + 6, 192 * l : 192 * (l + 1)].astype(BF)
        start = ONE + (4 + l) * width
        out[:, start : start + width] = merged[8 * l : 8 * l + 6].astype(BF)
    out[:, ONE + 8 * width :] = w_out[...]


def pack(w_qkv, w_out, w_in, w_back, vectors):
    rows, columns, units, spread = maps()
    return pl.pallas_call(
        pack_kernel,
        out_shape=jax.ShapeDtypeStruct((6, ONE + TWO), BF),
        scratch_shapes=[pltpu.VMEM((8, 128), F32), pltpu.VMEM((32, 768), F32)],
        name="pack",
    )(
        w_qkv, w_out, w_in, w_back, *vectors, jnp.asarray(rows),
        *(jnp.asarray(part, BF) for part in (columns, units, spread)),
    )


def exact_nt(a, b):
    return lax.dot_general(
        a, b, (((1,), (1,)), ((), ())), precision=lax.Precision.HIGHEST, preferred_element_type=F32
    )


def exact_tn(a, b):
    return lax.dot_general(
        a, b, (((0,), (0,)), ((), ())), precision=lax.Precision.HIGHEST, preferred_element_type=F32
    )


def finish_early_kernel(a, b, d, e, units, spread, g_in, g_back, g_out, stack, rows):
    width = g_back.shape[1]
    total = (a[...] + b[...]) + (d[...] + e[...])
    stack[...] = jnp.zeros_like(stack)
    rows[...] = jnp.zeros_like(rows)
    for l in range(4):
        for b in range(4):
            start = 2 * l * width + 192 * b
            stack[8 * b : 8 * b + 6, 192 * l : 192 * (l + 1)] = total[:, start : start + 192]
        rows[8 * l : 8 * l + 6] = total[:, (2 * l + 1) * width : (2 * l + 2) * width]
    moved = exact_nt(stack[...], units[...])
    for b in range(4):
        g_in[:, b * width : (b + 1) * width] = moved[8 * b : 8 * b + 6]
    g_back[...] = exact_tn(spread[...], rows[...])
    g_out[...] = total[:, 8 * width :]


def finish_early(parts):
    _, _, units, spread = maps()
    return pl.pallas_call(
        finish_early_kernel,
        out_shape=[jax.ShapeDtypeStruct(shape, F32) for shape in ((6, 3072), (24, 768), (6, 768))],
        scratch_shapes=[pltpu.VMEM((32, 768), F32)] * 2,
        name="finish_early",
    )(*parts, jnp.asarray(units), jnp.asarray(spread))


def finish_late_kernel(*refs):
    a, b, d, e, rows, columns, g_qkv = refs[:7]
    vectors, line = refs[7:-1], refs[-1]
    total = (a[...] + b[...]) + (d[...] + e[...])
    g_qkv[...] = total[:, :AT_VEC]
    line[...] = exact_nt(total[:, AT_VEC:], columns[...]) * rows[:6]
    line[0:1] = jnp.sum(line[...], axis=0, keepdims=True)
    at = 0
    for size, vector in zip(SIZES, vectors):
        vector[...] = line[0:1, at : at + size].reshape(size)
        at += size


def finish_late(parts):
    rows, columns, _, _ = maps()
    g_qkv, *vectors = pl.pallas_call(
        finish_late_kernel,
        out_shape=[
            jax.ShapeDtypeStruct(shape, F32) for shape in ((6, AT_VEC),) + tuple((n,) for n in SIZES)
        ],
        scratch_shapes=[pltpu.VMEM((6, 128), F32)],
        name="finish_late",
    )(*parts, jnp.asarray(rows), jnp.asarray(columns))
    return g_qkv, vectors


def interleave(parity):
    row = lax.broadcasted_iota(jnp.int32, (384, 768), 0)
    return (lax.broadcasted_iota(jnp.int32, (384, 768), 1) == 2 * row + parity).astype(BF)


def column_pairs(flip_c, flip_y):
    pairs = []
    for a in (0, 1):
        for b in (0, 1):
            for d in (0, 1):
                pairs.append((b * 4 + (a ^ flip_c) * 2 + (d ^ flip_y), a * 4 + b * 2 + d))
    return pairs


FLIPS = ((0, 0), (0, 1), (1, 0), (1, 1))


def gather_column(shard):
    parts = [lax.ppermute(shard, ("yl", "c", "yh"), column_pairs(*flip)) for flip in FLIPS]
    return jnp.concatenate(parts, axis=0)


def plane_pairs(step, stage):
    pairs = []
    for x in range(4):
        for z in range(4):
            for c in range(2):
                near = (x, (z + step) % 4) if c == stage else ((x + step) % 4, z)
                pairs.append(((near[0] * 4 + near[1]) * 2 + c, (x * 4 + z) * 2 + c))
    return pairs


def from_ring(block, stage):
    return [lax.ppermute(block, ("x", "z", "c"), plane_pairs(step, stage)) for step in STEPS[1:]]


def arrival():
    yl, x, z, c, yh = (lax.axis_index(name) for name in DEVICES)
    j = jnp.arange(384)
    steps = jnp.array(STEPS)
    last, early, flip = steps[j // 96], steps[(j % 96) // 24], (j % 24) // 6
    xx = (x + jnp.where(c == 0, last, early)) % 4
    zz = (z + jnp.where(c == 0, early, last)) % 4
    row = xx * 96 + zz * 24 + (yl ^ (flip // 2)) * 12 + (yh ^ (flip % 2)) * 6 + j % 6
    return (jnp.arange(384)[:, None] == row[None, :]).astype(BF)


def wide(columns):
    return next(n for n in (2304, 3072, columns) if columns % n == 0)


def sort_kernel(order, *refs):
    blocks, out = refs[:-1], refs[-1]
    out[...] = mm(order[...], jnp.concatenate([b[...] for b in blocks], axis=0)).astype(BF)


def sort_rows(order, blocks):
    rows, columns = blocks[0].shape
    lanes = wide(columns)
    return pl.pallas_call(
        sort_kernel,
        grid=(columns // lanes,),
        in_specs=[pl.BlockSpec(order.shape, lambda j: (0, 0))]
        + [pl.BlockSpec((rows, lanes), lambda j: (0, j))] * 4,
        out_specs=pl.BlockSpec((4 * rows, lanes), lambda j: (0, j)),
        out_shape=jax.ShapeDtypeStruct((4 * rows, columns), BF),
        name="sort_rows",
        **vmem(63, 2 * 384 * 384 * columns, 2 * 2 * 384 * columns),
    )(order, *blocks)


def split_kernel(order, mine, recv, *pieces):
    parts, _, lanes = mine.shape
    size = pieces[0].shape[0]
    for p in range(parts):
        total = (mine[p].astype(F32) + recv[p].astype(F32)).astype(BF)
        rows = mm_tn(order[...], total)
        for i, piece in enumerate(pieces):
            piece[:, p * lanes : (p + 1) * lanes] = rows[i * size : (i + 1) * size].astype(piece.dtype)


def split_rows(order, mine, recv):
    if mine.ndim == 2:
        mine, recv = mine[None], recv[None]
    parts, rows, lanes = mine.shape
    batch = 3 if parts % 3 == 0 else 1
    half = pl.BlockSpec((batch, rows, lanes), lambda p: (p, 0, 0))
    piece = pl.BlockSpec((rows // 4, batch * lanes), lambda p: (0, p))
    shape = (rows // 4, parts * lanes)
    return pl.pallas_call(
        split_kernel,
        grid=(parts // batch,),
        in_specs=[pl.BlockSpec(order.shape, lambda p: (0, 0)), half, half],
        out_specs=[piece] * 4,
        out_shape=[jax.ShapeDtypeStruct(shape, kind) for kind in (F32, BF, BF, BF)],
        name="split_rows",
        **vmem(63, 2 * 384 * 384 * parts * lanes, 3 * 2 * 384 * parts * lanes),
    )(order, mine, recv)


def fold_kernel(own, a, b, d, *pieces):
    total = own[...] + a[...].astype(F32) + b[...].astype(F32) + d[...].astype(F32)
    size = pieces[0].shape[0]
    for i, piece in enumerate(pieces):
        piece[...] = total[i * size : (i + 1) * size].astype(piece.dtype)


def fold_rows(own, received):
    rows, columns = own.shape
    lanes = wide(columns)
    block = pl.BlockSpec((rows, lanes), lambda j: (0, j))
    piece = pl.BlockSpec((rows // 4, lanes), lambda j: (0, j))
    return pl.pallas_call(
        fold_kernel,
        grid=(columns // lanes,),
        in_specs=[block] * 4,
        out_specs=[piece] * 4,
        out_shape=[jax.ShapeDtypeStruct((rows // 4, columns), kind) for kind in (F32, BF, BF, BF)],
        name="fold_rows",
        **vmem(63, 4 * rows * columns, 11 * rows * columns),
    )(own, *received)


def to_ring(pieces, stage):
    return [
        lax.ppermute(piece, ("x", "z", "c"), [(b, a) for a, b in plane_pairs(step, stage)])
        for step, piece in zip(STEPS[1:], pieces)
    ]


def column_parts(own, received):
    total = own
    for part in received:
        total += part.astype(F32)
    size = total.shape[0] // 4
    parts = []
    for i, flip in enumerate(FLIPS):
        pairs = [(user, owner) for owner, user in column_pairs(*flip)]
        parts.append(lax.ppermute(total[i * size : (i + 1) * size], ("yl", "c", "yh"), pairs))
    return parts


def sum_parts(parts):
    return (parts[0] + parts[1]) + (parts[2] + parts[3])


def apart(pair):
    lane = lax.broadcasted_iota(jnp.int32, pair.shape, 1)
    zero = jnp.zeros_like(pair)
    return jnp.concatenate(
        [jnp.where(lane < HD, pair, zero), jnp.where(lane < HD, zero, pair)], axis=0
    )


def beside(rows, span):
    return jnp.concatenate([rows[:HD, :span], rows[HD:, span:]], axis=0)


def attend_body(g, limits, x_own, x_oth, w_qkv, bias, own, oth, context, probs):
    span, width = context.shape
    key = lax.broadcasted_iota(jnp.int32, (span, 128), 0)
    lane = lax.broadcasted_iota(jnp.int32, (span, 128), 1)
    hidden = jnp.concatenate(
        [jnp.where((key >= limits[g, i]) & (lane == 0), -1e30, 0.0).astype(BF) for i in (0, 1)],
        axis=0,
    )
    unit = (lax.broadcasted_iota(jnp.int32, (2 * span, 128), 1) == 0).astype(BF)
    for j in range(3):
        at = pl.ds(j * width, width)
        own[:, at] = (mm(x_own[...], w_qkv[:, at]) + bias[0:1, at]).astype(BF)
        if j:
            oth[:, pl.ds((j - 1) * width, width)] = (
                mm(x_oth[...], w_qkv[:, at]) + bias[0:1, at]
            ).astype(BF)

    for at in range(0, width, 128):
        q = apart(own[:, pl.ds(at, 128)] * jnp.asarray(0.125, BF))
        k = jnp.concatenate([own[:, pl.ds(at + width, 128)], oth[:, pl.ds(at, 128)]], axis=0)
        v = jnp.concatenate(
            [own[:, pl.ds(at + 2 * width, 128)], oth[:, pl.ds(at + width, 128)]], axis=0
        )
        s = mm_nt(jnp.concatenate([k, hidden], axis=1), jnp.concatenate([q, unit], axis=1))
        e = jnp.exp(s - jnp.max(s, axis=0, keepdims=True))
        p_t = (e * (1.0 / jnp.sum(e, axis=0, keepdims=True))).astype(BF)
        probs[at // HD] = p_t[:, :span]
        probs[at // HD + 1] = p_t[:, span:]
        context[:, pl.ds(at, 128)] = beside(mm(v.T, p_t), span).T.astype(BF)


def attend_first_kernel(
    core, limits, x_own, x_oth, here, there, own, oth, context, probs, weights, bias, vec, arrived
):
    width = context.shape[1]
    half = width // 2

    @pl.when(pl.program_id(0) == 0)
    def _():
        copies = [
            pltpu.make_async_copy(
                source, weights.at[pl.ds(pl.multiple_of(start * half, half), half)], arrived.at[i]
            )
            for i, (source, start) in enumerate(((here, core[0]), (there, 1 - core[0])))
        ]
        for copy in copies:
            copy.start()
        for copy in copies:
            copy.wait()
        rows = weights[:, 3 * width :].astype(F32).T[:16]
        vec[...] = rows
        pairs = rows[V_QV : V_QV + 2].astype(BF)
        sides = [
            mm(pairs[0:1, k : k + half], interleave(0)) + mm(pairs[1:2, k : k + half], interleave(1))
            for k in (0, half)
        ]
        line = jnp.concatenate([sides[0], jnp.zeros((1, width), F32), sides[1]], axis=1)
        bias[...] = jnp.broadcast_to(line, bias.shape)

    attend_body(
        pl.program_id(0), limits, x_own, x_oth, weights, bias, own, oth, context, probs
    )


def attend_more_kernel(first, limits, x_own, x_oth, weights, bias, *rest):
    attend_body(pl.program_id(0) + first, limits, x_own, x_oth, weights, bias, *rest[-4:])


def attend_specs(micro, rows, width, first):
    span, heads = rows // micro, width // HD

    def block(n):
        return pl.BlockSpec((span, n), lambda g, *_: (g + first, 0))

    specs = [
        block(3 * width),
        block(2 * width),
        block(width),
        pl.BlockSpec((None, heads, 2 * span, span), lambda g, *_: (g + first, 0, 0, 0)),
    ]
    shapes = [
        jax.ShapeDtypeStruct((rows, 3 * width), BF),
        jax.ShapeDtypeStruct((rows, 2 * width), BF),
        jax.ShapeDtypeStruct((rows, width), BF),
        jax.ShapeDtypeStruct((micro, heads, 2 * span, span), BF),
    ]
    return block(width), specs, shapes


def attend_first(core, limits, x_own, x_oth, here, there, count):
    rows, width = x_own.shape
    block, specs, shapes = attend_specs(limits.shape[0], rows, width, 0)

    def whole(*shape):
        return pl.BlockSpec(shape, lambda g, *_: (0,) * len(shape))

    return pl.pallas_call(
        attend_first_kernel,
        grid_spec=pltpu.PrefetchScalarGridSpec(
            num_scalar_prefetch=2,
            grid=(count,),
            in_specs=[block, block] + [pl.BlockSpec(memory_space=pl.ANY)] * 2,
            out_specs=specs + [whole(width, ONE), whole(8, 3 * width), whole(16, width)],
            scratch_shapes=[pltpu.SemaphoreType.DMA((2,))],
        ),
        out_shape=shapes
        + [
            jax.ShapeDtypeStruct((width, ONE), BF),
            jax.ShapeDtypeStruct((8, 3 * width), F32),
            jax.ShapeDtypeStruct((16, width), F32),
        ],
        name="attend_first",
        **vmem(63, 10 * count << 30, 8 * count << 20),
    )(core, limits, x_own, x_oth, here, there)


def attend_more(limits, x_own, x_oth, weights, bias, first, earlier):
    micro = limits.shape[0]
    rows, width = x_own.shape
    block, specs, shapes = attend_specs(micro, rows, width, first)

    def whole(*shape):
        return pl.BlockSpec(shape, lambda g, *_: (0,) * len(shape))

    count = micro - first
    return pl.pallas_call(
        functools.partial(attend_more_kernel, first),
        grid_spec=pltpu.PrefetchScalarGridSpec(
            num_scalar_prefetch=1,
            grid=(count,),
            in_specs=[block, block, whole(width, 3 * width), whole(8, 3 * width)]
            + [pl.BlockSpec(memory_space=pl.ANY)] * len(earlier),
            out_specs=specs,
        ),
        out_shape=shapes,
        input_output_aliases={5 + i: i for i in range(len(earlier))},
        name="attend_more",
        **vmem(63, 10 * count << 30, 8 * count << 20),
    )(limits, x_own, x_oth, weights, bias, *earlier)


def attend_back_kernel(own, oth, probs, d_context, w_qkv, *rest):
    d_own, d_oth, sums, x_part = rest[-4:]
    span, width = d_context.shape
    for at in range(0, width, 128):
        q = apart(own[:, pl.ds(at, 128)] * jnp.asarray(0.125, BF))
        k = jnp.concatenate([own[:, pl.ds(at + width, 128)], oth[:, pl.ds(at, 128)]], axis=0)
        v = jnp.concatenate(
            [own[:, pl.ds(at + 2 * width, 128)], oth[:, pl.ds(at + width, 128)]], axis=0
        )
        d_c = apart(d_context[:, pl.ds(at, 128)])
        p_b = jnp.concatenate([probs[at // HD], probs[at // HD + 1]], axis=1)
        p_f = p_b.astype(F32)
        d_p = mm_nt(v, d_c)
        weighted = jnp.sum(p_f * d_p, axis=0, keepdims=True)
        d_s = (p_f * (d_p - weighted)).astype(BF)
        d_own[:, pl.ds(at, 128)] = (beside(mm(k.T, d_s), span).T * 0.125).astype(BF)
        d_k = mm(d_s, q).astype(BF)
        d_v = mm(p_b, d_c).astype(BF)
        d_own[:, pl.ds(at + width, 128)] = d_k[:span]
        d_own[:, pl.ds(at + 2 * width, 128)] = d_v[:span]
        d_oth[:, pl.ds(at, 128)] = d_k[span:]
        d_oth[:, pl.ds(at + width, 128)] = d_v[span:]
    x_part[...] = (
        mm_nt(d_oth[:, :width], w_qkv[:, width : 2 * width])
        + mm_nt(d_oth[:, width:], w_qkv[:, 2 * width :])
    ).astype(BF)
    of_queries = jnp.sum(d_own[:, :width].astype(F32), axis=0, keepdims=True)
    of_values = jnp.sum(
        d_own[:, 2 * width :].astype(F32) + d_oth[:, width:].astype(F32), axis=0, keepdims=True
    )
    sums[0] = rows_of(of_queries, of_values)


def attend_back(own, oth, probs, d_context, w_qkv, first, count, earlier=()):
    micro, heads, _, span = probs.shape
    rows, width = d_context.shape

    def block(n):
        return pl.BlockSpec((span, n), lambda g: (g + first, 0))

    return pl.pallas_call(
        attend_back_kernel,
        grid=(count,),
        in_specs=[
            block(3 * width),
            block(2 * width),
            pl.BlockSpec((None, heads, 2 * span, span), lambda g: (g + first, 0, 0, 0)),
            block(width),
            pl.BlockSpec((width, 3 * width), lambda g: (0, 0)),
        ]
        + [pl.BlockSpec(memory_space=pl.ANY)] * len(earlier),
        out_specs=[block(3 * width), block(2 * width)]
        + [pl.BlockSpec((1, 8, width), lambda g: (g + first, 0, 0))]
        + [pl.BlockSpec((span, width), lambda g: (g, 0))],
        out_shape=[
            jax.ShapeDtypeStruct((rows, 3 * width), BF),
            jax.ShapeDtypeStruct((rows, 2 * width), BF),
            jax.ShapeDtypeStruct((micro, 8, width), F32),
            jax.ShapeDtypeStruct((count * span, width), BF),
        ],
        input_output_aliases={5 + i: i for i in range(len(earlier))},
        name="attend_back",
        **vmem(63, 9 * count << 30, 8 * count << 20),
    )(own, oth, probs, d_context, w_qkv, *earlier)


def norm_parts(value):
    centre = value - jnp.mean(value, axis=-1, keepdims=True)
    inverse = lax.rsqrt(jnp.mean(centre * centre, axis=-1, keepdims=True) + EPS)
    return centre * inverse, inverse


def norm_back(grad, hat, inverse, gain):
    scaled = grad * gain
    return inverse * (
        scaled
        - jnp.mean(scaled, axis=-1, keepdims=True)
        - hat * jnp.mean(scaled * hat, axis=-1, keepdims=True)
    )


def rows_of(*terms):
    return jnp.concatenate(terms + (jnp.zeros((8 - len(terms), terms[0].shape[1]), F32),), axis=0)


def middle_kernel(
    core, vec, b_in, x, context, cot, w_mine, w_away,
    sums, in_sums, grad_mine, grad_away, block_out, d_first, d_context,
    x_in, c_in, cot_in, normed_b, hat_one, inv_one, outer, active, slope, d_outer, d_normed, result,
    d_ctx, weights, grads, from_rows, from_weights, to_rows, to_grads,
):
    t = pl.program_id(0)
    rows, width = x_in.shape
    half, parts, step = width // 2, active.shape[0], rows // 3
    mine, away = pl.multiple_of(core[0] * half, half), pl.multiple_of((1 - core[0]) * half, half)
    blocks = [pl.ds(r * step, step) for r in range(3)]
    w_out = weights.at[2 * parts]

    def row(i):
        return vec[i : i + 1, :]

    def fetch(i):
        lanes = pl.ds(i * width, width)
        return [
            pltpu.make_async_copy(
                source.at[:, lanes], weights.at[i, pl.ds(start, half)], from_weights.at[i, k]
            )
            for k, (source, start) in enumerate(((w_mine, mine), (w_away, away)))
        ]

    def rows_in(r, *which):
        ends = ((context, c_in), (x, x_in), (cot, cot_in))
        return [
            pltpu.make_async_copy(ends[k][0].at[blocks[r]], ends[k][1].at[blocks[r]], from_rows.at[k, r])
            for k in which
        ]

    def rows_out(k, r):
        source, into = ((result, block_out), (d_normed, d_first), (d_ctx, d_context))[k]
        return pltpu.make_async_copy(source.at[blocks[r]], into.at[blocks[r]], to_rows.at[k, r])

    def grads_out(i, slot, count):
        return [
            pltpu.make_async_copy(
                grads.at[slot, k, pl.ds(0, count)], into.at[pl.ds(i, count)], to_grads.at[slot, k]
            )
            for k, into in enumerate((grad_mine, grad_away))
        ]

    def wait_part(i):
        for copy in fetch(i) + fetch(parts + i):
            copy.wait()

    def forward(l):
        w_in, w_back = weights.at[l], weights.at[parts + l]

        def hidden(r):
            return mm(normed_b[blocks[r]], w_in[...]) + b_in[0]

        def bend(r, inner):
            phi = 0.5 + 0.5 * lax.erf(inner * (0.5**0.5))
            act = (inner * phi).astype(BF)
            active[l, blocks[r]] = act
            slope[l, blocks[r]] = phi + inner * jnp.exp(-0.5 * inner * inner) * 0.3989422804014327
            return act

        inner = [hidden(0), hidden(1)]
        for r in range(3):
            act = bend(r, inner[r])
            if r == 0:
                inner.append(hidden(2))
            outer[blocks[r]] += mm(act, w_back[...])

    def backward(l):
        w_in, w_back = weights.at[l], weights.at[parts + l]

        def back(r):
            return mm_nt(d_outer[blocks[r]], w_back[...])

        d_act = [back(0), back(1)]
        pieces = []
        bias = jnp.zeros((1, width), F32)
        for r, at in enumerate(blocks):
            d_inner = (d_act[r] * slope[l, at]).astype(BF)
            pieces.append(d_inner)
            if r == 0:
                d_act.append(back(2))
            bias += jnp.sum(d_inner.astype(F32), axis=0, keepdims=True)
            d_normed[at] += mm_nt(d_inner, w_in[...])
        d_inner = jnp.concatenate(pieces, axis=0)
        in_sums[0] = bias
        slot = l % 2 if isinstance(l, int) else lax.rem(l, 2)
        if not isinstance(l, int):

            @pl.when(l >= 2)
            def _():
                for copy in grads_out(2 * l - 4, slot, 2):
                    copy.wait()

        for k, start in enumerate((mine, away)):
            cols = pl.ds(start, half)
            grads[slot, k, 0] = mm_tn(normed_b[:, cols], d_inner).astype(BF)
            grads[slot, k, 1] = mm_tn(active[l, :, cols], d_outer[...]).astype(BF)
        for copy in grads_out(2 * l, slot, 2):
            copy.start()

    @pl.when(t == 0)
    def _():
        for copy in fetch(2 * parts):
            copy.start()
        for r in range(3):
            for copy in rows_in(r, 0, 1):
                copy.start()
        for i in range(parts):
            for copy in fetch(i) + fetch(parts + i):
                copy.start()
        for r in range(3):
            rows_in(r, 2)[0].start()
        for copy in fetch(2 * parts):
            copy.wait()
        wait_part(0)
        for r, at in enumerate(blocks):
            for copy in rows_in(r, 0, 1):
                copy.wait()
            hat, inverse = norm_parts(x_in[at].astype(F32) + mm(c_in[at], w_out[...]) + row(V_OUT))
            hat_one[at] = hat
            inv_one[at] = jnp.broadcast_to(inverse, (step, 128))
            value = hat * row(V_GAIN1) + row(V_SHIFT1)
            normed_b[at] = value.astype(BF)
            outer[at] = value + row(V_BACK)
        forward(0)

    @pl.when((t > 0) & (t < parts))
    def _():
        for i in range(1, parts):

            @pl.when(t == i)
            def _():
                wait_part(i)

        forward(t)

    @pl.when(t == parts)
    def _():
        total = [jnp.zeros((1, width), F32) for _ in range(3)]
        for r, at in enumerate(blocks):
            rows_in(r, 2)[0].wait()
            hat, inverse = norm_parts(outer[at])
            result[at] = (hat * row(V_GAIN2) + row(V_SHIFT2)).astype(BF)
            rows_out(0, r).start()
            grad = cot_in[at].astype(F32)
            d_second = norm_back(grad, hat, inverse, row(V_GAIN2))
            d_b = d_second.astype(BF)
            d_outer[at] = d_b
            d_normed[at] = d_second
            for i, term in enumerate((d_b.astype(F32), grad * hat, grad)):
                total[i] += jnp.sum(term, axis=0, keepdims=True)
        for i, term in zip((V_BACK, V_GAIN2, V_SHIFT2), total):
            sums[i : i + 1] = term
        backward(0)

    @pl.when((t > parts) & (t < 2 * parts))
    def _():
        backward(t - parts)

    @pl.when(t == 2 * parts)
    def _():
        total = [jnp.zeros((1, width), F32) for _ in range(3)]
        for r, at in enumerate(blocks):
            grad, hat = d_normed[at], hat_one[at]
            back = norm_back(grad, hat, inv_one[at, 0:1], row(V_GAIN1))
            d_normed[at] = back
            rows_out(1, r).start()
            d_b = back.astype(BF)
            d_outer[at] = d_b
            for i, term in enumerate((d_b.astype(F32), grad * hat, grad)):
                total[i] += jnp.sum(term, axis=0, keepdims=True)
            d_ctx[at] = mm_nt(d_b, w_out[...]).astype(BF)
            rows_out(2, r).start()
        for i, term in zip((V_OUT, V_GAIN1, V_SHIFT1), total):
            sums[i : i + 1] = term
        for copy in grads_out(2 * parts - 4, parts % 2, 2):
            copy.wait()
        for k, start in enumerate((mine, away)):
            grads[parts % 2, k, 0] = mm_tn(c_in[:, pl.ds(start, half)], d_outer[...]).astype(BF)
        for copy in grads_out(2 * parts, parts % 2, 1):
            copy.start()
        for copy in grads_out(2 * parts - 2, (parts - 1) % 2, 2) + grads_out(2 * parts, parts % 2, 1):
            copy.wait()
        for k in range(3):
            for r in range(3):
                rows_out(k, r).wait()


def middle(core, vec, b_in, x, context, cot, w_mine, w_away):
    rows, width = x.shape
    parts = b_in.shape[0]
    half = width // 2

    def whole(*shape):
        return pl.BlockSpec(shape, lambda t, *_: (0,) * len(shape))

    def later(t):
        return jnp.clip(t - parts, 0, parts - 1)

    anywhere = pl.BlockSpec(memory_space=pl.ANY)
    grads = ((2 * parts + 1, half, width), BF)
    shapes = (
        ((8, width), F32), ((parts, 1, width), F32), grads, grads,
        ((rows, width), BF), ((rows, width), F32), ((rows, width), BF),
    )
    return pl.pallas_call(
        middle_kernel,
        grid_spec=pltpu.PrefetchScalarGridSpec(
            num_scalar_prefetch=1,
            grid=(2 * parts + 1,),
            in_specs=[
                whole(16, width),
                pl.BlockSpec((1, 1, width), lambda t, *_: (jnp.minimum(t, parts - 1), 0, 0)),
            ]
            + [anywhere] * 5,
            out_specs=[whole(8, width)]
            + [pl.BlockSpec((1, 1, width), lambda t, *_: (later(t), 0, 0))]
            + [anywhere] * 5,
            scratch_shapes=[pltpu.VMEM((rows, width), BF)] * 4
            + [pltpu.VMEM((rows, width), F32), pltpu.VMEM((rows, 128), F32)]
            + [pltpu.VMEM((rows, width), F32)]
            + [pltpu.VMEM((parts, rows, width), BF), pltpu.VMEM((parts, rows, width), F32)]
            + [pltpu.VMEM((rows, width), BF), pltpu.VMEM((rows, width), F32)]
            + [pltpu.VMEM((rows, width), BF)] * 2
            + [
                pltpu.VMEM((2 * parts + 1, width, width), BF),
                pltpu.VMEM((2, 2, 2, half, width), BF),
                pltpu.SemaphoreType.DMA((3, 3)),
                pltpu.SemaphoreType.DMA((2 * parts + 1, 2)),
                pltpu.SemaphoreType.DMA((3, 3)),
                pltpu.SemaphoreType.DMA((2, 2)),
            ],
        ),
        out_shape=[jax.ShapeDtypeStruct(*shape) for shape in shapes],
        name="middle",
        **vmem(63, 24 << 30, 30 << 20),
    )(core, vec, b_in, x, context, cot, w_mine, w_away)


def mixed_grads_kernel(
    core, x_own, x_oth, d_own, d_oth, sums, in_sums, sums_qv, mine, away, columns, result, done,
):
    j = pl.program_id(0)
    width = x_own.shape[1]
    half = width // 2
    sides = (core[0], 1 - core[0])

    def send(k, start, lanes):
        return pltpu.make_async_copy(
            result.at[k, :, pl.ds(start, lanes)], (mine, away)[k].at[:, pl.ds(start, lanes)],
            done.at[k, start // width],
        )

    def sends():
        return [send(k, i * width, width if i < 3 else ONE - AT_VEC) for k in (0, 1) for i in range(4)]

    def place(k):
        return pl.ds(pl.multiple_of(sides[k] * half, half), half)

    @pl.when(j == 0)
    def _():
        qv = (sums_qv[0] + sums_qv[1] + sums_qv[2]).astype(BF)
        split = [
            jnp.concatenate([mm_nt(qv[i : i + 1], interleave(parity)) for i in (0, 1)], axis=1)
            for parity in (0, 1)
        ]
        rows = [sums[0:6]] + [in_sums[i] for i in range(4)] + split
        columns[...] = jnp.concatenate(rows + [jnp.zeros((116, width), F32)], axis=0).T.astype(BF)
        for k in (0, 1):
            result[k, :, AT_VEC:] = columns[place(k)]
            result[k, :, :width] = mm_tn(x_own[:, place(k)], d_own[...]).astype(BF)
            send(k, AT_VEC, ONE - AT_VEC).start()
            send(k, 0, width).start()

    for i in (1, 2):

        @pl.when(j == i)
        def _():
            for k in (0, 1):
                both = mm_tn(x_own[:, place(k)], d_own[...]) + mm_tn(x_oth[:, place(k)], d_oth[...])
                result[k, :, i * width : (i + 1) * width] = both.astype(BF)
                send(k, i * width, width).start()

    @pl.when(j == 2)
    def _():
        for copy in sends():
            copy.wait()


def mixed_grads(core, x_own, x_oth, d_own, d_oth, *sums):
    rows, width = x_own.shape
    half = width // 2

    def whole(*shape):
        return pl.BlockSpec(shape, lambda j, *_: (0,) * len(shape))

    own = pl.BlockSpec((rows, width), lambda j, *_: (0, j))
    oth = pl.BlockSpec((rows, width), lambda j, *_: (0, jnp.maximum(j - 1, 0)))
    return pl.pallas_call(
        mixed_grads_kernel,
        grid_spec=pltpu.PrefetchScalarGridSpec(
            num_scalar_prefetch=1,
            grid=(3,),
            in_specs=[whole(rows, width), whole(rows, width), own, oth]
            + [whole(*part.shape) for part in sums],
            out_specs=[pl.BlockSpec(memory_space=pl.ANY)] * 2,
            scratch_shapes=[
                pltpu.VMEM((width, 128), BF),
                pltpu.VMEM((2, half, ONE), BF),
                pltpu.SemaphoreType.DMA((2, 4)),
            ],
        ),
        out_shape=[jax.ShapeDtypeStruct((half, ONE), BF)] * 2,
        name="mixed_grads",
        **vmem(63, 6 << 30, 14 << 20),
    )(core, x_own, x_oth, d_own, d_oth, *sums)


def tokens_back_kernel(d_first, x_back, d_own, weights, d_tokens):
    d_tokens[...] = d_first[...] + x_back[...].astype(F32) + mm_nt(d_own[...], weights[...])


def tokens_back(d_first, x_back, d_own, weights, first, earlier=()):
    rows, width = d_first.shape
    span = 256

    def block(n, start=first):
        return pl.BlockSpec((span, n), lambda g: (g + start, 0))

    return pl.pallas_call(
        lambda *refs: tokens_back_kernel(*refs[:4], refs[-1]),
        grid=(x_back.shape[0] // span,),
        in_specs=[block(width), block(width, 0), block(3 * width)]
        + [pl.BlockSpec((width, 3 * width), lambda g: (0, 0))]
        + [pl.BlockSpec(memory_space=pl.ANY)] * len(earlier),
        out_specs=block(width),
        out_shape=jax.ShapeDtypeStruct((rows, width), F32),
        input_output_aliases={4 + i: i for i in range(len(earlier))},
        name="tokens_back",
        **vmem(63, 1 << 30, 6 << 20),
    )(d_first, x_back, d_own, weights, *earlier)


def on_device(
    tokens, lengths, cotangent, w_qkv, b_qv, w_out, b_out, w_in, b_in, w_back, b_back,
    gain_one, shift_one, gain_two, shift_two,
):
    micro, _, span, width = tokens.shape
    ff = w_in.shape[1]
    rows = micro * span
    yh = lax.axis_index("yh")
    c = lax.axis_index("c")
    core = c.reshape(1)
    x_own = tokens.reshape(rows, width)
    tie = lax.optimization_barrier
    order = arrival()

    packed = pack(
        w_qkv, w_out, w_in, w_back,
        (b_out, b_back, gain_one, shift_one, gain_two, shift_two, b_in, b_qv),
    )
    x_oth = lax.ppermute(x_own, "yh", SWAP)
    column = gather_column(packed)
    near = [column] + from_ring(column, 0)
    one = jnp.concatenate([part[:, :ONE] for part in near], axis=0)
    two = jnp.concatenate([part[:, ONE:] for part in near], axis=0)
    one_parts = [one] + from_ring(one, 1)
    one_parts, two, x_oth = tie((one_parts, two, x_oth))
    two_parts = [two] + from_ring(two, 1)
    one = sort_rows(order, one_parts)
    one_away = lax.ppermute(one, "c", SWAP)

    limits = jnp.stack([lengths[:, 0] - yh * span, lengths[:, 0] - (1 - yh) * span], axis=1)
    *seen, weights, bias, vec = attend_first(core, limits, x_own, x_oth, one, one_away, micro - 1)
    seen, two_parts = tie((seen, two_parts))
    two = sort_rows(order, two_parts)
    seen, two = tie((seen, two))
    two_away = lax.ppermute(two, "c", SWAP)
    mixed, mixed_oth, context, probs = attend_more(
        limits, x_own, x_oth, weights, bias, micro - 1, seen
    )
    b_in = vec[V_IN : V_IN + 4].reshape(4, 1, width)
    sums, in_sums, ff_mine, ff_away, block_out, d_first, d_context = middle(
        core, vec, b_in, x_own, context, cotangent.reshape(rows, width), two, two_away
    )
    ff_recv = lax.ppermute(ff_away, "c", SWAP)
    *part, x_near = attend_back(mixed, mixed_oth, probs, d_context, weights, 0, 1)
    x_near = lax.ppermute(x_near, "yh", SWAP)
    ff_recv, part = tie((ff_recv, part))
    ff_own, *ff_sent = split_rows(order, ff_mine, ff_recv)
    ff_sent, part = tie((ff_sent, part))
    ff_got = to_ring(ff_sent, 1)
    d_own, d_oth, sums_qv, x_part = attend_back(
        mixed, mixed_oth, probs, d_context, weights, 1, micro - 1, part
    )
    x_back = lax.ppermute(x_part, "yh", SWAP)
    d_own, x_near = tie((d_own, x_near))
    g_mine, g_away = mixed_grads(core, x_own, x_oth, d_own, d_oth, sums, in_sums, sums_qv)
    ff_got, g_away = tie((ff_got, g_away))
    g_recv = lax.ppermute(g_away, "c", SWAP)
    ff_own, *ff_sent = fold_rows(ff_own, ff_got)
    ff_got = to_ring(ff_sent, 0)
    g_recv, ff_sent = tie((g_recv, ff_sent))
    g_own, *g_sent = split_rows(order, g_mine, g_recv)
    g_sent, ff_got = tie((g_sent, ff_got))
    g_got = to_ring(g_sent, 1)
    ff_parts = column_parts(ff_own, ff_got)
    d_tokens = tokens_back(d_first, x_near, d_own, weights, 0)
    d_tokens = tokens_back(d_first, x_back, d_own, weights, 1, (d_tokens,))
    g_got, d_tokens = tie((g_got, d_tokens))
    g_own, *g_sent = fold_rows(g_own, g_got)
    g_got = to_ring(g_sent, 0)
    o_in, o_back, o_out = finish_early(ff_parts)
    g_got, o_in, o_back, o_out = tie((g_got, o_in, o_back, o_out))
    o_qkv, lines = finish_late(column_parts(g_own, g_got))
    return (
        block_out.reshape(tokens.shape),
        d_tokens.reshape(tokens.shape),
        o_qkv,
        lines[7],
        o_out,
        lines[0],
        o_in,
        lines[6],
        o_back,
        lines[1],
        lines[2],
        lines[3],
        lines[4],
        lines[5],
    )


def solution(mesh):
    fine = Mesh(mesh.devices.reshape(2, 4, 4, 2, 2), DEVICES)
    pairs = ("yl", "x", "z", "c")
    data = P(None, pairs, "yh", None)
    weight, vector = P(DEVICES, None), P(DEVICES)
    kinds = (weight, vector) * 4
    return jax.shard_map(
        on_device,
        mesh=fine,
        in_specs=(data, P(None, pairs), data) + kinds + (vector,) * 4,
        out_specs=(data, data) + kinds + (vector,) * 4,
        check_vma=False,
    )
```

```python
import functools

import jax
import jax.numpy as jnp
import numpy as np
from jax import lax
from jax.experimental import pallas as pl
from jax.experimental.pallas import tpu as pltpu
from jax.sharding import Mesh, PartitionSpec as P

HD = 64
EPS = 1e-05
F32 = jnp.float32
BF = jnp.bfloat16
DEVICES = ("yl", "x", "z", "c", "yh")
SWAP = ((0, 1), (1, 0))
STEPS = (0, 1, 3, 2)
AT_VEC = 3 * 768
ONE, TWO = AT_VEC + 128, 9 * 768
V_OUT, V_BACK, V_GAIN1, V_SHIFT1, V_GAIN2, V_SHIFT2, V_IN, V_QV = 0, 1, 2, 3, 4, 5, 6, 10


def mm(a, b):
    return lax.dot_general(a, b, (((1,), (0,)), ((), ())), preferred_element_type=F32)


def mm_nt(a, b):
    return lax.dot_general(a, b, (((1,), (1,)), ((), ())), preferred_element_type=F32)


def mm_tn(a, b):
    return lax.dot_general(a, b, (((0,), (0,)), ((), ())), preferred_element_type=F32)


def vmem(mib, flops=0, moved=0):
    return dict(
        compiler_params=pltpu.CompilerParams(vmem_limit_bytes=mib << 20),
        cost_estimate=pl.CostEstimate(flops=flops, bytes_accessed=moved, transcendentals=0),
    )


ROW = [i % 6 for i in range(36)] + [i // 4 for i in range(24)] + [i // 2 for i in range(12)]
COLUMN = [i // 6 for i in range(36)] + [V_IN + i % 4 for i in range(24)] + [V_QV + i % 2 for i in range(12)]


SIZES = (6, 6, 6, 6, 6, 6, 24, 12)


def maps():
    rows, columns = np.zeros((8, 128), np.float32), np.zeros((128, 128), np.float32)
    for i, (r, l) in enumerate(zip(ROW, COLUMN)):
        rows[r, i] = columns[i, l] = 1
    f, place = np.arange(768)[:, None], np.arange(768)[None, :]
    units = (f == 4 * (place % 192) + place // 192).astype(np.float32)
    r, f = np.arange(32)[:, None], np.arange(24)[None, :]
    spread = ((r % 8 < 6) & (f == 4 * (r % 8) + r // 8)).astype(np.float32)
    return rows, columns, units, spread


def pack_kernel(*refs):
    w_qkv, w_out, w_in, w_back = refs[:4]
    vectors = refs[4:12]
    rows, columns, units, spread, out, line, stack = refs[12:]
    width = w_out.shape[1]
    line[...] = jnp.zeros_like(line)
    stack[...] = jnp.zeros_like(stack)
    at = 0
    for size, vector in zip(SIZES, vectors):
        line[0:1, at : at + size] = vector[...].astype(F32).reshape(1, size)
        at += size
    out[:, : 3 * width] = w_qkv[...]
    out[:, AT_VEC:ONE] = mm((line[0:1] * rows[...]).astype(BF), columns[...])[:6].astype(BF)
    for b in range(4):
        stack[8 * b : 8 * b + 6] = w_in[:, b * width : (b + 1) * width].astype(F32)
    moved = mm(stack[...].astype(BF), units[...])
    merged = mm(spread[...], w_back[...])
    for l in range(4):
        for b in range(4):
            start = ONE + l * width + 192 * b
            out[:, start : start + 192] = moved[8 * b : 8 * b + 6, 192 * l : 192 * (l + 1)].astype(BF)
        start = ONE + (4 + l) * width
        out[:, start : start + width] = merged[8 * l : 8 * l + 6].astype(BF)
    out[:, ONE + 8 * width :] = w_out[...]


def pack(w_qkv, w_out, w_in, w_back, vectors):
    rows, columns, units, spread = maps()
    return pl.pallas_call(
        pack_kernel,
        out_shape=jax.ShapeDtypeStruct((6, ONE + TWO), BF),
        scratch_shapes=[pltpu.VMEM((8, 128), F32), pltpu.VMEM((32, 768), F32)],
        name="pack",
    )(
        w_qkv, w_out, w_in, w_back, *vectors, jnp.asarray(rows),
        *(jnp.asarray(part, BF) for part in (columns, units, spread)),
    )


def exact_nt(a, b):
    return lax.dot_general(
        a, b, (((1,), (1,)), ((), ())), precision=lax.Precision.HIGHEST, preferred_element_type=F32
    )


def exact_tn(a, b):
    return lax.dot_general(
        a, b, (((0,), (0,)), ((), ())), precision=lax.Precision.HIGHEST, preferred_element_type=F32
    )


def finish_early_kernel(a, b, d, e, units, spread, g_in, g_back, g_out, stack, rows):
    width = g_back.shape[1]
    total = (a[...] + b[...]) + (d[...] + e[...])
    stack[...] = jnp.zeros_like(stack)
    rows[...] = jnp.zeros_like(rows)
    for l in range(4):
        for b in range(4):
            start = 2 * l * width + 192 * b
            stack[8 * b : 8 * b + 6, 192 * l : 192 * (l + 1)] = total[:, start : start + 192]
        rows[8 * l : 8 * l + 6] = total[:, (2 * l + 1) * width : (2 * l + 2) * width]
    moved = exact_nt(stack[...], units[...])
    for b in range(4):
        g_in[:, b * width : (b + 1) * width] = moved[8 * b : 8 * b + 6]
    g_back[...] = exact_tn(spread[...], rows[...])
    g_out[...] = total[:, 8 * width :]


def finish_early(parts):
    _, _, units, spread = maps()
    return pl.pallas_call(
        finish_early_kernel,
        out_shape=[jax.ShapeDtypeStruct(shape, F32) for shape in ((6, 3072), (24, 768), (6, 768))],
        scratch_shapes=[pltpu.VMEM((32, 768), F32)] * 2,
        name="finish_early",
    )(*parts, jnp.asarray(units), jnp.asarray(spread))


def finish_late_kernel(*refs):
    a, b, d, e, rows, columns, g_qkv = refs[:7]
    vectors, line = refs[7:-1], refs[-1]
    total = (a[...] + b[...]) + (d[...] + e[...])
    g_qkv[...] = total[:, :AT_VEC]
    line[...] = exact_nt(total[:, AT_VEC:], columns[...]) * rows[:6]
    line[0:1] = jnp.sum(line[...], axis=0, keepdims=True)
    at = 0
    for size, vector in zip(SIZES, vectors):
        vector[...] = line[0:1, at : at + size].reshape(size)
        at += size


def finish_late(parts):
    rows, columns, _, _ = maps()
    g_qkv, *vectors = pl.pallas_call(
        finish_late_kernel,
        out_shape=[
            jax.ShapeDtypeStruct(shape, F32) for shape in ((6, AT_VEC),) + tuple((n,) for n in SIZES)
        ],
        scratch_shapes=[pltpu.VMEM((6, 128), F32)],
        name="finish_late",
    )(*parts, jnp.asarray(rows), jnp.asarray(columns))
    return g_qkv, vectors


def interleave(parity):
    row = lax.broadcasted_iota(jnp.int32, (384, 768), 0)
    return (lax.broadcasted_iota(jnp.int32, (384, 768), 1) == 2 * row + parity).astype(BF)


def column_pairs(flip_c, flip_y):
    pairs = []
    for a in (0, 1):
        for b in (0, 1):
            for d in (0, 1):
                pairs.append((b * 4 + (a ^ flip_c) * 2 + (d ^ flip_y), a * 4 + b * 2 + d))
    return pairs


FLIPS = ((0, 0), (0, 1), (1, 0), (1, 1))


def gather_column(shard):
    parts = [lax.ppermute(shard, ("yl", "c", "yh"), column_pairs(*flip)) for flip in FLIPS]
    return jnp.concatenate(parts, axis=0)


def plane_pairs(step, stage):
    pairs = []
    for x in range(4):
        for z in range(4):
            for c in range(2):
                near = (x, (z + step) % 4) if c == stage else ((x + step) % 4, z)
                pairs.append(((near[0] * 4 + near[1]) * 2 + c, (x * 4 + z) * 2 + c))
    return pairs


def from_ring(block, stage):
    return [lax.ppermute(block, ("x", "z", "c"), plane_pairs(step, stage)) for step in STEPS[1:]]


def arrival():
    yl, x, z, c, yh = (lax.axis_index(name) for name in DEVICES)
    j = jnp.arange(384)
    steps = jnp.array(STEPS)
    last, early, flip = steps[j // 96], steps[(j % 96) // 24], (j % 24) // 6
    xx = (x + jnp.where(c == 0, last, early)) % 4
    zz = (z + jnp.where(c == 0, early, last)) % 4
    row = xx * 96 + zz * 24 + (yl ^ (flip // 2)) * 12 + (yh ^ (flip % 2)) * 6 + j % 6
    return (jnp.arange(384)[:, None] == row[None, :]).astype(BF)


def wide(columns):
    return next(n for n in (2304, 3072, columns) if columns % n == 0)


def sort_kernel(order, *refs):
    blocks, out = refs[:-1], refs[-1]
    out[...] = mm(order[...], jnp.concatenate([b[...] for b in blocks], axis=0)).astype(BF)


def sort_rows(order, blocks):
    rows, columns = blocks[0].shape
    lanes = wide(columns)
    return pl.pallas_call(
        sort_kernel,
        grid=(columns // lanes,),
        in_specs=[pl.BlockSpec(order.shape, lambda j: (0, 0))]
        + [pl.BlockSpec((rows, lanes), lambda j: (0, j))] * 4,
        out_specs=pl.BlockSpec((4 * rows, lanes), lambda j: (0, j)),
        out_shape=jax.ShapeDtypeStruct((4 * rows, columns), BF),
        name="sort_rows",
        **vmem(63, 2 * 384 * 384 * columns, 2 * 2 * 384 * columns),
    )(order, *blocks)


def split_kernel(order, mine, recv, *pieces):
    parts, _, lanes = mine.shape
    size = pieces[0].shape[0]
    for p in range(parts):
        total = (mine[p].astype(F32) + recv[p].astype(F32)).astype(BF)
        rows = mm_tn(order[...], total)
        for i, piece in enumerate(pieces):
            piece[:, p * lanes : (p + 1) * lanes] = rows[i * size : (i + 1) * size].astype(piece.dtype)


def split_rows(order, mine, recv):
    if mine.ndim == 2:
        mine, recv = mine[None], recv[None]
    parts, rows, lanes = mine.shape
    batch = 3 if parts % 3 == 0 else 1
    half = pl.BlockSpec((batch, rows, lanes), lambda p: (p, 0, 0))
    piece = pl.BlockSpec((rows // 4, batch * lanes), lambda p: (0, p))
    shape = (rows // 4, parts * lanes)
    return pl.pallas_call(
        split_kernel,
        grid=(parts // batch,),
        in_specs=[pl.BlockSpec(order.shape, lambda p: (0, 0)), half, half],
        out_specs=[piece] * 4,
        out_shape=[jax.ShapeDtypeStruct(shape, BF)] * 4,
        name="split_rows",
        **vmem(63, 2 * 384 * 384 * parts * lanes, 3 * 2 * 384 * parts * lanes),
    )(order, mine, recv)


def fold_kernel(own, a, b, d, *pieces):
    total = own[...].astype(F32) + a[...].astype(F32) + b[...].astype(F32) + d[...].astype(F32)
    size = pieces[0].shape[0]
    for i, piece in enumerate(pieces):
        piece[...] = total[i * size : (i + 1) * size].astype(piece.dtype)


def fold_rows(own, received):
    rows, columns = own.shape
    lanes = wide(columns)
    block = pl.BlockSpec((rows, lanes), lambda j: (0, j))
    piece = pl.BlockSpec((rows // 4, lanes), lambda j: (0, j))
    return pl.pallas_call(
        fold_kernel,
        grid=(columns // lanes,),
        in_specs=[block] * 4,
        out_specs=[piece] * 4,
        out_shape=[jax.ShapeDtypeStruct((rows // 4, columns), kind) for kind in (F32, BF, BF, BF)],
        name="fold_rows",
        **vmem(63, 4 * rows * columns, 11 * rows * columns),
    )(own, *received)


def to_ring(pieces, stage):
    return [
        lax.ppermute(piece, ("x", "z", "c"), [(b, a) for a, b in plane_pairs(step, stage)])
        for step, piece in zip(STEPS[1:], pieces)
    ]


def column_parts(own, received):
    total = own
    for part in received:
        total += part.astype(F32)
    size = total.shape[0] // 4
    parts = []
    for i, flip in enumerate(FLIPS):
        pairs = [(user, owner) for owner, user in column_pairs(*flip)]
        parts.append(lax.ppermute(total[i * size : (i + 1) * size], ("yl", "c", "yh"), pairs))
    return parts


def sum_parts(parts):
    return (parts[0] + parts[1]) + (parts[2] + parts[3])


def apart(pair):
    lane = lax.broadcasted_iota(jnp.int32, pair.shape, 1)
    zero = jnp.zeros_like(pair)
    return jnp.concatenate(
        [jnp.where(lane < HD, pair, zero), jnp.where(lane < HD, zero, pair)], axis=0
    )


def beside(rows, span):
    return jnp.concatenate([rows[:HD, :span], rows[HD:, span:]], axis=0)


def attend_body(g, limits, x_own, x_oth, w_qkv, bias, own, oth, context, probs):
    span, width = context.shape
    key = lax.broadcasted_iota(jnp.int32, (span, 128), 0)
    lane = lax.broadcasted_iota(jnp.int32, (span, 128), 1)
    hidden = jnp.concatenate(
        [jnp.where((key >= limits[g, i]) & (lane == 0), -1e30, 0.0).astype(BF) for i in (0, 1)],
        axis=0,
    )
    unit = (lax.broadcasted_iota(jnp.int32, (2 * span, 128), 1) == 0).astype(BF)
    for j in range(3):
        at = pl.ds(j * width, width)
        own[:, at] = (mm(x_own[...], w_qkv[:, at]) + bias[0:1, at]).astype(BF)
        if j:
            oth[:, pl.ds((j - 1) * width, width)] = (
                mm(x_oth[...], w_qkv[:, at]) + bias[0:1, at]
            ).astype(BF)

    for at in range(0, width, 128):
        q = apart(own[:, pl.ds(at, 128)] * jnp.asarray(0.125, BF))
        k = jnp.concatenate([own[:, pl.ds(at + width, 128)], oth[:, pl.ds(at, 128)]], axis=0)
        v = jnp.concatenate(
            [own[:, pl.ds(at + 2 * width, 128)], oth[:, pl.ds(at + width, 128)]], axis=0
        )
        s = mm_nt(jnp.concatenate([k, hidden], axis=1), jnp.concatenate([q, unit], axis=1))
        e = jnp.exp(s - jnp.max(s, axis=0, keepdims=True))
        p_t = (e * (1.0 / jnp.sum(e, axis=0, keepdims=True))).astype(BF)
        probs[at // HD] = p_t[:, :span]
        probs[at // HD + 1] = p_t[:, span:]
        context[:, pl.ds(at, 128)] = beside(mm(v.T, p_t), span).T.astype(BF)


def attend_first_kernel(
    core, limits, x_own, x_oth, here, there, own, oth, context, probs, weights, bias, vec, arrived
):
    width = context.shape[1]
    half = width // 2

    @pl.when(pl.program_id(0) == 0)
    def _():
        copies = [
            pltpu.make_async_copy(
                source, weights.at[pl.ds(pl.multiple_of(start * half, half), half)], arrived.at[i]
            )
            for i, (source, start) in enumerate(((here, core[0]), (there, 1 - core[0])))
        ]
        for copy in copies:
            copy.start()
        for copy in copies:
            copy.wait()
        rows = weights[:, 3 * width :].astype(F32).T[:16]
        vec[...] = rows
        pairs = rows[V_QV : V_QV + 2].astype(BF)
        sides = [
            mm(pairs[0:1, k : k + half], interleave(0)) + mm(pairs[1:2, k : k + half], interleave(1))
            for k in (0, half)
        ]
        line = jnp.concatenate([sides[0], jnp.zeros((1, width), F32), sides[1]], axis=1)
        bias[...] = jnp.broadcast_to(line, bias.shape)

    attend_body(
        pl.program_id(0), limits, x_own, x_oth, weights, bias, own, oth, context, probs
    )


def attend_more_kernel(first, limits, x_own, x_oth, weights, bias, *rest):
    attend_body(pl.program_id(0) + first, limits, x_own, x_oth, weights, bias, *rest[-4:])


def attend_specs(micro, rows, width, first):
    span, heads = rows // micro, width // HD

    def block(n):
        return pl.BlockSpec((span, n), lambda g, *_: (g + first, 0))

    specs = [
        block(3 * width),
        block(2 * width),
        block(width),
        pl.BlockSpec((None, heads, 2 * span, span), lambda g, *_: (g + first, 0, 0, 0)),
    ]
    shapes = [
        jax.ShapeDtypeStruct((rows, 3 * width), BF),
        jax.ShapeDtypeStruct((rows, 2 * width), BF),
        jax.ShapeDtypeStruct((rows, width), BF),
        jax.ShapeDtypeStruct((micro, heads, 2 * span, span), BF),
    ]
    return block(width), specs, shapes


def attend_first(core, limits, x_own, x_oth, here, there, count):
    rows, width = x_own.shape
    block, specs, shapes = attend_specs(limits.shape[0], rows, width, 0)

    def whole(*shape):
        return pl.BlockSpec(shape, lambda g, *_: (0,) * len(shape))

    return pl.pallas_call(
        attend_first_kernel,
        grid_spec=pltpu.PrefetchScalarGridSpec(
            num_scalar_prefetch=2,
            grid=(count,),
            in_specs=[block, block] + [pl.BlockSpec(memory_space=pl.ANY)] * 2,
            out_specs=specs + [whole(width, ONE), whole(8, 3 * width), whole(16, width)],
            scratch_shapes=[pltpu.SemaphoreType.DMA((2,))],
        ),
        out_shape=shapes
        + [
            jax.ShapeDtypeStruct((width, ONE), BF),
            jax.ShapeDtypeStruct((8, 3 * width), F32),
            jax.ShapeDtypeStruct((16, width), F32),
        ],
        name="attend_first",
        **vmem(63, 10 * count << 30, 8 * count << 20),
    )(core, limits, x_own, x_oth, here, there)


def attend_more(limits, x_own, x_oth, weights, bias, first, earlier):
    micro = limits.shape[0]
    rows, width = x_own.shape
    block, specs, shapes = attend_specs(micro, rows, width, first)

    def whole(*shape):
        return pl.BlockSpec(shape, lambda g, *_: (0,) * len(shape))

    count = micro - first
    return pl.pallas_call(
        functools.partial(attend_more_kernel, first),
        grid_spec=pltpu.PrefetchScalarGridSpec(
            num_scalar_prefetch=1,
            grid=(count,),
            in_specs=[block, block, whole(width, 3 * width), whole(8, 3 * width)]
            + [pl.BlockSpec(memory_space=pl.ANY)] * len(earlier),
            out_specs=specs,
        ),
        out_shape=shapes,
        input_output_aliases={5 + i: i for i in range(len(earlier))},
        name="attend_more",
        **vmem(63, 10 * count << 30, 8 * count << 20),
    )(limits, x_own, x_oth, weights, bias, *earlier)


def attend_back_kernel(own, oth, probs, d_context, d_first, weights, *rest):
    d_own, d_oth, sums, d_tokens, x_part, w_qkv, arrived = rest[-7:]
    span, width = d_context.shape
    begin = pl.program_id(0) == 0
    fetch = pltpu.make_async_copy(weights.at[:, pl.ds(0, 3 * width)], w_qkv, arrived)

    @pl.when(begin)
    def _():
        fetch.start()

    for at in range(0, width, 128):
        q = apart(own[:, pl.ds(at, 128)] * jnp.asarray(0.125, BF))
        k = jnp.concatenate([own[:, pl.ds(at + width, 128)], oth[:, pl.ds(at, 128)]], axis=0)
        v = jnp.concatenate(
            [own[:, pl.ds(at + 2 * width, 128)], oth[:, pl.ds(at + width, 128)]], axis=0
        )
        d_c = apart(d_context[:, pl.ds(at, 128)])
        p_b = jnp.concatenate([probs[at // HD], probs[at // HD + 1]], axis=1)
        p_f = p_b.astype(F32)
        d_p = mm_nt(v, d_c)
        weighted = jnp.sum(p_f * d_p, axis=0, keepdims=True)
        d_s = (p_f * (d_p - weighted)).astype(BF)
        d_own[:, pl.ds(at, 128)] = (beside(mm(k.T, d_s), span).T * 0.125).astype(BF)
        d_k = mm(d_s, q).astype(BF)
        d_v = mm(p_b, d_c).astype(BF)
        d_own[:, pl.ds(at + width, 128)] = d_k[:span]
        d_own[:, pl.ds(at + 2 * width, 128)] = d_v[:span]
        d_oth[:, pl.ds(at, 128)] = d_k[span:]
        d_oth[:, pl.ds(at + width, 128)] = d_v[span:]

    @pl.when(begin)
    def _():
        fetch.wait()

    d_tokens[...] = d_first[...] + mm_nt(d_own[...], w_qkv[...])
    x_part[...] = (
        mm_nt(d_oth[:, :width], w_qkv[:, width : 2 * width])
        + mm_nt(d_oth[:, width:], w_qkv[:, 2 * width :])
    ).astype(BF)
    of_queries = jnp.sum(d_own[:, :width].astype(F32), axis=0, keepdims=True)
    of_values = jnp.sum(
        d_own[:, 2 * width :].astype(F32) + d_oth[:, width:].astype(F32), axis=0, keepdims=True
    )
    sums[0] = rows_of(of_queries, of_values)


def attend_back(own, oth, probs, d_context, d_first, weights, first, count, earlier=()):
    micro, heads, _, span = probs.shape
    rows, width = d_context.shape

    def block(n):
        return pl.BlockSpec((span, n), lambda g: (g + first, 0))

    return pl.pallas_call(
        attend_back_kernel,
        grid=(count,),
        in_specs=[
            block(3 * width),
            block(2 * width),
            pl.BlockSpec((None, heads, 2 * span, span), lambda g: (g + first, 0, 0, 0)),
            block(width),
            block(width),
        ]
        + [pl.BlockSpec(memory_space=pl.ANY)] * (1 + len(earlier)),
        out_specs=[block(3 * width), block(2 * width)]
        + [pl.BlockSpec((1, 8, width), lambda g: (g + first, 0, 0)), block(width)]
        + [pl.BlockSpec((span, width), lambda g: (g, 0))],
        out_shape=[
            jax.ShapeDtypeStruct((rows, 3 * width), BF),
            jax.ShapeDtypeStruct((rows, 2 * width), BF),
            jax.ShapeDtypeStruct((micro, 8, width), F32),
            jax.ShapeDtypeStruct((rows, width), F32),
            jax.ShapeDtypeStruct((count * span, width), BF),
        ],
        input_output_aliases={6 + i: i for i in range(len(earlier))},
        scratch_shapes=[pltpu.VMEM((width, 3 * width), BF), pltpu.SemaphoreType.DMA],
        name="attend_back",
        **vmem(63, 9 * count << 30, 8 * count << 20),
    )(own, oth, probs, d_context, d_first, weights, *earlier)


def norm_parts(value):
    centre = value - jnp.mean(value, axis=-1, keepdims=True)
    inverse = lax.rsqrt(jnp.mean(centre * centre, axis=-1, keepdims=True) + EPS)
    return centre * inverse, inverse


def norm_back(grad, hat, inverse, gain):
    scaled = grad * gain
    return inverse * (
        scaled
        - jnp.mean(scaled, axis=-1, keepdims=True)
        - hat * jnp.mean(scaled * hat, axis=-1, keepdims=True)
    )


def rows_of(*terms):
    return jnp.concatenate(terms + (jnp.zeros((8 - len(terms), terms[0].shape[1]), F32),), axis=0)


def middle_kernel(
    core, vec, b_in, x, context, cot, w_mine, w_away,
    sums, in_sums, grad_mine, grad_away, block_out, d_first, d_context,
    x_in, c_in, cot_in, normed_b, hat_one, inv_one, outer, active, slope, d_outer, d_normed, result,
    d_ctx, weights, grads, from_rows, from_weights, to_rows, to_grads,
):
    t = pl.program_id(0)
    rows, width = x_in.shape
    half, parts, step = width // 2, active.shape[0], rows // 3
    mine, away = pl.multiple_of(core[0] * half, half), pl.multiple_of((1 - core[0]) * half, half)
    blocks = [pl.ds(r * step, step) for r in range(3)]
    w_out = weights.at[2 * parts]

    def row(i):
        return vec[i : i + 1, :]

    def fetch(i):
        lanes = pl.ds(i * width, width)
        return [
            pltpu.make_async_copy(
                source.at[:, lanes], weights.at[i, pl.ds(start, half)], from_weights.at[i, k]
            )
            for k, (source, start) in enumerate(((w_mine, mine), (w_away, away)))
        ]

    def rows_in(r, *which):
        ends = ((context, c_in), (x, x_in), (cot, cot_in))
        return [
            pltpu.make_async_copy(ends[k][0].at[blocks[r]], ends[k][1].at[blocks[r]], from_rows.at[k, r])
            for k in which
        ]

    def rows_out(k, r):
        source, into = ((result, block_out), (d_normed, d_first), (d_ctx, d_context))[k]
        return pltpu.make_async_copy(source.at[blocks[r]], into.at[blocks[r]], to_rows.at[k, r])

    def grads_out(i, slot, count):
        return [
            pltpu.make_async_copy(
                grads.at[slot, k, pl.ds(0, count)], into.at[pl.ds(i, count)], to_grads.at[slot, k]
            )
            for k, into in enumerate((grad_mine, grad_away))
        ]

    def wait_part(i):
        for copy in fetch(i) + fetch(parts + i):
            copy.wait()

    def forward(l):
        w_in, w_back = weights.at[l], weights.at[parts + l]

        def hidden(r):
            return mm(normed_b[blocks[r]], w_in[...]) + b_in[0]

        def bend(r, inner):
            phi = 0.5 + 0.5 * lax.erf(inner * (0.5**0.5))
            act = (inner * phi).astype(BF)
            active[l, blocks[r]] = act
            slope[l, blocks[r]] = phi + inner * jnp.exp(-0.5 * inner * inner) * 0.3989422804014327
            return act

        inner = [hidden(0), hidden(1)]
        for r in range(3):
            act = bend(r, inner[r])
            if r == 0:
                inner.append(hidden(2))
            outer[blocks[r]] += mm(act, w_back[...])

    def backward(l):
        w_in, w_back = weights.at[l], weights.at[parts + l]

        def back(r):
            return mm_nt(d_outer[blocks[r]], w_back[...])

        d_act = [back(0), back(1)]
        pieces = []
        bias = jnp.zeros((1, width), F32)
        for r, at in enumerate(blocks):
            d_inner = (d_act[r] * slope[l, at]).astype(BF)
            pieces.append(d_inner)
            if r == 0:
                d_act.append(back(2))
            bias += jnp.sum(d_inner.astype(F32), axis=0, keepdims=True)
            d_normed[at] += mm_nt(d_inner, w_in[...])
        d_inner = jnp.concatenate(pieces, axis=0)
        in_sums[0] = bias
        slot = l % 2 if isinstance(l, int) else lax.rem(l, 2)
        if not isinstance(l, int):

            @pl.when(l >= 2)
            def _():
                for copy in grads_out(2 * l - 4, slot, 2):
                    copy.wait()

        for k, start in enumerate((mine, away)):
            cols = pl.ds(start, half)
            grads[slot, k, 0] = mm_tn(normed_b[:, cols], d_inner).astype(BF)
            grads[slot, k, 1] = mm_tn(active[l, :, cols], d_outer[...]).astype(BF)
        for copy in grads_out(2 * l, slot, 2):
            copy.start()

    @pl.when(t == 0)
    def _():
        for copy in fetch(2 * parts):
            copy.start()
        for r in range(3):
            for copy in rows_in(r, 0, 1):
                copy.start()
        for i in range(parts):
            for copy in fetch(i) + fetch(parts + i):
                copy.start()
        for r in range(3):
            rows_in(r, 2)[0].start()
        for copy in fetch(2 * parts):
            copy.wait()
        wait_part(0)
        for r, at in enumerate(blocks):
            for copy in rows_in(r, 0, 1):
                copy.wait()
            hat, inverse = norm_parts(x_in[at].astype(F32) + mm(c_in[at], w_out[...]) + row(V_OUT))
            hat_one[at] = hat
            inv_one[at] = jnp.broadcast_to(inverse, (step, 128))
            value = hat * row(V_GAIN1) + row(V_SHIFT1)
            normed_b[at] = value.astype(BF)
            outer[at] = value + row(V_BACK)
        forward(0)

    @pl.when((t > 0) & (t < parts))
    def _():
        for i in range(1, parts):

            @pl.when(t == i)
            def _():
                wait_part(i)

        forward(t)

    @pl.when(t == parts)
    def _():
        total = [jnp.zeros((1, width), F32) for _ in range(3)]
        for r, at in enumerate(blocks):
            rows_in(r, 2)[0].wait()
            hat, inverse = norm_parts(outer[at])
            result[at] = (hat * row(V_GAIN2) + row(V_SHIFT2)).astype(BF)
            rows_out(0, r).start()
            grad = cot_in[at].astype(F32)
            d_second = norm_back(grad, hat, inverse, row(V_GAIN2))
            d_b = d_second.astype(BF)
            d_outer[at] = d_b
            d_normed[at] = d_second
            for i, term in enumerate((d_b.astype(F32), grad * hat, grad)):
                total[i] += jnp.sum(term, axis=0, keepdims=True)
        for i, term in zip((V_BACK, V_GAIN2, V_SHIFT2), total):
            sums[i : i + 1] = term
        backward(0)

    @pl.when((t > parts) & (t < 2 * parts))
    def _():
        backward(t - parts)

    @pl.when(t == 2 * parts)
    def _():
        total = [jnp.zeros((1, width), F32) for _ in range(3)]
        for r, at in enumerate(blocks):
            grad, hat = d_normed[at], hat_one[at]
            back = norm_back(grad, hat, inv_one[at, 0:1], row(V_GAIN1))
            d_normed[at] = back
            rows_out(1, r).start()
            d_b = back.astype(BF)
            d_outer[at] = d_b
            for i, term in enumerate((d_b.astype(F32), grad * hat, grad)):
                total[i] += jnp.sum(term, axis=0, keepdims=True)
            d_ctx[at] = mm_nt(d_b, w_out[...]).astype(BF)
            rows_out(2, r).start()
        for i, term in zip((V_OUT, V_GAIN1, V_SHIFT1), total):
            sums[i : i + 1] = term
        for copy in grads_out(2 * parts - 4, parts % 2, 2):
            copy.wait()
        for k, start in enumerate((mine, away)):
            grads[parts % 2, k, 0] = mm_tn(c_in[:, pl.ds(start, half)], d_outer[...]).astype(BF)
        for copy in grads_out(2 * parts, parts % 2, 1):
            copy.start()
        for copy in grads_out(2 * parts - 2, (parts - 1) % 2, 2) + grads_out(2 * parts, parts % 2, 1):
            copy.wait()
        for k in range(3):
            for r in range(3):
                rows_out(k, r).wait()


def middle(core, vec, b_in, x, context, cot, w_mine, w_away):
    rows, width = x.shape
    parts = b_in.shape[0]
    half = width // 2

    def whole(*shape):
        return pl.BlockSpec(shape, lambda t, *_: (0,) * len(shape))

    def later(t):
        return jnp.clip(t - parts, 0, parts - 1)

    anywhere = pl.BlockSpec(memory_space=pl.ANY)
    grads = ((2 * parts + 1, half, width), BF)
    shapes = (
        ((8, width), F32), ((parts, 1, width), F32), grads, grads,
        ((rows, width), BF), ((rows, width), F32), ((rows, width), BF),
    )
    return pl.pallas_call(
        middle_kernel,
        grid_spec=pltpu.PrefetchScalarGridSpec(
            num_scalar_prefetch=1,
            grid=(2 * parts + 1,),
            in_specs=[
                whole(16, width),
                pl.BlockSpec((1, 1, width), lambda t, *_: (jnp.minimum(t, parts - 1), 0, 0)),
            ]
            + [anywhere] * 5,
            out_specs=[whole(8, width)]
            + [pl.BlockSpec((1, 1, width), lambda t, *_: (later(t), 0, 0))]
            + [anywhere] * 5,
            scratch_shapes=[pltpu.VMEM((rows, width), BF)] * 4
            + [pltpu.VMEM((rows, width), F32), pltpu.VMEM((rows, 128), F32)]
            + [pltpu.VMEM((rows, width), F32)]
            + [pltpu.VMEM((parts, rows, width), BF), pltpu.VMEM((parts, rows, width), F32)]
            + [pltpu.VMEM((rows, width), BF), pltpu.VMEM((rows, width), F32)]
            + [pltpu.VMEM((rows, width), BF)] * 2
            + [
                pltpu.VMEM((2 * parts + 1, width, width), BF),
                pltpu.VMEM((2, 2, 2, half, width), BF),
                pltpu.SemaphoreType.DMA((3, 3)),
                pltpu.SemaphoreType.DMA((2 * parts + 1, 2)),
                pltpu.SemaphoreType.DMA((3, 3)),
                pltpu.SemaphoreType.DMA((2, 2)),
            ],
        ),
        out_shape=[jax.ShapeDtypeStruct(*shape) for shape in shapes],
        name="middle",
        **vmem(63, 24 << 30, 30 << 20),
    )(core, vec, b_in, x, context, cot, w_mine, w_away)


def mixed_grads_kernel(
    core, x_own, x_oth, d_own, d_oth, sums, in_sums, sums_qv, mine, away, columns, result, done,
):
    j = pl.program_id(0)
    width = x_own.shape[1]
    half = width // 2
    sides = (core[0], 1 - core[0])

    def send(k, start, lanes):
        return pltpu.make_async_copy(
            result.at[k, :, pl.ds(start, lanes)], (mine, away)[k].at[:, pl.ds(start, lanes)],
            done.at[k, start // width],
        )

    def sends():
        return [send(k, i * width, width if i < 3 else ONE - AT_VEC) for k in (0, 1) for i in range(4)]

    def place(k):
        return pl.ds(pl.multiple_of(sides[k] * half, half), half)

    @pl.when(j == 0)
    def _():
        qv = (sums_qv[0] + sums_qv[1] + sums_qv[2]).astype(BF)
        split = [
            jnp.concatenate([mm_nt(qv[i : i + 1], interleave(parity)) for i in (0, 1)], axis=1)
            for parity in (0, 1)
        ]
        rows = [sums[0:6]] + [in_sums[i] for i in range(4)] + split
        columns[...] = jnp.concatenate(rows + [jnp.zeros((116, width), F32)], axis=0).T.astype(BF)
        for k in (0, 1):
            result[k, :, AT_VEC:] = columns[place(k)]
            result[k, :, :width] = mm_tn(x_own[:, place(k)], d_own[...]).astype(BF)
            send(k, AT_VEC, ONE - AT_VEC).start()
            send(k, 0, width).start()

    for i in (1, 2):

        @pl.when(j == i)
        def _():
            for k in (0, 1):
                both = mm_tn(x_own[:, place(k)], d_own[...]) + mm_tn(x_oth[:, place(k)], d_oth[...])
                result[k, :, i * width : (i + 1) * width] = both.astype(BF)
                send(k, i * width, width).start()

    @pl.when(j == 2)
    def _():
        for copy in sends():
            copy.wait()


def mixed_grads(core, x_own, x_oth, d_own, d_oth, *sums):
    rows, width = x_own.shape
    half = width // 2

    def whole(*shape):
        return pl.BlockSpec(shape, lambda j, *_: (0,) * len(shape))

    own = pl.BlockSpec((rows, width), lambda j, *_: (0, j))
    oth = pl.BlockSpec((rows, width), lambda j, *_: (0, jnp.maximum(j - 1, 0)))
    return pl.pallas_call(
        mixed_grads_kernel,
        grid_spec=pltpu.PrefetchScalarGridSpec(
            num_scalar_prefetch=1,
            grid=(3,),
            in_specs=[whole(rows, width), whole(rows, width), own, oth]
            + [whole(*part.shape) for part in sums],
            out_specs=[pl.BlockSpec(memory_space=pl.ANY)] * 2,
            scratch_shapes=[
                pltpu.VMEM((width, 128), BF),
                pltpu.VMEM((2, half, ONE), BF),
                pltpu.SemaphoreType.DMA((2, 4)),
            ],
        ),
        out_shape=[jax.ShapeDtypeStruct((half, ONE), BF)] * 2,
        name="mixed_grads",
        **vmem(63, 6 << 30, 14 << 20),
    )(core, x_own, x_oth, d_own, d_oth, *sums)


def on_device(
    tokens, lengths, cotangent, w_qkv, b_qv, w_out, b_out, w_in, b_in, w_back, b_back,
    gain_one, shift_one, gain_two, shift_two,
):
    micro, _, span, width = tokens.shape
    ff = w_in.shape[1]
    rows = micro * span
    yh = lax.axis_index("yh")
    c = lax.axis_index("c")
    core = c.reshape(1)
    x_own = tokens.reshape(rows, width)
    tie = lax.optimization_barrier
    order = arrival()

    packed = pack(
        w_qkv, w_out, w_in, w_back,
        (b_out, b_back, gain_one, shift_one, gain_two, shift_two, b_in, b_qv),
    )
    x_oth = lax.ppermute(x_own, "yh", SWAP)
    column = gather_column(packed)
    near = [column] + from_ring(column, 0)
    one = jnp.concatenate([part[:, :ONE] for part in near], axis=0)
    two = jnp.concatenate([part[:, ONE:] for part in near], axis=0)
    one_parts = [one] + from_ring(one, 1)
    one_parts, two, x_oth = tie((one_parts, two, x_oth))
    two_parts = [two] + from_ring(two, 1)
    one = sort_rows(order, one_parts)
    one_away = lax.ppermute(one, "c", SWAP)

    limits = jnp.stack([lengths[:, 0] - yh * span, lengths[:, 0] - (1 - yh) * span], axis=1)
    *seen, weights, bias, vec = attend_first(core, limits, x_own, x_oth, one, one_away, micro - 1)
    seen, two_parts = tie((seen, two_parts))
    two = sort_rows(order, two_parts)
    seen, two = tie((seen, two))
    two_away = lax.ppermute(two, "c", SWAP)
    mixed, mixed_oth, context, probs = attend_more(
        limits, x_own, x_oth, weights, bias, micro - 1, seen
    )
    b_in = vec[V_IN : V_IN + 4].reshape(4, 1, width)
    sums, in_sums, ff_mine, ff_away, block_out, d_first, d_context = middle(
        core, vec, b_in, x_own, context, cotangent.reshape(rows, width), two, two_away
    )
    ff_recv = lax.ppermute(ff_away, "c", SWAP)
    inputs = (mixed, mixed_oth, probs, d_context, d_first, weights)
    *part, x_near = attend_back(*inputs, 0, 1)
    x_near = lax.ppermute(x_near, "yh", SWAP)
    ff_recv, part = tie((ff_recv, part))
    ff_own, *ff_sent = split_rows(order, ff_mine, ff_recv)
    ff_sent, part = tie((ff_sent, part))
    ff_got = to_ring(ff_sent, 1)
    d_own, d_oth, sums_qv, d_tokens, x_part = attend_back(*inputs, 1, micro - 1, part)
    x_back = lax.ppermute(x_part, "yh", SWAP)
    d_own, x_near = tie((d_own, x_near))
    g_mine, g_away = mixed_grads(core, x_own, x_oth, d_own, d_oth, sums, in_sums, sums_qv)
    ff_got, g_away = tie((ff_got, g_away))
    g_recv = lax.ppermute(g_away, "c", SWAP)
    ff_own, *ff_sent = fold_rows(ff_own, ff_got)
    ff_got = to_ring(ff_sent, 0)
    g_recv, ff_sent = tie((g_recv, ff_sent))
    g_own, *g_sent = split_rows(order, g_mine, g_recv)
    g_sent, ff_got = tie((g_sent, ff_got))
    g_got = to_ring(g_sent, 1)
    ff_parts = column_parts(ff_own, ff_got)
    d_tokens = d_tokens + jnp.concatenate([x_near, x_back], axis=0).astype(F32)
    g_got, d_tokens = tie((g_got, d_tokens))
    g_own, *g_sent = fold_rows(g_own, g_got)
    g_got = to_ring(g_sent, 0)
    o_in, o_back, o_out = finish_early(ff_parts)
    g_got, o_in, o_back, o_out = tie((g_got, o_in, o_back, o_out))
    o_qkv, lines = finish_late(column_parts(g_own, g_got))
    return (
        block_out.reshape(tokens.shape),
        d_tokens.reshape(tokens.shape),
        o_qkv,
        lines[7],
        o_out,
        lines[0],
        o_in,
        lines[6],
        o_back,
        lines[1],
        lines[2],
        lines[3],
        lines[4],
        lines[5],
    )


def solution(mesh):
    fine = Mesh(mesh.devices.reshape(2, 4, 4, 2, 2), DEVICES)
    pairs = ("yl", "x", "z", "c")
    data = P(None, pairs, "yh", None)
    weight, vector = P(DEVICES, None), P(DEVICES)
    kinds = (weight, vector) * 4
    return jax.shard_map(
        on_device,
        mesh=fine,
        in_specs=(data, P(None, pairs), data) + kinds + (vector,) * 4,
        out_specs=(data, data) + kinds + (vector,) * 4,
        check_vma=False,
    )
```

```python
import functools

import jax
import jax.numpy as jnp
import numpy as np
from jax import lax
from jax.experimental import pallas as pl
from jax.experimental.pallas import tpu as pltpu
from jax.sharding import Mesh, PartitionSpec as P

HD = 64
EPS = 1e-05
F32 = jnp.float32
BF = jnp.bfloat16
DEVICES = ("yl", "x", "z", "c", "yh")
SWAP = ((0, 1), (1, 0))
STEPS = (0, 1, 3, 2)
AT_VEC = 3 * 768
ONE, TWO = AT_VEC + 128, 9 * 768
V_OUT, V_BACK, V_GAIN1, V_SHIFT1, V_GAIN2, V_SHIFT2, V_IN, V_QV = 0, 1, 2, 3, 4, 5, 6, 10


def mm(a, b):
    return lax.dot_general(a, b, (((1,), (0,)), ((), ())), preferred_element_type=F32)


def mm_nt(a, b):
    return lax.dot_general(a, b, (((1,), (1,)), ((), ())), preferred_element_type=F32)


def mm_tn(a, b):
    return lax.dot_general(a, b, (((0,), (0,)), ((), ())), preferred_element_type=F32)


def vmem(mib, flops=0, moved=0):
    return dict(
        compiler_params=pltpu.CompilerParams(vmem_limit_bytes=mib << 20),
        cost_estimate=pl.CostEstimate(flops=flops, bytes_accessed=moved, transcendentals=0),
    )


ROW = [i % 6 for i in range(36)] + [i // 4 for i in range(24)] + [i // 2 for i in range(12)]
COLUMN = [i // 6 for i in range(36)] + [V_IN + i % 4 for i in range(24)] + [V_QV + i % 2 for i in range(12)]


SIZES = (6, 6, 6, 6, 6, 6, 24, 12)


def maps():
    rows, columns = np.zeros((8, 128), np.float32), np.zeros((128, 128), np.float32)
    for i, (r, l) in enumerate(zip(ROW, COLUMN)):
        rows[r, i] = columns[i, l] = 1
    f, place = np.arange(768)[:, None], np.arange(768)[None, :]
    units = (f == 4 * (place % 192) + place // 192).astype(np.float32)
    r, f = np.arange(32)[:, None], np.arange(24)[None, :]
    spread = ((r % 8 < 6) & (f == 4 * (r % 8) + r // 8)).astype(np.float32)
    return rows, columns, units, spread


def pack_kernel(*refs):
    w_qkv, w_out, w_in, w_back = refs[:4]
    vectors = refs[4:12]
    rows, columns, units, spread, out, line, stack = refs[12:]
    width = w_out.shape[1]
    line[...] = jnp.zeros_like(line)
    stack[...] = jnp.zeros_like(stack)
    at = 0
    for size, vector in zip(SIZES, vectors):
        line[0:1, at : at + size] = vector[...].astype(F32).reshape(1, size)
        at += size
    out[:, : 3 * width] = w_qkv[...]
    out[:, AT_VEC:ONE] = mm((line[0:1] * rows[...]).astype(BF), columns[...])[:6].astype(BF)
    for b in range(4):
        stack[8 * b : 8 * b + 6] = w_in[:, b * width : (b + 1) * width].astype(F32)
    moved = mm(stack[...].astype(BF), units[...])
    merged = mm(spread[...], w_back[...])
    for l in range(4):
        for b in range(4):
            start = ONE + l * width + 192 * b
            out[:, start : start + 192] = moved[8 * b : 8 * b + 6, 192 * l : 192 * (l + 1)].astype(BF)
        start = ONE + (4 + l) * width
        out[:, start : start + width] = merged[8 * l : 8 * l + 6].astype(BF)
    out[:, ONE + 8 * width :] = w_out[...]


def pack(w_qkv, w_out, w_in, w_back, vectors):
    rows, columns, units, spread = maps()
    return pl.pallas_call(
        pack_kernel,
        out_shape=jax.ShapeDtypeStruct((6, ONE + TWO), BF),
        scratch_shapes=[pltpu.VMEM((8, 128), F32), pltpu.VMEM((32, 768), F32)],
        name="pack",
    )(
        w_qkv, w_out, w_in, w_back, *vectors, jnp.asarray(rows),
        *(jnp.asarray(part, BF) for part in (columns, units, spread)),
    )


def exact_nt(a, b):
    return lax.dot_general(
        a, b, (((1,), (1,)), ((), ())), precision=lax.Precision.HIGHEST, preferred_element_type=F32
    )


def exact_tn(a, b):
    return lax.dot_general(
        a, b, (((0,), (0,)), ((), ())), precision=lax.Precision.HIGHEST, preferred_element_type=F32
    )


def finish_early_kernel(a, b, d, e, units, spread, g_in, g_back, g_out, stack, rows):
    width = g_back.shape[1]
    total = (a[...] + b[...]) + (d[...] + e[...])
    stack[...] = jnp.zeros_like(stack)
    rows[...] = jnp.zeros_like(rows)
    for l in range(4):
        for b in range(4):
            start = 2 * l * width + 192 * b
            stack[8 * b : 8 * b + 6, 192 * l : 192 * (l + 1)] = total[:, start : start + 192]
        rows[8 * l : 8 * l + 6] = total[:, (2 * l + 1) * width : (2 * l + 2) * width]
    moved = exact_nt(stack[...], units[...])
    for b in range(4):
        g_in[:, b * width : (b + 1) * width] = moved[8 * b : 8 * b + 6]
    g_back[...] = exact_tn(spread[...], rows[...])
    g_out[...] = total[:, 8 * width :]


def finish_early(parts):
    _, _, units, spread = maps()
    return pl.pallas_call(
        finish_early_kernel,
        out_shape=[jax.ShapeDtypeStruct(shape, F32) for shape in ((6, 3072), (24, 768), (6, 768))],
        scratch_shapes=[pltpu.VMEM((32, 768), F32)] * 2,
        name="finish_early",
    )(*parts, jnp.asarray(units), jnp.asarray(spread))


def finish_late_kernel(*refs):
    a, b, d, e, rows, columns, g_qkv = refs[:7]
    vectors, line = refs[7:-1], refs[-1]
    total = (a[...] + b[...]) + (d[...] + e[...])
    g_qkv[...] = total[:, :AT_VEC]
    line[...] = exact_nt(total[:, AT_VEC:], columns[...]) * rows[:6]
    line[0:1] = jnp.sum(line[...], axis=0, keepdims=True)
    at = 0
    for size, vector in zip(SIZES, vectors):
        vector[...] = line[0:1, at : at + size].reshape(size)
        at += size


def finish_late(parts):
    rows, columns, _, _ = maps()
    g_qkv, *vectors = pl.pallas_call(
        finish_late_kernel,
        out_shape=[
            jax.ShapeDtypeStruct(shape, F32) for shape in ((6, AT_VEC),) + tuple((n,) for n in SIZES)
        ],
        scratch_shapes=[pltpu.VMEM((6, 128), F32)],
        name="finish_late",
    )(*parts, jnp.asarray(rows), jnp.asarray(columns))
    return g_qkv, vectors


def interleave(parity):
    row = lax.broadcasted_iota(jnp.int32, (384, 768), 0)
    return (lax.broadcasted_iota(jnp.int32, (384, 768), 1) == 2 * row + parity).astype(BF)


def column_pairs(flip_c, flip_y):
    pairs = []
    for a in (0, 1):
        for b in (0, 1):
            for d in (0, 1):
                pairs.append((b * 4 + (a ^ flip_c) * 2 + (d ^ flip_y), a * 4 + b * 2 + d))
    return pairs


FLIPS = ((0, 0), (0, 1), (1, 0), (1, 1))


def gather_column(shard):
    parts = [lax.ppermute(shard, ("yl", "c", "yh"), column_pairs(*flip)) for flip in FLIPS]
    return jnp.concatenate(parts, axis=0)


def plane_pairs(step, stage):
    pairs = []
    for x in range(4):
        for z in range(4):
            for c in range(2):
                near = (x, (z + step) % 4) if c == stage else ((x + step) % 4, z)
                pairs.append(((near[0] * 4 + near[1]) * 2 + c, (x * 4 + z) * 2 + c))
    return pairs


def from_ring(block, stage):
    return [lax.ppermute(block, ("x", "z", "c"), plane_pairs(step, stage)) for step in STEPS[1:]]


def arrival():
    yl, x, z, c, yh = (lax.axis_index(name) for name in DEVICES)
    j = jnp.arange(384)
    steps = jnp.array(STEPS)
    last, early, flip = steps[j // 96], steps[(j % 96) // 24], (j % 24) // 6
    xx = (x + jnp.where(c == 0, last, early)) % 4
    zz = (z + jnp.where(c == 0, early, last)) % 4
    row = xx * 96 + zz * 24 + (yl ^ (flip // 2)) * 12 + (yh ^ (flip % 2)) * 6 + j % 6
    return (jnp.arange(384)[:, None] == row[None, :]).astype(BF)


def wide(columns):
    return next(n for n in (2304, 3072, columns) if columns % n == 0)


def sort_kernel(order, *refs):
    blocks, out = refs[:-1], refs[-1]
    out[...] = mm(order[...], jnp.concatenate([b[...] for b in blocks], axis=0)).astype(BF)


def sort_rows(order, blocks):
    rows, columns = blocks[0].shape
    lanes = wide(columns)
    return pl.pallas_call(
        sort_kernel,
        grid=(columns // lanes,),
        in_specs=[pl.BlockSpec(order.shape, lambda j: (0, 0))]
        + [pl.BlockSpec((rows, lanes), lambda j: (0, j))] * 4,
        out_specs=pl.BlockSpec((4 * rows, lanes), lambda j: (0, j)),
        out_shape=jax.ShapeDtypeStruct((4 * rows, columns), BF),
        name="sort_rows",
        **vmem(24, 2 * 384 * 384 * columns, 2 * 2 * 384 * columns),
    )(order, *blocks)


def split_kernel(order, mine, recv, *pieces):
    parts, _, lanes = mine.shape
    size = pieces[0].shape[0]
    for p in range(parts):
        total = (mine[p].astype(F32) + recv[p].astype(F32)).astype(BF)
        rows = mm_tn(order[...], total)
        for i, piece in enumerate(pieces):
            piece[:, p * lanes : (p + 1) * lanes] = rows[i * size : (i + 1) * size].astype(piece.dtype)


def split_rows(order, mine, recv):
    if mine.ndim == 2:
        mine, recv = mine[None], recv[None]
    parts, rows, lanes = mine.shape
    batch = 3 if parts % 3 == 0 else 1
    half = pl.BlockSpec((batch, rows, lanes), lambda p: (p, 0, 0))
    piece = pl.BlockSpec((rows // 4, batch * lanes), lambda p: (0, p))
    shape = (rows // 4, parts * lanes)
    return pl.pallas_call(
        split_kernel,
        grid=(parts // batch,),
        in_specs=[pl.BlockSpec(order.shape, lambda p: (0, 0)), half, half],
        out_specs=[piece] * 4,
        out_shape=[jax.ShapeDtypeStruct(shape, BF)] * 4,
        name="split_rows",
        **vmem(24, 2 * 384 * 384 * parts * lanes, 3 * 2 * 384 * parts * lanes),
    )(order, mine, recv)


def fold_kernel(own, a, b, d, *pieces):
    total = own[...].astype(F32) + a[...].astype(F32) + b[...].astype(F32) + d[...].astype(F32)
    size = pieces[0].shape[0]
    for i, piece in enumerate(pieces):
        piece[...] = total[i * size : (i + 1) * size].astype(piece.dtype)


def fold_rows(own, received):
    rows, columns = own.shape
    lanes = wide(columns)
    block = pl.BlockSpec((rows, lanes), lambda j: (0, j))
    piece = pl.BlockSpec((rows // 4, lanes), lambda j: (0, j))
    return pl.pallas_call(
        fold_kernel,
        grid=(columns // lanes,),
        in_specs=[block] * 4,
        out_specs=[piece] * 4,
        out_shape=[jax.ShapeDtypeStruct((rows // 4, columns), kind) for kind in (F32, BF, BF, BF)],
        name="fold_rows",
        **vmem(24, 4 * rows * columns, 11 * rows * columns),
    )(own, *received)


def to_ring(pieces, stage):
    return [
        lax.ppermute(piece, ("x", "z", "c"), [(b, a) for a, b in plane_pairs(step, stage)])
        for step, piece in zip(STEPS[1:], pieces)
    ]


def column_parts(own, received):
    total = own
    for part in received:
        total += part.astype(F32)
    size = total.shape[0] // 4
    parts = []
    for i, flip in enumerate(FLIPS):
        pairs = [(user, owner) for owner, user in column_pairs(*flip)]
        parts.append(lax.ppermute(total[i * size : (i + 1) * size], ("yl", "c", "yh"), pairs))
    return parts


def sum_parts(parts):
    return (parts[0] + parts[1]) + (parts[2] + parts[3])


def apart(pair):
    lane = lax.broadcasted_iota(jnp.int32, pair.shape, 1)
    zero = jnp.zeros_like(pair)
    return jnp.concatenate(
        [jnp.where(lane < HD, pair, zero), jnp.where(lane < HD, zero, pair)], axis=0
    )


def beside(rows, span):
    return jnp.concatenate([rows[:HD, :span], rows[HD:, span:]], axis=0)


def attend_body(g, limits, x_own, x_oth, w_qkv, bias, own, oth, context, probs):
    span, width = context.shape
    key = lax.broadcasted_iota(jnp.int32, (span, 128), 0)
    lane = lax.broadcasted_iota(jnp.int32, (span, 128), 1)
    hidden = jnp.concatenate(
        [jnp.where((key >= limits[g, i]) & (lane == 0), -1e30, 0.0).astype(BF) for i in (0, 1)],
        axis=0,
    )
    unit = (lax.broadcasted_iota(jnp.int32, (2 * span, 128), 1) == 0).astype(BF)
    for j in range(3):
        at = pl.ds(j * width, width)
        own[:, at] = (mm(x_own[...], w_qkv[:, at]) + bias[0:1, at]).astype(BF)
        if j:
            oth[:, pl.ds((j - 1) * width, width)] = (
                mm(x_oth[...], w_qkv[:, at]) + bias[0:1, at]
            ).astype(BF)

    for at in range(0, width, 128):
        q = apart(own[:, pl.ds(at, 128)] * jnp.asarray(0.125, BF))
        k = jnp.concatenate([own[:, pl.ds(at + width, 128)], oth[:, pl.ds(at, 128)]], axis=0)
        v = jnp.concatenate(
            [own[:, pl.ds(at + 2 * width, 128)], oth[:, pl.ds(at + width, 128)]], axis=0
        )
        s = mm_nt(jnp.concatenate([k, hidden], axis=1), jnp.concatenate([q, unit], axis=1))
        e = jnp.exp(s - jnp.max(s, axis=0, keepdims=True))
        p_t = (e * (1.0 / jnp.sum(e, axis=0, keepdims=True))).astype(BF)
        probs[at // HD] = p_t[:, :span]
        probs[at // HD + 1] = p_t[:, span:]
        context[:, pl.ds(at, 128)] = beside(mm(v.T, p_t), span).T.astype(BF)


def attend_first_kernel(
    core, limits, x_own, x_oth, here, there,
    own, oth, context, probs, weights, bias, vec, b_in, arrived,
):
    width = context.shape[1]
    half = width // 2

    @pl.when(pl.program_id(0) == 0)
    def _():
        copies = [
            pltpu.make_async_copy(
                source, weights.at[pl.ds(pl.multiple_of(start * half, half), half)], arrived.at[i]
            )
            for i, (source, start) in enumerate(((here, core[0]), (there, 1 - core[0])))
        ]
        for copy in copies:
            copy.start()
        for copy in copies:
            copy.wait()
        rows = weights[:, 3 * width :].astype(F32).T[:16]
        vec[...] = rows
        for l in range(4):
            b_in[l] = rows[V_IN + l : V_IN + l + 1]
        pairs = rows[V_QV : V_QV + 2].astype(BF)
        sides = [
            mm(pairs[0:1, k : k + half], interleave(0)) + mm(pairs[1:2, k : k + half], interleave(1))
            for k in (0, half)
        ]
        line = jnp.concatenate([sides[0], jnp.zeros((1, width), F32), sides[1]], axis=1)
        bias[...] = jnp.broadcast_to(line, bias.shape)

    attend_body(
        pl.program_id(0), limits, x_own, x_oth, weights, bias, own, oth, context, probs
    )


def attend_more_kernel(first, limits, x_own, x_oth, weights, bias, *rest):
    attend_body(pl.program_id(0) + first, limits, x_own, x_oth, weights, bias, *rest[-4:])


def attend_specs(micro, rows, width, first):
    span, heads = rows // micro, width // HD

    def block(n):
        return pl.BlockSpec((span, n), lambda g, *_: (g + first, 0))

    specs = [
        block(3 * width),
        block(2 * width),
        block(width),
        pl.BlockSpec((None, heads, 2 * span, span), lambda g, *_: (g + first, 0, 0, 0)),
    ]
    shapes = [
        jax.ShapeDtypeStruct((rows, 3 * width), BF),
        jax.ShapeDtypeStruct((rows, 2 * width), BF),
        jax.ShapeDtypeStruct((rows, width), BF),
        jax.ShapeDtypeStruct((micro, heads, 2 * span, span), BF),
    ]
    return block(width), specs, shapes


def attend_first(core, limits, x_own, x_oth, here, there, count):
    rows, width = x_own.shape
    block, specs, shapes = attend_specs(limits.shape[0], rows, width, 0)

    def whole(*shape):
        return pl.BlockSpec(shape, lambda g, *_: (0,) * len(shape))

    return pl.pallas_call(
        attend_first_kernel,
        grid_spec=pltpu.PrefetchScalarGridSpec(
            num_scalar_prefetch=2,
            grid=(count,),
            in_specs=[block, block] + [pl.BlockSpec(memory_space=pl.ANY)] * 2,
            out_specs=specs
            + [whole(width, ONE), whole(8, 3 * width), whole(16, width), whole(4, 1, width)],
            scratch_shapes=[pltpu.SemaphoreType.DMA((2,))],
        ),
        out_shape=shapes
        + [
            jax.ShapeDtypeStruct((width, ONE), BF),
            jax.ShapeDtypeStruct((8, 3 * width), F32),
            jax.ShapeDtypeStruct((16, width), F32),
            jax.ShapeDtypeStruct((4, 1, width), F32),
        ],
        name="attend_first",
        **vmem(56, 10 * count << 30, 8 * count << 20),
    )(core, limits, x_own, x_oth, here, there)


def attend_more(limits, x_own, x_oth, weights, bias, first, earlier):
    micro = limits.shape[0]
    rows, width = x_own.shape
    block, specs, shapes = attend_specs(micro, rows, width, first)

    def whole(*shape):
        return pl.BlockSpec(shape, lambda g, *_: (0,) * len(shape))

    count = micro - first
    return pl.pallas_call(
        functools.partial(attend_more_kernel, first),
        grid_spec=pltpu.PrefetchScalarGridSpec(
            num_scalar_prefetch=1,
            grid=(count,),
            in_specs=[block, block, whole(width, 3 * width), whole(8, 3 * width)]
            + [pl.BlockSpec(memory_space=pl.ANY)] * len(earlier),
            out_specs=specs,
        ),
        out_shape=shapes,
        input_output_aliases={5 + i: i for i in range(len(earlier))},
        name="attend_more",
        **vmem(63, 10 * count << 30, 8 * count << 20),
    )(limits, x_own, x_oth, weights, bias, *earlier)


def attend_back_kernel(own, oth, probs, d_context, d_first, weights, *rest):
    d_own, d_oth, sums, d_tokens, x_part, w_qkv, arrived = rest[-7:]
    span, width = d_context.shape
    begin = pl.program_id(0) == 0
    fetch = pltpu.make_async_copy(weights.at[:, pl.ds(0, 3 * width)], w_qkv, arrived)

    @pl.when(begin)
    def _():
        fetch.start()

    for at in range(0, width, 128):
        q = apart(own[:, pl.ds(at, 128)] * jnp.asarray(0.125, BF))
        k = jnp.concatenate([own[:, pl.ds(at + width, 128)], oth[:, pl.ds(at, 128)]], axis=0)
        v = jnp.concatenate(
            [own[:, pl.ds(at + 2 * width, 128)], oth[:, pl.ds(at + width, 128)]], axis=0
        )
        d_c = apart(d_context[:, pl.ds(at, 128)])
        p_b = jnp.concatenate([probs[at // HD], probs[at // HD + 1]], axis=1)
        p_f = p_b.astype(F32)
        d_p = mm_nt(v, d_c)
        weighted = jnp.sum(p_f * d_p, axis=0, keepdims=True)
        d_s = (p_f * (d_p - weighted)).astype(BF)
        d_own[:, pl.ds(at, 128)] = (beside(mm(k.T, d_s), span).T * 0.125).astype(BF)
        d_k = mm(d_s, q).astype(BF)
        d_v = mm(p_b, d_c).astype(BF)
        d_own[:, pl.ds(at + width, 128)] = d_k[:span]
        d_own[:, pl.ds(at + 2 * width, 128)] = d_v[:span]
        d_oth[:, pl.ds(at, 128)] = d_k[span:]
        d_oth[:, pl.ds(at + width, 128)] = d_v[span:]

    @pl.when(begin)
    def _():
        fetch.wait()

    d_tokens[...] = d_first[...] + mm_nt(d_own[...], w_qkv[...])
    x_part[...] = (
        mm_nt(d_oth[:, :width], w_qkv[:, width : 2 * width])
        + mm_nt(d_oth[:, width:], w_qkv[:, 2 * width :])
    ).astype(BF)
    of_queries = jnp.sum(d_own[:, :width].astype(F32), axis=0, keepdims=True)
    of_values = jnp.sum(
        d_own[:, 2 * width :].astype(F32) + d_oth[:, width:].astype(F32), axis=0, keepdims=True
    )
    sums[0] = rows_of(of_queries, of_values)


def attend_back(own, oth, probs, d_context, d_first, weights, first, count, earlier=()):
    micro, heads, _, span = probs.shape
    rows, width = d_context.shape

    def block(n):
        return pl.BlockSpec((span, n), lambda g: (g + first, 0))

    return pl.pallas_call(
        attend_back_kernel,
        grid=(count,),
        in_specs=[
            block(3 * width),
            block(2 * width),
            pl.BlockSpec((None, heads, 2 * span, span), lambda g: (g + first, 0, 0, 0)),
            block(width),
            block(width),
        ]
        + [pl.BlockSpec(memory_space=pl.ANY)] * (1 + len(earlier)),
        out_specs=[block(3 * width), block(2 * width)]
        + [pl.BlockSpec((1, 8, width), lambda g: (g + first, 0, 0)), block(width)]
        + [pl.BlockSpec((span, width), lambda g: (g, 0))],
        out_shape=[
            jax.ShapeDtypeStruct((rows, 3 * width), BF),
            jax.ShapeDtypeStruct((rows, 2 * width), BF),
            jax.ShapeDtypeStruct((micro, 8, width), F32),
            jax.ShapeDtypeStruct((rows, width), F32),
            jax.ShapeDtypeStruct((count * span, width), BF),
        ],
        input_output_aliases={6 + i: i for i in range(len(earlier))},
        scratch_shapes=[pltpu.VMEM((width, 3 * width), BF), pltpu.SemaphoreType.DMA],
        name="attend_back",
        **vmem(52, 9 * count << 30, 8 * count << 20),
    )(own, oth, probs, d_context, d_first, weights, *earlier)


def norm_parts(value):
    centre = value - jnp.mean(value, axis=-1, keepdims=True)
    inverse = lax.rsqrt(jnp.mean(centre * centre, axis=-1, keepdims=True) + EPS)
    return centre * inverse, inverse


def norm_back(grad, hat, inverse, gain):
    scaled = grad * gain
    return inverse * (
        scaled
        - jnp.mean(scaled, axis=-1, keepdims=True)
        - hat * jnp.mean(scaled * hat, axis=-1, keepdims=True)
    )


def rows_of(*terms):
    return jnp.concatenate(terms + (jnp.zeros((8 - len(terms), terms[0].shape[1]), F32),), axis=0)


def middle_kernel(
    core, vec, b_in, x, context, cot, w_mine, w_away,
    sums, in_sums, grad_mine, grad_away, block_out, d_first, d_context,
    x_in, c_in, cot_in, normed_b, hat_one, inv_one, outer, active, slope, d_outer, d_normed, result,
    d_ctx, weights, grads, from_rows, from_weights, to_rows, to_grads,
):
    t = pl.program_id(0)
    rows, width = x_in.shape
    half, parts, step = width // 2, active.shape[0], rows // 3
    mine, away = pl.multiple_of(core[0] * half, half), pl.multiple_of((1 - core[0]) * half, half)
    blocks = [pl.ds(r * step, step) for r in range(3)]
    w_out = weights.at[2 * parts]

    def row(i):
        return vec[i : i + 1, :]

    def fetch(i):
        lanes = pl.ds(i * width, width)
        return [
            pltpu.make_async_copy(
                source.at[:, lanes], weights.at[i, pl.ds(start, half)], from_weights.at[i, k]
            )
            for k, (source, start) in enumerate(((w_mine, mine), (w_away, away)))
        ]

    def rows_in(r, *which):
        ends = ((context, c_in), (x, x_in), (cot, cot_in))
        return [
            pltpu.make_async_copy(ends[k][0].at[blocks[r]], ends[k][1].at[blocks[r]], from_rows.at[k, r])
            for k in which
        ]

    def rows_out(k, r):
        source, into = ((result, block_out), (d_normed, d_first), (d_ctx, d_context))[k]
        return pltpu.make_async_copy(source.at[blocks[r]], into.at[blocks[r]], to_rows.at[k, r])

    def grads_out(i, slot, count):
        return [
            pltpu.make_async_copy(
                grads.at[slot, k, pl.ds(0, count)], into.at[pl.ds(i, count)], to_grads.at[slot, k]
            )
            for k, into in enumerate((grad_mine, grad_away))
        ]

    def wait_part(i):
        for copy in fetch(i) + fetch(parts + i):
            copy.wait()

    def forward(l):
        w_in, w_back = weights.at[l], weights.at[parts + l]

        def hidden(r):
            return mm(normed_b[blocks[r]], w_in[...]) + b_in[0]

        def bend(r, inner):
            phi = 0.5 + 0.5 * lax.erf(inner * (0.5**0.5))
            act = (inner * phi).astype(BF)
            active[l, blocks[r]] = act
            slope[l, blocks[r]] = phi + inner * jnp.exp(-0.5 * inner * inner) * 0.3989422804014327
            return act

        inner = [hidden(0), hidden(1)]
        for r in range(3):
            act = bend(r, inner[r])
            if r == 0:
                inner.append(hidden(2))
            outer[blocks[r]] += mm(act, w_back[...])

    def backward(l):
        w_in, w_back = weights.at[l], weights.at[parts + l]

        def back(r):
            return mm_nt(d_outer[blocks[r]], w_back[...])

        d_act = [back(0), back(1)]
        pieces = []
        bias = jnp.zeros((1, width), F32)
        for r, at in enumerate(blocks):
            d_inner = (d_act[r] * slope[l, at]).astype(BF)
            pieces.append(d_inner)
            if r == 0:
                d_act.append(back(2))
            bias += jnp.sum(d_inner.astype(F32), axis=0, keepdims=True)
            d_normed[at] += mm_nt(d_inner, w_in[...])
        d_inner = jnp.concatenate(pieces, axis=0)
        in_sums[0] = bias
        slot = l % 2 if isinstance(l, int) else lax.rem(l, 2)
        if not isinstance(l, int):

            @pl.when(l >= 2)
            def _():
                for copy in grads_out(2 * l - 4, slot, 2):
                    copy.wait()

        for k, start in enumerate((mine, away)):
            cols = pl.ds(start, half)
            grads[slot, k, 0] = mm_tn(normed_b[:, cols], d_inner).astype(BF)
            grads[slot, k, 1] = mm_tn(active[l, :, cols], d_outer[...]).astype(BF)
        for copy in grads_out(2 * l, slot, 2):
            copy.start()

    @pl.when(t == 0)
    def _():
        for copy in fetch(2 * parts):
            copy.start()
        for r in range(3):
            for copy in rows_in(r, 0, 1):
                copy.start()
        for i in range(parts):
            for copy in fetch(i) + fetch(parts + i):
                copy.start()
        for r in range(3):
            rows_in(r, 2)[0].start()
        for copy in fetch(2 * parts):
            copy.wait()
        wait_part(0)
        for r, at in enumerate(blocks):
            for copy in rows_in(r, 0, 1):
                copy.wait()
            hat, inverse = norm_parts(x_in[at].astype(F32) + mm(c_in[at], w_out[...]) + row(V_OUT))
            hat_one[at] = hat
            inv_one[at] = jnp.broadcast_to(inverse, (step, 128))
            value = hat * row(V_GAIN1) + row(V_SHIFT1)
            normed_b[at] = value.astype(BF)
            outer[at] = value + row(V_BACK)
        forward(0)

    @pl.when((t > 0) & (t < parts))
    def _():
        for i in range(1, parts):

            @pl.when(t == i)
            def _():
                wait_part(i)

        forward(t)

    @pl.when(t == parts)
    def _():
        total = [jnp.zeros((1, width), F32) for _ in range(3)]
        for r, at in enumerate(blocks):
            rows_in(r, 2)[0].wait()
            hat, inverse = norm_parts(outer[at])
            result[at] = (hat * row(V_GAIN2) + row(V_SHIFT2)).astype(BF)
            rows_out(0, r).start()
            grad = cot_in[at].astype(F32)
            d_second = norm_back(grad, hat, inverse, row(V_GAIN2))
            d_b = d_second.astype(BF)
            d_outer[at] = d_b
            d_normed[at] = d_second
            for i, term in enumerate((d_b.astype(F32), grad * hat, grad)):
                total[i] += jnp.sum(term, axis=0, keepdims=True)
        for i, term in zip((V_BACK, V_GAIN2, V_SHIFT2), total):
            sums[i : i + 1] = term
        backward(0)

    @pl.when((t > parts) & (t < 2 * parts))
    def _():
        backward(t - parts)

    @pl.when(t == 2 * parts)
    def _():
        total = [jnp.zeros((1, width), F32) for _ in range(3)]
        for r, at in enumerate(blocks):
            grad, hat = d_normed[at], hat_one[at]
            back = norm_back(grad, hat, inv_one[at, 0:1], row(V_GAIN1))
            d_normed[at] = back
            rows_out(1, r).start()
            d_b = back.astype(BF)
            d_outer[at] = d_b
            for i, term in enumerate((d_b.astype(F32), grad * hat, grad)):
                total[i] += jnp.sum(term, axis=0, keepdims=True)
            d_ctx[at] = mm_nt(d_b, w_out[...]).astype(BF)
            rows_out(2, r).start()
        for i, term in zip((V_OUT, V_GAIN1, V_SHIFT1), total):
            sums[i : i + 1] = term
        for copy in grads_out(2 * parts - 4, parts % 2, 2):
            copy.wait()
        for k, start in enumerate((mine, away)):
            grads[parts % 2, k, 0] = mm_tn(c_in[:, pl.ds(start, half)], d_outer[...]).astype(BF)
        for copy in grads_out(2 * parts, parts % 2, 1):
            copy.start()
        for copy in grads_out(2 * parts - 2, (parts - 1) % 2, 2) + grads_out(2 * parts, parts % 2, 1):
            copy.wait()
        for k in range(3):
            for r in range(3):
                rows_out(k, r).wait()


def middle(core, vec, b_in, x, context, cot, w_mine, w_away):
    rows, width = x.shape
    parts = b_in.shape[0]
    half = width // 2

    def whole(*shape):
        return pl.BlockSpec(shape, lambda t, *_: (0,) * len(shape))

    def later(t):
        return jnp.clip(t - parts, 0, parts - 1)

    anywhere = pl.BlockSpec(memory_space=pl.ANY)
    grads = ((2 * parts + 1, half, width), BF)
    shapes = (
        ((8, width), F32), ((parts, 1, width), F32), grads, grads,
        ((rows, width), BF), ((rows, width), F32), ((rows, width), BF),
    )
    return pl.pallas_call(
        middle_kernel,
        grid_spec=pltpu.PrefetchScalarGridSpec(
            num_scalar_prefetch=1,
            grid=(2 * parts + 1,),
            in_specs=[
                whole(16, width),
                pl.BlockSpec((1, 1, width), lambda t, *_: (jnp.minimum(t, parts - 1), 0, 0)),
            ]
            + [anywhere] * 5,
            out_specs=[whole(8, width)]
            + [pl.BlockSpec((1, 1, width), lambda t, *_: (later(t), 0, 0))]
            + [anywhere] * 5,
            scratch_shapes=[pltpu.VMEM((rows, width), BF)] * 4
            + [pltpu.VMEM((rows, width), F32), pltpu.VMEM((rows, 128), F32)]
            + [pltpu.VMEM((rows, width), F32)]
            + [pltpu.VMEM((parts, rows, width), BF), pltpu.VMEM((parts, rows, width), F32)]
            + [pltpu.VMEM((rows, width), BF), pltpu.VMEM((rows, width), F32)]
            + [pltpu.VMEM((rows, width), BF)] * 2
            + [
                pltpu.VMEM((2 * parts + 1, width, width), BF),
                pltpu.VMEM((2, 2, 2, half, width), BF),
                pltpu.SemaphoreType.DMA((3, 3)),
                pltpu.SemaphoreType.DMA((2 * parts + 1, 2)),
                pltpu.SemaphoreType.DMA((3, 3)),
                pltpu.SemaphoreType.DMA((2, 2)),
            ],
        ),
        out_shape=[jax.ShapeDtypeStruct(*shape) for shape in shapes],
        name="middle",
        **vmem(63, 24 << 30, 30 << 20),
    )(core, vec, b_in, x, context, cot, w_mine, w_away)


def mixed_grads_kernel(
    core, x_own, x_oth, d_own, d_oth, sums, in_sums, sums_qv, mine, away, columns, result, done,
):
    j = pl.program_id(0)
    width = x_own.shape[1]
    half = width // 2
    sides = (core[0], 1 - core[0])

    def send(k, start, lanes):
        return pltpu.make_async_copy(
            result.at[k, :, pl.ds(start, lanes)], (mine, away)[k].at[:, pl.ds(start, lanes)],
            done.at[k, start // width],
        )

    def sends():
        return [send(k, i * width, width if i < 3 else ONE - AT_VEC) for k in (0, 1) for i in range(4)]

    def place(k):
        return pl.ds(pl.multiple_of(sides[k] * half, half), half)

    @pl.when(j == 0)
    def _():
        qv = (sums_qv[0] + sums_qv[1] + sums_qv[2]).astype(BF)
        split = [
            jnp.concatenate([mm_nt(qv[i : i + 1], interleave(parity)) for i in (0, 1)], axis=1)
            for parity in (0, 1)
        ]
        rows = [sums[0:6]] + [in_sums[i] for i in range(4)] + split
        columns[...] = jnp.concatenate(rows + [jnp.zeros((116, width), F32)], axis=0).T.astype(BF)
        for k in (0, 1):
            result[k, :, AT_VEC:] = columns[place(k)]
            result[k, :, :width] = mm_tn(x_own[:, place(k)], d_own[...]).astype(BF)
            send(k, AT_VEC, ONE - AT_VEC).start()
            send(k, 0, width).start()

    for i in (1, 2):

        @pl.when(j == i)
        def _():
            for k in (0, 1):
                both = mm_tn(x_own[:, place(k)], d_own[...]) + mm_tn(x_oth[:, place(k)], d_oth[...])
                result[k, :, i * width : (i + 1) * width] = both.astype(BF)
                send(k, i * width, width).start()

    @pl.when(j == 2)
    def _():
        for copy in sends():
            copy.wait()


def mixed_grads(core, x_own, x_oth, d_own, d_oth, *sums):
    rows, width = x_own.shape
    half = width // 2

    def whole(*shape):
        return pl.BlockSpec(shape, lambda j, *_: (0,) * len(shape))

    own = pl.BlockSpec((rows, width), lambda j, *_: (0, j))
    oth = pl.BlockSpec((rows, width), lambda j, *_: (0, jnp.maximum(j - 1, 0)))
    return pl.pallas_call(
        mixed_grads_kernel,
        grid_spec=pltpu.PrefetchScalarGridSpec(
            num_scalar_prefetch=1,
            grid=(3,),
            in_specs=[whole(rows, width), whole(rows, width), own, oth]
            + [whole(*part.shape) for part in sums],
            out_specs=[pl.BlockSpec(memory_space=pl.ANY)] * 2,
            scratch_shapes=[
                pltpu.VMEM((width, 128), BF),
                pltpu.VMEM((2, half, ONE), BF),
                pltpu.SemaphoreType.DMA((2, 4)),
            ],
        ),
        out_shape=[jax.ShapeDtypeStruct((half, ONE), BF)] * 2,
        name="mixed_grads",
        **vmem(48, 6 << 30, 14 << 20),
    )(core, x_own, x_oth, d_own, d_oth, *sums)


def on_device(
    tokens, lengths, cotangent, w_qkv, b_qv, w_out, b_out, w_in, b_in, w_back, b_back,
    gain_one, shift_one, gain_two, shift_two,
):
    micro, _, span, width = tokens.shape
    ff = w_in.shape[1]
    rows = micro * span
    yh = lax.axis_index("yh")
    c = lax.axis_index("c")
    core = c.reshape(1)
    x_own = tokens.reshape(rows, width)
    tie = lax.optimization_barrier
    order = arrival()

    packed = pack(
        w_qkv, w_out, w_in, w_back,
        (b_out, b_back, gain_one, shift_one, gain_two, shift_two, b_in, b_qv),
    )
    x_oth = lax.ppermute(x_own, "yh", SWAP)
    column = gather_column(packed)
    near = [column] + from_ring(column, 0)
    one = jnp.concatenate([part[:, :ONE] for part in near], axis=0)
    two = jnp.concatenate([part[:, ONE:] for part in near], axis=0)
    one_parts = [one] + from_ring(one, 1)
    limits = jnp.stack([lengths[:, 0] - yh * span, lengths[:, 0] - (1 - yh) * span], axis=1)
    one_parts, two, x_oth, limits = tie((one_parts, two, x_oth, limits))
    two_parts = [two] + from_ring(two, 1)
    one = sort_rows(order, one_parts)
    one_away = lax.ppermute(one, "c", SWAP)

    *seen, weights, bias, vec, b_in = attend_first(core, limits, x_own, x_oth, one, one_away, micro - 1)
    seen, two_parts = tie((seen, two_parts))
    two = sort_rows(order, two_parts)
    seen, two = tie((seen, two))
    two_away = lax.ppermute(two, "c", SWAP)
    mixed, mixed_oth, context, probs = attend_more(
        limits, x_own, x_oth, weights, bias, micro - 1, seen
    )
    sums, in_sums, ff_mine, ff_away, block_out, d_first, d_context = middle(
        core, vec, b_in, x_own, context, cotangent.reshape(rows, width), two, two_away
    )
    ff_recv = lax.ppermute(ff_away, "c", SWAP)
    inputs = (mixed, mixed_oth, probs, d_context, d_first, weights)
    *part, x_near = attend_back(*inputs, 0, 1)
    x_near = lax.ppermute(x_near, "yh", SWAP)
    ff_recv, part = tie((ff_recv, part))
    ff_own, *ff_sent = split_rows(order, ff_mine, ff_recv)
    ff_sent, part = tie((ff_sent, part))
    ff_got = to_ring(ff_sent, 1)
    d_own, d_oth, sums_qv, d_tokens, x_part = attend_back(*inputs, 1, micro - 1, part)
    x_back = lax.ppermute(x_part, "yh", SWAP)
    d_own, x_near = tie((d_own, x_near))
    g_mine, g_away = mixed_grads(core, x_own, x_oth, d_own, d_oth, sums, in_sums, sums_qv)
    ff_got, g_away = tie((ff_got, g_away))
    g_recv = lax.ppermute(g_away, "c", SWAP)
    ff_own, *ff_sent = fold_rows(ff_own, ff_got)
    ff_got = to_ring(ff_sent, 0)
    g_recv, ff_sent = tie((g_recv, ff_sent))
    g_own, *g_sent = split_rows(order, g_mine, g_recv)
    g_sent, ff_got, x_back = tie((g_sent, ff_got, x_back))
    g_got = to_ring(g_sent, 1)
    ff_parts = column_parts(ff_own, ff_got)
    d_tokens = d_tokens + jnp.concatenate([x_near, x_back], axis=0).astype(F32)
    g_got, d_tokens = tie((g_got, d_tokens))
    g_own, *g_sent = fold_rows(g_own, g_got)
    g_got = to_ring(g_sent, 0)
    o_in, o_back, o_out = finish_early(ff_parts)
    g_got, o_in, o_back, o_out = tie((g_got, o_in, o_back, o_out))
    o_qkv, lines = finish_late(column_parts(g_own, g_got))
    return (
        block_out.reshape(tokens.shape),
        d_tokens.reshape(tokens.shape),
        o_qkv,
        lines[7],
        o_out,
        lines[0],
        o_in,
        lines[6],
        o_back,
        lines[1],
        lines[2],
        lines[3],
        lines[4],
        lines[5],
    )


def solution(mesh):
    fine = Mesh(mesh.devices.reshape(2, 4, 4, 2, 2), DEVICES)
    pairs = ("yl", "x", "z", "c")
    data = P(None, pairs, "yh", None)
    weight, vector = P(DEVICES, None), P(DEVICES)
    kinds = (weight, vector) * 4
    return jax.shard_map(
        on_device,
        mesh=fine,
        in_specs=(data, P(None, pairs), data) + kinds + (vector,) * 4,
        out_specs=(data, data) + kinds + (vector,) * 4,
        check_vma=False,
    )
```

```python
import functools

import jax
import jax.numpy as jnp
import numpy as np
from jax import lax
from jax.experimental import pallas as pl
from jax.experimental.pallas import tpu as pltpu
from jax.sharding import Mesh, PartitionSpec as P

HD = 64
EPS = 1e-05
F32 = jnp.float32
BF = jnp.bfloat16
DEVICES = ("yl", "x", "z", "c", "yh")
SWAP = ((0, 1), (1, 0))
STEPS = (0, 1, 3, 2)
AT_VEC = 3 * 768
ONE, TWO = AT_VEC + 128, 9 * 768
V_OUT, V_BACK, V_GAIN1, V_SHIFT1, V_GAIN2, V_SHIFT2, V_IN, V_QV = 0, 1, 2, 3, 4, 5, 6, 10


def mm(a, b):
    return lax.dot_general(a, b, (((1,), (0,)), ((), ())), preferred_element_type=F32)


def mm_nt(a, b):
    return lax.dot_general(a, b, (((1,), (1,)), ((), ())), preferred_element_type=F32)


def mm_tn(a, b):
    return lax.dot_general(a, b, (((0,), (0,)), ((), ())), preferred_element_type=F32)


def vmem(mib, flops=0, moved=0):
    return dict(
        compiler_params=pltpu.CompilerParams(vmem_limit_bytes=mib << 20),
        cost_estimate=pl.CostEstimate(flops=flops, bytes_accessed=moved, transcendentals=0),
    )


ROW = [i % 6 for i in range(36)] + [i // 4 for i in range(24)] + [i // 2 for i in range(12)]
COLUMN = [i // 6 for i in range(36)] + [V_IN + i % 4 for i in range(24)] + [V_QV + i % 2 for i in range(12)]


SIZES = (6, 6, 6, 6, 6, 6, 24, 12)


def maps():
    rows, columns = np.zeros((8, 128), np.float32), np.zeros((128, 128), np.float32)
    for i, (r, l) in enumerate(zip(ROW, COLUMN)):
        rows[r, i] = columns[i, l] = 1
    f, place = np.arange(768)[:, None], np.arange(768)[None, :]
    units = (f == 4 * (place % 192) + place // 192).astype(np.float32)
    r, f = np.arange(32)[:, None], np.arange(24)[None, :]
    spread = ((r % 8 < 6) & (f == 4 * (r % 8) + r // 8)).astype(np.float32)
    return rows, columns, units, spread


def pack_kernel(*refs):
    w_qkv, w_out, w_in, w_back = refs[:4]
    vectors = refs[4:12]
    rows, columns, units, spread, out, line, stack = refs[12:]
    width = w_out.shape[1]
    line[...] = jnp.zeros_like(line)
    stack[...] = jnp.zeros_like(stack)
    at = 0
    for size, vector in zip(SIZES, vectors):
        line[0:1, at : at + size] = vector[...].astype(F32).reshape(1, size)
        at += size
    out[:, : 3 * width] = w_qkv[...]
    out[:, AT_VEC:ONE] = mm((line[0:1] * rows[...]).astype(BF), columns[...])[:6].astype(BF)
    for b in range(4):
        stack[8 * b : 8 * b + 6] = w_in[:, b * width : (b + 1) * width].astype(F32)
    moved = mm(stack[...].astype(BF), units[...])
    merged = mm(spread[...], w_back[...])
    for l in range(4):
        for b in range(4):
            start = ONE + l * width + 192 * b
            out[:, start : start + 192] = moved[8 * b : 8 * b + 6, 192 * l : 192 * (l + 1)].astype(BF)
        start = ONE + (4 + l) * width
        out[:, start : start + width] = merged[8 * l : 8 * l + 6].astype(BF)
    out[:, ONE + 8 * width :] = w_out[...]


def pack(w_qkv, w_out, w_in, w_back, vectors):
    rows, columns, units, spread = maps()
    return pl.pallas_call(
        pack_kernel,
        out_shape=jax.ShapeDtypeStruct((6, ONE + TWO), BF),
        scratch_shapes=[pltpu.VMEM((8, 128), F32), pltpu.VMEM((32, 768), F32)],
        name="pack",
    )(
        w_qkv, w_out, w_in, w_back, *vectors, jnp.asarray(rows),
        *(jnp.asarray(part, BF) for part in (columns, units, spread)),
    )


def exact_nt(a, b):
    return lax.dot_general(
        a, b, (((1,), (1,)), ((), ())), precision=lax.Precision.HIGHEST, preferred_element_type=F32
    )


def exact_tn(a, b):
    return lax.dot_general(
        a, b, (((0,), (0,)), ((), ())), precision=lax.Precision.HIGHEST, preferred_element_type=F32
    )


def thirds(value):
    high = value.astype(BF)
    rest = value - high.astype(F32)
    middle_ = rest.astype(BF)
    return jnp.concatenate([high, middle_, (rest - middle_.astype(F32)).astype(BF)], axis=0)


def finish_early_kernel(a, b, d, e, units, spread, g_in, g_back, g_out, stack, rows):
    width = g_back.shape[1]
    total = (a[...] + b[...]) + (d[...] + e[...])
    stack[...] = jnp.zeros_like(stack)
    rows[...] = jnp.zeros_like(rows)
    for l in range(4):
        for b_ in range(4):
            start = 2 * l * width + 192 * b_
            stack[8 * b_ : 8 * b_ + 6, 192 * l : 192 * (l + 1)] = total[:, start : start + 192]
        rows[8 * l : 8 * l + 6] = total[:, (2 * l + 1) * width : (2 * l + 2) * width]
    moved = mm_nt(thirds(stack[...]), units[...])
    moved = moved[:32] + moved[32:64] + moved[64:]
    for b_ in range(4):
        g_in[:, b_ * width : (b_ + 1) * width] = moved[8 * b_ : 8 * b_ + 6]
    g_back[...] = exact_tn(spread[...], rows[...])
    g_out[...] = total[:, 8 * width :]


def finish_early(parts):
    _, _, units, spread = maps()
    return pl.pallas_call(
        finish_early_kernel,
        out_shape=[jax.ShapeDtypeStruct(shape, F32) for shape in ((6, 3072), (24, 768), (6, 768))],
        scratch_shapes=[pltpu.VMEM((32, 768), F32)] * 2,
        name="finish_early",
    )(*parts, jnp.asarray(units, BF), jnp.asarray(spread))


def finish_late_kernel(*refs):
    a, b, d, e, rows, columns, g_qkv = refs[:7]
    vectors, line = refs[7:-1], refs[-1]
    total = (a[...] + b[...]) + (d[...] + e[...])
    g_qkv[...] = total[:, :AT_VEC]
    line[...] = exact_nt(total[:, AT_VEC:], columns[...]) * rows[:6]
    line[0:1] = jnp.sum(line[...], axis=0, keepdims=True)
    at = 0
    for size, vector in zip(SIZES, vectors):
        vector[...] = line[0:1, at : at + size].reshape(size)
        at += size


def finish_late(parts):
    rows, columns, _, _ = maps()
    g_qkv, *vectors = pl.pallas_call(
        finish_late_kernel,
        out_shape=[
            jax.ShapeDtypeStruct(shape, F32) for shape in ((6, AT_VEC),) + tuple((n,) for n in SIZES)
        ],
        scratch_shapes=[pltpu.VMEM((6, 128), F32)],
        name="finish_late",
    )(*parts, jnp.asarray(rows), jnp.asarray(columns))
    return g_qkv, vectors


def interleave(parity):
    row = lax.broadcasted_iota(jnp.int32, (384, 768), 0)
    return (lax.broadcasted_iota(jnp.int32, (384, 768), 1) == 2 * row + parity).astype(BF)


def column_pairs(flip_c, flip_y):
    pairs = []
    for a in (0, 1):
        for b in (0, 1):
            for d in (0, 1):
                pairs.append((b * 4 + (a ^ flip_c) * 2 + (d ^ flip_y), a * 4 + b * 2 + d))
    return pairs


FLIPS = ((0, 0), (0, 1), (1, 0), (1, 1))


def gather_column(shard):
    parts = [lax.ppermute(shard, ("yl", "c", "yh"), column_pairs(*flip)) for flip in FLIPS]
    return jnp.concatenate(parts, axis=0)


def plane_pairs(step, stage):
    pairs = []
    for x in range(4):
        for z in range(4):
            for c in range(2):
                near = (x, (z + step) % 4) if c == stage else ((x + step) % 4, z)
                pairs.append(((near[0] * 4 + near[1]) * 2 + c, (x * 4 + z) * 2 + c))
    return pairs


def from_ring(block, stage):
    return [lax.ppermute(block, ("x", "z", "c"), plane_pairs(step, stage)) for step in STEPS[1:]]


def arrival():
    yl, x, z, c, yh = (lax.axis_index(name) for name in DEVICES)
    j = jnp.arange(384)
    steps = jnp.array(STEPS)
    last, early, flip = steps[j // 96], steps[(j % 96) // 24], (j % 24) // 6
    xx = (x + jnp.where(c == 0, last, early)) % 4
    zz = (z + jnp.where(c == 0, early, last)) % 4
    row = xx * 96 + zz * 24 + (yl ^ (flip // 2)) * 12 + (yh ^ (flip % 2)) * 6 + j % 6
    return (jnp.arange(384)[:, None] == row[None, :]).astype(BF)


def wide(columns):
    return next(n for n in (2304, 3072, columns) if columns % n == 0)


def sort_kernel(order, *refs):
    blocks, out = refs[:-1], refs[-1]
    out[...] = mm(order[...], jnp.concatenate([b[...] for b in blocks], axis=0)).astype(BF)


def sort_rows(order, blocks):
    rows, columns = blocks[0].shape
    lanes = wide(columns)
    return pl.pallas_call(
        sort_kernel,
        grid=(columns // lanes,),
        in_specs=[pl.BlockSpec(order.shape, lambda j: (0, 0))]
        + [pl.BlockSpec((rows, lanes), lambda j: (0, j))] * 4,
        out_specs=pl.BlockSpec((4 * rows, lanes), lambda j: (0, j)),
        out_shape=jax.ShapeDtypeStruct((4 * rows, columns), BF),
        name="sort_rows",
        **vmem(24, 2 * 384 * 384 * columns, 2 * 2 * 384 * columns),
    )(order, *blocks)


def split_kernel(order, mine, recv, *pieces):
    parts, _, lanes = mine.shape
    size = pieces[0].shape[0]
    for p in range(parts):
        total = (mine[p].astype(F32) + recv[p].astype(F32)).astype(BF)
        rows = mm_tn(order[...], total)
        for i, piece in enumerate(pieces):
            piece[:, p * lanes : (p + 1) * lanes] = rows[i * size : (i + 1) * size].astype(piece.dtype)


def split_rows(order, mine, recv):
    if mine.ndim == 2:
        mine, recv = mine[None], recv[None]
    parts, rows, lanes = mine.shape
    batch = 3 if parts % 3 == 0 else 1
    half = pl.BlockSpec((batch, rows, lanes), lambda p: (p, 0, 0))
    piece = pl.BlockSpec((rows // 4, batch * lanes), lambda p: (0, p))
    shape = (rows // 4, parts * lanes)
    return pl.pallas_call(
        split_kernel,
        grid=(parts // batch,),
        in_specs=[pl.BlockSpec(order.shape, lambda p: (0, 0)), half, half],
        out_specs=[piece] * 4,
        out_shape=[jax.ShapeDtypeStruct(shape, BF)] * 4,
        name="split_rows",
        **vmem(24, 2 * 384 * 384 * parts * lanes, 3 * 2 * 384 * parts * lanes),
    )(order, mine, recv)


def fold_kernel(own, a, b, d, *pieces):
    total = own[...].astype(F32) + a[...].astype(F32) + b[...].astype(F32) + d[...].astype(F32)
    size = pieces[0].shape[0]
    for i, piece in enumerate(pieces):
        piece[...] = total[i * size : (i + 1) * size].astype(piece.dtype)


def fold_rows(own, received):
    rows, columns = own.shape
    lanes = wide(columns)
    block = pl.BlockSpec((rows, lanes), lambda j: (0, j))
    piece = pl.BlockSpec((rows // 4, lanes), lambda j: (0, j))
    return pl.pallas_call(
        fold_kernel,
        grid=(columns // lanes,),
        in_specs=[block] * 4,
        out_specs=[piece] * 4,
        out_shape=[jax.ShapeDtypeStruct((rows // 4, columns), kind) for kind in (F32, BF, BF, BF)],
        name="fold_rows",
        **vmem(24, 4 * rows * columns, 11 * rows * columns),
    )(own, *received)


def to_ring(pieces, stage):
    return [
        lax.ppermute(piece, ("x", "z", "c"), [(b, a) for a, b in plane_pairs(step, stage)])
        for step, piece in zip(STEPS[1:], pieces)
    ]


def column_parts(own, received):
    total = own
    for part in received:
        total += part.astype(F32)
    size = total.shape[0] // 4
    parts = []
    for i, flip in enumerate(FLIPS):
        pairs = [(user, owner) for owner, user in column_pairs(*flip)]
        parts.append(lax.ppermute(total[i * size : (i + 1) * size], ("yl", "c", "yh"), pairs))
    return parts


def sum_parts(parts):
    return (parts[0] + parts[1]) + (parts[2] + parts[3])


def apart(pair):
    lane = lax.broadcasted_iota(jnp.int32, pair.shape, 1)
    zero = jnp.zeros_like(pair)
    return jnp.concatenate(
        [jnp.where(lane < HD, pair, zero), jnp.where(lane < HD, zero, pair)], axis=0
    )


def beside(rows, span):
    return jnp.concatenate([rows[:HD, :span], rows[HD:, span:]], axis=0)


def attend_body(g, limits, x_own, x_oth, w_qkv, bias, own, oth, context, probs):
    span, width = context.shape
    key = lax.broadcasted_iota(jnp.int32, (span, 128), 0)
    lane = lax.broadcasted_iota(jnp.int32, (span, 128), 1)
    hidden = jnp.concatenate(
        [jnp.where((key >= limits[g, i]) & (lane == 0), -1e30, 0.0).astype(BF) for i in (0, 1)],
        axis=0,
    )
    unit = (lax.broadcasted_iota(jnp.int32, (2 * span, 128), 1) == 0).astype(BF)
    for j in range(3):
        at = pl.ds(j * width, width)
        own[:, at] = (mm(x_own[...], w_qkv[:, at]) + bias[0:1, at]).astype(BF)
        if j:
            oth[:, pl.ds((j - 1) * width, width)] = (
                mm(x_oth[...], w_qkv[:, at]) + bias[0:1, at]
            ).astype(BF)

    for at in range(0, width, 128):
        q = apart(own[:, pl.ds(at, 128)] * jnp.asarray(0.125, BF))
        k = jnp.concatenate([own[:, pl.ds(at + width, 128)], oth[:, pl.ds(at, 128)]], axis=0)
        v = jnp.concatenate(
            [own[:, pl.ds(at + 2 * width, 128)], oth[:, pl.ds(at + width, 128)]], axis=0
        )
        s = mm_nt(jnp.concatenate([k, hidden], axis=1), jnp.concatenate([q, unit], axis=1))
        e = jnp.exp(s - jnp.max(s, axis=0, keepdims=True))
        p_t = (e * (1.0 / jnp.sum(e, axis=0, keepdims=True))).astype(BF)
        probs[at // HD] = p_t[:, :span]
        probs[at // HD + 1] = p_t[:, span:]
        context[:, pl.ds(at, 128)] = beside(mm(v.T, p_t), span).T.astype(BF)


def attend_first_kernel(
    core, limits, x_own, x_oth, here, there,
    own, oth, context, probs, weights, bias, vec, b_in, arrived,
):
    width = context.shape[1]
    half = width // 2

    @pl.when(pl.program_id(0) == 0)
    def _():
        copies = [
            pltpu.make_async_copy(
                source, weights.at[pl.ds(pl.multiple_of(start * half, half), half)], arrived.at[i]
            )
            for i, (source, start) in enumerate(((here, core[0]), (there, 1 - core[0])))
        ]
        for copy in copies:
            copy.start()
        for copy in copies:
            copy.wait()
        rows = weights[:, 3 * width :].astype(F32).T[:16]
        vec[...] = rows
        for l in range(4):
            b_in[l] = rows[V_IN + l : V_IN + l + 1]
        pairs = rows[V_QV : V_QV + 2].astype(BF)
        sides = [
            mm(pairs[0:1, k : k + half], interleave(0)) + mm(pairs[1:2, k : k + half], interleave(1))
            for k in (0, half)
        ]
        line = jnp.concatenate([sides[0], jnp.zeros((1, width), F32), sides[1]], axis=1)
        bias[...] = jnp.broadcast_to(line, bias.shape)

    attend_body(
        pl.program_id(0), limits, x_own, x_oth, weights, bias, own, oth, context, probs
    )


def attend_more_kernel(first, limits, x_own, x_oth, weights, bias, *rest):
    attend_body(pl.program_id(0) + first, limits, x_own, x_oth, weights, bias, *rest[-4:])


def attend_specs(micro, rows, width, first):
    span, heads = rows // micro, width // HD

    def block(n):
        return pl.BlockSpec((span, n), lambda g, *_: (g + first, 0))

    specs = [
        block(3 * width),
        block(2 * width),
        block(width),
        pl.BlockSpec((None, heads, 2 * span, span), lambda g, *_: (g + first, 0, 0, 0)),
    ]
    shapes = [
        jax.ShapeDtypeStruct((rows, 3 * width), BF),
        jax.ShapeDtypeStruct((rows, 2 * width), BF),
        jax.ShapeDtypeStruct((rows, width), BF),
        jax.ShapeDtypeStruct((micro, heads, 2 * span, span), BF),
    ]
    return block(width), specs, shapes


def attend_first(core, limits, x_own, x_oth, here, there, count):
    rows, width = x_own.shape
    block, specs, shapes = attend_specs(limits.shape[0], rows, width, 0)

    def whole(*shape):
        return pl.BlockSpec(shape, lambda g, *_: (0,) * len(shape))

    return pl.pallas_call(
        attend_first_kernel,
        grid_spec=pltpu.PrefetchScalarGridSpec(
            num_scalar_prefetch=2,
            grid=(count,),
            in_specs=[block, block] + [pl.BlockSpec(memory_space=pl.ANY)] * 2,
            out_specs=specs
            + [whole(width, ONE), whole(8, 3 * width), whole(16, width), whole(4, 1, width)],
            scratch_shapes=[pltpu.SemaphoreType.DMA((2,))],
        ),
        out_shape=shapes
        + [
            jax.ShapeDtypeStruct((width, ONE), BF),
            jax.ShapeDtypeStruct((8, 3 * width), F32),
            jax.ShapeDtypeStruct((16, width), F32),
            jax.ShapeDtypeStruct((4, 1, width), F32),
        ],
        name="attend_first",
        **vmem(56, 10 * count << 30, 8 * count << 20),
    )(core, limits, x_own, x_oth, here, there)


def attend_more(limits, x_own, x_oth, weights, bias, first, earlier):
    micro = limits.shape[0]
    rows, width = x_own.shape
    block, specs, shapes = attend_specs(micro, rows, width, first)

    def whole(*shape):
        return pl.BlockSpec(shape, lambda g, *_: (0,) * len(shape))

    count = micro - first
    return pl.pallas_call(
        functools.partial(attend_more_kernel, first),
        grid_spec=pltpu.PrefetchScalarGridSpec(
            num_scalar_prefetch=1,
            grid=(count,),
            in_specs=[block, block, whole(width, 3 * width), whole(8, 3 * width)]
            + [pl.BlockSpec(memory_space=pl.ANY)] * len(earlier),
            out_specs=specs,
        ),
        out_shape=shapes,
        input_output_aliases={5 + i: i for i in range(len(earlier))},
        name="attend_more",
        **vmem(63, 10 * count << 30, 8 * count << 20),
    )(limits, x_own, x_oth, weights, bias, *earlier)


def attend_back_body(own, oth, probs, d_context, d_own, d_oth):
    span, width = d_context.shape
    for at in range(0, width, 128):
        q = apart(own[:, pl.ds(at, 128)] * jnp.asarray(0.125, BF))
        k = jnp.concatenate([own[:, pl.ds(at + width, 128)], oth[:, pl.ds(at, 128)]], axis=0)
        v = jnp.concatenate(
            [own[:, pl.ds(at + 2 * width, 128)], oth[:, pl.ds(at + width, 128)]], axis=0
        )
        d_c = apart(d_context[:, pl.ds(at, 128)])
        p_b = jnp.concatenate([probs[at // HD], probs[at // HD + 1]], axis=1)
        p_f = p_b.astype(F32)
        d_p = mm_nt(v, d_c)
        weighted = jnp.sum(p_f * d_p, axis=0, keepdims=True)
        d_s = (p_f * (d_p - weighted)).astype(BF)
        d_own[:, pl.ds(at, 128)] = (beside(mm(k.T, d_s), span).T * 0.125).astype(BF)
        d_k = mm(d_s, q).astype(BF)
        d_v = mm(p_b, d_c).astype(BF)
        d_own[:, pl.ds(at + width, 128)] = d_k[:span]
        d_own[:, pl.ds(at + 2 * width, 128)] = d_v[:span]
        d_oth[:, pl.ds(at, 128)] = d_k[span:]
        d_oth[:, pl.ds(at + width, 128)] = d_v[span:]


def token_parts(d_own, d_oth, w_qkv, d_first, d_tokens, x_part):
    width = d_first.shape[1]
    d_tokens[...] = d_first[...] + mm_nt(d_own[...], w_qkv[...])
    x_part[...] = (
        mm_nt(d_oth[:, :width], w_qkv[:, width : 2 * width])
        + mm_nt(d_oth[:, width:], w_qkv[:, 2 * width :])
    ).astype(BF)


def bias_sums(d_own, d_oth):
    width = d_oth.shape[1] // 2
    of_queries = jnp.sum(d_own[:, :width].astype(F32), axis=0, keepdims=True)
    of_values = jnp.sum(
        d_own[:, 2 * width :].astype(F32) + d_oth[:, width:].astype(F32), axis=0, keepdims=True
    )
    return rows_of(of_queries, of_values)


def attend_back_kernel(
    own, oth, probs, d_context, d_first, weights, d_own, d_oth, sums, d_tokens, x_part, w_qkv, arrived
):
    fetch = pltpu.make_async_copy(weights.at[:, pl.ds(0, w_qkv.shape[1])], w_qkv, arrived)
    fetch.start()
    attend_back_body(own, oth, probs, d_context, d_own, d_oth)
    fetch.wait()
    token_parts(d_own, d_oth, w_qkv, d_first, d_tokens, x_part)
    sums[...] = bias_sums(d_own, d_oth)


def attend_back(own, oth, probs, d_context, d_first, weights):
    _, heads, _, span = probs.shape
    rows, width = d_context.shape

    def block(n):
        return pl.BlockSpec((span, n), lambda g: (0, 0))

    return pl.pallas_call(
        attend_back_kernel,
        grid=(1,),
        in_specs=[block(3 * width), block(2 * width)]
        + [pl.BlockSpec((None, heads, 2 * span, span), lambda g: (0, 0, 0, 0))]
        + [block(width), block(width), pl.BlockSpec(memory_space=pl.ANY)],
        out_specs=[block(3 * width), block(2 * width), pl.BlockSpec((8, width), lambda g: (0, 0))]
        + [block(width), block(width)],
        out_shape=[
            jax.ShapeDtypeStruct((span, 3 * width), BF),
            jax.ShapeDtypeStruct((span, 2 * width), BF),
            jax.ShapeDtypeStruct((8, width), F32),
            jax.ShapeDtypeStruct((rows, width), F32),
            jax.ShapeDtypeStruct((span, width), BF),
        ],
        scratch_shapes=[pltpu.VMEM((width, 3 * width), BF), pltpu.SemaphoreType.DMA],
        name="attend_back",
        **vmem(63, 9 << 30, 8 << 20),
    )(own, oth, probs, d_context, d_first, weights)


def attend_last_kernel(
    core, own, oth, probs, d_context, d_first, sums_qv, sums, in_sums,
    weights, d_own_first, d_oth_first, x_own, x_oth, _,
    d_tokens, x_part, mine, away,
    w_qkv, d_own, d_oth, x_here, x_there, total, columns, result, arrived, done,
):
    g, last = pl.program_id(0), pl.num_programs(0) - 1
    span, width = d_context.shape
    half = width // 2
    rows = pl.ds(pl.multiple_of((g + 1) * span, span), span)
    d_own_here, d_oth_here = d_own.at[rows], d_oth.at[rows]
    first = pl.ds(0, span)
    copies = [
        pltpu.make_async_copy(source, into, arrived.at[i])
        for i, (source, into) in enumerate(
            (
                (weights.at[:, pl.ds(0, 3 * width)], w_qkv),
                (d_own_first, d_own.at[first]),
                (d_oth_first, d_oth.at[first]),
                (x_own, x_here),
                (x_oth, x_there),
            )
        )
    ]

    def send(k, start, lanes):
        return pltpu.make_async_copy(
            result.at[k, :, pl.ds(start, lanes)], (mine, away)[k].at[:, pl.ds(start, lanes)],
            done.at[k, start // width],
        )

    @pl.when(g == 0)
    def _():
        for copy in copies:
            copy.start()
        total[...] = sums_qv[...]

    attend_back_body(own, oth, probs, d_context, d_own_here, d_oth_here)

    @pl.when(g == 0)
    def _():
        for copy in copies:
            copy.wait()

    token_parts(d_own_here, d_oth_here, w_qkv, d_first, d_tokens, x_part)
    total[...] += bias_sums(d_own_here, d_oth_here)

    @pl.when(g == last)
    def _():
        qv = total[0:2].astype(BF)
        split = [
            jnp.concatenate([mm_nt(qv[i : i + 1], interleave(parity)) for i in (0, 1)], axis=1)
            for parity in (0, 1)
        ]
        lines = [sums[0:6]] + [in_sums[i] for i in range(4)] + split
        columns[...] = jnp.concatenate(lines + [jnp.zeros((116, width), F32)], axis=0).T.astype(BF)
        for k, side in enumerate((core[0], 1 - core[0])):
            place = pl.ds(pl.multiple_of(side * half, half), half)
            result[k, :, AT_VEC:] = columns[place]
            send(k, AT_VEC, ONE - AT_VEC).start()
            here, there = x_here[:, place], x_there[:, place]
            for j in range(3):
                lanes = slice(j * width, (j + 1) * width)
                grad = mm_tn(here, d_own[:, lanes])
                if j:
                    grad += mm_tn(there, d_oth[:, (j - 1) * width : j * width])
                result[k, :, lanes] = grad.astype(BF)
                send(k, j * width, width).start()
        for k in (0, 1):
            for i in range(4):
                send(k, i * width, width if i < 3 else ONE - AT_VEC).wait()


def attend_last(core, own, oth, probs, d_context, d_first, weights, part, x_own, x_oth, sums, in_sums):
    micro, heads, _, span = probs.shape
    rows, width = d_context.shape
    half = width // 2
    d_own, d_oth, sums_qv, d_tokens = part

    def block(n):
        return pl.BlockSpec((span, n), lambda g, *_: (g + 1, 0))

    def whole(*shape):
        return pl.BlockSpec(shape, lambda g, *_: (0,) * len(shape))

    anywhere = pl.BlockSpec(memory_space=pl.ANY)
    return pl.pallas_call(
        attend_last_kernel,
        grid_spec=pltpu.PrefetchScalarGridSpec(
            num_scalar_prefetch=1,
            grid=(micro - 1,),
            in_specs=[block(3 * width), block(2 * width)]
            + [pl.BlockSpec((None, heads, 2 * span, span), lambda g, *_: (g + 1, 0, 0, 0))]
            + [block(width), block(width), whole(8, width), whole(8, width), whole(4, 1, width)]
            + [anywhere] * 6,
            out_specs=[block(width), pl.BlockSpec((span, width), lambda g, *_: (g, 0))]
            + [anywhere] * 2,
            scratch_shapes=[
                pltpu.VMEM((width, 3 * width), BF),
                pltpu.VMEM((rows, 3 * width), BF),
                pltpu.VMEM((rows, 2 * width), BF),
                pltpu.VMEM((rows, width), BF),
                pltpu.VMEM((rows, width), BF),
                pltpu.VMEM((8, width), F32),
                pltpu.VMEM((width, 128), BF),
                pltpu.VMEM((2, half, ONE), BF),
                pltpu.SemaphoreType.DMA((5,)),
                pltpu.SemaphoreType.DMA((2, 4)),
            ],
        ),
        out_shape=[
            jax.ShapeDtypeStruct((rows, width), F32),
            jax.ShapeDtypeStruct((rows - span, width), BF),
            jax.ShapeDtypeStruct((half, ONE), BF),
            jax.ShapeDtypeStruct((half, ONE), BF),
        ],
        input_output_aliases={14: 0},
        name="attend_last",
        **vmem(40, 24 << 30, 20 << 20),
    )(
        core, own, oth, probs, d_context, d_first, sums_qv, sums, in_sums,
        weights, d_own, d_oth, x_own, x_oth, d_tokens,
    )


def norm_parts(value):
    centre = value - jnp.mean(value, axis=-1, keepdims=True)
    inverse = lax.rsqrt(jnp.mean(centre * centre, axis=-1, keepdims=True) + EPS)
    return centre * inverse, inverse


def norm_back(grad, hat, inverse, gain):
    scaled = grad * gain
    return inverse * (
        scaled
        - jnp.mean(scaled, axis=-1, keepdims=True)
        - hat * jnp.mean(scaled * hat, axis=-1, keepdims=True)
    )


def rows_of(*terms):
    return jnp.concatenate(terms + (jnp.zeros((8 - len(terms), terms[0].shape[1]), F32),), axis=0)


def middle_kernel(
    core, vec, b_in, x, context, cot, w_mine, w_away,
    sums, in_sums, grad_mine, grad_away, block_out, d_first, d_context,
    x_in, c_in, cot_in, normed_b, hat_one, inv_one, outer, active, slope, d_outer, d_normed, result,
    d_ctx, weights, grads, from_rows, from_weights, to_rows, to_grads,
):
    t = pl.program_id(0)
    rows, width = x_in.shape
    half, parts, step = width // 2, active.shape[0], rows // 3
    mine, away = pl.multiple_of(core[0] * half, half), pl.multiple_of((1 - core[0]) * half, half)
    blocks = [pl.ds(r * step, step) for r in range(3)]
    w_out = weights.at[2 * parts]

    def row(i):
        return vec[i : i + 1, :]

    def fetch(i):
        lanes = pl.ds(i * width, width)
        return [
            pltpu.make_async_copy(
                source.at[:, lanes], weights.at[i, pl.ds(start, half)], from_weights.at[i, k]
            )
            for k, (source, start) in enumerate(((w_mine, mine), (w_away, away)))
        ]

    def rows_in(r, *which):
        ends = ((context, c_in), (x, x_in), (cot, cot_in))
        return [
            pltpu.make_async_copy(ends[k][0].at[blocks[r]], ends[k][1].at[blocks[r]], from_rows.at[k, r])
            for k in which
        ]

    def rows_out(k, r):
        source, into = ((result, block_out), (d_normed, d_first), (d_ctx, d_context))[k]
        return pltpu.make_async_copy(source.at[blocks[r]], into.at[blocks[r]], to_rows.at[k, r])

    def grads_out(i, slot, count):
        return [
            pltpu.make_async_copy(
                grads.at[slot, k, pl.ds(0, count)], into.at[pl.ds(i, count)], to_grads.at[slot, k]
            )
            for k, into in enumerate((grad_mine, grad_away))
        ]

    def wait_part(i):
        for copy in fetch(i) + fetch(parts + i):
            copy.wait()

    def forward(l):
        w_in, w_back = weights.at[l], weights.at[parts + l]

        def hidden(r):
            return mm(normed_b[blocks[r]], w_in[...]) + b_in[0]

        def bend(r, inner):
            phi = 0.5 + 0.5 * lax.erf(inner * (0.5**0.5))
            act = (inner * phi).astype(BF)
            active[l, blocks[r]] = act
            slope[l, blocks[r]] = phi + inner * jnp.exp(-0.5 * inner * inner) * 0.3989422804014327
            return act

        inner = [hidden(0), hidden(1)]
        for r in range(3):
            act = bend(r, inner[r])
            if r == 0:
                inner.append(hidden(2))
            outer[blocks[r]] += mm(act, w_back[...])

    def backward(l):
        w_in, w_back = weights.at[l], weights.at[parts + l]

        def back(r):
            return mm_nt(d_outer[blocks[r]], w_back[...])

        d_act = [back(0), back(1)]
        pieces = []
        bias = jnp.zeros((1, width), F32)
        for r, at in enumerate(blocks):
            d_inner = (d_act[r] * slope[l, at]).astype(BF)
            pieces.append(d_inner)
            if r == 0:
                d_act.append(back(2))
            bias += jnp.sum(d_inner.astype(F32), axis=0, keepdims=True)
            d_normed[at] += mm_nt(d_inner, w_in[...])
        d_inner = jnp.concatenate(pieces, axis=0)
        in_sums[0] = bias
        slot = l % 2 if isinstance(l, int) else lax.rem(l, 2)
        if not isinstance(l, int):

            @pl.when(l >= 2)
            def _():
                for copy in grads_out(2 * l - 4, slot, 2):
                    copy.wait()

        for k, start in enumerate((mine, away)):
            cols = pl.ds(start, half)
            grads[slot, k, 0] = mm_tn(normed_b[:, cols], d_inner).astype(BF)
            grads[slot, k, 1] = mm_tn(active[l, :, cols], d_outer[...]).astype(BF)
        for copy in grads_out(2 * l, slot, 2):
            copy.start()

    @pl.when(t == 0)
    def _():
        for copy in fetch(2 * parts):
            copy.start()
        for r in range(3):
            for copy in rows_in(r, 0, 1):
                copy.start()
        for i in range(parts):
            for copy in fetch(i) + fetch(parts + i):
                copy.start()
        for r in range(3):
            rows_in(r, 2)[0].start()
        for copy in fetch(2 * parts):
            copy.wait()
        wait_part(0)
        for r, at in enumerate(blocks):
            for copy in rows_in(r, 0, 1):
                copy.wait()
            hat, inverse = norm_parts(x_in[at].astype(F32) + mm(c_in[at], w_out[...]) + row(V_OUT))
            hat_one[at] = hat
            inv_one[at] = jnp.broadcast_to(inverse, (step, 128))
            value = hat * row(V_GAIN1) + row(V_SHIFT1)
            normed_b[at] = value.astype(BF)
            outer[at] = value + row(V_BACK)
        forward(0)

    @pl.when((t > 0) & (t < parts))
    def _():
        for i in range(1, parts):

            @pl.when(t == i)
            def _():
                wait_part(i)

        forward(t)

    @pl.when(t == parts)
    def _():
        total = [jnp.zeros((1, width), F32) for _ in range(3)]
        for r, at in enumerate(blocks):
            rows_in(r, 2)[0].wait()
            hat, inverse = norm_parts(outer[at])
            result[at] = (hat * row(V_GAIN2) + row(V_SHIFT2)).astype(BF)
            rows_out(0, r).start()
            grad = cot_in[at].astype(F32)
            d_second = norm_back(grad, hat, inverse, row(V_GAIN2))
            d_b = d_second.astype(BF)
            d_outer[at] = d_b
            d_normed[at] = d_second
            for i, term in enumerate((d_b.astype(F32), grad * hat, grad)):
                total[i] += jnp.sum(term, axis=0, keepdims=True)
        for i, term in zip((V_BACK, V_GAIN2, V_SHIFT2), total):
            sums[i : i + 1] = term
        backward(0)

    @pl.when((t > parts) & (t < 2 * parts))
    def _():
        backward(t - parts)

    @pl.when(t == 2 * parts)
    def _():
        total = [jnp.zeros((1, width), F32) for _ in range(3)]
        for r, at in enumerate(blocks):
            grad, hat = d_normed[at], hat_one[at]
            back = norm_back(grad, hat, inv_one[at, 0:1], row(V_GAIN1))
            d_normed[at] = back
            rows_out(1, r).start()
            d_b = back.astype(BF)
            d_outer[at] = d_b
            for i, term in enumerate((d_b.astype(F32), grad * hat, grad)):
                total[i] += jnp.sum(term, axis=0, keepdims=True)
            d_ctx[at] = mm_nt(d_b, w_out[...]).astype(BF)
            rows_out(2, r).start()
        for i, term in zip((V_OUT, V_GAIN1, V_SHIFT1), total):
            sums[i : i + 1] = term
        for copy in grads_out(2 * parts - 4, parts % 2, 2):
            copy.wait()
        for k, start in enumerate((mine, away)):
            grads[parts % 2, k, 0] = mm_tn(c_in[:, pl.ds(start, half)], d_outer[...]).astype(BF)
        for copy in grads_out(2 * parts, parts % 2, 1):
            copy.start()
        for copy in grads_out(2 * parts - 2, (parts - 1) % 2, 2) + grads_out(2 * parts, parts % 2, 1):
            copy.wait()
        for k in range(3):
            for r in range(3):
                rows_out(k, r).wait()


def middle(core, vec, b_in, x, context, cot, w_mine, w_away):
    rows, width = x.shape
    parts = b_in.shape[0]
    half = width // 2

    def whole(*shape):
        return pl.BlockSpec(shape, lambda t, *_: (0,) * len(shape))

    def later(t):
        return jnp.clip(t - parts, 0, parts - 1)

    anywhere = pl.BlockSpec(memory_space=pl.ANY)
    grads = ((2 * parts + 1, half, width), BF)
    shapes = (
        ((8, width), F32), ((parts, 1, width), F32), grads, grads,
        ((rows, width), BF), ((rows, width), F32), ((rows, width), BF),
    )
    return pl.pallas_call(
        middle_kernel,
        grid_spec=pltpu.PrefetchScalarGridSpec(
            num_scalar_prefetch=1,
            grid=(2 * parts + 1,),
            in_specs=[
                whole(16, width),
                pl.BlockSpec((1, 1, width), lambda t, *_: (jnp.minimum(t, parts - 1), 0, 0)),
            ]
            + [anywhere] * 5,
            out_specs=[whole(8, width)]
            + [pl.BlockSpec((1, 1, width), lambda t, *_: (later(t), 0, 0))]
            + [anywhere] * 5,
            scratch_shapes=[pltpu.VMEM((rows, width), BF)] * 4
            + [pltpu.VMEM((rows, width), F32), pltpu.VMEM((rows, 128), F32)]
            + [pltpu.VMEM((rows, width), F32)]
            + [pltpu.VMEM((parts, rows, width), BF), pltpu.VMEM((parts, rows, width), F32)]
            + [pltpu.VMEM((rows, width), BF), pltpu.VMEM((rows, width), F32)]
            + [pltpu.VMEM((rows, width), BF)] * 2
            + [
                pltpu.VMEM((2 * parts + 1, width, width), BF),
                pltpu.VMEM((2, 2, 2, half, width), BF),
                pltpu.SemaphoreType.DMA((3, 3)),
                pltpu.SemaphoreType.DMA((2 * parts + 1, 2)),
                pltpu.SemaphoreType.DMA((3, 3)),
                pltpu.SemaphoreType.DMA((2, 2)),
            ],
        ),
        out_shape=[jax.ShapeDtypeStruct(*shape) for shape in shapes],
        name="middle",
        **vmem(63, 24 << 30, 30 << 20),
    )(core, vec, b_in, x, context, cot, w_mine, w_away)


def on_device(
    tokens, lengths, cotangent, w_qkv, b_qv, w_out, b_out, w_in, b_in, w_back, b_back,
    gain_one, shift_one, gain_two, shift_two,
):
    micro, _, span, width = tokens.shape
    ff = w_in.shape[1]
    rows = micro * span
    yh = lax.axis_index("yh")
    c = lax.axis_index("c")
    core = c.reshape(1)
    x_own = tokens.reshape(rows, width)
    tie = lax.optimization_barrier
    order = arrival()

    packed = pack(
        w_qkv, w_out, w_in, w_back,
        (b_out, b_back, gain_one, shift_one, gain_two, shift_two, b_in, b_qv),
    )
    x_oth = lax.ppermute(x_own, "yh", SWAP)
    column = gather_column(packed)
    near = [column] + from_ring(column, 0)
    one = jnp.concatenate([part[:, :ONE] for part in near], axis=0)
    two = jnp.concatenate([part[:, ONE:] for part in near], axis=0)
    one_parts = [one] + from_ring(one, 1)
    limits = jnp.stack([lengths[:, 0] - yh * span, lengths[:, 0] - (1 - yh) * span], axis=1)
    one_parts, two, x_oth, limits = tie((one_parts, two, x_oth, limits))
    two_parts = [two] + from_ring(two, 1)
    one = sort_rows(order, one_parts)
    one_away = lax.ppermute(one, "c", SWAP)

    *seen, weights, bias, vec, b_in = attend_first(core, limits, x_own, x_oth, one, one_away, micro - 1)
    seen, two_parts = tie((seen, two_parts))
    two = sort_rows(order, two_parts)
    seen, two = tie((seen, two))
    two_away = lax.ppermute(two, "c", SWAP)
    mixed, mixed_oth, context, probs = attend_more(
        limits, x_own, x_oth, weights, bias, micro - 1, seen
    )
    sums, in_sums, ff_mine, ff_away, block_out, d_first, d_context = middle(
        core, vec, b_in, x_own, context, cotangent.reshape(rows, width), two, two_away
    )
    ff_recv = lax.ppermute(ff_away, "c", SWAP)
    inputs = (mixed, mixed_oth, probs, d_context, d_first, weights)
    *part, x_near = attend_back(*inputs)
    x_near = lax.ppermute(x_near, "yh", SWAP)
    ff_recv, part = tie((ff_recv, part))
    ff_own, *ff_sent = split_rows(order, ff_mine, ff_recv)
    ff_sent, part = tie((ff_sent, part))
    ff_got = to_ring(ff_sent, 1)
    d_tokens, x_part, g_mine, g_away = attend_last(
        core, *inputs, part, x_own, x_oth, sums, in_sums
    )
    g_away, x_near = tie((g_away, x_near))
    x_back = lax.ppermute(x_part, "yh", SWAP)
    ff_got, g_away = tie((ff_got, g_away))
    g_recv = lax.ppermute(g_away, "c", SWAP)
    ff_own, *ff_sent = fold_rows(ff_own, ff_got)
    ff_got = to_ring(ff_sent, 0)
    g_recv, ff_sent = tie((g_recv, ff_sent))
    g_own, *g_sent = split_rows(order, g_mine, g_recv)
    g_sent, ff_got[0] = tie((g_sent, ff_got[0]))
    g_got = to_ring(g_sent, 1)
    ff_parts = column_parts(ff_own, ff_got)
    d_tokens = d_tokens + jnp.concatenate([x_near, x_back], axis=0).astype(F32)
    g_got, d_tokens = tie((g_got, d_tokens))
    g_own, *g_sent = fold_rows(g_own, g_got)
    g_got = to_ring(g_sent, 0)
    o_in, o_back, o_out = finish_early(ff_parts)
    g_got, o_in, o_back, o_out = tie((g_got, o_in, o_back, o_out))
    o_qkv, lines = finish_late(column_parts(g_own, g_got))
    return (
        block_out.reshape(tokens.shape),
        d_tokens.reshape(tokens.shape),
        o_qkv,
        lines[7],
        o_out,
        lines[0],
        o_in,
        lines[6],
        o_back,
        lines[1],
        lines[2],
        lines[3],
        lines[4],
        lines[5],
    )


def solution(mesh):
    fine = Mesh(mesh.devices.reshape(2, 4, 4, 2, 2), DEVICES)
    pairs = ("yl", "x", "z", "c")
    data = P(None, pairs, "yh", None)
    weight, vector = P(DEVICES, None), P(DEVICES)
    kinds = (weight, vector) * 4
    return jax.shard_map(
        on_device,
        mesh=fine,
        in_specs=(data, P(None, pairs), data) + kinds + (vector,) * 4,
        out_specs=(data, data) + kinds + (vector,) * 4,
        check_vma=False,
    )
```

```python
import functools

import jax
import jax.numpy as jnp
import numpy as np
from jax import lax
from jax.experimental import pallas as pl
from jax.experimental.pallas import tpu as pltpu
from jax.sharding import Mesh, PartitionSpec as P

HD = 64
EPS = 1e-05
F32 = jnp.float32
BF = jnp.bfloat16
DEVICES = ("yl", "x", "z", "c", "yh")
SWAP = ((0, 1), (1, 0))
STEPS = (0, 1, 3, 2)
AT_VEC = 3 * 768
ONE, TWO = AT_VEC + 128, 9 * 768
V_OUT, V_BACK, V_GAIN1, V_SHIFT1, V_GAIN2, V_SHIFT2, V_IN, V_QV = 0, 1, 2, 3, 4, 5, 6, 10


def mm(a, b):
    return lax.dot_general(a, b, (((1,), (0,)), ((), ())), preferred_element_type=F32)


def mm_nt(a, b):
    return lax.dot_general(a, b, (((1,), (1,)), ((), ())), preferred_element_type=F32)


def mm_tn(a, b):
    return lax.dot_general(a, b, (((0,), (0,)), ((), ())), preferred_element_type=F32)


def vmem(mib, flops=0, moved=0):
    return dict(
        compiler_params=pltpu.CompilerParams(vmem_limit_bytes=mib << 20),
        cost_estimate=pl.CostEstimate(flops=flops, bytes_accessed=moved, transcendentals=0),
    )


ROW = [i % 6 for i in range(36)] + [i // 4 for i in range(24)] + [i // 2 for i in range(12)]
COLUMN = [i // 6 for i in range(36)] + [V_IN + i % 4 for i in range(24)] + [V_QV + i % 2 for i in range(12)]


SIZES = (6, 6, 6, 6, 6, 6, 24, 12)


def maps():
    rows, columns = np.zeros((8, 128), np.float32), np.zeros((128, 128), np.float32)
    for i, (r, l) in enumerate(zip(ROW, COLUMN)):
        rows[r, i] = columns[i, l] = 1
    f, place = np.arange(768)[:, None], np.arange(768)[None, :]
    units = (f == 4 * (place % 192) + place // 192).astype(np.float32)
    r, f = np.arange(32)[:, None], np.arange(24)[None, :]
    spread = ((r % 8 < 6) & (f == 4 * (r % 8) + r // 8)).astype(np.float32)
    return rows, columns, units, spread


def pack_kernel(*refs):
    w_qkv, w_out, w_in, w_back = refs[:4]
    vectors = refs[4:12]
    rows, columns, units, spread, out, line, stack = refs[12:]
    width = w_out.shape[1]
    line[...] = jnp.zeros_like(line)
    stack[...] = jnp.zeros_like(stack)
    at = 0
    for size, vector in zip(SIZES, vectors):
        line[0:1, at : at + size] = vector[...].astype(F32).reshape(1, size)
        at += size
    out[:, : 3 * width] = w_qkv[...]
    out[:, AT_VEC:ONE] = mm((line[0:1] * rows[...]).astype(BF), columns[...])[:6].astype(BF)
    for b in range(4):
        stack[8 * b : 8 * b + 6] = w_in[:, b * width : (b + 1) * width].astype(F32)
    moved = mm(stack[...].astype(BF), units[...])
    merged = mm(spread[...], w_back[...])
    for l in range(4):
        for b in range(4):
            start = ONE + l * width + 192 * b
            out[:, start : start + 192] = moved[8 * b : 8 * b + 6, 192 * l : 192 * (l + 1)].astype(BF)
        start = ONE + (4 + l) * width
        out[:, start : start + width] = merged[8 * l : 8 * l + 6].astype(BF)
    out[:, ONE + 8 * width :] = w_out[...]


def pack(w_qkv, w_out, w_in, w_back, vectors):
    rows, columns, units, spread = maps()
    return pl.pallas_call(
        pack_kernel,
        out_shape=jax.ShapeDtypeStruct((6, ONE + TWO), BF),
        scratch_shapes=[pltpu.VMEM((8, 128), F32), pltpu.VMEM((32, 768), F32)],
        name="pack",
    )(
        w_qkv, w_out, w_in, w_back, *vectors, jnp.asarray(rows),
        *(jnp.asarray(part, BF) for part in (columns, units, spread)),
    )


def exact_nt(a, b):
    return lax.dot_general(
        a, b, (((1,), (1,)), ((), ())), precision=lax.Precision.HIGHEST, preferred_element_type=F32
    )


def exact_tn(a, b):
    return lax.dot_general(
        a, b, (((0,), (0,)), ((), ())), precision=lax.Precision.HIGHEST, preferred_element_type=F32
    )


def thirds(value):
    high = value.astype(BF)
    rest = value - high.astype(F32)
    middle_ = rest.astype(BF)
    return jnp.concatenate([high, middle_, (rest - middle_.astype(F32)).astype(BF)], axis=0)


def finish_early_kernel(a, b, d, e, units, spread, g_in, g_back, g_out, stack, rows):
    width = g_back.shape[1]
    total = (a[...] + b[...]) + (d[...] + e[...])
    stack[...] = jnp.zeros_like(stack)
    rows[...] = jnp.zeros_like(rows)
    for l in range(4):
        for b_ in range(4):
            start = 2 * l * width + 192 * b_
            stack[8 * b_ : 8 * b_ + 6, 192 * l : 192 * (l + 1)] = total[:, start : start + 192]
        rows[8 * l : 8 * l + 6] = total[:, (2 * l + 1) * width : (2 * l + 2) * width]
    moved = mm_nt(thirds(stack[...]), units[...])
    moved = moved[:32] + moved[32:64] + moved[64:]
    for b_ in range(4):
        g_in[:, b_ * width : (b_ + 1) * width] = moved[8 * b_ : 8 * b_ + 6]
    g_back[...] = exact_tn(spread[...], rows[...])
    g_out[...] = total[:, 8 * width :]


def finish_early(parts):
    _, _, units, spread = maps()
    return pl.pallas_call(
        finish_early_kernel,
        out_shape=[jax.ShapeDtypeStruct(shape, F32) for shape in ((6, 3072), (24, 768), (6, 768))],
        scratch_shapes=[pltpu.VMEM((32, 768), F32)] * 2,
        name="finish_early",
        **vmem(16, 1 << 28, 1 << 20),
    )(*parts, jnp.asarray(units, BF), jnp.asarray(spread))


def finish_late_kernel(*refs):
    a, b, d, e, rows, columns, g_qkv = refs[:7]
    vectors, line = refs[7:-1], refs[-1]
    total = (a[...] + b[...]) + (d[...] + e[...])
    g_qkv[...] = total[:, :AT_VEC]
    line[...] = exact_nt(total[:, AT_VEC:], columns[...]) * rows[:6]
    line[0:1] = jnp.sum(line[...], axis=0, keepdims=True)
    at = 0
    for size, vector in zip(SIZES, vectors):
        vector[...] = line[0:1, at : at + size].reshape(size)
        at += size


def finish_late(parts):
    rows, columns, _, _ = maps()
    g_qkv, *vectors = pl.pallas_call(
        finish_late_kernel,
        out_shape=[
            jax.ShapeDtypeStruct(shape, F32) for shape in ((6, AT_VEC),) + tuple((n,) for n in SIZES)
        ],
        scratch_shapes=[pltpu.VMEM((6, 128), F32)],
        name="finish_late",
        **vmem(16, 1 << 24, 1 << 18),
    )(*parts, jnp.asarray(rows), jnp.asarray(columns))
    return g_qkv, vectors


def interleave(parity):
    row = lax.broadcasted_iota(jnp.int32, (384, 768), 0)
    return (lax.broadcasted_iota(jnp.int32, (384, 768), 1) == 2 * row + parity).astype(BF)


def column_pairs(flip_c, flip_y):
    pairs = []
    for a in (0, 1):
        for b in (0, 1):
            for d in (0, 1):
                pairs.append((b * 4 + (a ^ flip_c) * 2 + (d ^ flip_y), a * 4 + b * 2 + d))
    return pairs


FLIPS = ((0, 0), (0, 1), (1, 0), (1, 1))


def gather_column(shard):
    parts = [lax.ppermute(shard, ("yl", "c", "yh"), column_pairs(*flip)) for flip in FLIPS]
    return jnp.concatenate(parts, axis=0)


def plane_pairs(step, stage):
    pairs = []
    for x in range(4):
        for z in range(4):
            for c in range(2):
                near = (x, (z + step) % 4) if c == stage else ((x + step) % 4, z)
                pairs.append(((near[0] * 4 + near[1]) * 2 + c, (x * 4 + z) * 2 + c))
    return pairs


def from_ring(block, stage):
    return [lax.ppermute(block, ("x", "z", "c"), plane_pairs(step, stage)) for step in STEPS[1:]]


def arrival():
    yl, x, z, c, yh = (lax.axis_index(name) for name in DEVICES)
    j = jnp.arange(384)
    steps = jnp.array(STEPS)
    last, early, flip = steps[j // 96], steps[(j % 96) // 24], (j % 24) // 6
    xx = (x + jnp.where(c == 0, last, early)) % 4
    zz = (z + jnp.where(c == 0, early, last)) % 4
    row = xx * 96 + zz * 24 + (yl ^ (flip // 2)) * 12 + (yh ^ (flip % 2)) * 6 + j % 6
    return (jnp.arange(384)[:, None] == row[None, :]).astype(BF)


def wide(columns):
    return next(n for n in (2304, 3072, columns) if columns % n == 0)


def sort_kernel(order, *refs):
    blocks, out = refs[:-1], refs[-1]
    out[...] = mm(order[...], jnp.concatenate([b[...] for b in blocks], axis=0)).astype(BF)


def sort_rows(order, blocks):
    rows, columns = blocks[0].shape
    lanes = wide(columns)
    return pl.pallas_call(
        sort_kernel,
        grid=(columns // lanes,),
        in_specs=[pl.BlockSpec(order.shape, lambda j: (0, 0))]
        + [pl.BlockSpec((rows, lanes), lambda j: (0, j))] * 4,
        out_specs=pl.BlockSpec((4 * rows, lanes), lambda j: (0, j)),
        out_shape=jax.ShapeDtypeStruct((4 * rows, columns), BF),
        name="sort_rows",
        **vmem(24, 2 * 384 * 384 * columns, 2 * 2 * 384 * columns),
    )(order, *blocks)


def split_kernel(order, mine, recv, *pieces):
    parts, _, lanes = mine.shape
    size = pieces[0].shape[0]
    for p in range(parts):
        total = (mine[p].astype(F32) + recv[p].astype(F32)).astype(BF)
        rows = mm_tn(order[...], total)
        for i, piece in enumerate(pieces):
            piece[:, p * lanes : (p + 1) * lanes] = rows[i * size : (i + 1) * size].astype(piece.dtype)


def split_rows(order, mine, recv):
    if mine.ndim == 2:
        mine, recv = mine[None], recv[None]
    parts, rows, lanes = mine.shape
    batch = 3 if parts % 3 == 0 else 1
    half = pl.BlockSpec((batch, rows, lanes), lambda p: (p, 0, 0))
    piece = pl.BlockSpec((rows // 4, batch * lanes), lambda p: (0, p))
    shape = (rows // 4, parts * lanes)
    return pl.pallas_call(
        split_kernel,
        grid=(parts // batch,),
        in_specs=[pl.BlockSpec(order.shape, lambda p: (0, 0)), half, half],
        out_specs=[piece] * 4,
        out_shape=[jax.ShapeDtypeStruct(shape, BF)] * 4,
        name="split_rows",
        **vmem(24, 2 * 384 * 384 * parts * lanes, 3 * 2 * 384 * parts * lanes),
    )(order, mine, recv)


def fold_kernel(own, a, b, d, *pieces):
    total = own[...].astype(F32) + a[...].astype(F32) + b[...].astype(F32) + d[...].astype(F32)
    size = pieces[0].shape[0]
    for i, piece in enumerate(pieces):
        piece[...] = total[i * size : (i + 1) * size].astype(piece.dtype)


def fold_rows(own, received):
    rows, columns = own.shape
    lanes = wide(columns)
    block = pl.BlockSpec((rows, lanes), lambda j: (0, j))
    piece = pl.BlockSpec((rows // 4, lanes), lambda j: (0, j))
    return pl.pallas_call(
        fold_kernel,
        grid=(columns // lanes,),
        in_specs=[block] * 4,
        out_specs=[piece] * 4,
        out_shape=[jax.ShapeDtypeStruct((rows // 4, columns), kind) for kind in (F32, BF, BF, BF)],
        name="fold_rows",
        **vmem(24, 4 * rows * columns, 11 * rows * columns),
    )(own, *received)


def to_ring(pieces, stage):
    return [
        lax.ppermute(piece, ("x", "z", "c"), [(b, a) for a, b in plane_pairs(step, stage)])
        for step, piece in zip(STEPS[1:], pieces)
    ]


def column_parts(own, received):
    total = own
    for part in received:
        total += part.astype(F32)
    size = total.shape[0] // 4
    parts = []
    for i, flip in enumerate(FLIPS):
        pairs = [(user, owner) for owner, user in column_pairs(*flip)]
        parts.append(lax.ppermute(total[i * size : (i + 1) * size], ("yl", "c", "yh"), pairs))
    return parts


def sum_parts(parts):
    return (parts[0] + parts[1]) + (parts[2] + parts[3])


def apart(pair):
    lane = lax.broadcasted_iota(jnp.int32, pair.shape, 1)
    zero = jnp.zeros_like(pair)
    return jnp.concatenate(
        [jnp.where(lane < HD, pair, zero), jnp.where(lane < HD, zero, pair)], axis=0
    )


def beside(rows, span):
    return jnp.concatenate([rows[:HD, :span], rows[HD:, span:]], axis=0)


def attend_body(g, limits, x_own, x_oth, w_qkv, bias, own, oth, context, probs):
    span, width = context.shape
    key = lax.broadcasted_iota(jnp.int32, (span, 128), 0)
    lane = lax.broadcasted_iota(jnp.int32, (span, 128), 1)
    hidden = jnp.concatenate(
        [jnp.where((key >= limits[g, i]) & (lane == 0), -1e30, 0.0).astype(BF) for i in (0, 1)],
        axis=0,
    )
    unit = (lax.broadcasted_iota(jnp.int32, (2 * span, 128), 1) == 0).astype(BF)
    for j in range(3):
        at = pl.ds(j * width, width)
        own[:, at] = (mm(x_own[...], w_qkv[:, at]) + bias[0:1, at]).astype(BF)
        if j:
            oth[:, pl.ds((j - 1) * width, width)] = (
                mm(x_oth[...], w_qkv[:, at]) + bias[0:1, at]
            ).astype(BF)

    for at in range(0, width, 128):
        q = apart(own[:, pl.ds(at, 128)] * jnp.asarray(0.125, BF))
        k = jnp.concatenate([own[:, pl.ds(at + width, 128)], oth[:, pl.ds(at, 128)]], axis=0)
        v = jnp.concatenate(
            [own[:, pl.ds(at + 2 * width, 128)], oth[:, pl.ds(at + width, 128)]], axis=0
        )
        s = mm_nt(jnp.concatenate([k, hidden], axis=1), jnp.concatenate([q, unit], axis=1))
        e = jnp.exp(s - jnp.max(s, axis=0, keepdims=True))
        p_t = (e * (1.0 / jnp.sum(e, axis=0, keepdims=True))).astype(BF)
        probs[at // HD] = p_t[:, :span]
        probs[at // HD + 1] = p_t[:, span:]
        context[:, pl.ds(at, 128)] = beside(mm(v.T, p_t), span).T.astype(BF)


def attend_first_kernel(
    core, limits, x_own, x_oth, here, there,
    own, oth, context, probs, weights, bias, vec, b_in, arrived,
):
    width = context.shape[1]
    half = width // 2

    @pl.when(pl.program_id(0) == 0)
    def _():
        copies = [
            pltpu.make_async_copy(
                source, weights.at[pl.ds(pl.multiple_of(start * half, half), half)], arrived.at[i]
            )
            for i, (source, start) in enumerate(((here, core[0]), (there, 1 - core[0])))
        ]
        for copy in copies:
            copy.start()
        for copy in copies:
            copy.wait()
        rows = weights[:, 3 * width :].astype(F32).T[:16]
        vec[...] = rows
        for l in range(4):
            b_in[l] = rows[V_IN + l : V_IN + l + 1]
        pairs = rows[V_QV : V_QV + 2].astype(BF)
        sides = [
            mm(pairs[0:1, k : k + half], interleave(0)) + mm(pairs[1:2, k : k + half], interleave(1))
            for k in (0, half)
        ]
        line = jnp.concatenate([sides[0], jnp.zeros((1, width), F32), sides[1]], axis=1)
        bias[...] = jnp.broadcast_to(line, bias.shape)

    attend_body(
        pl.program_id(0), limits, x_own, x_oth, weights, bias, own, oth, context, probs
    )


def attend_more_kernel(first, limits, x_own, x_oth, weights, bias, *rest):
    attend_body(pl.program_id(0) + first, limits, x_own, x_oth, weights, bias, *rest[-4:])


def attend_specs(micro, rows, width, first):
    span, heads = rows // micro, width // HD

    def block(n):
        return pl.BlockSpec((span, n), lambda g, *_: (g + first, 0))

    specs = [
        block(3 * width),
        block(2 * width),
        block(width),
        pl.BlockSpec((None, heads, 2 * span, span), lambda g, *_: (g + first, 0, 0, 0)),
    ]
    shapes = [
        jax.ShapeDtypeStruct((rows, 3 * width), BF),
        jax.ShapeDtypeStruct((rows, 2 * width), BF),
        jax.ShapeDtypeStruct((rows, width), BF),
        jax.ShapeDtypeStruct((micro, heads, 2 * span, span), BF),
    ]
    return block(width), specs, shapes


def attend_first(core, limits, x_own, x_oth, here, there, count):
    rows, width = x_own.shape
    block, specs, shapes = attend_specs(limits.shape[0], rows, width, 0)

    def whole(*shape):
        return pl.BlockSpec(shape, lambda g, *_: (0,) * len(shape))

    return pl.pallas_call(
        attend_first_kernel,
        grid_spec=pltpu.PrefetchScalarGridSpec(
            num_scalar_prefetch=2,
            grid=(count,),
            in_specs=[block, block] + [pl.BlockSpec(memory_space=pl.ANY)] * 2,
            out_specs=specs
            + [whole(width, ONE), whole(8, 3 * width), whole(16, width), whole(4, 1, width)],
            scratch_shapes=[pltpu.SemaphoreType.DMA((2,))],
        ),
        out_shape=shapes
        + [
            jax.ShapeDtypeStruct((width, ONE), BF),
            jax.ShapeDtypeStruct((8, 3 * width), F32),
            jax.ShapeDtypeStruct((16, width), F32),
            jax.ShapeDtypeStruct((4, 1, width), F32),
        ],
        name="attend_first",
        **vmem(56, 10 * count << 30, 8 * count << 20),
    )(core, limits, x_own, x_oth, here, there)


def attend_more(limits, x_own, x_oth, weights, bias, first, earlier):
    micro = limits.shape[0]
    rows, width = x_own.shape
    block, specs, shapes = attend_specs(micro, rows, width, first)

    def whole(*shape):
        return pl.BlockSpec(shape, lambda g, *_: (0,) * len(shape))

    count = micro - first
    return pl.pallas_call(
        functools.partial(attend_more_kernel, first),
        grid_spec=pltpu.PrefetchScalarGridSpec(
            num_scalar_prefetch=1,
            grid=(count,),
            in_specs=[block, block, whole(width, 3 * width), whole(8, 3 * width)]
            + [pl.BlockSpec(memory_space=pl.ANY)] * len(earlier),
            out_specs=specs,
        ),
        out_shape=shapes,
        input_output_aliases={5 + i: i for i in range(len(earlier))},
        name="attend_more",
        **vmem(63, 10 * count << 30, 8 * count << 20),
    )(limits, x_own, x_oth, weights, bias, *earlier)


def attend_back_body(own, oth, probs, d_context, d_own, d_oth):
    span, width = d_context.shape
    for at in range(0, width, 128):
        q = apart(own[:, pl.ds(at, 128)] * jnp.asarray(0.125, BF))
        k = jnp.concatenate([own[:, pl.ds(at + width, 128)], oth[:, pl.ds(at, 128)]], axis=0)
        v = jnp.concatenate(
            [own[:, pl.ds(at + 2 * width, 128)], oth[:, pl.ds(at + width, 128)]], axis=0
        )
        d_c = apart(d_context[:, pl.ds(at, 128)])
        p_b = jnp.concatenate([probs[at // HD], probs[at // HD + 1]], axis=1)
        p_f = p_b.astype(F32)
        d_p = mm_nt(v, d_c)
        weighted = jnp.sum(p_f * d_p, axis=0, keepdims=True)
        d_s = (p_f * (d_p - weighted)).astype(BF)
        d_own[:, pl.ds(at, 128)] = (beside(mm(k.T, d_s), span).T * 0.125).astype(BF)
        d_k = mm(d_s, q).astype(BF)
        d_v = mm(p_b, d_c).astype(BF)
        d_own[:, pl.ds(at + width, 128)] = d_k[:span]
        d_own[:, pl.ds(at + 2 * width, 128)] = d_v[:span]
        d_oth[:, pl.ds(at, 128)] = d_k[span:]
        d_oth[:, pl.ds(at + width, 128)] = d_v[span:]


def token_parts(d_own, d_oth, w_qkv, d_first, d_tokens, x_part):
    width = d_first.shape[1]
    d_tokens[...] = d_first[...] + mm_nt(d_own[...], w_qkv[...])
    x_part[...] = (
        mm_nt(d_oth[:, :width], w_qkv[:, width : 2 * width])
        + mm_nt(d_oth[:, width:], w_qkv[:, 2 * width :])
    ).astype(BF)


def bias_sums(d_own, d_oth):
    width = d_oth.shape[1] // 2
    of_queries = jnp.sum(d_own[:, :width].astype(F32), axis=0, keepdims=True)
    of_values = jnp.sum(
        d_own[:, 2 * width :].astype(F32) + d_oth[:, width:].astype(F32), axis=0, keepdims=True
    )
    return rows_of(of_queries, of_values)


def attend_back_kernel(
    own, oth, probs, d_context, d_first, weights, d_own, d_oth, sums, d_tokens, x_part, w_qkv, arrived
):
    fetch = pltpu.make_async_copy(weights.at[:, pl.ds(0, w_qkv.shape[1])], w_qkv, arrived)
    fetch.start()
    attend_back_body(own, oth, probs, d_context, d_own, d_oth)
    fetch.wait()
    token_parts(d_own, d_oth, w_qkv, d_first, d_tokens, x_part)
    sums[...] = bias_sums(d_own, d_oth)


def attend_back(own, oth, probs, d_context, d_first, weights):
    _, heads, _, span = probs.shape
    rows, width = d_context.shape

    def block(n):
        return pl.BlockSpec((span, n), lambda g: (0, 0))

    return pl.pallas_call(
        attend_back_kernel,
        grid=(1,),
        in_specs=[block(3 * width), block(2 * width)]
        + [pl.BlockSpec((None, heads, 2 * span, span), lambda g: (0, 0, 0, 0))]
        + [block(width), block(width), pl.BlockSpec(memory_space=pl.ANY)],
        out_specs=[block(3 * width), block(2 * width), pl.BlockSpec((8, width), lambda g: (0, 0))]
        + [block(width), block(width)],
        out_shape=[
            jax.ShapeDtypeStruct((span, 3 * width), BF),
            jax.ShapeDtypeStruct((span, 2 * width), BF),
            jax.ShapeDtypeStruct((8, width), F32),
            jax.ShapeDtypeStruct((rows, width), F32),
            jax.ShapeDtypeStruct((span, width), BF),
        ],
        scratch_shapes=[pltpu.VMEM((width, 3 * width), BF), pltpu.SemaphoreType.DMA],
        name="attend_back",
        **vmem(63, 9 << 30, 8 << 20),
    )(own, oth, probs, d_context, d_first, weights)


def attend_last_kernel(
    core, own, oth, probs, d_context, d_first, sums_qv, sums, in_sums,
    weights, d_own_first, d_oth_first, x_own, x_oth, _,
    d_tokens, x_part, mine, away,
    w_qkv, d_own, d_oth, x_here, x_there, total, columns, result, arrived, done,
):
    g, last = pl.program_id(0), pl.num_programs(0) - 1
    span, width = d_context.shape
    half = width // 2
    rows = pl.ds(pl.multiple_of((g + 1) * span, span), span)
    d_own_here, d_oth_here = d_own.at[rows], d_oth.at[rows]
    first = pl.ds(0, span)
    copies = [
        pltpu.make_async_copy(source, into, arrived.at[i])
        for i, (source, into) in enumerate(
            (
                (weights.at[:, pl.ds(0, 3 * width)], w_qkv),
                (d_own_first, d_own.at[first]),
                (d_oth_first, d_oth.at[first]),
                (x_own, x_here),
                (x_oth, x_there),
            )
        )
    ]

    def send(k, start, lanes):
        return pltpu.make_async_copy(
            result.at[k, :, pl.ds(start, lanes)], (mine, away)[k].at[:, pl.ds(start, lanes)],
            done.at[k, start // width],
        )

    @pl.when(g == 0)
    def _():
        for copy in copies:
            copy.start()
        total[...] = sums_qv[...]

    attend_back_body(own, oth, probs, d_context, d_own_here, d_oth_here)

    @pl.when(g == 0)
    def _():
        for copy in copies:
            copy.wait()

    token_parts(d_own_here, d_oth_here, w_qkv, d_first, d_tokens, x_part)
    total[...] += bias_sums(d_own_here, d_oth_here)

    @pl.when(g == last)
    def _():
        qv = total[0:2].astype(BF)
        split = [
            jnp.concatenate([mm_nt(qv[i : i + 1], interleave(parity)) for i in (0, 1)], axis=1)
            for parity in (0, 1)
        ]
        lines = [sums[0:6]] + [in_sums[i] for i in range(4)] + split
        columns[...] = jnp.concatenate(lines + [jnp.zeros((116, width), F32)], axis=0).T.astype(BF)
        for k, side in enumerate((core[0], 1 - core[0])):
            place = pl.ds(pl.multiple_of(side * half, half), half)
            result[k, :, AT_VEC:] = columns[place]
            send(k, AT_VEC, ONE - AT_VEC).start()
            here, there = x_here[:, place], x_there[:, place]
            for j in range(3):
                lanes = slice(j * width, (j + 1) * width)
                grad = mm_tn(here, d_own[:, lanes])
                if j:
                    grad += mm_tn(there, d_oth[:, (j - 1) * width : j * width])
                result[k, :, lanes] = grad.astype(BF)
                send(k, j * width, width).start()
        for k in (0, 1):
            for i in range(4):
                send(k, i * width, width if i < 3 else ONE - AT_VEC).wait()


def attend_last(core, own, oth, probs, d_context, d_first, weights, part, x_own, x_oth, sums, in_sums):
    micro, heads, _, span = probs.shape
    rows, width = d_context.shape
    half = width // 2
    d_own, d_oth, sums_qv, d_tokens = part

    def block(n):
        return pl.BlockSpec((span, n), lambda g, *_: (g + 1, 0))

    def whole(*shape):
        return pl.BlockSpec(shape, lambda g, *_: (0,) * len(shape))

    anywhere = pl.BlockSpec(memory_space=pl.ANY)
    return pl.pallas_call(
        attend_last_kernel,
        grid_spec=pltpu.PrefetchScalarGridSpec(
            num_scalar_prefetch=1,
            grid=(micro - 1,),
            in_specs=[block(3 * width), block(2 * width)]
            + [pl.BlockSpec((None, heads, 2 * span, span), lambda g, *_: (g + 1, 0, 0, 0))]
            + [block(width), block(width), whole(8, width), whole(8, width), whole(4, 1, width)]
            + [anywhere] * 6,
            out_specs=[block(width), pl.BlockSpec((span, width), lambda g, *_: (g, 0))]
            + [anywhere] * 2,
            scratch_shapes=[
                pltpu.VMEM((width, 3 * width), BF),
                pltpu.VMEM((rows, 3 * width), BF),
                pltpu.VMEM((rows, 2 * width), BF),
                pltpu.VMEM((rows, width), BF),
                pltpu.VMEM((rows, width), BF),
                pltpu.VMEM((8, width), F32),
                pltpu.VMEM((width, 128), BF),
                pltpu.VMEM((2, half, ONE), BF),
                pltpu.SemaphoreType.DMA((5,)),
                pltpu.SemaphoreType.DMA((2, 4)),
            ],
        ),
        out_shape=[
            jax.ShapeDtypeStruct((rows, width), F32),
            jax.ShapeDtypeStruct((rows - span, width), BF),
            jax.ShapeDtypeStruct((half, ONE), BF),
            jax.ShapeDtypeStruct((half, ONE), BF),
        ],
        input_output_aliases={14: 0},
        name="attend_last",
        **vmem(40, 24 << 30, 20 << 20),
    )(
        core, own, oth, probs, d_context, d_first, sums_qv, sums, in_sums,
        weights, d_own, d_oth, x_own, x_oth, d_tokens,
    )


def norm_parts(value):
    centre = value - jnp.mean(value, axis=-1, keepdims=True)
    inverse = lax.rsqrt(jnp.mean(centre * centre, axis=-1, keepdims=True) + EPS)
    return centre * inverse, inverse


def norm_back(grad, hat, inverse, gain):
    scaled = grad * gain
    return inverse * (
        scaled
        - jnp.mean(scaled, axis=-1, keepdims=True)
        - hat * jnp.mean(scaled * hat, axis=-1, keepdims=True)
    )


def rows_of(*terms):
    return jnp.concatenate(terms + (jnp.zeros((8 - len(terms), terms[0].shape[1]), F32),), axis=0)


def middle_kernel(
    core, vec, b_in, x, context, cot, w_mine, w_away,
    sums, in_sums, grad_mine, grad_away, block_out, d_first, d_context,
    x_in, c_in, cot_in, normed_b, hat_one, inv_one, outer, active, slope, d_outer, d_normed, result,
    d_ctx, weights, grads, from_rows, from_weights, to_rows, to_grads,
):
    t = pl.program_id(0)
    rows, width = x_in.shape
    half, parts, step = width // 2, active.shape[0], rows // 3
    mine, away = pl.multiple_of(core[0] * half, half), pl.multiple_of((1 - core[0]) * half, half)
    blocks = [pl.ds(r * step, step) for r in range(3)]
    w_out = weights.at[2 * parts]

    def row(i):
        return vec[i : i + 1, :]

    def fetch(i):
        lanes = pl.ds(i * width, width)
        return [
            pltpu.make_async_copy(
                source.at[:, lanes], weights.at[i, pl.ds(start, half)], from_weights.at[i, k]
            )
            for k, (source, start) in enumerate(((w_mine, mine), (w_away, away)))
        ]

    def rows_in(r, *which):
        ends = ((context, c_in), (x, x_in), (cot, cot_in))
        return [
            pltpu.make_async_copy(ends[k][0].at[blocks[r]], ends[k][1].at[blocks[r]], from_rows.at[k, r])
            for k in which
        ]

    def rows_out(k, r):
        source, into = ((result, block_out), (d_normed, d_first), (d_ctx, d_context))[k]
        return pltpu.make_async_copy(source.at[blocks[r]], into.at[blocks[r]], to_rows.at[k, r])

    def grads_out(i, slot, count):
        return [
            pltpu.make_async_copy(
                grads.at[slot, k, pl.ds(0, count)], into.at[pl.ds(i, count)], to_grads.at[slot, k]
            )
            for k, into in enumerate((grad_mine, grad_away))
        ]

    def wait_part(i):
        for copy in fetch(i) + fetch(parts + i):
            copy.wait()

    def forward(l):
        w_in, w_back = weights.at[l], weights.at[parts + l]

        def hidden(r):
            return mm(normed_b[blocks[r]], w_in[...]) + b_in[0]

        def bend(r, inner):
            phi = 0.5 + 0.5 * lax.erf(inner * (0.5**0.5))
            act = (inner * phi).astype(BF)
            active[l, blocks[r]] = act
            slope[l, blocks[r]] = phi + inner * jnp.exp(-0.5 * inner * inner) * 0.3989422804014327
            return act

        inner = [hidden(0), hidden(1)]
        for r in range(3):
            act = bend(r, inner[r])
            if r == 0:
                inner.append(hidden(2))
            outer[blocks[r]] += mm(act, w_back[...])

    def backward(l):
        w_in, w_back = weights.at[l], weights.at[parts + l]

        def back(r):
            return mm_nt(d_outer[blocks[r]], w_back[...])

        d_act = [back(0), back(1)]
        pieces = []
        bias = jnp.zeros((1, width), F32)
        for r, at in enumerate(blocks):
            d_inner = (d_act[r] * slope[l, at]).astype(BF)
            pieces.append(d_inner)
            if r == 0:
                d_act.append(back(2))
            bias += jnp.sum(d_inner.astype(F32), axis=0, keepdims=True)
            d_normed[at] += mm_nt(d_inner, w_in[...])
        d_inner = jnp.concatenate(pieces, axis=0)
        in_sums[0] = bias
        slot = l % 2 if isinstance(l, int) else lax.rem(l, 2)
        if not isinstance(l, int):

            @pl.when(l >= 2)
            def _():
                for copy in grads_out(2 * l - 4, slot, 2):
                    copy.wait()

        for k, start in enumerate((mine, away)):
            cols = pl.ds(start, half)
            grads[slot, k, 0] = mm_tn(normed_b[:, cols], d_inner).astype(BF)
            grads[slot, k, 1] = mm_tn(active[l, :, cols], d_outer[...]).astype(BF)
        for copy in grads_out(2 * l, slot, 2):
            copy.start()

    @pl.when(t == 0)
    def _():
        for copy in fetch(2 * parts):
            copy.start()
        for r in range(3):
            for copy in rows_in(r, 0, 1):
                copy.start()
        for i in range(parts):
            for copy in fetch(i) + fetch(parts + i):
                copy.start()
        for r in range(3):
            rows_in(r, 2)[0].start()
        for copy in fetch(2 * parts):
            copy.wait()
        wait_part(0)
        for r, at in enumerate(blocks):
            for copy in rows_in(r, 0, 1):
                copy.wait()
            hat, inverse = norm_parts(x_in[at].astype(F32) + mm(c_in[at], w_out[...]) + row(V_OUT))
            hat_one[at] = hat
            inv_one[at] = jnp.broadcast_to(inverse, (step, 128))
            value = hat * row(V_GAIN1) + row(V_SHIFT1)
            normed_b[at] = value.astype(BF)
            outer[at] = value + row(V_BACK)
        forward(0)

    @pl.when((t > 0) & (t < parts))
    def _():
        for i in range(1, parts):

            @pl.when(t == i)
            def _():
                wait_part(i)

        forward(t)

    @pl.when(t == parts)
    def _():
        total = [jnp.zeros((1, width), F32) for _ in range(3)]
        for r, at in enumerate(blocks):
            rows_in(r, 2)[0].wait()
            hat, inverse = norm_parts(outer[at])
            result[at] = (hat * row(V_GAIN2) + row(V_SHIFT2)).astype(BF)
            rows_out(0, r).start()
            grad = cot_in[at].astype(F32)
            d_second = norm_back(grad, hat, inverse, row(V_GAIN2))
            d_b = d_second.astype(BF)
            d_outer[at] = d_b
            d_normed[at] = d_second
            for i, term in enumerate((d_b.astype(F32), grad * hat, grad)):
                total[i] += jnp.sum(term, axis=0, keepdims=True)
        for i, term in zip((V_BACK, V_GAIN2, V_SHIFT2), total):
            sums[i : i + 1] = term
        backward(0)

    @pl.when((t > parts) & (t < 2 * parts))
    def _():
        backward(t - parts)

    @pl.when(t == 2 * parts)
    def _():
        total = [jnp.zeros((1, width), F32) for _ in range(3)]
        for r, at in enumerate(blocks):
            grad, hat = d_normed[at], hat_one[at]
            back = norm_back(grad, hat, inv_one[at, 0:1], row(V_GAIN1))
            d_normed[at] = back
            rows_out(1, r).start()
            d_b = back.astype(BF)
            d_outer[at] = d_b
            for i, term in enumerate((d_b.astype(F32), grad * hat, grad)):
                total[i] += jnp.sum(term, axis=0, keepdims=True)
            d_ctx[at] = mm_nt(d_b, w_out[...]).astype(BF)
            rows_out(2, r).start()
        for i, term in zip((V_OUT, V_GAIN1, V_SHIFT1), total):
            sums[i : i + 1] = term
        for copy in grads_out(2 * parts - 4, parts % 2, 2):
            copy.wait()
        for k, start in enumerate((mine, away)):
            grads[parts % 2, k, 0] = mm_tn(c_in[:, pl.ds(start, half)], d_outer[...]).astype(BF)
        for copy in grads_out(2 * parts, parts % 2, 1):
            copy.start()
        for copy in grads_out(2 * parts - 2, (parts - 1) % 2, 2) + grads_out(2 * parts, parts % 2, 1):
            copy.wait()
        for k in range(3):
            for r in range(3):
                rows_out(k, r).wait()


def middle(core, vec, b_in, x, context, cot, w_mine, w_away):
    rows, width = x.shape
    parts = b_in.shape[0]
    half = width // 2

    def whole(*shape):
        return pl.BlockSpec(shape, lambda t, *_: (0,) * len(shape))

    def later(t):
        return jnp.clip(t - parts, 0, parts - 1)

    anywhere = pl.BlockSpec(memory_space=pl.ANY)
    grads = ((2 * parts + 1, half, width), BF)
    shapes = (
        ((8, width), F32), ((parts, 1, width), F32), grads, grads,
        ((rows, width), BF), ((rows, width), F32), ((rows, width), BF),
    )
    return pl.pallas_call(
        middle_kernel,
        grid_spec=pltpu.PrefetchScalarGridSpec(
            num_scalar_prefetch=1,
            grid=(2 * parts + 1,),
            in_specs=[
                whole(16, width),
                pl.BlockSpec((1, 1, width), lambda t, *_: (jnp.minimum(t, parts - 1), 0, 0)),
            ]
            + [anywhere] * 5,
            out_specs=[whole(8, width)]
            + [pl.BlockSpec((1, 1, width), lambda t, *_: (later(t), 0, 0))]
            + [anywhere] * 5,
            scratch_shapes=[pltpu.VMEM((rows, width), BF)] * 4
            + [pltpu.VMEM((rows, width), F32), pltpu.VMEM((rows, 128), F32)]
            + [pltpu.VMEM((rows, width), F32)]
            + [pltpu.VMEM((parts, rows, width), BF), pltpu.VMEM((parts, rows, width), F32)]
            + [pltpu.VMEM((rows, width), BF), pltpu.VMEM((rows, width), F32)]
            + [pltpu.VMEM((rows, width), BF)] * 2
            + [
                pltpu.VMEM((2 * parts + 1, width, width), BF),
                pltpu.VMEM((2, 2, 2, half, width), BF),
                pltpu.SemaphoreType.DMA((3, 3)),
                pltpu.SemaphoreType.DMA((2 * parts + 1, 2)),
                pltpu.SemaphoreType.DMA((3, 3)),
                pltpu.SemaphoreType.DMA((2, 2)),
            ],
        ),
        out_shape=[jax.ShapeDtypeStruct(*shape) for shape in shapes],
        name="middle",
        **vmem(63, 24 << 30, 30 << 20),
    )(core, vec, b_in, x, context, cot, w_mine, w_away)


def on_device(
    tokens, lengths, cotangent, w_qkv, b_qv, w_out, b_out, w_in, b_in, w_back, b_back,
    gain_one, shift_one, gain_two, shift_two,
):
    micro, _, span, width = tokens.shape
    ff = w_in.shape[1]
    rows = micro * span
    yh = lax.axis_index("yh")
    c = lax.axis_index("c")
    core = c.reshape(1)
    x_own = tokens.reshape(rows, width)
    tie = lax.optimization_barrier
    order = arrival()

    packed = pack(
        w_qkv, w_out, w_in, w_back,
        (b_out, b_back, gain_one, shift_one, gain_two, shift_two, b_in, b_qv),
    )
    x_oth = lax.ppermute(x_own, "yh", SWAP)
    column = gather_column(packed)
    near = [column] + from_ring(column, 0)
    one = jnp.concatenate([part[:, :ONE] for part in near], axis=0)
    two = jnp.concatenate([part[:, ONE:] for part in near], axis=0)
    one_parts = [one] + from_ring(one, 1)
    limits = jnp.stack([lengths[:, 0] - yh * span, lengths[:, 0] - (1 - yh) * span], axis=1)
    one_parts, two, x_oth, limits = tie((one_parts, two, x_oth, limits))
    two_parts = [two] + from_ring(two, 1)
    one = sort_rows(order, one_parts)
    one_away = lax.ppermute(one, "c", SWAP)

    *seen, weights, bias, vec, b_in = attend_first(core, limits, x_own, x_oth, one, one_away, micro - 1)
    seen, two_parts = tie((seen, two_parts))
    two = sort_rows(order, two_parts)
    seen, two = tie((seen, two))
    two_away = lax.ppermute(two, "c", SWAP)
    mixed, mixed_oth, context, probs = attend_more(
        limits, x_own, x_oth, weights, bias, micro - 1, seen
    )
    sums, in_sums, ff_mine, ff_away, block_out, d_first, d_context = middle(
        core, vec, b_in, x_own, context, cotangent.reshape(rows, width), two, two_away
    )
    ff_recv = lax.ppermute(ff_away, "c", SWAP)
    inputs = (mixed, mixed_oth, probs, d_context, d_first, weights)
    *part, x_near = attend_back(*inputs)
    x_near = lax.ppermute(x_near, "yh", SWAP)
    ff_recv, part = tie((ff_recv, part))
    ff_own, *ff_sent = split_rows(order, ff_mine, ff_recv)
    ff_sent, part = tie((ff_sent, part))
    ff_got = to_ring(ff_sent, 1)
    d_tokens, x_part, g_mine, g_away = attend_last(
        core, *inputs, part, x_own, x_oth, sums, in_sums
    )
    g_away, x_near = tie((g_away, x_near))
    x_middle = lax.ppermute(x_part[:span], "yh", SWAP)
    x_back = lax.ppermute(x_part[span:], "yh", SWAP)
    ff_got, g_away = tie((ff_got, g_away))
    g_recv = lax.ppermute(g_away, "c", SWAP)
    ff_own, *ff_sent = fold_rows(ff_own, ff_got)
    ff_got = to_ring(ff_sent, 0)
    g_recv, ff_sent = tie((g_recv, ff_sent))
    g_own, *g_sent = split_rows(order, g_mine, g_recv)
    g_sent, ff_got[0], x_middle = tie((g_sent, ff_got[0], x_middle))
    g_got = to_ring(g_sent, 1)
    ff_parts = column_parts(ff_own, ff_got)
    d_tokens = d_tokens + jnp.concatenate([x_near, x_middle, x_back], axis=0).astype(F32)
    g_got, d_tokens = tie((g_got, d_tokens))
    g_own, *g_sent = fold_rows(g_own, g_got)
    g_got = to_ring(g_sent, 0)
    o_in, o_back, o_out = finish_early(ff_parts)
    g_got, o_in, o_back, o_out = tie((g_got, o_in, o_back, o_out))
    o_qkv, lines = finish_late(column_parts(g_own, g_got))
    return (
        block_out.reshape(tokens.shape),
        d_tokens.reshape(tokens.shape),
        o_qkv,
        lines[7],
        o_out,
        lines[0],
        o_in,
        lines[6],
        o_back,
        lines[1],
        lines[2],
        lines[3],
        lines[4],
        lines[5],
    )


def solution(mesh):
    fine = Mesh(mesh.devices.reshape(2, 4, 4, 2, 2), DEVICES)
    pairs = ("yl", "x", "z", "c")
    data = P(None, pairs, "yh", None)
    weight, vector = P(DEVICES, None), P(DEVICES)
    kinds = (weight, vector) * 4
    return jax.shard_map(
        on_device,
        mesh=fine,
        in_specs=(data, P(None, pairs), data) + kinds + (vector,) * 4,
        out_specs=(data, data) + kinds + (vector,) * 4,
        check_vma=False,
    )
```

```python
import functools

import jax
import jax.numpy as jnp
import numpy as np
from jax import lax
from jax.experimental import pallas as pl
from jax.experimental.pallas import tpu as pltpu
from jax.sharding import Mesh, PartitionSpec as P

HD = 64
EPS = 1e-05
F32 = jnp.float32
BF = jnp.bfloat16
DEVICES = ("yl", "x", "z", "c", "yh")
SWAP = ((0, 1), (1, 0))
STEPS = (0, 1, 3, 2)
AT_VEC = 3 * 768
ONE, TWO = AT_VEC + 128, 9 * 768
V_OUT, V_BACK, V_GAIN1, V_SHIFT1, V_GAIN2, V_SHIFT2, V_IN, V_QV = 0, 1, 2, 3, 4, 5, 6, 10


def mm(a, b):
    return lax.dot_general(a, b, (((1,), (0,)), ((), ())), preferred_element_type=F32)


def mm_nt(a, b):
    return lax.dot_general(a, b, (((1,), (1,)), ((), ())), preferred_element_type=F32)


def mm_tn(a, b):
    return lax.dot_general(a, b, (((0,), (0,)), ((), ())), preferred_element_type=F32)


def vmem(mib, flops=0, moved=0):
    return dict(
        compiler_params=pltpu.CompilerParams(vmem_limit_bytes=mib << 20),
        cost_estimate=pl.CostEstimate(flops=flops, bytes_accessed=moved, transcendentals=0),
    )


ROW = [i % 6 for i in range(36)] + [i // 4 for i in range(24)] + [i // 2 for i in range(12)]
COLUMN = [i // 6 for i in range(36)] + [V_IN + i % 4 for i in range(24)] + [V_QV + i % 2 for i in range(12)]


SIZES = (6, 6, 6, 6, 6, 6, 24, 12)


def maps():
    rows, columns = np.zeros((8, 128), np.float32), np.zeros((128, 128), np.float32)
    for i, (r, l) in enumerate(zip(ROW, COLUMN)):
        rows[r, i] = columns[i, l] = 1
    f, place = np.arange(768)[:, None], np.arange(768)[None, :]
    units = (f == 4 * (place % 192) + place // 192).astype(np.float32)
    r, f = np.arange(32)[:, None], np.arange(24)[None, :]
    spread = ((r % 8 < 6) & (f == 4 * (r % 8) + r // 8)).astype(np.float32)
    return rows, columns, units, spread


def pack_kernel(*refs):
    w_qkv, w_out, w_in, w_back = refs[:4]
    vectors = refs[4:12]
    rows, columns, units, spread, out, line, stack = refs[12:]
    width = w_out.shape[1]
    line[...] = jnp.zeros_like(line)
    stack[...] = jnp.zeros_like(stack)
    at = 0
    for size, vector in zip(SIZES, vectors):
        line[0:1, at : at + size] = vector[...].astype(F32).reshape(1, size)
        at += size
    out[:, : 3 * width] = w_qkv[...]
    out[:, AT_VEC:ONE] = mm((line[0:1] * rows[...]).astype(BF), columns[...])[:6].astype(BF)
    for b in range(4):
        stack[8 * b : 8 * b + 6] = w_in[:, b * width : (b + 1) * width].astype(F32)
    moved = mm(stack[...].astype(BF), units[...])
    merged = mm(spread[...], w_back[...])
    for l in range(4):
        for b in range(4):
            start = ONE + l * width + 192 * b
            out[:, start : start + 192] = moved[8 * b : 8 * b + 6, 192 * l : 192 * (l + 1)].astype(BF)
        start = ONE + (4 + l) * width
        out[:, start : start + width] = merged[8 * l : 8 * l + 6].astype(BF)
    out[:, ONE + 8 * width :] = w_out[...]


def pack(w_qkv, w_out, w_in, w_back, vectors):
    rows, columns, units, spread = maps()
    return pl.pallas_call(
        pack_kernel,
        out_shape=jax.ShapeDtypeStruct((6, ONE + TWO), BF),
        scratch_shapes=[pltpu.VMEM((8, 128), F32), pltpu.VMEM((32, 768), F32)],
        name="pack",
    )(
        w_qkv, w_out, w_in, w_back, *vectors, jnp.asarray(rows),
        *(jnp.asarray(part, BF) for part in (columns, units, spread)),
    )


def exact_nt(a, b):
    return lax.dot_general(
        a, b, (((1,), (1,)), ((), ())), precision=lax.Precision.HIGHEST, preferred_element_type=F32
    )


def exact_tn(a, b):
    return lax.dot_general(
        a, b, (((0,), (0,)), ((), ())), precision=lax.Precision.HIGHEST, preferred_element_type=F32
    )


def thirds(value):
    high = value.astype(BF)
    rest = value - high.astype(F32)
    middle_ = rest.astype(BF)
    return jnp.concatenate([high, middle_, (rest - middle_.astype(F32)).astype(BF)], axis=0)


def finish_early_kernel(a, b, d, e, units, spread, g_in, g_back, g_out, stack, rows):
    width = g_back.shape[1]
    total = (a[...] + b[...]) + (d[...] + e[...])
    stack[...] = jnp.zeros_like(stack)
    rows[...] = jnp.zeros_like(rows)
    for l in range(4):
        for b_ in range(4):
            start = 2 * l * width + 192 * b_
            stack[8 * b_ : 8 * b_ + 6, 192 * l : 192 * (l + 1)] = total[:, start : start + 192]
        rows[8 * l : 8 * l + 6] = total[:, (2 * l + 1) * width : (2 * l + 2) * width]
    moved = mm_nt(thirds(stack[...]), units[...])
    moved = moved[:32] + moved[32:64] + moved[64:]
    for b_ in range(4):
        g_in[:, b_ * width : (b_ + 1) * width] = moved[8 * b_ : 8 * b_ + 6]
    g_back[...] = exact_tn(spread[...], rows[...])
    g_out[...] = total[:, 8 * width :]


def finish_early(parts):
    _, _, units, spread = maps()
    return pl.pallas_call(
        finish_early_kernel,
        out_shape=[jax.ShapeDtypeStruct(shape, F32) for shape in ((6, 3072), (24, 768), (6, 768))],
        scratch_shapes=[pltpu.VMEM((32, 768), F32)] * 2,
        name="finish_early",
        **vmem(16, 1 << 28, 1 << 20),
    )(*parts, jnp.asarray(units, BF), jnp.asarray(spread))


def finish_late_kernel(*refs):
    a, b, d, e, rows, columns, g_qkv = refs[:7]
    vectors, line = refs[7:-1], refs[-1]
    total = (a[...] + b[...]) + (d[...] + e[...])
    g_qkv[...] = total[:, :AT_VEC]
    line[...] = exact_nt(total[:, AT_VEC:], columns[...]) * rows[:6]
    line[0:1] = jnp.sum(line[...], axis=0, keepdims=True)
    at = 0
    for size, vector in zip(SIZES, vectors):
        vector[...] = line[0:1, at : at + size].reshape(size)
        at += size


def finish_late(parts):
    rows, columns, _, _ = maps()
    g_qkv, *vectors = pl.pallas_call(
        finish_late_kernel,
        out_shape=[
            jax.ShapeDtypeStruct(shape, F32) for shape in ((6, AT_VEC),) + tuple((n,) for n in SIZES)
        ],
        scratch_shapes=[pltpu.VMEM((6, 128), F32)],
        name="finish_late",
        **vmem(16, 1 << 24, 1 << 18),
    )(*parts, jnp.asarray(rows), jnp.asarray(columns))
    return g_qkv, vectors


def interleave(parity):
    row = lax.broadcasted_iota(jnp.int32, (384, 768), 0)
    return (lax.broadcasted_iota(jnp.int32, (384, 768), 1) == 2 * row + parity).astype(BF)


def column_pairs(flip_c, flip_y):
    pairs = []
    for a in (0, 1):
        for b in (0, 1):
            for d in (0, 1):
                pairs.append((b * 4 + (a ^ flip_c) * 2 + (d ^ flip_y), a * 4 + b * 2 + d))
    return pairs


FLIPS = ((0, 0), (0, 1), (1, 0), (1, 1))


def gather_column(shard):
    parts = [lax.ppermute(shard, ("yl", "c", "yh"), column_pairs(*flip)) for flip in FLIPS]
    return jnp.concatenate(parts, axis=0)


def plane_pairs(step, stage):
    pairs = []
    for x in range(4):
        for z in range(4):
            for c in range(2):
                near = (x, (z + step) % 4) if c == stage else ((x + step) % 4, z)
                pairs.append(((near[0] * 4 + near[1]) * 2 + c, (x * 4 + z) * 2 + c))
    return pairs


def from_ring(block, stage):
    return [lax.ppermute(block, ("x", "z", "c"), plane_pairs(step, stage)) for step in STEPS[1:]]


def arrival():
    yl, x, z, c, yh = (lax.axis_index(name) for name in DEVICES)
    j = jnp.arange(384)
    steps = jnp.array(STEPS)
    last, early, flip = steps[j // 96], steps[(j % 96) // 24], (j % 24) // 6
    xx = (x + jnp.where(c == 0, last, early)) % 4
    zz = (z + jnp.where(c == 0, early, last)) % 4
    row = xx * 96 + zz * 24 + (yl ^ (flip // 2)) * 12 + (yh ^ (flip % 2)) * 6 + j % 6
    return (jnp.arange(384)[:, None] == row[None, :]).astype(BF)


def wide(columns):
    return next(n for n in (2304, 3072, columns) if columns % n == 0)


def sort_kernel(order, *refs):
    blocks, out = refs[:-1], refs[-1]
    out[...] = mm(order[...], jnp.concatenate([b[...] for b in blocks], axis=0)).astype(BF)


def sort_rows(order, blocks):
    rows, columns = blocks[0].shape
    lanes = wide(columns)
    return pl.pallas_call(
        sort_kernel,
        grid=(columns // lanes,),
        in_specs=[pl.BlockSpec(order.shape, lambda j: (0, 0))]
        + [pl.BlockSpec((rows, lanes), lambda j: (0, j))] * 4,
        out_specs=pl.BlockSpec((4 * rows, lanes), lambda j: (0, j)),
        out_shape=jax.ShapeDtypeStruct((4 * rows, columns), BF),
        name="sort_rows",
        **vmem(24, 2 * 384 * 384 * columns, 2 * 2 * 384 * columns),
    )(order, *blocks)


def split_kernel(order, mine, recv, *pieces):
    parts, _, lanes = mine.shape
    size = pieces[0].shape[0]
    for p in range(parts):
        total = (mine[p].astype(F32) + recv[p].astype(F32)).astype(BF)
        rows = mm_tn(order[...], total)
        for i, piece in enumerate(pieces):
            piece[:, p * lanes : (p + 1) * lanes] = rows[i * size : (i + 1) * size].astype(piece.dtype)


def split_rows(order, mine, recv, room=24):
    if mine.ndim == 2:
        mine, recv = mine[None], recv[None]
    parts, rows, lanes = mine.shape
    batch = 3 if parts % 3 == 0 else 1
    half = pl.BlockSpec((batch, rows, lanes), lambda p: (p, 0, 0))
    piece = pl.BlockSpec((rows // 4, batch * lanes), lambda p: (0, p))
    shape = (rows // 4, parts * lanes)
    return pl.pallas_call(
        split_kernel,
        grid=(parts // batch,),
        in_specs=[pl.BlockSpec(order.shape, lambda p: (0, 0)), half, half],
        out_specs=[piece] * 4,
        out_shape=[jax.ShapeDtypeStruct(shape, BF)] * 4,
        name="split_rows",
        **vmem(room, 2 * 384 * 384 * parts * lanes, 3 * 2 * 384 * parts * lanes),
    )(order, mine, recv)


def fold_kernel(own, a, b, d, *pieces):
    total = own[...].astype(F32) + a[...].astype(F32) + b[...].astype(F32) + d[...].astype(F32)
    size = pieces[0].shape[0]
    for i, piece in enumerate(pieces):
        piece[...] = total[i * size : (i + 1) * size].astype(piece.dtype)


def fold_rows(own, received):
    rows, columns = own.shape
    lanes = wide(columns)
    block = pl.BlockSpec((rows, lanes), lambda j: (0, j))
    piece = pl.BlockSpec((rows // 4, lanes), lambda j: (0, j))
    return pl.pallas_call(
        fold_kernel,
        grid=(columns // lanes,),
        in_specs=[block] * 4,
        out_specs=[piece] * 4,
        out_shape=[jax.ShapeDtypeStruct((rows // 4, columns), kind) for kind in (F32, BF, BF, BF)],
        name="fold_rows",
        **vmem(24, 4 * rows * columns, 11 * rows * columns),
    )(own, *received)


def to_ring(pieces, stage):
    return [
        lax.ppermute(piece, ("x", "z", "c"), [(b, a) for a, b in plane_pairs(step, stage)])
        for step, piece in zip(STEPS[1:], pieces)
    ]


def column_parts(own, received):
    total = own
    for part in received:
        total += part.astype(F32)
    size = total.shape[0] // 4
    parts = []
    for i, flip in enumerate(FLIPS):
        pairs = [(user, owner) for owner, user in column_pairs(*flip)]
        parts.append(lax.ppermute(total[i * size : (i + 1) * size], ("yl", "c", "yh"), pairs))
    return parts


def sum_parts(parts):
    return (parts[0] + parts[1]) + (parts[2] + parts[3])


def apart(pair):
    lane = lax.broadcasted_iota(jnp.int32, pair.shape, 1)
    zero = jnp.zeros_like(pair)
    return jnp.concatenate(
        [jnp.where(lane < HD, pair, zero), jnp.where(lane < HD, zero, pair)], axis=0
    )


def beside(rows, span):
    return jnp.concatenate([rows[:HD, :span], rows[HD:, span:]], axis=0)


def attend_body(g, limits, x_own, x_oth, w_qkv, bias, own, oth, context, probs):
    span, width = context.shape
    key = lax.broadcasted_iota(jnp.int32, (span, 128), 0)
    lane = lax.broadcasted_iota(jnp.int32, (span, 128), 1)
    hidden = jnp.concatenate(
        [jnp.where((key >= limits[g, i]) & (lane == 0), -1e30, 0.0).astype(BF) for i in (0, 1)],
        axis=0,
    )
    unit = (lax.broadcasted_iota(jnp.int32, (2 * span, 128), 1) == 0).astype(BF)
    for j in range(3):
        at = pl.ds(j * width, width)
        own[:, at] = (mm(x_own[...], w_qkv[:, at]) + bias[0:1, at]).astype(BF)
        if j:
            oth[:, pl.ds((j - 1) * width, width)] = (
                mm(x_oth[...], w_qkv[:, at]) + bias[0:1, at]
            ).astype(BF)

    for at in range(0, width, 128):
        q = apart(own[:, pl.ds(at, 128)] * jnp.asarray(0.125, BF))
        k = jnp.concatenate([own[:, pl.ds(at + width, 128)], oth[:, pl.ds(at, 128)]], axis=0)
        v = jnp.concatenate(
            [own[:, pl.ds(at + 2 * width, 128)], oth[:, pl.ds(at + width, 128)]], axis=0
        )
        s = mm_nt(jnp.concatenate([k, hidden], axis=1), jnp.concatenate([q, unit], axis=1))
        e = jnp.exp(s - jnp.max(s, axis=0, keepdims=True))
        p_t = (e * (1.0 / jnp.sum(e, axis=0, keepdims=True))).astype(BF)
        probs[at // HD] = p_t[:, :span]
        probs[at // HD + 1] = p_t[:, span:]
        context[:, pl.ds(at, 128)] = beside(mm(v.T, p_t), span).T.astype(BF)


def attend_first_kernel(
    core, limits, x_own, x_oth, here, there,
    own, oth, context, probs, weights, bias, vec, b_in, arrived,
):
    width = context.shape[1]
    half = width // 2

    @pl.when(pl.program_id(0) == 0)
    def _():
        copies = [
            pltpu.make_async_copy(
                source, weights.at[pl.ds(pl.multiple_of(start * half, half), half)], arrived.at[i]
            )
            for i, (source, start) in enumerate(((here, core[0]), (there, 1 - core[0])))
        ]
        for copy in copies:
            copy.start()
        for copy in copies:
            copy.wait()
        rows = weights[:, 3 * width :].astype(F32).T[:16]
        vec[...] = rows
        for l in range(4):
            b_in[l] = rows[V_IN + l : V_IN + l + 1]
        pairs = rows[V_QV : V_QV + 2].astype(BF)
        sides = [
            mm(pairs[0:1, k : k + half], interleave(0)) + mm(pairs[1:2, k : k + half], interleave(1))
            for k in (0, half)
        ]
        line = jnp.concatenate([sides[0], jnp.zeros((1, width), F32), sides[1]], axis=1)
        bias[...] = jnp.broadcast_to(line, bias.shape)

    attend_body(
        pl.program_id(0), limits, x_own, x_oth, weights, bias, own, oth, context, probs
    )


def attend_more_kernel(first, limits, x_own, x_oth, weights, bias, *rest):
    attend_body(pl.program_id(0) + first, limits, x_own, x_oth, weights, bias, *rest[-4:])


def attend_specs(micro, rows, width, first):
    span, heads = rows // micro, width // HD

    def block(n):
        return pl.BlockSpec((span, n), lambda g, *_: (g + first, 0))

    specs = [
        block(3 * width),
        block(2 * width),
        block(width),
        pl.BlockSpec((None, heads, 2 * span, span), lambda g, *_: (g + first, 0, 0, 0)),
    ]
    shapes = [
        jax.ShapeDtypeStruct((rows, 3 * width), BF),
        jax.ShapeDtypeStruct((rows, 2 * width), BF),
        jax.ShapeDtypeStruct((rows, width), BF),
        jax.ShapeDtypeStruct((micro, heads, 2 * span, span), BF),
    ]
    return block(width), specs, shapes


def attend_first(core, limits, x_own, x_oth, here, there, count):
    rows, width = x_own.shape
    block, specs, shapes = attend_specs(limits.shape[0], rows, width, 0)

    def whole(*shape):
        return pl.BlockSpec(shape, lambda g, *_: (0,) * len(shape))

    return pl.pallas_call(
        attend_first_kernel,
        grid_spec=pltpu.PrefetchScalarGridSpec(
            num_scalar_prefetch=2,
            grid=(count,),
            in_specs=[block, block] + [pl.BlockSpec(memory_space=pl.ANY)] * 2,
            out_specs=specs
            + [whole(width, ONE), whole(8, 3 * width), whole(16, width), whole(4, 1, width)],
            scratch_shapes=[pltpu.SemaphoreType.DMA((2,))],
        ),
        out_shape=shapes
        + [
            jax.ShapeDtypeStruct((width, ONE), BF),
            jax.ShapeDtypeStruct((8, 3 * width), F32),
            jax.ShapeDtypeStruct((16, width), F32),
            jax.ShapeDtypeStruct((4, 1, width), F32),
        ],
        name="attend_first",
        **vmem(56, 10 * count << 30, 8 * count << 20),
    )(core, limits, x_own, x_oth, here, there)


def attend_more(limits, x_own, x_oth, weights, bias, first, earlier):
    micro = limits.shape[0]
    rows, width = x_own.shape
    block, specs, shapes = attend_specs(micro, rows, width, first)

    def whole(*shape):
        return pl.BlockSpec(shape, lambda g, *_: (0,) * len(shape))

    count = micro - first
    return pl.pallas_call(
        functools.partial(attend_more_kernel, first),
        grid_spec=pltpu.PrefetchScalarGridSpec(
            num_scalar_prefetch=1,
            grid=(count,),
            in_specs=[block, block, whole(width, 3 * width), whole(8, 3 * width)]
            + [pl.BlockSpec(memory_space=pl.ANY)] * len(earlier),
            out_specs=specs,
        ),
        out_shape=shapes,
        input_output_aliases={5 + i: i for i in range(len(earlier))},
        name="attend_more",
        **vmem(52, 10 * count << 30, 8 * count << 20),
    )(limits, x_own, x_oth, weights, bias, *earlier)


def attend_back_body(own, oth, probs, d_context, d_own, d_oth):
    span, width = d_context.shape
    for at in range(0, width, 128):
        q = apart(own[:, pl.ds(at, 128)] * jnp.asarray(0.125, BF))
        k = jnp.concatenate([own[:, pl.ds(at + width, 128)], oth[:, pl.ds(at, 128)]], axis=0)
        v = jnp.concatenate(
            [own[:, pl.ds(at + 2 * width, 128)], oth[:, pl.ds(at + width, 128)]], axis=0
        )
        d_c = apart(d_context[:, pl.ds(at, 128)])
        p_b = jnp.concatenate([probs[at // HD], probs[at // HD + 1]], axis=1)
        p_f = p_b.astype(F32)
        d_p = mm_nt(v, d_c)
        weighted = jnp.sum(p_f * d_p, axis=0, keepdims=True)
        d_s = (p_f * (d_p - weighted)).astype(BF)
        d_own[:, pl.ds(at, 128)] = (beside(mm(k.T, d_s), span).T * 0.125).astype(BF)
        d_k = mm(d_s, q).astype(BF)
        d_v = mm(p_b, d_c).astype(BF)
        d_own[:, pl.ds(at + width, 128)] = d_k[:span]
        d_own[:, pl.ds(at + 2 * width, 128)] = d_v[:span]
        d_oth[:, pl.ds(at, 128)] = d_k[span:]
        d_oth[:, pl.ds(at + width, 128)] = d_v[span:]


def token_parts(d_own, d_oth, w_qkv, d_first, d_tokens, x_part):
    width = d_first.shape[1]
    d_tokens[...] = d_first[...] + mm_nt(d_own[...], w_qkv[...])
    x_part[...] = (
        mm_nt(d_oth[:, :width], w_qkv[:, width : 2 * width])
        + mm_nt(d_oth[:, width:], w_qkv[:, 2 * width :])
    ).astype(BF)


def bias_sums(d_own, d_oth):
    width = d_oth.shape[1] // 2
    of_queries = jnp.sum(d_own[:, :width].astype(F32), axis=0, keepdims=True)
    of_values = jnp.sum(
        d_own[:, 2 * width :].astype(F32) + d_oth[:, width:].astype(F32), axis=0, keepdims=True
    )
    return rows_of(of_queries, of_values)


def attend_back_kernel(
    own, oth, probs, d_context, d_first, weights, d_own, d_oth, sums, d_tokens, x_part, w_qkv, arrived
):
    fetch = pltpu.make_async_copy(weights.at[:, pl.ds(0, w_qkv.shape[1])], w_qkv, arrived)
    fetch.start()
    attend_back_body(own, oth, probs, d_context, d_own, d_oth)
    fetch.wait()
    token_parts(d_own, d_oth, w_qkv, d_first, d_tokens, x_part)
    sums[...] = bias_sums(d_own, d_oth)


def attend_back(own, oth, probs, d_context, d_first, weights):
    _, heads, _, span = probs.shape
    rows, width = d_context.shape

    def block(n):
        return pl.BlockSpec((span, n), lambda g: (0, 0))

    return pl.pallas_call(
        attend_back_kernel,
        grid=(1,),
        in_specs=[block(3 * width), block(2 * width)]
        + [pl.BlockSpec((None, heads, 2 * span, span), lambda g: (0, 0, 0, 0))]
        + [block(width), block(width), pl.BlockSpec(memory_space=pl.ANY)],
        out_specs=[block(3 * width), block(2 * width), pl.BlockSpec((8, width), lambda g: (0, 0))]
        + [block(width), block(width)],
        out_shape=[
            jax.ShapeDtypeStruct((span, 3 * width), BF),
            jax.ShapeDtypeStruct((span, 2 * width), BF),
            jax.ShapeDtypeStruct((8, width), F32),
            jax.ShapeDtypeStruct((rows, width), F32),
            jax.ShapeDtypeStruct((span, width), BF),
        ],
        scratch_shapes=[pltpu.VMEM((width, 3 * width), BF), pltpu.SemaphoreType.DMA],
        name="attend_back",
        **vmem(56, 9 << 30, 8 << 20),
    )(own, oth, probs, d_context, d_first, weights)


def attend_last_kernel(
    core, own, oth, probs, d_context, d_first, sums_qv, sums, in_sums,
    weights, d_own_first, d_oth_first, x_own, x_oth, _,
    d_tokens, x_part, mine, away,
    w_qkv, d_own, d_oth, x_here, x_there, total, columns, result, arrived, done,
):
    g, last = pl.program_id(0), pl.num_programs(0) - 1
    span, width = d_context.shape
    half = width // 2
    rows = pl.ds(pl.multiple_of((g + 1) * span, span), span)
    d_own_here, d_oth_here = d_own.at[rows], d_oth.at[rows]
    first = pl.ds(0, span)
    copies = [
        pltpu.make_async_copy(source, into, arrived.at[i])
        for i, (source, into) in enumerate(
            (
                (weights.at[:, pl.ds(0, 3 * width)], w_qkv),
                (d_own_first, d_own.at[first]),
                (d_oth_first, d_oth.at[first]),
                (x_own, x_here),
                (x_oth, x_there),
            )
        )
    ]

    def send(k, start, lanes):
        return pltpu.make_async_copy(
            result.at[k, :, pl.ds(start, lanes)], (mine, away)[k].at[:, pl.ds(start, lanes)],
            done.at[k, start // width],
        )

    @pl.when(g == 0)
    def _():
        for copy in copies:
            copy.start()
        total[...] = sums_qv[...]

    attend_back_body(own, oth, probs, d_context, d_own_here, d_oth_here)

    @pl.when(g == 0)
    def _():
        for copy in copies:
            copy.wait()

    token_parts(d_own_here, d_oth_here, w_qkv, d_first, d_tokens, x_part)
    total[...] += bias_sums(d_own_here, d_oth_here)

    @pl.when(g == last)
    def _():
        qv = total[0:2].astype(BF)
        split = [
            jnp.concatenate([mm_nt(qv[i : i + 1], interleave(parity)) for i in (0, 1)], axis=1)
            for parity in (0, 1)
        ]
        lines = [sums[0:6]] + [in_sums[i] for i in range(4)] + split
        columns[...] = jnp.concatenate(lines + [jnp.zeros((116, width), F32)], axis=0).T.astype(BF)
        for k, side in enumerate((core[0], 1 - core[0])):
            place = pl.ds(pl.multiple_of(side * half, half), half)
            result[k, :, AT_VEC:] = columns[place]
            send(k, AT_VEC, ONE - AT_VEC).start()
            here, there = x_here[:, place], x_there[:, place]
            for j in range(3):
                lanes = slice(j * width, (j + 1) * width)
                grad = mm_tn(here, d_own[:, lanes])
                if j:
                    grad += mm_tn(there, d_oth[:, (j - 1) * width : j * width])
                result[k, :, lanes] = grad.astype(BF)
                send(k, j * width, width).start()
        for k in (0, 1):
            for i in range(4):
                send(k, i * width, width if i < 3 else ONE - AT_VEC).wait()


def attend_last(core, own, oth, probs, d_context, d_first, weights, part, x_own, x_oth, sums, in_sums):
    micro, heads, _, span = probs.shape
    rows, width = d_context.shape
    half = width // 2
    d_own, d_oth, sums_qv, d_tokens = part

    def block(n):
        return pl.BlockSpec((span, n), lambda g, *_: (g + 1, 0))

    def whole(*shape):
        return pl.BlockSpec(shape, lambda g, *_: (0,) * len(shape))

    anywhere = pl.BlockSpec(memory_space=pl.ANY)
    return pl.pallas_call(
        attend_last_kernel,
        grid_spec=pltpu.PrefetchScalarGridSpec(
            num_scalar_prefetch=1,
            grid=(micro - 1,),
            in_specs=[block(3 * width), block(2 * width)]
            + [pl.BlockSpec((None, heads, 2 * span, span), lambda g, *_: (g + 1, 0, 0, 0))]
            + [block(width), block(width), whole(8, width), whole(8, width), whole(4, 1, width)]
            + [anywhere] * 6,
            out_specs=[block(width), pl.BlockSpec((span, width), lambda g, *_: (g, 0))]
            + [anywhere] * 2,
            scratch_shapes=[
                pltpu.VMEM((width, 3 * width), BF),
                pltpu.VMEM((rows, 3 * width), BF),
                pltpu.VMEM((rows, 2 * width), BF),
                pltpu.VMEM((rows, width), BF),
                pltpu.VMEM((rows, width), BF),
                pltpu.VMEM((8, width), F32),
                pltpu.VMEM((width, 128), BF),
                pltpu.VMEM((2, half, ONE), BF),
                pltpu.SemaphoreType.DMA((5,)),
                pltpu.SemaphoreType.DMA((2, 4)),
            ],
        ),
        out_shape=[
            jax.ShapeDtypeStruct((rows, width), F32),
            jax.ShapeDtypeStruct((rows - span, width), BF),
            jax.ShapeDtypeStruct((half, ONE), BF),
            jax.ShapeDtypeStruct((half, ONE), BF),
        ],
        input_output_aliases={14: 0},
        name="attend_last",
        **vmem(40, 24 << 30, 20 << 20),
    )(
        core, own, oth, probs, d_context, d_first, sums_qv, sums, in_sums,
        weights, d_own, d_oth, x_own, x_oth, d_tokens,
    )


def norm_parts(value):
    centre = value - jnp.mean(value, axis=-1, keepdims=True)
    inverse = lax.rsqrt(jnp.mean(centre * centre, axis=-1, keepdims=True) + EPS)
    return centre * inverse, inverse


def norm_back(grad, hat, inverse, gain):
    scaled = grad * gain
    return inverse * (
        scaled
        - jnp.mean(scaled, axis=-1, keepdims=True)
        - hat * jnp.mean(scaled * hat, axis=-1, keepdims=True)
    )


def rows_of(*terms):
    return jnp.concatenate(terms + (jnp.zeros((8 - len(terms), terms[0].shape[1]), F32),), axis=0)


def middle_kernel(
    core, vec, b_in, x, context, cot, w_mine, w_away,
    sums, in_sums, grad_mine, grad_away, block_out, d_first, d_context,
    x_in, c_in, cot_in, normed_b, hat_one, inv_one, outer, active, slope, d_outer, d_normed, result,
    d_ctx, weights, grads, from_rows, from_weights, to_rows, to_grads,
):
    t = pl.program_id(0)
    rows, width = x_in.shape
    half, parts, step = width // 2, active.shape[0], rows // 3
    mine, away = pl.multiple_of(core[0] * half, half), pl.multiple_of((1 - core[0]) * half, half)
    blocks = [pl.ds(r * step, step) for r in range(3)]
    w_out = weights.at[2 * parts]

    def row(i):
        return vec[i : i + 1, :]

    def fetch(i):
        lanes = pl.ds(i * width, width)
        return [
            pltpu.make_async_copy(
                source.at[:, lanes], weights.at[i, pl.ds(start, half)], from_weights.at[i, k]
            )
            for k, (source, start) in enumerate(((w_mine, mine), (w_away, away)))
        ]

    def rows_in(r, *which):
        ends = ((context, c_in), (x, x_in), (cot, cot_in))
        return [
            pltpu.make_async_copy(ends[k][0].at[blocks[r]], ends[k][1].at[blocks[r]], from_rows.at[k, r])
            for k in which
        ]

    def rows_out(k, r):
        source, into = ((result, block_out), (d_normed, d_first), (d_ctx, d_context))[k]
        return pltpu.make_async_copy(source.at[blocks[r]], into.at[blocks[r]], to_rows.at[k, r])

    def grads_out(i, slot, count):
        return [
            pltpu.make_async_copy(
                grads.at[slot, k, pl.ds(0, count)], into.at[pl.ds(i, count)], to_grads.at[slot, k]
            )
            for k, into in enumerate((grad_mine, grad_away))
        ]

    def wait_part(i):
        for copy in fetch(i) + fetch(parts + i):
            copy.wait()

    def forward(l):
        w_in, w_back = weights.at[l], weights.at[parts + l]

        def hidden(r):
            return mm(normed_b[blocks[r]], w_in[...]) + b_in[0]

        def bend(r, inner):
            phi = 0.5 + 0.5 * lax.erf(inner * (0.5**0.5))
            act = (inner * phi).astype(BF)
            active[l, blocks[r]] = act
            slope[l, blocks[r]] = phi + inner * jnp.exp(-0.5 * inner * inner) * 0.3989422804014327
            return act

        inner = [hidden(0), hidden(1)]
        for r in range(3):
            act = bend(r, inner[r])
            if r == 0:
                inner.append(hidden(2))
            outer[blocks[r]] += mm(act, w_back[...])

    def backward(l):
        w_in, w_back = weights.at[l], weights.at[parts + l]

        def back(r):
            return mm_nt(d_outer[blocks[r]], w_back[...])

        d_act = [back(0), back(1)]
        pieces = []
        bias = jnp.zeros((1, width), F32)
        for r, at in enumerate(blocks):
            d_inner = (d_act[r] * slope[l, at]).astype(BF)
            pieces.append(d_inner)
            if r == 0:
                d_act.append(back(2))
            bias += jnp.sum(d_inner.astype(F32), axis=0, keepdims=True)
            d_normed[at] += mm_nt(d_inner, w_in[...])
        d_inner = jnp.concatenate(pieces, axis=0)
        in_sums[0] = bias
        slot = l % 2 if isinstance(l, int) else lax.rem(l, 2)
        if not isinstance(l, int):

            @pl.when(l >= 2)
            def _():
                for copy in grads_out(2 * l - 4, slot, 2):
                    copy.wait()

        for k, start in enumerate((mine, away)):
            cols = pl.ds(start, half)
            grads[slot, k, 0] = mm_tn(normed_b[:, cols], d_inner).astype(BF)
            grads[slot, k, 1] = mm_tn(active[l, :, cols], d_outer[...]).astype(BF)
        for copy in grads_out(2 * l, slot, 2):
            copy.start()

    @pl.when(t == 0)
    def _():
        for copy in fetch(2 * parts):
            copy.start()
        for r in range(3):
            for copy in rows_in(r, 0, 1):
                copy.start()
        for i in range(parts):
            for copy in fetch(i) + fetch(parts + i):
                copy.start()
        for r in range(3):
            rows_in(r, 2)[0].start()
        for copy in fetch(2 * parts):
            copy.wait()
        wait_part(0)
        for r, at in enumerate(blocks):
            for copy in rows_in(r, 0, 1):
                copy.wait()
            hat, inverse = norm_parts(x_in[at].astype(F32) + mm(c_in[at], w_out[...]) + row(V_OUT))
            hat_one[at] = hat
            inv_one[at] = jnp.broadcast_to(inverse, (step, 128))
            value = hat * row(V_GAIN1) + row(V_SHIFT1)
            normed_b[at] = value.astype(BF)
            outer[at] = value + row(V_BACK)
        forward(0)

    @pl.when((t > 0) & (t < parts))
    def _():
        for i in range(1, parts):

            @pl.when(t == i)
            def _():
                wait_part(i)

        forward(t)

    @pl.when(t == parts)
    def _():
        total = [jnp.zeros((1, width), F32) for _ in range(3)]
        for r, at in enumerate(blocks):
            rows_in(r, 2)[0].wait()
            hat, inverse = norm_parts(outer[at])
            result[at] = (hat * row(V_GAIN2) + row(V_SHIFT2)).astype(BF)
            rows_out(0, r).start()
            grad = cot_in[at].astype(F32)
            d_second = norm_back(grad, hat, inverse, row(V_GAIN2))
            d_b = d_second.astype(BF)
            d_outer[at] = d_b
            d_normed[at] = d_second
            for i, term in enumerate((d_b.astype(F32), grad * hat, grad)):
                total[i] += jnp.sum(term, axis=0, keepdims=True)
        for i, term in zip((V_BACK, V_GAIN2, V_SHIFT2), total):
            sums[i : i + 1] = term
        backward(0)

    @pl.when((t > parts) & (t < 2 * parts))
    def _():
        backward(t - parts)

    @pl.when(t == 2 * parts)
    def _():
        total = [jnp.zeros((1, width), F32) for _ in range(3)]
        for r, at in enumerate(blocks):
            grad, hat = d_normed[at], hat_one[at]
            back = norm_back(grad, hat, inv_one[at, 0:1], row(V_GAIN1))
            d_normed[at] = back
            rows_out(1, r).start()
            d_b = back.astype(BF)
            d_outer[at] = d_b
            for i, term in enumerate((d_b.astype(F32), grad * hat, grad)):
                total[i] += jnp.sum(term, axis=0, keepdims=True)
            d_ctx[at] = mm_nt(d_b, w_out[...]).astype(BF)
            rows_out(2, r).start()
        for i, term in zip((V_OUT, V_GAIN1, V_SHIFT1), total):
            sums[i : i + 1] = term
        for copy in grads_out(2 * parts - 4, parts % 2, 2):
            copy.wait()
        for k, start in enumerate((mine, away)):
            grads[parts % 2, k, 0] = mm_tn(c_in[:, pl.ds(start, half)], d_outer[...]).astype(BF)
        for copy in grads_out(2 * parts, parts % 2, 1):
            copy.start()
        for copy in grads_out(2 * parts - 2, (parts - 1) % 2, 2) + grads_out(2 * parts, parts % 2, 1):
            copy.wait()
        for k in range(3):
            for r in range(3):
                rows_out(k, r).wait()


def middle(core, vec, b_in, x, context, cot, w_mine, w_away):
    rows, width = x.shape
    parts = b_in.shape[0]
    half = width // 2

    def whole(*shape):
        return pl.BlockSpec(shape, lambda t, *_: (0,) * len(shape))

    def later(t):
        return jnp.clip(t - parts, 0, parts - 1)

    anywhere = pl.BlockSpec(memory_space=pl.ANY)
    grads = ((2 * parts + 1, half, width), BF)
    shapes = (
        ((8, width), F32), ((parts, 1, width), F32), grads, grads,
        ((rows, width), BF), ((rows, width), F32), ((rows, width), BF),
    )
    return pl.pallas_call(
        middle_kernel,
        grid_spec=pltpu.PrefetchScalarGridSpec(
            num_scalar_prefetch=1,
            grid=(2 * parts + 1,),
            in_specs=[
                whole(16, width),
                pl.BlockSpec((1, 1, width), lambda t, *_: (jnp.minimum(t, parts - 1), 0, 0)),
            ]
            + [anywhere] * 5,
            out_specs=[whole(8, width)]
            + [pl.BlockSpec((1, 1, width), lambda t, *_: (later(t), 0, 0))]
            + [anywhere] * 5,
            scratch_shapes=[pltpu.VMEM((rows, width), BF)] * 4
            + [pltpu.VMEM((rows, width), F32), pltpu.VMEM((rows, 128), F32)]
            + [pltpu.VMEM((rows, width), F32)]
            + [pltpu.VMEM((parts, rows, width), BF), pltpu.VMEM((parts, rows, width), F32)]
            + [pltpu.VMEM((rows, width), BF), pltpu.VMEM((rows, width), F32)]
            + [pltpu.VMEM((rows, width), BF)] * 2
            + [
                pltpu.VMEM((2 * parts + 1, width, width), BF),
                pltpu.VMEM((2, 2, 2, half, width), BF),
                pltpu.SemaphoreType.DMA((3, 3)),
                pltpu.SemaphoreType.DMA((2 * parts + 1, 2)),
                pltpu.SemaphoreType.DMA((3, 3)),
                pltpu.SemaphoreType.DMA((2, 2)),
            ],
        ),
        out_shape=[jax.ShapeDtypeStruct(*shape) for shape in shapes],
        name="middle",
        **vmem(63, 24 << 30, 30 << 20),
    )(core, vec, b_in, x, context, cot, w_mine, w_away)


def on_device(
    tokens, lengths, cotangent, w_qkv, b_qv, w_out, b_out, w_in, b_in, w_back, b_back,
    gain_one, shift_one, gain_two, shift_two,
):
    micro, _, span, width = tokens.shape
    ff = w_in.shape[1]
    rows = micro * span
    yh = lax.axis_index("yh")
    c = lax.axis_index("c")
    core = c.reshape(1)
    x_own = tokens.reshape(rows, width)
    tie = lax.optimization_barrier
    order = arrival()

    packed = pack(
        w_qkv, w_out, w_in, w_back,
        (b_out, b_back, gain_one, shift_one, gain_two, shift_two, b_in, b_qv),
    )
    x_oth = lax.ppermute(x_own, "yh", SWAP)
    column = gather_column(packed)
    near = [column] + from_ring(column, 0)
    one = jnp.concatenate([part[:, :ONE] for part in near], axis=0)
    two = jnp.concatenate([part[:, ONE:] for part in near], axis=0)
    one_parts = [one] + from_ring(one, 1)
    limits = jnp.stack([lengths[:, 0] - yh * span, lengths[:, 0] - (1 - yh) * span], axis=1)
    one_parts, two, x_oth, limits = tie((one_parts, two, x_oth, limits))
    two_parts = [two] + from_ring(two, 1)
    one = sort_rows(order, one_parts)
    one_away = lax.ppermute(one, "c", SWAP)

    *seen, weights, bias, vec, b_in = attend_first(core, limits, x_own, x_oth, one, one_away, micro - 1)
    seen, two_parts = tie((seen, two_parts))
    two = sort_rows(order, two_parts)
    seen, two = tie((seen, two))
    two_away = lax.ppermute(two, "c", SWAP)
    mixed, mixed_oth, context, probs = attend_more(
        limits, x_own, x_oth, weights, bias, micro - 1, seen
    )
    sums, in_sums, ff_mine, ff_away, block_out, d_first, d_context = middle(
        core, vec, b_in, x_own, context, cotangent.reshape(rows, width), two, two_away
    )
    ff_recv = lax.ppermute(ff_away, "c", SWAP)
    inputs = (mixed, mixed_oth, probs, d_context, d_first, weights)
    *part, x_near = attend_back(*inputs)
    ff_recv, part = tie((ff_recv, part))
    ff_own, *ff_sent = split_rows(order, ff_mine, ff_recv)
    ff_sent, part, x_near = tie((ff_sent, part, x_near))
    x_near = lax.ppermute(x_near, "yh", SWAP)
    ff_got = to_ring(ff_sent, 1)
    d_tokens, x_part, g_mine, g_away = attend_last(
        core, *inputs, part, x_own, x_oth, sums, in_sums
    )
    g_away, x_near = tie((g_away, x_near))
    x_middle = lax.ppermute(x_part[:span], "yh", SWAP)
    x_back = lax.ppermute(x_part[span:], "yh", SWAP)
    ff_got, g_away = tie((ff_got, g_away))
    g_recv = lax.ppermute(g_away, "c", SWAP)
    ff_own, *ff_sent = fold_rows(ff_own, ff_got)
    ff_got = to_ring(ff_sent, 0)
    g_recv, ff_sent = tie((g_recv, ff_sent))
    g_own, *g_sent = split_rows(order, g_mine, g_recv)
    g_sent, ff_got[0], x_middle = tie((g_sent, ff_got[0], x_middle))
    g_got = to_ring(g_sent, 1)
    ff_parts = column_parts(ff_own, ff_got)
    g_own, *g_sent = fold_rows(g_own, g_got)
    g_got = to_ring(g_sent, 0)
    o_in, o_back, o_out = finish_early(ff_parts)
    d_tokens = d_tokens + jnp.concatenate([x_near, x_middle, x_back], axis=0).astype(F32)
    g_got, o_in, o_back, o_out, d_tokens = tie((g_got, o_in, o_back, o_out, d_tokens))
    g_parts = column_parts(g_own, g_got)
    o_qkv, lines = finish_late(g_parts)
    return (
        block_out.reshape(tokens.shape),
        d_tokens.reshape(tokens.shape),
        o_qkv,
        lines[7],
        o_out,
        lines[0],
        o_in,
        lines[6],
        o_back,
        lines[1],
        lines[2],
        lines[3],
        lines[4],
        lines[5],
    )


def solution(mesh):
    fine = Mesh(mesh.devices.reshape(2, 4, 4, 2, 2), DEVICES)
    pairs = ("yl", "x", "z", "c")
    data = P(None, pairs, "yh", None)
    weight, vector = P(DEVICES, None), P(DEVICES)
    kinds = (weight, vector) * 4
    return jax.shard_map(
        on_device,
        mesh=fine,
        in_specs=(data, P(None, pairs), data) + kinds + (vector,) * 4,
        out_specs=(data, data) + kinds + (vector,) * 4,
        check_vma=False,
    )
```

```python
import functools

import jax
import jax.numpy as jnp
import numpy as np
from jax import lax
from jax.experimental import pallas as pl
from jax.experimental.pallas import tpu as pltpu
from jax.sharding import Mesh, PartitionSpec as P

HD = 64
EPS = 1e-05
F32 = jnp.float32
BF = jnp.bfloat16
DEVICES = ("yl", "x", "z", "c", "yh")
SWAP = ((0, 1), (1, 0))
STEPS = (0, 1, 3, 2)
AT_VEC = 3 * 768
ONE, TWO = AT_VEC + 128, 9 * 768
V_OUT, V_BACK, V_GAIN1, V_SHIFT1, V_GAIN2, V_SHIFT2, V_IN, V_QV = 0, 1, 2, 3, 4, 5, 6, 10


def mm(a, b):
    return lax.dot_general(a, b, (((1,), (0,)), ((), ())), preferred_element_type=F32)


def mm_nt(a, b):
    return lax.dot_general(a, b, (((1,), (1,)), ((), ())), preferred_element_type=F32)


def mm_tn(a, b):
    return lax.dot_general(a, b, (((0,), (0,)), ((), ())), preferred_element_type=F32)


def vmem(mib, flops=0, moved=0):
    return dict(
        compiler_params=pltpu.CompilerParams(vmem_limit_bytes=mib << 20),
        cost_estimate=pl.CostEstimate(flops=flops, bytes_accessed=moved, transcendentals=0),
    )


ROW = [i % 6 for i in range(36)] + [i // 4 for i in range(24)] + [i // 2 for i in range(12)]
COLUMN = [i // 6 for i in range(36)] + [V_IN + i % 4 for i in range(24)] + [V_QV + i % 2 for i in range(12)]


SIZES = (6, 6, 6, 6, 6, 6, 24, 12)


def maps():
    rows, columns = np.zeros((8, 128), np.float32), np.zeros((128, 128), np.float32)
    for i, (r, l) in enumerate(zip(ROW, COLUMN)):
        rows[r, i] = columns[i, l] = 1
    f, place = np.arange(768)[:, None], np.arange(768)[None, :]
    units = (f == 4 * (place % 192) + place // 192).astype(np.float32)
    r, f = np.arange(32)[:, None], np.arange(24)[None, :]
    spread = ((r % 8 < 6) & (f == 4 * (r % 8) + r // 8)).astype(np.float32)
    return rows, columns, units, spread


def pack_kernel(*refs):
    w_qkv, w_out, w_in, w_back = refs[:4]
    vectors = refs[4:12]
    rows, columns, units, spread, out, line, stack = refs[12:]
    width = w_out.shape[1]
    line[...] = jnp.zeros_like(line)
    stack[...] = jnp.zeros_like(stack)
    at = 0
    for size, vector in zip(SIZES, vectors):
        line[0:1, at : at + size] = vector[...].astype(F32).reshape(1, size)
        at += size
    out[:, : 3 * width] = w_qkv[...]
    out[:, AT_VEC:ONE] = mm((line[0:1] * rows[...]).astype(BF), columns[...])[:6].astype(BF)
    for b in range(4):
        stack[8 * b : 8 * b + 6] = w_in[:, b * width : (b + 1) * width].astype(F32)
    moved = mm(stack[...].astype(BF), units[...])
    merged = mm(spread[...], w_back[...])
    for l in range(4):
        for b in range(4):
            start = ONE + l * width + 192 * b
            out[:, start : start + 192] = moved[8 * b : 8 * b + 6, 192 * l : 192 * (l + 1)].astype(BF)
        start = ONE + (4 + l) * width
        out[:, start : start + width] = merged[8 * l : 8 * l + 6].astype(BF)
    out[:, ONE + 8 * width :] = w_out[...]


def pack(w_qkv, w_out, w_in, w_back, vectors):
    rows, columns, units, spread = maps()
    return pl.pallas_call(
        pack_kernel,
        out_shape=jax.ShapeDtypeStruct((6, ONE + TWO), BF),
        scratch_shapes=[pltpu.VMEM((8, 128), F32), pltpu.VMEM((32, 768), F32)],
        name="pack",
    )(
        w_qkv, w_out, w_in, w_back, *vectors, jnp.asarray(rows),
        *(jnp.asarray(part, BF) for part in (columns, units, spread)),
    )


def exact_nt(a, b):
    return lax.dot_general(
        a, b, (((1,), (1,)), ((), ())), precision=lax.Precision.HIGHEST, preferred_element_type=F32
    )


def exact_tn(a, b):
    return lax.dot_general(
        a, b, (((0,), (0,)), ((), ())), precision=lax.Precision.HIGHEST, preferred_element_type=F32
    )


def thirds(value):
    high = value.astype(BF)
    rest = value - high.astype(F32)
    middle_ = rest.astype(BF)
    return jnp.concatenate([high, middle_, (rest - middle_.astype(F32)).astype(BF)], axis=0)


def finish_early_kernel(a, b, d, e, units, spread, g_in, g_back, g_out, stack, rows):
    width = g_back.shape[1]
    total = (a[...] + b[...]) + (d[...] + e[...])
    stack[...] = jnp.zeros_like(stack)
    rows[...] = jnp.zeros_like(rows)
    for l in range(4):
        for b_ in range(4):
            start = 2 * l * width + 192 * b_
            stack[8 * b_ : 8 * b_ + 6, 192 * l : 192 * (l + 1)] = total[:, start : start + 192]
        rows[8 * l : 8 * l + 6] = total[:, (2 * l + 1) * width : (2 * l + 2) * width]
    moved = mm_nt(thirds(stack[...]), units[...])
    moved = moved[:32] + moved[32:64] + moved[64:]
    for b_ in range(4):
        g_in[:, b_ * width : (b_ + 1) * width] = moved[8 * b_ : 8 * b_ + 6]
    g_back[...] = exact_tn(spread[...], rows[...])
    g_out[...] = total[:, 8 * width :]


def finish_early(parts):
    _, _, units, spread = maps()
    return pl.pallas_call(
        finish_early_kernel,
        out_shape=[jax.ShapeDtypeStruct(shape, F32) for shape in ((6, 3072), (24, 768), (6, 768))],
        scratch_shapes=[pltpu.VMEM((32, 768), F32)] * 2,
        name="finish_early",
        **vmem(16, 1 << 28, 1 << 20),
    )(*parts, jnp.asarray(units, BF), jnp.asarray(spread))


def finish_late_kernel(*refs):
    a, b, d, e, rows, columns, g_qkv = refs[:7]
    vectors, line = refs[7:-1], refs[-1]
    total = (a[...] + b[...]) + (d[...] + e[...])
    g_qkv[...] = total[:, :AT_VEC]
    line[...] = exact_nt(total[:, AT_VEC:], columns[...]) * rows[:6]
    line[0:1] = jnp.sum(line[...], axis=0, keepdims=True)
    at = 0
    for size, vector in zip(SIZES, vectors):
        vector[...] = line[0:1, at : at + size].reshape(size)
        at += size


def finish_late(parts):
    rows, columns, _, _ = maps()
    g_qkv, *vectors = pl.pallas_call(
        finish_late_kernel,
        out_shape=[
            jax.ShapeDtypeStruct(shape, F32) for shape in ((6, AT_VEC),) + tuple((n,) for n in SIZES)
        ],
        scratch_shapes=[pltpu.VMEM((6, 128), F32)],
        name="finish_late",
        **vmem(16, 1 << 24, 1 << 18),
    )(*parts, jnp.asarray(rows), jnp.asarray(columns))
    return g_qkv, vectors


def interleave(parity):
    row = lax.broadcasted_iota(jnp.int32, (384, 768), 0)
    return (lax.broadcasted_iota(jnp.int32, (384, 768), 1) == 2 * row + parity).astype(BF)


def column_pairs(flip_c, flip_y):
    pairs = []
    for a in (0, 1):
        for b in (0, 1):
            for d in (0, 1):
                pairs.append((b * 4 + (a ^ flip_c) * 2 + (d ^ flip_y), a * 4 + b * 2 + d))
    return pairs


FLIPS = ((0, 0), (0, 1), (1, 0), (1, 1))


def gather_column(shard):
    parts = [lax.ppermute(shard, ("yl", "c", "yh"), column_pairs(*flip)) for flip in FLIPS]
    return jnp.concatenate(parts, axis=0)


def plane_pairs(step, stage):
    pairs = []
    for x in range(4):
        for z in range(4):
            for c in range(2):
                near = (x, (z + step) % 4) if c == stage else ((x + step) % 4, z)
                pairs.append(((near[0] * 4 + near[1]) * 2 + c, (x * 4 + z) * 2 + c))
    return pairs


def from_ring(block, stage):
    return [lax.ppermute(block, ("x", "z", "c"), plane_pairs(step, stage)) for step in STEPS[1:]]


def arrival():
    yl, x, z, c, yh = (lax.axis_index(name) for name in DEVICES)
    j = jnp.arange(384)
    steps = jnp.array(STEPS)
    last, early, flip = steps[j // 96], steps[(j % 96) // 24], (j % 24) // 6
    xx = (x + jnp.where(c == 0, last, early)) % 4
    zz = (z + jnp.where(c == 0, early, last)) % 4
    row = xx * 96 + zz * 24 + (yl ^ (flip // 2)) * 12 + (yh ^ (flip % 2)) * 6 + j % 6
    return (jnp.arange(384)[:, None] == row[None, :]).astype(BF)


def wide(columns):
    return next(n for n in (2304, 3072, columns) if columns % n == 0)


def sort_kernel(order, *refs):
    blocks, out = refs[:-1], refs[-1]
    out[...] = mm(order[...], jnp.concatenate([b[...] for b in blocks], axis=0)).astype(BF)


def sort_rows(order, blocks):
    rows, columns = blocks[0].shape
    lanes = wide(columns)
    return pl.pallas_call(
        sort_kernel,
        grid=(columns // lanes,),
        in_specs=[pl.BlockSpec(order.shape, lambda j: (0, 0))]
        + [pl.BlockSpec((rows, lanes), lambda j: (0, j))] * 4,
        out_specs=pl.BlockSpec((4 * rows, lanes), lambda j: (0, j)),
        out_shape=jax.ShapeDtypeStruct((4 * rows, columns), BF),
        name="sort_rows",
        **vmem(24, 2 * 384 * 384 * columns, 2 * 2 * 384 * columns),
    )(order, *blocks)


def split_kernel(order, mine, recv, *pieces):
    parts, _, lanes = mine.shape
    size = pieces[0].shape[0]
    for p in range(parts):
        total = (mine[p].astype(F32) + recv[p].astype(F32)).astype(BF)
        rows = mm_tn(order[...], total)
        for i, piece in enumerate(pieces):
            piece[:, p * lanes : (p + 1) * lanes] = rows[i * size : (i + 1) * size].astype(piece.dtype)


def split_rows(order, mine, recv, room=24):
    if mine.ndim == 2:
        mine, recv = mine[None], recv[None]
    parts, rows, lanes = mine.shape
    batch = 3 if parts % 3 == 0 else 1
    half = pl.BlockSpec((batch, rows, lanes), lambda p: (p, 0, 0))
    piece = pl.BlockSpec((rows // 4, batch * lanes), lambda p: (0, p))
    shape = (rows // 4, parts * lanes)
    return pl.pallas_call(
        split_kernel,
        grid=(parts // batch,),
        in_specs=[pl.BlockSpec(order.shape, lambda p: (0, 0)), half, half],
        out_specs=[piece] * 4,
        out_shape=[jax.ShapeDtypeStruct(shape, BF)] * 4,
        name="split_rows",
        **vmem(room, 2 * 384 * 384 * parts * lanes, 3 * 2 * 384 * parts * lanes),
    )(order, mine, recv)


def fold_kernel(own, a, b, d, *pieces):
    total = own[...].astype(F32) + a[...].astype(F32) + b[...].astype(F32) + d[...].astype(F32)
    size = pieces[0].shape[0]
    for i, piece in enumerate(pieces):
        piece[...] = total[i * size : (i + 1) * size].astype(piece.dtype)


def fold_rows(own, received):
    rows, columns = own.shape
    lanes = wide(columns)
    block = pl.BlockSpec((rows, lanes), lambda j: (0, j))
    piece = pl.BlockSpec((rows // 4, lanes), lambda j: (0, j))
    return pl.pallas_call(
        fold_kernel,
        grid=(columns // lanes,),
        in_specs=[block] * 4,
        out_specs=[piece] * 4,
        out_shape=[jax.ShapeDtypeStruct((rows // 4, columns), kind) for kind in (F32, BF, BF, BF)],
        name="fold_rows",
        **vmem(24, 4 * rows * columns, 11 * rows * columns),
    )(own, *received)


def to_ring(pieces, stage):
    return [
        lax.ppermute(piece, ("x", "z", "c"), [(b, a) for a, b in plane_pairs(step, stage)])
        for step, piece in zip(STEPS[1:], pieces)
    ]


def column_parts(own, received):
    total = own
    for part in received:
        total += part.astype(F32)
    size = total.shape[0] // 4
    parts = []
    for i, flip in enumerate(FLIPS):
        pairs = [(user, owner) for owner, user in column_pairs(*flip)]
        parts.append(lax.ppermute(total[i * size : (i + 1) * size], ("yl", "c", "yh"), pairs))
    return parts


def sum_parts(parts):
    return (parts[0] + parts[1]) + (parts[2] + parts[3])


def apart(pair):
    lane = lax.broadcasted_iota(jnp.int32, pair.shape, 1)
    zero = jnp.zeros_like(pair)
    return jnp.concatenate(
        [jnp.where(lane < HD, pair, zero), jnp.where(lane < HD, zero, pair)], axis=0
    )


def beside(rows, span):
    return jnp.concatenate([rows[:HD, :span], rows[HD:, span:]], axis=0)


def attend_body(g, limits, x_own, x_oth, w_qkv, bias, own, oth, context, probs):
    span, width = context.shape
    key = lax.broadcasted_iota(jnp.int32, (span, 128), 0)
    lane = lax.broadcasted_iota(jnp.int32, (span, 128), 1)
    hidden = jnp.concatenate(
        [jnp.where((key >= limits[g, i]) & (lane == 0), -1e30, 0.0).astype(BF) for i in (0, 1)],
        axis=0,
    )
    unit = (lax.broadcasted_iota(jnp.int32, (2 * span, 128), 1) == 0).astype(BF)
    for j in range(3):
        at = pl.ds(j * width, width)
        own[:, at] = (mm(x_own[...], w_qkv[:, at]) + bias[0:1, at]).astype(BF)
        if j:
            oth[:, pl.ds((j - 1) * width, width)] = (
                mm(x_oth[...], w_qkv[:, at]) + bias[0:1, at]
            ).astype(BF)

    for at in range(0, width, 128):
        q = apart(own[:, pl.ds(at, 128)] * jnp.asarray(0.125, BF))
        k = jnp.concatenate([own[:, pl.ds(at + width, 128)], oth[:, pl.ds(at, 128)]], axis=0)
        v = jnp.concatenate(
            [own[:, pl.ds(at + 2 * width, 128)], oth[:, pl.ds(at + width, 128)]], axis=0
        )
        s = mm_nt(jnp.concatenate([k, hidden], axis=1), jnp.concatenate([q, unit], axis=1))
        e = jnp.exp(s - jnp.max(s, axis=0, keepdims=True))
        p_t = (e * (1.0 / jnp.sum(e, axis=0, keepdims=True))).astype(BF)
        probs[at // HD] = p_t[:, :span]
        probs[at // HD + 1] = p_t[:, span:]
        context[:, pl.ds(at, 128)] = beside(mm(v.T, p_t), span).T.astype(BF)


def attend_first_kernel(
    core, limits, x_own, x_oth, here, there,
    own, oth, context, probs, weights, bias, vec, b_in, arrived,
):
    width = context.shape[1]
    half = width // 2

    @pl.when(pl.program_id(0) == 0)
    def _():
        copies = [
            pltpu.make_async_copy(
                source, weights.at[pl.ds(pl.multiple_of(start * half, half), half)], arrived.at[i]
            )
            for i, (source, start) in enumerate(((here, core[0]), (there, 1 - core[0])))
        ]
        for copy in copies:
            copy.start()
        for copy in copies:
            copy.wait()
        rows = weights[:, 3 * width :].astype(F32).T[:16]
        vec[...] = rows
        for l in range(4):
            b_in[l] = rows[V_IN + l : V_IN + l + 1]
        pairs = rows[V_QV : V_QV + 2].astype(BF)
        sides = [
            mm(pairs[0:1, k : k + half], interleave(0)) + mm(pairs[1:2, k : k + half], interleave(1))
            for k in (0, half)
        ]
        line = jnp.concatenate([sides[0], jnp.zeros((1, width), F32), sides[1]], axis=1)
        bias[...] = jnp.broadcast_to(line, bias.shape)

    attend_body(
        pl.program_id(0), limits, x_own, x_oth, weights, bias, own, oth, context, probs
    )


def attend_more_kernel(first, limits, x_own, x_oth, weights, bias, *rest):
    attend_body(pl.program_id(0) + first, limits, x_own, x_oth, weights, bias, *rest[-4:])


def attend_specs(micro, rows, width, first):
    span, heads = rows // micro, width // HD

    def block(n):
        return pl.BlockSpec((span, n), lambda g, *_: (g + first, 0))

    specs = [
        block(3 * width),
        block(2 * width),
        block(width),
        pl.BlockSpec((None, heads, 2 * span, span), lambda g, *_: (g + first, 0, 0, 0)),
    ]
    shapes = [
        jax.ShapeDtypeStruct((rows, 3 * width), BF),
        jax.ShapeDtypeStruct((rows, 2 * width), BF),
        jax.ShapeDtypeStruct((rows, width), BF),
        jax.ShapeDtypeStruct((micro, heads, 2 * span, span), BF),
    ]
    return block(width), specs, shapes


def attend_first(core, limits, x_own, x_oth, here, there, count):
    rows, width = x_own.shape
    block, specs, shapes = attend_specs(limits.shape[0], rows, width, 0)

    def whole(*shape):
        return pl.BlockSpec(shape, lambda g, *_: (0,) * len(shape))

    return pl.pallas_call(
        attend_first_kernel,
        grid_spec=pltpu.PrefetchScalarGridSpec(
            num_scalar_prefetch=2,
            grid=(count,),
            in_specs=[block, block] + [pl.BlockSpec(memory_space=pl.ANY)] * 2,
            out_specs=specs
            + [whole(width, ONE), whole(8, 3 * width), whole(16, width), whole(4, 1, width)],
            scratch_shapes=[pltpu.SemaphoreType.DMA((2,))],
        ),
        out_shape=shapes
        + [
            jax.ShapeDtypeStruct((width, ONE), BF),
            jax.ShapeDtypeStruct((8, 3 * width), F32),
            jax.ShapeDtypeStruct((16, width), F32),
            jax.ShapeDtypeStruct((4, 1, width), F32),
        ],
        name="attend_first",
        **vmem(56, 10 * count << 30, 8 * count << 20),
    )(core, limits, x_own, x_oth, here, there)


def attend_more(limits, x_own, x_oth, weights, bias, first, earlier):
    micro = limits.shape[0]
    rows, width = x_own.shape
    block, specs, shapes = attend_specs(micro, rows, width, first)

    def whole(*shape):
        return pl.BlockSpec(shape, lambda g, *_: (0,) * len(shape))

    count = micro - first
    return pl.pallas_call(
        functools.partial(attend_more_kernel, first),
        grid_spec=pltpu.PrefetchScalarGridSpec(
            num_scalar_prefetch=1,
            grid=(count,),
            in_specs=[block, block, whole(width, 3 * width), whole(8, 3 * width)]
            + [pl.BlockSpec(memory_space=pl.ANY)] * len(earlier),
            out_specs=specs,
        ),
        out_shape=shapes,
        input_output_aliases={5 + i: i for i in range(len(earlier))},
        name="attend_more",
        **vmem(63, 10 * count << 30, 8 * count << 20),
    )(limits, x_own, x_oth, weights, bias, *earlier)


def attend_back_body(own, oth, probs, d_context, d_own, d_oth):
    span, width = d_context.shape
    for at in range(0, width, 128):
        q = apart(own[:, pl.ds(at, 128)] * jnp.asarray(0.125, BF))
        k = jnp.concatenate([own[:, pl.ds(at + width, 128)], oth[:, pl.ds(at, 128)]], axis=0)
        v = jnp.concatenate(
            [own[:, pl.ds(at + 2 * width, 128)], oth[:, pl.ds(at + width, 128)]], axis=0
        )
        d_c = apart(d_context[:, pl.ds(at, 128)])
        p_b = jnp.concatenate([probs[at // HD], probs[at // HD + 1]], axis=1)
        p_f = p_b.astype(F32)
        d_p = mm_nt(v, d_c)
        weighted = jnp.sum(p_f * d_p, axis=0, keepdims=True)
        d_s = (p_f * (d_p - weighted)).astype(BF)
        d_own[:, pl.ds(at, 128)] = (beside(mm(k.T, d_s), span).T * 0.125).astype(BF)
        d_k = mm(d_s, q).astype(BF)
        d_v = mm(p_b, d_c).astype(BF)
        d_own[:, pl.ds(at + width, 128)] = d_k[:span]
        d_own[:, pl.ds(at + 2 * width, 128)] = d_v[:span]
        d_oth[:, pl.ds(at, 128)] = d_k[span:]
        d_oth[:, pl.ds(at + width, 128)] = d_v[span:]


def token_parts(d_own, d_oth, w_qkv, d_first, d_tokens, x_part):
    width = d_first.shape[1]
    d_tokens[...] = d_first[...] + mm_nt(d_own[...], w_qkv[...])
    x_part[...] = (
        mm_nt(d_oth[:, :width], w_qkv[:, width : 2 * width])
        + mm_nt(d_oth[:, width:], w_qkv[:, 2 * width :])
    ).astype(BF)


def bias_sums(d_own, d_oth):
    width = d_oth.shape[1] // 2
    of_queries = jnp.sum(d_own[:, :width].astype(F32), axis=0, keepdims=True)
    of_values = jnp.sum(
        d_own[:, 2 * width :].astype(F32) + d_oth[:, width:].astype(F32), axis=0, keepdims=True
    )
    return rows_of(of_queries, of_values)


def attend_back_kernel(
    own, oth, probs, d_context, d_first, weights, d_own, d_oth, sums, d_tokens, x_part, w_qkv, arrived
):
    fetch = pltpu.make_async_copy(weights.at[:, pl.ds(0, w_qkv.shape[1])], w_qkv, arrived)
    fetch.start()
    attend_back_body(own, oth, probs, d_context, d_own, d_oth)
    fetch.wait()
    token_parts(d_own, d_oth, w_qkv, d_first, d_tokens, x_part)
    sums[...] = bias_sums(d_own, d_oth)


def attend_back(own, oth, probs, d_context, d_first, weights):
    _, heads, _, span = probs.shape
    rows, width = d_context.shape

    def block(n):
        return pl.BlockSpec((span, n), lambda g: (0, 0))

    return pl.pallas_call(
        attend_back_kernel,
        grid=(1,),
        in_specs=[block(3 * width), block(2 * width)]
        + [pl.BlockSpec((None, heads, 2 * span, span), lambda g: (0, 0, 0, 0))]
        + [block(width), block(width), pl.BlockSpec(memory_space=pl.ANY)],
        out_specs=[block(3 * width), block(2 * width), pl.BlockSpec((8, width), lambda g: (0, 0))]
        + [block(width), block(width)],
        out_shape=[
            jax.ShapeDtypeStruct((span, 3 * width), BF),
            jax.ShapeDtypeStruct((span, 2 * width), BF),
            jax.ShapeDtypeStruct((8, width), F32),
            jax.ShapeDtypeStruct((rows, width), F32),
            jax.ShapeDtypeStruct((span, width), BF),
        ],
        scratch_shapes=[pltpu.VMEM((width, 3 * width), BF), pltpu.SemaphoreType.DMA],
        name="attend_back",
        **vmem(56, 9 << 30, 8 << 20),
    )(own, oth, probs, d_context, d_first, weights)


def attend_last_kernel(
    core, own, oth, probs, d_context, d_first, sums_qv, sums, in_sums,
    weights, d_own_first, d_oth_first, x_own, x_oth, _,
    d_tokens, x_part, mine, away,
    w_qkv, d_own, d_oth, x_here, x_there, total, columns, result, arrived, done,
):
    g, last = pl.program_id(0), pl.num_programs(0) - 1
    span, width = d_context.shape
    half = width // 2
    rows = pl.ds(pl.multiple_of((g + 1) * span, span), span)
    d_own_here, d_oth_here = d_own.at[rows], d_oth.at[rows]
    first = pl.ds(0, span)
    copies = [
        pltpu.make_async_copy(source, into, arrived.at[i])
        for i, (source, into) in enumerate(
            (
                (weights.at[:, pl.ds(0, 3 * width)], w_qkv),
                (d_own_first, d_own.at[first]),
                (d_oth_first, d_oth.at[first]),
                (x_own, x_here),
                (x_oth, x_there),
            )
        )
    ]

    def send(k, start, lanes):
        return pltpu.make_async_copy(
            result.at[k, :, pl.ds(start, lanes)], (mine, away)[k].at[:, pl.ds(start, lanes)],
            done.at[k, start // width],
        )

    @pl.when(g == 0)
    def _():
        for copy in copies:
            copy.start()
        total[...] = sums_qv[...]

    attend_back_body(own, oth, probs, d_context, d_own_here, d_oth_here)

    @pl.when(g == 0)
    def _():
        for copy in copies:
            copy.wait()

    token_parts(d_own_here, d_oth_here, w_qkv, d_first, d_tokens, x_part)
    total[...] += bias_sums(d_own_here, d_oth_here)

    @pl.when(g == last)
    def _():
        qv = total[0:2].astype(BF)
        split = [
            jnp.concatenate([mm_nt(qv[i : i + 1], interleave(parity)) for i in (0, 1)], axis=1)
            for parity in (0, 1)
        ]
        lines = [sums[0:6]] + [in_sums[i] for i in range(4)] + split
        columns[...] = jnp.concatenate(lines + [jnp.zeros((116, width), F32)], axis=0).T.astype(BF)
        for k, side in enumerate((core[0], 1 - core[0])):
            place = pl.ds(pl.multiple_of(side * half, half), half)
            result[k, :, AT_VEC:] = columns[place]
            send(k, AT_VEC, ONE - AT_VEC).start()
            here, there = x_here[:, place], x_there[:, place]
            for j in range(3):
                lanes = slice(j * width, (j + 1) * width)
                grad = mm_tn(here, d_own[:, lanes])
                if j:
                    grad += mm_tn(there, d_oth[:, (j - 1) * width : j * width])
                result[k, :, lanes] = grad.astype(BF)
                send(k, j * width, width).start()
        for k in (0, 1):
            for i in range(4):
                send(k, i * width, width if i < 3 else ONE - AT_VEC).wait()


def attend_last(core, own, oth, probs, d_context, d_first, weights, part, x_own, x_oth, sums, in_sums):
    micro, heads, _, span = probs.shape
    rows, width = d_context.shape
    half = width // 2
    d_own, d_oth, sums_qv, d_tokens = part

    def block(n):
        return pl.BlockSpec((span, n), lambda g, *_: (g + 1, 0))

    def whole(*shape):
        return pl.BlockSpec(shape, lambda g, *_: (0,) * len(shape))

    anywhere = pl.BlockSpec(memory_space=pl.ANY)
    return pl.pallas_call(
        attend_last_kernel,
        grid_spec=pltpu.PrefetchScalarGridSpec(
            num_scalar_prefetch=1,
            grid=(micro - 1,),
            in_specs=[block(3 * width), block(2 * width)]
            + [pl.BlockSpec((None, heads, 2 * span, span), lambda g, *_: (g + 1, 0, 0, 0))]
            + [block(width), block(width), whole(8, width), whole(8, width), whole(4, 1, width)]
            + [anywhere] * 6,
            out_specs=[block(width), pl.BlockSpec((span, width), lambda g, *_: (g, 0))]
            + [anywhere] * 2,
            scratch_shapes=[
                pltpu.VMEM((width, 3 * width), BF),
                pltpu.VMEM((rows, 3 * width), BF),
                pltpu.VMEM((rows, 2 * width), BF),
                pltpu.VMEM((rows, width), BF),
                pltpu.VMEM((rows, width), BF),
                pltpu.VMEM((8, width), F32),
                pltpu.VMEM((width, 128), BF),
                pltpu.VMEM((2, half, ONE), BF),
                pltpu.SemaphoreType.DMA((5,)),
                pltpu.SemaphoreType.DMA((2, 4)),
            ],
        ),
        out_shape=[
            jax.ShapeDtypeStruct((rows, width), F32),
            jax.ShapeDtypeStruct((rows - span, width), BF),
            jax.ShapeDtypeStruct((half, ONE), BF),
            jax.ShapeDtypeStruct((half, ONE), BF),
        ],
        input_output_aliases={14: 0},
        name="attend_last",
        **vmem(40, 24 << 30, 20 << 20),
    )(
        core, own, oth, probs, d_context, d_first, sums_qv, sums, in_sums,
        weights, d_own, d_oth, x_own, x_oth, d_tokens,
    )


def norm_parts(value):
    centre = value - jnp.mean(value, axis=-1, keepdims=True)
    inverse = lax.rsqrt(jnp.mean(centre * centre, axis=-1, keepdims=True) + EPS)
    return centre * inverse, inverse


def norm_back(grad, hat, inverse, gain):
    scaled = grad * gain
    return inverse * (
        scaled
        - jnp.mean(scaled, axis=-1, keepdims=True)
        - hat * jnp.mean(scaled * hat, axis=-1, keepdims=True)
    )


def rows_of(*terms):
    return jnp.concatenate(terms + (jnp.zeros((8 - len(terms), terms[0].shape[1]), F32),), axis=0)


def middle_kernel(
    core, vec, b_in, x, context, cot, w_mine, w_away,
    sums, in_sums, grad_mine, grad_away, block_out, d_first, d_context,
    x_in, c_in, cot_in, normed_b, hat_one, inv_one, outer, active, slope, d_outer, d_normed, result,
    d_ctx, weights, grads, from_rows, from_weights, to_rows, to_grads,
):
    t = pl.program_id(0)
    rows, width = x_in.shape
    half, parts, step = width // 2, active.shape[0], rows // 3
    mine, away = pl.multiple_of(core[0] * half, half), pl.multiple_of((1 - core[0]) * half, half)
    blocks = [pl.ds(r * step, step) for r in range(3)]
    w_out = weights.at[2 * parts]

    def row(i):
        return vec[i : i + 1, :]

    def fetch(i):
        lanes = pl.ds(i * width, width)
        return [
            pltpu.make_async_copy(
                source.at[:, lanes], weights.at[i, pl.ds(start, half)], from_weights.at[i, k]
            )
            for k, (source, start) in enumerate(((w_mine, mine), (w_away, away)))
        ]

    def rows_in(r, *which):
        ends = ((context, c_in), (x, x_in), (cot, cot_in))
        return [
            pltpu.make_async_copy(ends[k][0].at[blocks[r]], ends[k][1].at[blocks[r]], from_rows.at[k, r])
            for k in which
        ]

    def rows_out(k, r):
        source, into = ((result, block_out), (d_normed, d_first), (d_ctx, d_context))[k]
        return pltpu.make_async_copy(source.at[blocks[r]], into.at[blocks[r]], to_rows.at[k, r])

    def grads_out(i, slot, count):
        return [
            pltpu.make_async_copy(
                grads.at[slot, k, pl.ds(0, count)], into.at[pl.ds(i, count)], to_grads.at[slot, k]
            )
            for k, into in enumerate((grad_mine, grad_away))
        ]

    def wait_part(i):
        for copy in fetch(i) + fetch(parts + i):
            copy.wait()

    def forward(l):
        w_in, w_back = weights.at[l], weights.at[parts + l]

        def hidden(r):
            return mm(normed_b[blocks[r]], w_in[...]) + b_in[0]

        def bend(r, inner):
            phi = 0.5 + 0.5 * lax.erf(inner * (0.5**0.5))
            act = (inner * phi).astype(BF)
            active[l, blocks[r]] = act
            slope[l, blocks[r]] = phi + inner * jnp.exp(-0.5 * inner * inner) * 0.3989422804014327
            return act

        inner = [hidden(0), hidden(1)]
        for r in range(3):
            act = bend(r, inner[r])
            if r == 0:
                inner.append(hidden(2))
            outer[blocks[r]] += mm(act, w_back[...])

    def backward(l):
        w_in, w_back = weights.at[l], weights.at[parts + l]

        def back(r):
            return mm_nt(d_outer[blocks[r]], w_back[...])

        d_act = [back(0), back(1)]
        pieces = []
        bias = jnp.zeros((1, width), F32)
        for r, at in enumerate(blocks):
            d_inner = (d_act[r] * slope[l, at]).astype(BF)
            pieces.append(d_inner)
            if r == 0:
                d_act.append(back(2))
            bias += jnp.sum(d_inner.astype(F32), axis=0, keepdims=True)
            d_normed[at] += mm_nt(d_inner, w_in[...])
        d_inner = jnp.concatenate(pieces, axis=0)
        in_sums[0] = bias
        slot = l % 2 if isinstance(l, int) else lax.rem(l, 2)
        if not isinstance(l, int):

            @pl.when(l >= 2)
            def _():
                for copy in grads_out(2 * l - 4, slot, 2):
                    copy.wait()

        for k, start in enumerate((mine, away)):
            cols = pl.ds(start, half)
            grads[slot, k, 0] = mm_tn(normed_b[:, cols], d_inner).astype(BF)
            grads[slot, k, 1] = mm_tn(active[l, :, cols], d_outer[...]).astype(BF)
        for copy in grads_out(2 * l, slot, 2):
            copy.start()

    @pl.when(t == 0)
    def _():
        for copy in fetch(2 * parts):
            copy.start()
        for r in range(3):
            for copy in rows_in(r, 0, 1):
                copy.start()
        for i in range(parts):
            for copy in fetch(i) + fetch(parts + i):
                copy.start()
        for r in range(3):
            rows_in(r, 2)[0].start()
        for copy in fetch(2 * parts):
            copy.wait()
        wait_part(0)
        for r, at in enumerate(blocks):
            for copy in rows_in(r, 0, 1):
                copy.wait()
            hat, inverse = norm_parts(x_in[at].astype(F32) + mm(c_in[at], w_out[...]) + row(V_OUT))
            hat_one[at] = hat
            inv_one[at] = jnp.broadcast_to(inverse, (step, 128))
            value = hat * row(V_GAIN1) + row(V_SHIFT1)
            normed_b[at] = value.astype(BF)
            outer[at] = value + row(V_BACK)
        forward(0)

    @pl.when((t > 0) & (t < parts))
    def _():
        for i in range(1, parts):

            @pl.when(t == i)
            def _():
                wait_part(i)

        forward(t)

    @pl.when(t == parts)
    def _():
        total = [jnp.zeros((1, width), F32) for _ in range(3)]
        for r, at in enumerate(blocks):
            rows_in(r, 2)[0].wait()
            hat, inverse = norm_parts(outer[at])
            result[at] = (hat * row(V_GAIN2) + row(V_SHIFT2)).astype(BF)
            rows_out(0, r).start()
            grad = cot_in[at].astype(F32)
            d_second = norm_back(grad, hat, inverse, row(V_GAIN2))
            d_b = d_second.astype(BF)
            d_outer[at] = d_b
            d_normed[at] = d_second
            for i, term in enumerate((d_b.astype(F32), grad * hat, grad)):
                total[i] += jnp.sum(term, axis=0, keepdims=True)
        for i, term in zip((V_BACK, V_GAIN2, V_SHIFT2), total):
            sums[i : i + 1] = term
        backward(0)

    @pl.when((t > parts) & (t < 2 * parts))
    def _():
        backward(t - parts)

    @pl.when(t == 2 * parts)
    def _():
        total = [jnp.zeros((1, width), F32) for _ in range(3)]
        for r, at in enumerate(blocks):
            grad, hat = d_normed[at], hat_one[at]
            back = norm_back(grad, hat, inv_one[at, 0:1], row(V_GAIN1))
            d_normed[at] = back
            rows_out(1, r).start()
            d_b = back.astype(BF)
            d_outer[at] = d_b
            for i, term in enumerate((d_b.astype(F32), grad * hat, grad)):
                total[i] += jnp.sum(term, axis=0, keepdims=True)
            d_ctx[at] = mm_nt(d_b, w_out[...]).astype(BF)
            rows_out(2, r).start()
        for i, term in zip((V_OUT, V_GAIN1, V_SHIFT1), total):
            sums[i : i + 1] = term
        for copy in grads_out(2 * parts - 4, parts % 2, 2):
            copy.wait()
        for k, start in enumerate((mine, away)):
            grads[parts % 2, k, 0] = mm_tn(c_in[:, pl.ds(start, half)], d_outer[...]).astype(BF)
        for copy in grads_out(2 * parts, parts % 2, 1):
            copy.start()
        for copy in grads_out(2 * parts - 2, (parts - 1) % 2, 2) + grads_out(2 * parts, parts % 2, 1):
            copy.wait()
        for k in range(3):
            for r in range(3):
                rows_out(k, r).wait()


def middle(core, vec, b_in, x, context, cot, w_mine, w_away):
    rows, width = x.shape
    parts = b_in.shape[0]
    half = width // 2

    def whole(*shape):
        return pl.BlockSpec(shape, lambda t, *_: (0,) * len(shape))

    def later(t):
        return jnp.clip(t - parts, 0, parts - 1)

    anywhere = pl.BlockSpec(memory_space=pl.ANY)
    grads = ((2 * parts + 1, half, width), BF)
    shapes = (
        ((8, width), F32), ((parts, 1, width), F32), grads, grads,
        ((rows, width), BF), ((rows, width), F32), ((rows, width), BF),
    )
    return pl.pallas_call(
        middle_kernel,
        grid_spec=pltpu.PrefetchScalarGridSpec(
            num_scalar_prefetch=1,
            grid=(2 * parts + 1,),
            in_specs=[
                whole(16, width),
                pl.BlockSpec((1, 1, width), lambda t, *_: (jnp.minimum(t, parts - 1), 0, 0)),
            ]
            + [anywhere] * 5,
            out_specs=[whole(8, width)]
            + [pl.BlockSpec((1, 1, width), lambda t, *_: (later(t), 0, 0))]
            + [anywhere] * 5,
            scratch_shapes=[pltpu.VMEM((rows, width), BF)] * 4
            + [pltpu.VMEM((rows, width), F32), pltpu.VMEM((rows, 128), F32)]
            + [pltpu.VMEM((rows, width), F32)]
            + [pltpu.VMEM((parts, rows, width), BF), pltpu.VMEM((parts, rows, width), F32)]
            + [pltpu.VMEM((rows, width), BF), pltpu.VMEM((rows, width), F32)]
            + [pltpu.VMEM((rows, width), BF)] * 2
            + [
                pltpu.VMEM((2 * parts + 1, width, width), BF),
                pltpu.VMEM((2, 2, 2, half, width), BF),
                pltpu.SemaphoreType.DMA((3, 3)),
                pltpu.SemaphoreType.DMA((2 * parts + 1, 2)),
                pltpu.SemaphoreType.DMA((3, 3)),
                pltpu.SemaphoreType.DMA((2, 2)),
            ],
        ),
        out_shape=[jax.ShapeDtypeStruct(*shape) for shape in shapes],
        name="middle",
        **vmem(63, 24 << 30, 30 << 20),
    )(core, vec, b_in, x, context, cot, w_mine, w_away)


def on_device(
    tokens, lengths, cotangent, w_qkv, b_qv, w_out, b_out, w_in, b_in, w_back, b_back,
    gain_one, shift_one, gain_two, shift_two,
):
    micro, _, span, width = tokens.shape
    ff = w_in.shape[1]
    rows = micro * span
    yh = lax.axis_index("yh")
    c = lax.axis_index("c")
    core = c.reshape(1)
    x_own = tokens.reshape(rows, width)
    tie = lax.optimization_barrier
    order = arrival()

    packed = pack(
        w_qkv, w_out, w_in, w_back,
        (b_out, b_back, gain_one, shift_one, gain_two, shift_two, b_in, b_qv),
    )
    x_oth = lax.ppermute(x_own, "yh", SWAP)
    column = gather_column(packed)
    near = [column] + from_ring(column, 0)
    one = jnp.concatenate([part[:, :ONE] for part in near], axis=0)
    two = jnp.concatenate([part[:, ONE:] for part in near], axis=0)
    one_parts = [one] + from_ring(one, 1)
    limits = jnp.stack([lengths[:, 0] - yh * span, lengths[:, 0] - (1 - yh) * span], axis=1)
    one_parts, two, x_oth, limits = tie((one_parts, two, x_oth, limits))
    two_parts = [two] + from_ring(two, 1)
    one = sort_rows(order, one_parts)
    one_away = lax.ppermute(one, "c", SWAP)

    *seen, weights, bias, vec, b_in = attend_first(core, limits, x_own, x_oth, one, one_away, micro - 1)
    seen, two_parts = tie((seen, two_parts))
    two = sort_rows(order, two_parts)
    seen, two = tie((seen, two))
    two_away = lax.ppermute(two, "c", SWAP)
    mixed, mixed_oth, context, probs = attend_more(
        limits, x_own, x_oth, weights, bias, micro - 1, seen
    )
    sums, in_sums, ff_mine, ff_away, block_out, d_first, d_context = middle(
        core, vec, b_in, x_own, context, cotangent.reshape(rows, width), two, two_away
    )
    ff_recv = lax.ppermute(ff_away, "c", SWAP)
    inputs = (mixed, mixed_oth, probs, d_context, d_first, weights)
    *part, x_near = attend_back(*inputs)
    ff_recv, part = tie((ff_recv, part))
    ff_own, *ff_sent = split_rows(order, ff_mine, ff_recv)
    ff_sent, part = tie((ff_sent, part))
    ff_got = to_ring(ff_sent, 1)
    d_tokens, x_part, g_mine, g_away = attend_last(
        core, *inputs, part, x_own, x_oth, sums, in_sums
    )
    g_away, x_near = tie((g_away, x_near))
    x_near = lax.ppermute(x_near, "yh", SWAP)
    x_rest = x_part
    ff_got, g_away = tie((ff_got, g_away))
    g_recv = lax.ppermute(g_away, "c", SWAP)
    ff_own, *ff_sent = fold_rows(ff_own, ff_got)
    ff_got = to_ring(ff_sent, 0)
    g_recv, ff_sent = tie((g_recv, ff_sent))
    g_own, *g_sent = split_rows(order, g_mine, g_recv)
    g_sent, ff_got[0], x_near = tie((g_sent, ff_got[0], x_near))
    g_got = to_ring(g_sent, 1)
    x_rest = lax.ppermute(x_rest, "yh", SWAP)
    ff_parts = column_parts(ff_own, ff_got)
    g_own, *g_sent = fold_rows(g_own, g_got)
    g_got = to_ring(g_sent, 0)
    o_in, o_back, o_out = finish_early(ff_parts)
    d_tokens = d_tokens + jnp.concatenate([x_near, x_rest], axis=0).astype(F32)
    g_got, o_in, o_back, o_out, d_tokens = tie((g_got, o_in, o_back, o_out, d_tokens))
    g_parts = column_parts(g_own, g_got)
    o_qkv, lines = finish_late(g_parts)
    return (
        block_out.reshape(tokens.shape),
        d_tokens.reshape(tokens.shape),
        o_qkv,
        lines[7],
        o_out,
        lines[0],
        o_in,
        lines[6],
        o_back,
        lines[1],
        lines[2],
        lines[3],
        lines[4],
        lines[5],
    )


def solution(mesh):
    fine = Mesh(mesh.devices.reshape(2, 4, 4, 2, 2), DEVICES)
    pairs = ("yl", "x", "z", "c")
    data = P(None, pairs, "yh", None)
    weight, vector = P(DEVICES, None), P(DEVICES)
    kinds = (weight, vector) * 4
    return jax.shard_map(
        on_device,
        mesh=fine,
        in_specs=(data, P(None, pairs), data) + kinds + (vector,) * 4,
        out_specs=(data, data) + kinds + (vector,) * 4,
        check_vma=False,
    )
```

```python
import functools

import jax
import jax.numpy as jnp
import numpy as np
from jax import lax
from jax.experimental import pallas as pl
from jax.experimental.pallas import tpu as pltpu
from jax.sharding import Mesh, PartitionSpec as P

HD = 64
EPS = 1e-05
F32 = jnp.float32
BF = jnp.bfloat16
DEVICES = ("yl", "x", "z", "c", "yh")
SWAP = ((0, 1), (1, 0))
STEPS = (0, 1, 3, 2)
AT_VEC = 3 * 768
ONE, TWO = AT_VEC + 128, 9 * 768
V_OUT, V_BACK, V_GAIN1, V_SHIFT1, V_GAIN2, V_SHIFT2, V_IN, V_QV = 0, 1, 2, 3, 4, 5, 6, 10


def mm(a, b):
    return lax.dot_general(a, b, (((1,), (0,)), ((), ())), preferred_element_type=F32)


def mm_nt(a, b):
    return lax.dot_general(a, b, (((1,), (1,)), ((), ())), preferred_element_type=F32)


def mm_tn(a, b):
    return lax.dot_general(a, b, (((0,), (0,)), ((), ())), preferred_element_type=F32)


def vmem(mib, flops=0, moved=0):
    return dict(
        compiler_params=pltpu.CompilerParams(vmem_limit_bytes=mib << 20),
        cost_estimate=pl.CostEstimate(flops=flops, bytes_accessed=moved, transcendentals=0),
    )


ROW = [i % 6 for i in range(36)] + [i // 4 for i in range(24)] + [i // 2 for i in range(12)]
COLUMN = [i // 6 for i in range(36)] + [V_IN + i % 4 for i in range(24)] + [V_QV + i % 2 for i in range(12)]


SIZES = (6, 6, 6, 6, 6, 6, 24, 12)


def maps():
    rows, columns = np.zeros((8, 128), np.float32), np.zeros((128, 128), np.float32)
    for i, (r, l) in enumerate(zip(ROW, COLUMN)):
        rows[r, i] = columns[i, l] = 1
    f, place = np.arange(768)[:, None], np.arange(768)[None, :]
    units = (f == 4 * (place % 192) + place // 192).astype(np.float32)
    r, f = np.arange(32)[:, None], np.arange(24)[None, :]
    spread = ((r % 8 < 6) & (f == 4 * (r % 8) + r // 8)).astype(np.float32)
    return rows, columns, units, spread


def pack_kernel(*refs):
    w_qkv, w_out, w_in, w_back = refs[:4]
    vectors = refs[4:12]
    rows, columns, units, spread, out, line, stack = refs[12:]
    width = w_out.shape[1]
    line[...] = jnp.zeros_like(line)
    stack[...] = jnp.zeros_like(stack)
    at = 0
    for size, vector in zip(SIZES, vectors):
        line[0:1, at : at + size] = vector[...].astype(F32).reshape(1, size)
        at += size
    out[:, : 3 * width] = w_qkv[...]
    out[:, AT_VEC:ONE] = mm((line[0:1] * rows[...]).astype(BF), columns[...])[:6].astype(BF)
    for b in range(4):
        stack[8 * b : 8 * b + 6] = w_in[:, b * width : (b + 1) * width].astype(F32)
    moved = mm(stack[...].astype(BF), units[...])
    merged = mm(spread[...], w_back[...])
    for l in range(4):
        for b in range(4):
            start = ONE + l * width + 192 * b
            out[:, start : start + 192] = moved[8 * b : 8 * b + 6, 192 * l : 192 * (l + 1)].astype(BF)
        start = ONE + (4 + l) * width
        out[:, start : start + width] = merged[8 * l : 8 * l + 6].astype(BF)
    out[:, ONE + 8 * width :] = w_out[...]


def pack(w_qkv, w_out, w_in, w_back, vectors):
    rows, columns, units, spread = maps()
    return pl.pallas_call(
        pack_kernel,
        out_shape=jax.ShapeDtypeStruct((6, ONE + TWO), BF),
        scratch_shapes=[pltpu.VMEM((8, 128), F32), pltpu.VMEM((32, 768), F32)],
        name="pack",
    )(
        w_qkv, w_out, w_in, w_back, *vectors, jnp.asarray(rows),
        *(jnp.asarray(part, BF) for part in (columns, units, spread)),
    )


def exact_nt(a, b):
    return lax.dot_general(
        a, b, (((1,), (1,)), ((), ())), precision=lax.Precision.HIGHEST, preferred_element_type=F32
    )


def exact_tn(a, b):
    return lax.dot_general(
        a, b, (((0,), (0,)), ((), ())), precision=lax.Precision.HIGHEST, preferred_element_type=F32
    )


def thirds(value):
    high = value.astype(BF)
    rest = value - high.astype(F32)
    middle_ = rest.astype(BF)
    return jnp.concatenate([high, middle_, (rest - middle_.astype(F32)).astype(BF)], axis=0)


def finish_early_kernel(a, b, d, e, units, spread, g_in, g_back, g_out, stack, rows):
    width = g_back.shape[1]
    terms = [part[...].astype(F32) for part in (a, b, d, e)]
    total = (terms[0] + terms[1]) + (terms[2] + terms[3])
    stack[...] = jnp.zeros_like(stack)
    rows[...] = jnp.zeros_like(rows)
    for l in range(4):
        for b_ in range(4):
            start = 2 * l * width + 192 * b_
            stack[8 * b_ : 8 * b_ + 6, 192 * l : 192 * (l + 1)] = total[:, start : start + 192]
        rows[8 * l : 8 * l + 6] = total[:, (2 * l + 1) * width : (2 * l + 2) * width]
    moved = mm_nt(thirds(stack[...]), units[...])
    moved = moved[:32] + moved[32:64] + moved[64:]
    for b_ in range(4):
        g_in[:, b_ * width : (b_ + 1) * width] = moved[8 * b_ : 8 * b_ + 6]
    g_back[...] = exact_tn(spread[...], rows[...])
    g_out[...] = total[:, 8 * width :]


def finish_early(parts):
    _, _, units, spread = maps()
    return pl.pallas_call(
        finish_early_kernel,
        out_shape=[jax.ShapeDtypeStruct(shape, F32) for shape in ((6, 3072), (24, 768), (6, 768))],
        scratch_shapes=[pltpu.VMEM((32, 768), F32)] * 2,
        name="finish_early",
        **vmem(16, 1 << 28, 1 << 20),
    )(*parts, jnp.asarray(units, BF), jnp.asarray(spread))


def finish_late_kernel(*refs):
    a, b, d, e, rows, columns, g_qkv = refs[:7]
    vectors, line = refs[7:-1], refs[-1]
    total = (a[...] + b[...]) + (d[...] + e[...])
    g_qkv[...] = total[:, :AT_VEC]
    line[...] = exact_nt(total[:, AT_VEC:], columns[...]) * rows[:6]
    line[0:1] = jnp.sum(line[...], axis=0, keepdims=True)
    at = 0
    for size, vector in zip(SIZES, vectors):
        vector[...] = line[0:1, at : at + size].reshape(size)
        at += size


def finish_late(parts):
    rows, columns, _, _ = maps()
    g_qkv, *vectors = pl.pallas_call(
        finish_late_kernel,
        out_shape=[
            jax.ShapeDtypeStruct(shape, F32) for shape in ((6, AT_VEC),) + tuple((n,) for n in SIZES)
        ],
        scratch_shapes=[pltpu.VMEM((6, 128), F32)],
        name="finish_late",
        **vmem(16, 1 << 24, 1 << 18),
    )(*parts, jnp.asarray(rows), jnp.asarray(columns))
    return g_qkv, vectors


def interleave(parity):
    row = lax.broadcasted_iota(jnp.int32, (384, 768), 0)
    return (lax.broadcasted_iota(jnp.int32, (384, 768), 1) == 2 * row + parity).astype(BF)


def column_pairs(flip_c, flip_y):
    pairs = []
    for a in (0, 1):
        for b in (0, 1):
            for d in (0, 1):
                pairs.append((b * 4 + (a ^ flip_c) * 2 + (d ^ flip_y), a * 4 + b * 2 + d))
    return pairs


FLIPS = ((0, 0), (0, 1), (1, 0), (1, 1))


def gather_column(shard):
    parts = [lax.ppermute(shard, ("yl", "c", "yh"), column_pairs(*flip)) for flip in FLIPS]
    return jnp.concatenate(parts, axis=0)


def plane_pairs(step, stage):
    pairs = []
    for x in range(4):
        for z in range(4):
            for c in range(2):
                near = (x, (z + step) % 4) if c == stage else ((x + step) % 4, z)
                pairs.append(((near[0] * 4 + near[1]) * 2 + c, (x * 4 + z) * 2 + c))
    return pairs


def from_ring(block, stage):
    return [lax.ppermute(block, ("x", "z", "c"), plane_pairs(step, stage)) for step in STEPS[1:]]


def arrival():
    yl, x, z, c, yh = (lax.axis_index(name) for name in DEVICES)
    j = jnp.arange(384)
    steps = jnp.array(STEPS)
    last, early, flip = steps[j // 96], steps[(j % 96) // 24], (j % 24) // 6
    xx = (x + jnp.where(c == 0, last, early)) % 4
    zz = (z + jnp.where(c == 0, early, last)) % 4
    row = xx * 96 + zz * 24 + (yl ^ (flip // 2)) * 12 + (yh ^ (flip % 2)) * 6 + j % 6
    return (jnp.arange(384)[:, None] == row[None, :]).astype(BF)


def wide(columns):
    return next(n for n in (2304, 3072, columns) if columns % n == 0)


def sort_kernel(order, *refs):
    blocks, out = refs[:-1], refs[-1]
    out[...] = mm(order[...], jnp.concatenate([b[...] for b in blocks], axis=0)).astype(BF)


def sort_rows(order, blocks):
    rows, columns = blocks[0].shape
    lanes = wide(columns)
    return pl.pallas_call(
        sort_kernel,
        grid=(columns // lanes,),
        in_specs=[pl.BlockSpec(order.shape, lambda j: (0, 0))]
        + [pl.BlockSpec((rows, lanes), lambda j: (0, j))] * 4,
        out_specs=pl.BlockSpec((4 * rows, lanes), lambda j: (0, j)),
        out_shape=jax.ShapeDtypeStruct((4 * rows, columns), BF),
        name="sort_rows",
        **vmem(24, 2 * 384 * 384 * columns, 2 * 2 * 384 * columns),
    )(order, *blocks)


def split_kernel(order, mine, recv, *pieces):
    parts, _, lanes = mine.shape
    size = pieces[0].shape[0]
    for p in range(parts):
        total = (mine[p].astype(F32) + recv[p].astype(F32)).astype(BF)
        rows = mm_tn(order[...], total)
        for i, piece in enumerate(pieces):
            piece[:, p * lanes : (p + 1) * lanes] = rows[i * size : (i + 1) * size].astype(piece.dtype)


def split_rows(order, mine, recv, room=24):
    if mine.ndim == 2:
        mine, recv = mine[None], recv[None]
    parts, rows, lanes = mine.shape
    batch = 3 if parts % 3 == 0 else 1
    half = pl.BlockSpec((batch, rows, lanes), lambda p: (p, 0, 0))
    piece = pl.BlockSpec((rows // 4, batch * lanes), lambda p: (0, p))
    shape = (rows // 4, parts * lanes)
    return pl.pallas_call(
        split_kernel,
        grid=(parts // batch,),
        in_specs=[pl.BlockSpec(order.shape, lambda p: (0, 0)), half, half],
        out_specs=[piece] * 4,
        out_shape=[jax.ShapeDtypeStruct(shape, BF)] * 4,
        name="split_rows",
        **vmem(room, 2 * 384 * 384 * parts * lanes, 3 * 2 * 384 * parts * lanes),
    )(order, mine, recv)


def fold_kernel(own, a, b, d, *pieces):
    total = own[...].astype(F32) + a[...].astype(F32) + b[...].astype(F32) + d[...].astype(F32)
    size = pieces[0].shape[0]
    for i, piece in enumerate(pieces):
        piece[...] = total[i * size : (i + 1) * size].astype(piece.dtype)


def fold_rows(own, received):
    rows, columns = own.shape
    lanes = wide(columns)
    block = pl.BlockSpec((rows, lanes), lambda j: (0, j))
    piece = pl.BlockSpec((rows // 4, lanes), lambda j: (0, j))
    return pl.pallas_call(
        fold_kernel,
        grid=(columns // lanes,),
        in_specs=[block] * 4,
        out_specs=[piece] * 4,
        out_shape=[jax.ShapeDtypeStruct((rows // 4, columns), kind) for kind in (F32, BF, BF, BF)],
        name="fold_rows",
        **vmem(24, 4 * rows * columns, 11 * rows * columns),
    )(own, *received)


def to_ring(pieces, stage):
    return [
        lax.ppermute(piece, ("x", "z", "c"), [(b, a) for a, b in plane_pairs(step, stage)])
        for step, piece in zip(STEPS[1:], pieces)
    ]


def column_parts(own, received, kind=F32):
    total = own
    for part in received:
        total += part.astype(F32)
    size = total.shape[0] // 4
    parts = []
    for i, flip in enumerate(FLIPS):
        pairs = [(user, owner) for owner, user in column_pairs(*flip)]
        piece = total[i * size : (i + 1) * size].astype(kind)
        parts.append(lax.ppermute(piece, ("yl", "c", "yh"), pairs))
    return parts


def sum_parts(parts):
    return (parts[0] + parts[1]) + (parts[2] + parts[3])


def apart(pair):
    lane = lax.broadcasted_iota(jnp.int32, pair.shape, 1)
    zero = jnp.zeros_like(pair)
    return jnp.concatenate(
        [jnp.where(lane < HD, pair, zero), jnp.where(lane < HD, zero, pair)], axis=0
    )


def beside(rows, span):
    return jnp.concatenate([rows[:HD, :span], rows[HD:, span:]], axis=0)


def attend_body(g, limits, x_own, x_oth, w_qkv, bias, own, oth, context, probs):
    span, width = context.shape
    key = lax.broadcasted_iota(jnp.int32, (span, 128), 0)
    lane = lax.broadcasted_iota(jnp.int32, (span, 128), 1)
    hidden = jnp.concatenate(
        [jnp.where((key >= limits[g, i]) & (lane == 0), -1e30, 0.0).astype(BF) for i in (0, 1)],
        axis=0,
    )
    unit = (lax.broadcasted_iota(jnp.int32, (2 * span, 128), 1) == 0).astype(BF)
    for j in range(3):
        at = pl.ds(j * width, width)
        own[:, at] = (mm(x_own[...], w_qkv[:, at]) + bias[0:1, at]).astype(BF)
        if j:
            oth[:, pl.ds((j - 1) * width, width)] = (
                mm(x_oth[...], w_qkv[:, at]) + bias[0:1, at]
            ).astype(BF)

    for at in range(0, width, 128):
        q = apart(own[:, pl.ds(at, 128)] * jnp.asarray(0.125, BF))
        k = jnp.concatenate([own[:, pl.ds(at + width, 128)], oth[:, pl.ds(at, 128)]], axis=0)
        v = jnp.concatenate(
            [own[:, pl.ds(at + 2 * width, 128)], oth[:, pl.ds(at + width, 128)]], axis=0
        )
        s = mm_nt(jnp.concatenate([k, hidden], axis=1), jnp.concatenate([q, unit], axis=1))
        e = jnp.exp(s - jnp.max(s, axis=0, keepdims=True))
        p_t = (e * (1.0 / jnp.sum(e, axis=0, keepdims=True))).astype(BF)
        probs[at // HD] = p_t[:, :span]
        probs[at // HD + 1] = p_t[:, span:]
        context[:, pl.ds(at, 128)] = beside(mm(v.T, p_t), span).T.astype(BF)


def attend_first_kernel(
    core, limits, x_own, x_oth, here, there,
    own, oth, context, probs, weights, bias, vec, b_in, arrived,
):
    width = context.shape[1]
    half = width // 2

    @pl.when(pl.program_id(0) == 0)
    def _():
        copies = [
            pltpu.make_async_copy(
                source, weights.at[pl.ds(pl.multiple_of(start * half, half), half)], arrived.at[i]
            )
            for i, (source, start) in enumerate(((here, core[0]), (there, 1 - core[0])))
        ]
        for copy in copies:
            copy.start()
        for copy in copies:
            copy.wait()
        rows = weights[:, 3 * width :].astype(F32).T[:16]
        vec[...] = rows
        for l in range(4):
            b_in[l] = rows[V_IN + l : V_IN + l + 1]
        pairs = rows[V_QV : V_QV + 2].astype(BF)
        sides = [
            mm(pairs[0:1, k : k + half], interleave(0)) + mm(pairs[1:2, k : k + half], interleave(1))
            for k in (0, half)
        ]
        line = jnp.concatenate([sides[0], jnp.zeros((1, width), F32), sides[1]], axis=1)
        bias[...] = jnp.broadcast_to(line, bias.shape)

    attend_body(
        pl.program_id(0), limits, x_own, x_oth, weights, bias, own, oth, context, probs
    )


def attend_more_kernel(first, limits, x_own, x_oth, weights, bias, *rest):
    attend_body(pl.program_id(0) + first, limits, x_own, x_oth, weights, bias, *rest[-4:])


def attend_specs(micro, rows, width, first):
    span, heads = rows // micro, width // HD

    def block(n):
        return pl.BlockSpec((span, n), lambda g, *_: (g + first, 0))

    specs = [
        block(3 * width),
        block(2 * width),
        block(width),
        pl.BlockSpec((None, heads, 2 * span, span), lambda g, *_: (g + first, 0, 0, 0)),
    ]
    shapes = [
        jax.ShapeDtypeStruct((rows, 3 * width), BF),
        jax.ShapeDtypeStruct((rows, 2 * width), BF),
        jax.ShapeDtypeStruct((rows, width), BF),
        jax.ShapeDtypeStruct((micro, heads, 2 * span, span), BF),
    ]
    return block(width), specs, shapes


def attend_first(core, limits, x_own, x_oth, here, there, count):
    rows, width = x_own.shape
    block, specs, shapes = attend_specs(limits.shape[0], rows, width, 0)

    def whole(*shape):
        return pl.BlockSpec(shape, lambda g, *_: (0,) * len(shape))

    return pl.pallas_call(
        attend_first_kernel,
        grid_spec=pltpu.PrefetchScalarGridSpec(
            num_scalar_prefetch=2,
            grid=(count,),
            in_specs=[block, block] + [pl.BlockSpec(memory_space=pl.ANY)] * 2,
            out_specs=specs
            + [whole(width, ONE), whole(8, 3 * width), whole(16, width), whole(4, 1, width)],
            scratch_shapes=[pltpu.SemaphoreType.DMA((2,))],
        ),
        out_shape=shapes
        + [
            jax.ShapeDtypeStruct((width, ONE), BF),
            jax.ShapeDtypeStruct((8, 3 * width), F32),
            jax.ShapeDtypeStruct((16, width), F32),
            jax.ShapeDtypeStruct((4, 1, width), F32),
        ],
        name="attend_first",
        **vmem(56, 10 * count << 30, 8 * count << 20),
    )(core, limits, x_own, x_oth, here, there)


def attend_more(limits, x_own, x_oth, weights, bias, first, earlier):
    micro = limits.shape[0]
    rows, width = x_own.shape
    block, specs, shapes = attend_specs(micro, rows, width, first)

    def whole(*shape):
        return pl.BlockSpec(shape, lambda g, *_: (0,) * len(shape))

    count = micro - first
    return pl.pallas_call(
        functools.partial(attend_more_kernel, first),
        grid_spec=pltpu.PrefetchScalarGridSpec(
            num_scalar_prefetch=1,
            grid=(count,),
            in_specs=[block, block, whole(width, 3 * width), whole(8, 3 * width)]
            + [pl.BlockSpec(memory_space=pl.ANY)] * len(earlier),
            out_specs=specs,
        ),
        out_shape=shapes,
        input_output_aliases={5 + i: i for i in range(len(earlier))},
        name="attend_more",
        **vmem(63, 10 * count << 30, 8 * count << 20),
    )(limits, x_own, x_oth, weights, bias, *earlier)


def attend_back_body(own, oth, probs, d_context, d_own, d_oth):
    span, width = d_context.shape
    for at in range(0, width, 128):
        q = apart(own[:, pl.ds(at, 128)] * jnp.asarray(0.125, BF))
        k = jnp.concatenate([own[:, pl.ds(at + width, 128)], oth[:, pl.ds(at, 128)]], axis=0)
        v = jnp.concatenate(
            [own[:, pl.ds(at + 2 * width, 128)], oth[:, pl.ds(at + width, 128)]], axis=0
        )
        d_c = apart(d_context[:, pl.ds(at, 128)])
        p_b = jnp.concatenate([probs[at // HD], probs[at // HD + 1]], axis=1)
        p_f = p_b.astype(F32)
        d_p = mm_nt(v, d_c)
        weighted = jnp.sum(p_f * d_p, axis=0, keepdims=True)
        d_s = (p_f * (d_p - weighted)).astype(BF)
        d_own[:, pl.ds(at, 128)] = (beside(mm(k.T, d_s), span).T * 0.125).astype(BF)
        d_k = mm(d_s, q).astype(BF)
        d_v = mm(p_b, d_c).astype(BF)
        d_own[:, pl.ds(at + width, 128)] = d_k[:span]
        d_own[:, pl.ds(at + 2 * width, 128)] = d_v[:span]
        d_oth[:, pl.ds(at, 128)] = d_k[span:]
        d_oth[:, pl.ds(at + width, 128)] = d_v[span:]


def token_parts(d_own, d_oth, w_qkv, d_first, d_tokens, x_part):
    width = d_first.shape[1]
    d_tokens[...] = d_first[...] + mm_nt(d_own[...], w_qkv[...])
    x_part[...] = (
        mm_nt(d_oth[:, :width], w_qkv[:, width : 2 * width])
        + mm_nt(d_oth[:, width:], w_qkv[:, 2 * width :])
    ).astype(BF)


def bias_sums(d_own, d_oth):
    width = d_oth.shape[1] // 2
    of_queries = jnp.sum(d_own[:, :width].astype(F32), axis=0, keepdims=True)
    of_values = jnp.sum(
        d_own[:, 2 * width :].astype(F32) + d_oth[:, width:].astype(F32), axis=0, keepdims=True
    )
    return rows_of(of_queries, of_values)


def attend_back_kernel(
    own, oth, probs, d_context, d_first, weights, d_own, d_oth, sums, d_tokens, x_part, w_qkv, arrived
):
    fetch = pltpu.make_async_copy(weights.at[:, pl.ds(0, w_qkv.shape[1])], w_qkv, arrived)
    fetch.start()
    attend_back_body(own, oth, probs, d_context, d_own, d_oth)
    fetch.wait()
    token_parts(d_own, d_oth, w_qkv, d_first, d_tokens, x_part)
    sums[...] = bias_sums(d_own, d_oth)


def attend_back(own, oth, probs, d_context, d_first, weights):
    _, heads, _, span = probs.shape
    rows, width = d_context.shape

    def block(n):
        return pl.BlockSpec((span, n), lambda g: (0, 0))

    return pl.pallas_call(
        attend_back_kernel,
        grid=(1,),
        in_specs=[block(3 * width), block(2 * width)]
        + [pl.BlockSpec((None, heads, 2 * span, span), lambda g: (0, 0, 0, 0))]
        + [block(width), block(width), pl.BlockSpec(memory_space=pl.ANY)],
        out_specs=[block(3 * width), block(2 * width), pl.BlockSpec((8, width), lambda g: (0, 0))]
        + [block(width), block(width)],
        out_shape=[
            jax.ShapeDtypeStruct((span, 3 * width), BF),
            jax.ShapeDtypeStruct((span, 2 * width), BF),
            jax.ShapeDtypeStruct((8, width), F32),
            jax.ShapeDtypeStruct((rows, width), F32),
            jax.ShapeDtypeStruct((span, width), BF),
        ],
        scratch_shapes=[pltpu.VMEM((width, 3 * width), BF), pltpu.SemaphoreType.DMA],
        name="attend_back",
        **vmem(56, 9 << 30, 8 << 20),
    )(own, oth, probs, d_context, d_first, weights)


def attend_last_kernel(
    core, own, oth, probs, d_context, d_first, sums_qv, sums, in_sums,
    weights, d_own_first, d_oth_first, x_own, x_oth, _,
    d_tokens, x_part, mine, away,
    w_qkv, d_own, d_oth, x_here, x_there, total, columns, result, arrived, done,
):
    g, last = pl.program_id(0), pl.num_programs(0) - 1
    span, width = d_context.shape
    half = width // 2
    rows = pl.ds(pl.multiple_of((g + 1) * span, span), span)
    d_own_here, d_oth_here = d_own.at[rows], d_oth.at[rows]
    first = pl.ds(0, span)
    copies = [
        pltpu.make_async_copy(source, into, arrived.at[i])
        for i, (source, into) in enumerate(
            (
                (weights.at[:, pl.ds(0, 3 * width)], w_qkv),
                (d_own_first, d_own.at[first]),
                (d_oth_first, d_oth.at[first]),
                (x_own, x_here),
                (x_oth, x_there),
            )
        )
    ]

    def send(k, start, lanes):
        return pltpu.make_async_copy(
            result.at[k, :, pl.ds(start, lanes)], (mine, away)[k].at[:, pl.ds(start, lanes)],
            done.at[k, start // width],
        )

    @pl.when(g == 0)
    def _():
        for copy in copies:
            copy.start()
        total[...] = sums_qv[...]

    attend_back_body(own, oth, probs, d_context, d_own_here, d_oth_here)

    @pl.when(g == 0)
    def _():
        for copy in copies:
            copy.wait()

    token_parts(d_own_here, d_oth_here, w_qkv, d_first, d_tokens, x_part)
    total[...] += bias_sums(d_own_here, d_oth_here)

    @pl.when(g == last)
    def _():
        qv = total[0:2].astype(BF)
        split = [
            jnp.concatenate([mm_nt(qv[i : i + 1], interleave(parity)) for i in (0, 1)], axis=1)
            for parity in (0, 1)
        ]
        lines = [sums[0:6]] + [in_sums[i] for i in range(4)] + split
        columns[...] = jnp.concatenate(lines + [jnp.zeros((116, width), F32)], axis=0).T.astype(BF)
        for k, side in enumerate((core[0], 1 - core[0])):
            place = pl.ds(pl.multiple_of(side * half, half), half)
            result[k, :, AT_VEC:] = columns[place]
            send(k, AT_VEC, ONE - AT_VEC).start()
            here, there = x_here[:, place], x_there[:, place]
            for j in range(3):
                lanes = slice(j * width, (j + 1) * width)
                grad = mm_tn(here, d_own[:, lanes])
                if j:
                    grad += mm_tn(there, d_oth[:, (j - 1) * width : j * width])
                result[k, :, lanes] = grad.astype(BF)
                send(k, j * width, width).start()
        for k in (0, 1):
            for i in range(4):
                send(k, i * width, width if i < 3 else ONE - AT_VEC).wait()


def attend_last(core, own, oth, probs, d_context, d_first, weights, part, x_own, x_oth, sums, in_sums):
    micro, heads, _, span = probs.shape
    rows, width = d_context.shape
    half = width // 2
    d_own, d_oth, sums_qv, d_tokens = part

    def block(n):
        return pl.BlockSpec((span, n), lambda g, *_: (g + 1, 0))

    def whole(*shape):
        return pl.BlockSpec(shape, lambda g, *_: (0,) * len(shape))

    anywhere = pl.BlockSpec(memory_space=pl.ANY)
    return pl.pallas_call(
        attend_last_kernel,
        grid_spec=pltpu.PrefetchScalarGridSpec(
            num_scalar_prefetch=1,
            grid=(micro - 1,),
            in_specs=[block(3 * width), block(2 * width)]
            + [pl.BlockSpec((None, heads, 2 * span, span), lambda g, *_: (g + 1, 0, 0, 0))]
            + [block(width), block(width), whole(8, width), whole(8, width), whole(4, 1, width)]
            + [anywhere] * 6,
            out_specs=[block(width), pl.BlockSpec((span, width), lambda g, *_: (g, 0))]
            + [anywhere] * 2,
            scratch_shapes=[
                pltpu.VMEM((width, 3 * width), BF),
                pltpu.VMEM((rows, 3 * width), BF),
                pltpu.VMEM((rows, 2 * width), BF),
                pltpu.VMEM((rows, width), BF),
                pltpu.VMEM((rows, width), BF),
                pltpu.VMEM((8, width), F32),
                pltpu.VMEM((width, 128), BF),
                pltpu.VMEM((2, half, ONE), BF),
                pltpu.SemaphoreType.DMA((5,)),
                pltpu.SemaphoreType.DMA((2, 4)),
            ],
        ),
        out_shape=[
            jax.ShapeDtypeStruct((rows, width), F32),
            jax.ShapeDtypeStruct((rows - span, width), BF),
            jax.ShapeDtypeStruct((half, ONE), BF),
            jax.ShapeDtypeStruct((half, ONE), BF),
        ],
        input_output_aliases={14: 0},
        name="attend_last",
        **vmem(40, 24 << 30, 20 << 20),
    )(
        core, own, oth, probs, d_context, d_first, sums_qv, sums, in_sums,
        weights, d_own, d_oth, x_own, x_oth, d_tokens,
    )


def norm_parts(value):
    centre = value - jnp.mean(value, axis=-1, keepdims=True)
    inverse = lax.rsqrt(jnp.mean(centre * centre, axis=-1, keepdims=True) + EPS)
    return centre * inverse, inverse


def norm_back(grad, hat, inverse, gain):
    scaled = grad * gain
    return inverse * (
        scaled
        - jnp.mean(scaled, axis=-1, keepdims=True)
        - hat * jnp.mean(scaled * hat, axis=-1, keepdims=True)
    )


def rows_of(*terms):
    return jnp.concatenate(terms + (jnp.zeros((8 - len(terms), terms[0].shape[1]), F32),), axis=0)


def middle_kernel(
    core, vec, b_in, x, context, cot, w_mine, w_away,
    sums, in_sums, grad_mine, grad_away, block_out, d_first, d_context,
    x_in, c_in, cot_in, normed_b, hat_one, inv_one, outer, active, slope, d_outer, d_normed, result,
    d_ctx, weights, grads, from_rows, from_weights, to_rows, to_grads,
):
    t = pl.program_id(0)
    rows, width = x_in.shape
    half, parts, step = width // 2, active.shape[0], rows // 3
    mine, away = pl.multiple_of(core[0] * half, half), pl.multiple_of((1 - core[0]) * half, half)
    blocks = [pl.ds(r * step, step) for r in range(3)]
    w_out = weights.at[2 * parts]

    def row(i):
        return vec[i : i + 1, :]

    def fetch(i):
        lanes = pl.ds(i * width, width)
        return [
            pltpu.make_async_copy(
                source.at[:, lanes], weights.at[i, pl.ds(start, half)], from_weights.at[i, k]
            )
            for k, (source, start) in enumerate(((w_mine, mine), (w_away, away)))
        ]

    def rows_in(r, *which):
        ends = ((context, c_in), (x, x_in), (cot, cot_in))
        return [
            pltpu.make_async_copy(ends[k][0].at[blocks[r]], ends[k][1].at[blocks[r]], from_rows.at[k, r])
            for k in which
        ]

    def rows_out(k, r):
        source, into = ((result, block_out), (d_normed, d_first), (d_ctx, d_context))[k]
        return pltpu.make_async_copy(source.at[blocks[r]], into.at[blocks[r]], to_rows.at[k, r])

    def grads_out(i, slot, count):
        return [
            pltpu.make_async_copy(
                grads.at[slot, k, pl.ds(0, count)], into.at[pl.ds(i, count)], to_grads.at[slot, k]
            )
            for k, into in enumerate((grad_mine, grad_away))
        ]

    def wait_part(i):
        for copy in fetch(i) + fetch(parts + i):
            copy.wait()

    def forward(l):
        w_in, w_back = weights.at[l], weights.at[parts + l]

        def hidden(r):
            return mm(normed_b[blocks[r]], w_in[...]) + b_in[0]

        def bend(r, inner):
            phi = 0.5 + 0.5 * lax.erf(inner * (0.5**0.5))
            act = (inner * phi).astype(BF)
            active[l, blocks[r]] = act
            slope[l, blocks[r]] = phi + inner * jnp.exp(-0.5 * inner * inner) * 0.3989422804014327
            return act

        inner = [hidden(0), hidden(1)]
        for r in range(3):
            act = bend(r, inner[r])
            if r == 0:
                inner.append(hidden(2))
            outer[blocks[r]] += mm(act, w_back[...])

    def backward(l):
        w_in, w_back = weights.at[l], weights.at[parts + l]

        def back(r):
            return mm_nt(d_outer[blocks[r]], w_back[...])

        d_act = [back(0), back(1)]
        pieces = []
        bias = jnp.zeros((1, width), F32)
        for r, at in enumerate(blocks):
            d_inner = (d_act[r] * slope[l, at]).astype(BF)
            pieces.append(d_inner)
            if r == 0:
                d_act.append(back(2))
            bias += jnp.sum(d_inner.astype(F32), axis=0, keepdims=True)
            d_normed[at] += mm_nt(d_inner, w_in[...])
        d_inner = jnp.concatenate(pieces, axis=0)
        in_sums[0] = bias
        slot = l % 2 if isinstance(l, int) else lax.rem(l, 2)
        if not isinstance(l, int):

            @pl.when(l >= 2)
            def _():
                for copy in grads_out(2 * l - 4, slot, 2):
                    copy.wait()

        for k, start in enumerate((mine, away)):
            cols = pl.ds(start, half)
            grads[slot, k, 0] = mm_tn(normed_b[:, cols], d_inner).astype(BF)
            grads[slot, k, 1] = mm_tn(active[l, :, cols], d_outer[...]).astype(BF)
        for copy in grads_out(2 * l, slot, 2):
            copy.start()

    @pl.when(t == 0)
    def _():
        for copy in fetch(2 * parts):
            copy.start()
        for r in range(3):
            for copy in rows_in(r, 0, 1):
                copy.start()
        for i in range(parts):
            for copy in fetch(i) + fetch(parts + i):
                copy.start()
        for r in range(3):
            rows_in(r, 2)[0].start()
        for copy in fetch(2 * parts):
            copy.wait()
        wait_part(0)
        for r, at in enumerate(blocks):
            for copy in rows_in(r, 0, 1):
                copy.wait()
            hat, inverse = norm_parts(x_in[at].astype(F32) + mm(c_in[at], w_out[...]) + row(V_OUT))
            hat_one[at] = hat
            inv_one[at] = jnp.broadcast_to(inverse, (step, 128))
            value = hat * row(V_GAIN1) + row(V_SHIFT1)
            normed_b[at] = value.astype(BF)
            outer[at] = value + row(V_BACK)
        forward(0)

    @pl.when((t > 0) & (t < parts))
    def _():
        for i in range(1, parts):

            @pl.when(t == i)
            def _():
                wait_part(i)

        forward(t)

    @pl.when(t == parts)
    def _():
        total = [jnp.zeros((1, width), F32) for _ in range(3)]
        for r, at in enumerate(blocks):
            rows_in(r, 2)[0].wait()
            hat, inverse = norm_parts(outer[at])
            result[at] = (hat * row(V_GAIN2) + row(V_SHIFT2)).astype(BF)
            rows_out(0, r).start()
            grad = cot_in[at].astype(F32)
            d_second = norm_back(grad, hat, inverse, row(V_GAIN2))
            d_b = d_second.astype(BF)
            d_outer[at] = d_b
            d_normed[at] = d_second
            for i, term in enumerate((d_b.astype(F32), grad * hat, grad)):
                total[i] += jnp.sum(term, axis=0, keepdims=True)
        for i, term in zip((V_BACK, V_GAIN2, V_SHIFT2), total):
            sums[i : i + 1] = term
        backward(0)

    @pl.when((t > parts) & (t < 2 * parts))
    def _():
        backward(t - parts)

    @pl.when(t == 2 * parts)
    def _():
        total = [jnp.zeros((1, width), F32) for _ in range(3)]
        for r, at in enumerate(blocks):
            grad, hat = d_normed[at], hat_one[at]
            back = norm_back(grad, hat, inv_one[at, 0:1], row(V_GAIN1))
            d_normed[at] = back
            rows_out(1, r).start()
            d_b = back.astype(BF)
            d_outer[at] = d_b
            for i, term in enumerate((d_b.astype(F32), grad * hat, grad)):
                total[i] += jnp.sum(term, axis=0, keepdims=True)
            d_ctx[at] = mm_nt(d_b, w_out[...]).astype(BF)
            rows_out(2, r).start()
        for i, term in zip((V_OUT, V_GAIN1, V_SHIFT1), total):
            sums[i : i + 1] = term
        for copy in grads_out(2 * parts - 4, parts % 2, 2):
            copy.wait()
        for k, start in enumerate((mine, away)):
            grads[parts % 2, k, 0] = mm_tn(c_in[:, pl.ds(start, half)], d_outer[...]).astype(BF)
        for copy in grads_out(2 * parts, parts % 2, 1):
            copy.start()
        for copy in grads_out(2 * parts - 2, (parts - 1) % 2, 2) + grads_out(2 * parts, parts % 2, 1):
            copy.wait()
        for k in range(3):
            for r in range(3):
                rows_out(k, r).wait()


def middle(core, vec, b_in, x, context, cot, w_mine, w_away):
    rows, width = x.shape
    parts = b_in.shape[0]
    half = width // 2

    def whole(*shape):
        return pl.BlockSpec(shape, lambda t, *_: (0,) * len(shape))

    def later(t):
        return jnp.clip(t - parts, 0, parts - 1)

    anywhere = pl.BlockSpec(memory_space=pl.ANY)
    grads = ((2 * parts + 1, half, width), BF)
    shapes = (
        ((8, width), F32), ((parts, 1, width), F32), grads, grads,
        ((rows, width), BF), ((rows, width), F32), ((rows, width), BF),
    )
    return pl.pallas_call(
        middle_kernel,
        grid_spec=pltpu.PrefetchScalarGridSpec(
            num_scalar_prefetch=1,
            grid=(2 * parts + 1,),
            in_specs=[
                whole(16, width),
                pl.BlockSpec((1, 1, width), lambda t, *_: (jnp.minimum(t, parts - 1), 0, 0)),
            ]
            + [anywhere] * 5,
            out_specs=[whole(8, width)]
            + [pl.BlockSpec((1, 1, width), lambda t, *_: (later(t), 0, 0))]
            + [anywhere] * 5,
            scratch_shapes=[pltpu.VMEM((rows, width), BF)] * 4
            + [pltpu.VMEM((rows, width), F32), pltpu.VMEM((rows, 128), F32)]
            + [pltpu.VMEM((rows, width), F32)]
            + [pltpu.VMEM((parts, rows, width), BF), pltpu.VMEM((parts, rows, width), F32)]
            + [pltpu.VMEM((rows, width), BF), pltpu.VMEM((rows, width), F32)]
            + [pltpu.VMEM((rows, width), BF)] * 2
            + [
                pltpu.VMEM((2 * parts + 1, width, width), BF),
                pltpu.VMEM((2, 2, 2, half, width), BF),
                pltpu.SemaphoreType.DMA((3, 3)),
                pltpu.SemaphoreType.DMA((2 * parts + 1, 2)),
                pltpu.SemaphoreType.DMA((3, 3)),
                pltpu.SemaphoreType.DMA((2, 2)),
            ],
        ),
        out_shape=[jax.ShapeDtypeStruct(*shape) for shape in shapes],
        name="middle",
        **vmem(63, 24 << 30, 30 << 20),
    )(core, vec, b_in, x, context, cot, w_mine, w_away)


def on_device(
    tokens, lengths, cotangent, w_qkv, b_qv, w_out, b_out, w_in, b_in, w_back, b_back,
    gain_one, shift_one, gain_two, shift_two,
):
    micro, _, span, width = tokens.shape
    ff = w_in.shape[1]
    rows = micro * span
    yh = lax.axis_index("yh")
    c = lax.axis_index("c")
    core = c.reshape(1)
    x_own = tokens.reshape(rows, width)
    tie = lax.optimization_barrier
    order = arrival()

    packed = pack(
        w_qkv, w_out, w_in, w_back,
        (b_out, b_back, gain_one, shift_one, gain_two, shift_two, b_in, b_qv),
    )
    x_oth = lax.ppermute(x_own, "yh", SWAP)
    column = gather_column(packed)
    near = [column] + from_ring(column, 0)
    one = jnp.concatenate([part[:, :ONE] for part in near], axis=0)
    two = jnp.concatenate([part[:, ONE:] for part in near], axis=0)
    one_parts = [one] + from_ring(one, 1)
    limits = jnp.stack([lengths[:, 0] - yh * span, lengths[:, 0] - (1 - yh) * span], axis=1)
    one_parts, two, x_oth, limits = tie((one_parts, two, x_oth, limits))
    two_parts = [two] + from_ring(two, 1)
    one = sort_rows(order, one_parts)
    one_away = lax.ppermute(one, "c", SWAP)

    *seen, weights, bias, vec, b_in = attend_first(core, limits, x_own, x_oth, one, one_away, micro - 1)
    seen, two_parts = tie((seen, two_parts))
    two = sort_rows(order, two_parts)
    seen, two = tie((seen, two))
    two_away = lax.ppermute(two, "c", SWAP)
    mixed, mixed_oth, context, probs = attend_more(
        limits, x_own, x_oth, weights, bias, micro - 1, seen
    )
    sums, in_sums, ff_mine, ff_away, block_out, d_first, d_context = middle(
        core, vec, b_in, x_own, context, cotangent.reshape(rows, width), two, two_away
    )
    ff_recv = lax.ppermute(ff_away, "c", SWAP)
    inputs = (mixed, mixed_oth, probs, d_context, d_first, weights)
    *part, x_near = attend_back(*inputs)
    ff_recv, part = tie((ff_recv, part))
    ff_own, *ff_sent = split_rows(order, ff_mine, ff_recv)
    ff_sent, part = tie((ff_sent, part))
    ff_got = to_ring(ff_sent, 1)
    d_tokens, x_part, g_mine, g_away = attend_last(
        core, *inputs, part, x_own, x_oth, sums, in_sums
    )
    g_away, x_near = tie((g_away, x_near))
    x_near = lax.ppermute(x_near, "yh", SWAP)
    x_rest = x_part
    ff_got, g_away = tie((ff_got, g_away))
    g_recv = lax.ppermute(g_away, "c", SWAP)
    ff_own, *ff_sent = fold_rows(ff_own, ff_got)
    ff_got = to_ring(ff_sent, 0)
    g_recv, ff_sent = tie((g_recv, ff_sent))
    g_own, *g_sent = split_rows(order, g_mine, g_recv)
    g_sent, ff_got[0], x_near = tie((g_sent, ff_got[0], x_near))
    g_got = to_ring(g_sent, 1)
    x_rest = lax.ppermute(x_rest, "yh", SWAP)
    ff_parts = column_parts(ff_own, ff_got, BF)
    g_own, *g_sent = fold_rows(g_own, g_got)
    g_got = to_ring(g_sent, 0)
    o_in, o_back, o_out = finish_early(ff_parts)
    d_tokens = d_tokens + jnp.concatenate([x_near, x_rest], axis=0).astype(F32)
    g_got, o_in, o_back, o_out, d_tokens = tie((g_got, o_in, o_back, o_out, d_tokens))
    g_parts = column_parts(g_own, g_got)
    o_qkv, lines = finish_late(g_parts)
    return (
        block_out.reshape(tokens.shape),
        d_tokens.reshape(tokens.shape),
        o_qkv,
        lines[7],
        o_out,
        lines[0],
        o_in,
        lines[6],
        o_back,
        lines[1],
        lines[2],
        lines[3],
        lines[4],
        lines[5],
    )


def solution(mesh):
    fine = Mesh(mesh.devices.reshape(2, 4, 4, 2, 2), DEVICES)
    pairs = ("yl", "x", "z", "c")
    data = P(None, pairs, "yh", None)
    weight, vector = P(DEVICES, None), P(DEVICES)
    kinds = (weight, vector) * 4
    return jax.shard_map(
        on_device,
        mesh=fine,
        in_specs=(data, P(None, pairs), data) + kinds + (vector,) * 4,
        out_specs=(data, data) + kinds + (vector,) * 4,
        check_vma=False,
    )
```
